32 devices in a mesh: fsdp: 4 (over x, core), ctx: 8 (over z, y).
Axes of the slice: x: 2, y: 2, z: 4, core: 2. Of those that a mesh axis runs over, the one named last changes fastest.
Arguments:
- frames: bfloat16 [4, 4096, 1536], P('fsdp', 'ctx'), may hold values from -120 to 120
- lengths: int32 [4], P('fsdp'), may hold values from 1024 to 4096, as said below
- ln_gain: float32 [1536], replicated, may hold values from 0.1 to 1.9
- w_in: bfloat16 [1536, 1536], P('fsdp'), may hold values from -0.15625 to 0.15625
- dw_kernel: float32 [31, 768], replicated, may hold values from -1 to 1
- bn_gain: float32 [768], replicated, may hold values from 0.1 to 1.9
- bn_shift: float32 [768], replicated, may hold values from -3 to 3
- w_out: bfloat16 [768, 1536], P('fsdp'), may hold values from -0.21875 to 0.21875
Outputs:
- result: bfloat16 [4, 4096, 1536], P('fsdp', 'ctx')
The draws below stay inside these ranges and needn't reach their ends.
Inputs may be any that keep to these rules, and one draw needn't show every extreme that they name: frames 0 to lengths[r] - 1 of recording r are valid; one recording is full and one has exactly 1024 valid frames.
All inputs are finite; a program needn't handle non-finite values.
Results may differ from the reference program's by a relative error of at most 0.0076.
Values may be sent and summed in bfloat16 or wider, within the bound.
No kernel may reach another device: no remote copies, remote signals or barrier semaphores. Data moves between devices by JAX's collectives and lax.ppermute only.
A program may use at most 64 MiB of HBM per device.

```python
import math
import jax
import jax.numpy as jnp
from jax import lax

D = 1536
CH = 768
KERNEL = 31
HALF = 15
ROWS = 512
FRAMES = 4096
RECS = 4


def draw_lengths(key, part):
    first_key, second_key = jax.random.split(jax.random.fold_in(key, 11))
    drawn = jax.random.randint(first_key, (RECS,), FRAMES // 4, FRAMES + 1, dtype=jnp.int32)
    order = jax.random.permutation(second_key, RECS)
    drawn = jnp.where(order == 0, FRAMES, drawn)
    drawn = jnp.where(order == 1, FRAMES // 4, drawn)
    return drawn.astype(jnp.int32)


def draw_frames(key, part):
    noise_key, start_key, drift_key, scale_key = jax.random.split(jax.random.fold_in(key, 23), 4)
    lag_count = 12
    weights = [math.exp(-lag / 4.0) for lag in range(lag_count)]
    weight_norm = math.sqrt(sum((value * value for value in weights)))
    ramp = (jnp.arange(FRAMES, dtype=jnp.float32) / FRAMES)[None, :, None]
    block_count = FRAMES // ROWS
    white = jax.random.normal(noise_key, (RECS, FRAMES + lag_count - 1, D), jnp.float32)
    row_scale = 1.0
    level = 1.5
    noise = jnp.zeros((RECS, FRAMES, D), jnp.float32)
    for lag in range(lag_count):
        noise = noise + white[:, lag:lag + FRAMES] * (weights[lag] / weight_norm)
    block_start = jax.random.normal(start_key, (RECS, block_count, 1, D), jnp.float32) * level
    start = jnp.broadcast_to(block_start, (RECS, block_count, ROWS, D)).reshape(RECS, FRAMES, D)
    drift = jax.random.normal(drift_key, (RECS, 1, D), jnp.float32) * 0.7
    return jnp.clip((noise + start + drift * ramp) * row_scale, -120.0, 120.0).astype(jnp.bfloat16)


def levels(key, shape, shards, low, high):
    factor_of, own = 1.0, jax.random.fold_in(key, 6)
    for axis_at, parts in shards:
        steps = jnp.exp(jax.random.uniform(jax.random.fold_in(own, axis_at), (parts,), jnp.float32, low / len(shards), high / len(shards)))
        factor_of = factor_of * jnp.repeat(steps, shape[axis_at] // parts).reshape([-1 if axis == axis_at else 1 for axis in range(len(shape))])
    return factor_of


def scatter_about(rng, shape, deviation, bound, pieces=(), kind=jnp.bfloat16):
    entries = jax.random.normal(rng, shape, jnp.float32) * deviation
    if len(pieces) > 0:
        entries = levels(rng, shape, pieces, -0.22, 0.18) * entries
    return jnp.clip(entries, min=-bound, max=bound).astype(kind)


def setup_inputs(seed: int = 0) -> dict:
    keys = jax.random.split(jax.random.key(seed), 9)
    frames = draw_frames(jax.random.fold_in(keys[8], 71), 0)
    lengths = draw_lengths(jax.random.fold_in(keys[8], 71), 0)
    ln_gain = jnp.clip(1.0 + 0.18 * jax.random.normal(keys[2], (D,), jnp.float32), 0.1, 1.9)
    w_in = scatter_about(keys[3], (D, 2 * CH), D ** -0.5, 0.15625, ((0, 4),))
    dw_kernel = scatter_about(keys[4], (KERNEL, CH), KERNEL ** -0.5, 1.0, (), jnp.float32)
    bn_gain = jnp.clip(1.0 + 0.18 * jax.random.normal(keys[5], (CH,), jnp.float32), 0.1, 1.9)
    bn_shift = scatter_about(keys[6], (CH,), 0.5, 3.0, (), jnp.float32)
    w_out = scatter_about(keys[7], (CH, D), CH ** -0.5, 0.21875, ((0, 4),))
    return dict(frames=frames, lengths=lengths, ln_gain=ln_gain, w_in=w_in, dw_kernel=dw_kernel, bn_gain=bn_gain, bn_shift=bn_shift, w_out=w_out)


def normalize_rows(rows_in, ln_gain):
    values = rows_in.astype(jnp.float32)
    centre = lax.optimization_barrier(jnp.mean(values, axis=-1, keepdims=True))
    deviate = values - centre
    spread = lax.optimization_barrier(jnp.mean(deviate * deviate, axis=-1, keepdims=True))
    return (deviate * lax.rsqrt(spread + 1e-05) * ln_gain).astype(jnp.bfloat16)

def reference(frames, lengths, ln_gain, w_in, dw_kernel, bn_gain, bn_shift, w_out):
    position = jnp.arange(FRAMES, dtype=jnp.int32)

    def front_half(record_pair):
        record, length = record_pair
        normed = normalize_rows(record, ln_gain)
        projected = jnp.dot(normed, w_in, preferred_element_type=jnp.float32)
        valid_rows = (position < length)[:, None]
        gated = jnp.where(valid_rows, projected[:, :CH] * jax.nn.sigmoid(projected[:, CH:]), 0.0).astype(jnp.bfloat16)
        padded = jnp.pad(gated.astype(jnp.float32), ((HALF, HALF), (0, 0)))
        convolved = jnp.zeros((FRAMES, CH), jnp.float32)
        for tap_index in range(KERNEL):
            convolved = convolved + padded[tap_index:tap_index + FRAMES] * dw_kernel[tap_index]
        return convolved
    convolved = lax.map(front_half, (frames, lengths.astype(jnp.int32)))
    valid_mask = (position[None, :] < lengths[:, None]).astype(jnp.float32)[:, :, None]
    valid_count = jnp.sum(valid_mask)
    chan_mean = lax.optimization_barrier(jnp.sum(convolved * valid_mask, axis=(0, 1))) / valid_count
    centered = (convolved - chan_mean) * valid_mask
    chan_var = lax.optimization_barrier(jnp.sum(centered * centered, axis=(0, 1))) / valid_count

    def back_half(record_pair):
        conv_block, length = record_pair
        scaled = (conv_block - chan_mean) * lax.rsqrt(chan_var + 1e-05) * bn_gain + bn_shift
        activated = jax.nn.silu(scaled).astype(jnp.bfloat16)
        result_rows = jnp.dot(activated, w_out, preferred_element_type=jnp.float32)
        valid_rows = (position < length)[:, None]
        return jnp.where(valid_rows, result_rows, 0.0).astype(jnp.bfloat16)
    return lax.map(back_half, (convolved, lengths.astype(jnp.int32)))
```

```python
import jax
import jax.numpy as jnp
from jax import lax
from jax.sharding import PartitionSpec as P


def normalize_rows(rows_in, ln_gain):
    values = rows_in.astype(jnp.float32)
    centre = jnp.mean(values, axis=-1, keepdims=True)
    deviate = values - centre
    spread = jnp.mean(deviate * deviate, axis=-1, keepdims=True)
    return (deviate * lax.rsqrt(spread + 1e-05) * ln_gain).astype(jnp.bfloat16)


def radices(count):
    found = []
    factor = 2
    while count > 1:
        while count % factor == 0:
            found.append(factor)
            count //= factor
        factor += 1
    return found


def merge(first, second):
    count = first[2] + second[2]
    share = second[2] / jnp.maximum(count, 1.0)
    delta = second[0] - first[0]
    mean = first[0] + delta * share
    square = first[1] + second[1] + delta * delta * (first[2] * share)
    return jnp.stack([mean, square, count])


def merge_over(stats, axis):
    count = lax.axis_size(axis)
    stride = 1
    for radix in radices(count):
        got = []
        for step in range(1, radix):
            perm = []
            for i in range(count):
                digit = (i // stride) % radix
                perm.append((i, i + ((digit + step) % radix - digit) * stride))
            got.append(lax.ppermute(stats, axis, perm))
        for other in got:
            stats = merge(stats, other)
        stride *= radix
    return stats


def gather_all(shard):
    parts = lax.axis_size("ctx")
    rows = shard.shape[0] // parts
    piece = lax.dynamic_slice_in_dim(shard, lax.axis_index("ctx") * rows, rows, axis=0)
    return lax.all_gather(piece, ("fsdp", "ctx"), axis=0, tiled=True)


def body(frames, lengths, ln_gain, w_in, dw_kernel, bn_gain, bn_shift, w_out):
    _, row_count, model_width = frames.shape
    kernel_taps, channels = dw_kernel.shape
    halo = 16
    reach = (kernel_taps - 1) // 2
    rows = frames[0]
    ends = lax.axis_size("ctx") - 1
    before = lax.ppermute(rows[-halo:], "ctx", [(i, i + 1) for i in range(ends)])
    after = lax.ppermute(rows[:halo], "ctx", [(i + 1, i) for i in range(ends)])
    full_in = gather_all(w_in)
    full_out = lax.all_gather(w_out, "fsdp", axis=0, tiled=True)
    extended = jnp.concatenate([before, rows, after], axis=0)
    normed = normalize_rows(extended, ln_gain)
    start = lax.axis_index("ctx") * row_count
    position = start - halo + jnp.arange(row_count + 2 * halo, dtype=jnp.int32)
    length = lengths[0]
    valid = ((position >= 0) & (position < length))[:, None]
    projected = jnp.dot(normed, full_in, preferred_element_type=jnp.float32)
    gated = jnp.where(valid, projected[:, :channels] * jax.nn.sigmoid(projected[:, channels:]), 0.0)
    padded = gated.astype(jnp.bfloat16).astype(jnp.float32)
    convolved = jnp.zeros((row_count, channels), jnp.float32)
    first = halo - reach
    for tap in range(kernel_taps):
        convolved = convolved + padded[first + tap : first + tap + row_count] * dw_kernel[tap]
    mask = valid[halo : halo + row_count].astype(jnp.float32)
    local_count = jnp.clip(length - start, 0, row_count).astype(jnp.float32)
    local_mean = jnp.sum(convolved * mask, axis=0) / jnp.maximum(local_count, 1.0)
    centered = (convolved - local_mean) * mask
    local_square = jnp.sum(centered * centered, axis=0)
    stats = jnp.stack([local_mean, local_square, jnp.full((channels,), local_count)])
    stats = merge_over(stats, "fsdp")
    stats = merge_over(stats, "ctx")
    chan_mean = stats[0]
    chan_var = stats[1] / stats[2]
    scaled = (convolved - chan_mean) * lax.rsqrt(chan_var + 1e-05) * bn_gain + bn_shift
    activated = jax.nn.silu(scaled).astype(jnp.bfloat16)
    result = jnp.dot(activated, full_out, preferred_element_type=jnp.float32)
    result = jnp.where(mask > 0, result, 0.0).astype(jnp.bfloat16)
    return result[None]


def solution(mesh):
    return jax.shard_map(
        body,
        mesh=mesh,
        in_specs=(
            P("fsdp", "ctx", None),
            P("fsdp"),
            P(),
            P("fsdp", None),
            P(),
            P(),
            P(),
            P("fsdp", None),
        ),
        out_specs=P("fsdp", "ctx", None),
        check_vma=False,
    )
```

```python
import functools

import jax
import jax.numpy as jnp
from jax import lax
from jax.experimental import pallas as pl
from jax.experimental.pallas import tpu as pltpu
from jax.sharding import PartitionSpec as P

HALO = 16
LANES = 128
MIB = 1024 * 1024
VMEM = pltpu.VMEM


def params(mib):
    return pltpu.CompilerParams(vmem_limit_bytes=mib * MIB)


def radices(count):
    found = []
    factor = 2
    while count > 1:
        while count % factor == 0:
            found.append(factor)
            count //= factor
        factor += 1
    return found


def merge(first, second):
    count = first[2] + second[2]
    share = second[2] / jnp.maximum(count, 1.0)
    delta = second[0] - first[0]
    mean = first[0] + delta * share
    square = first[1] + second[1] + delta * delta * (first[2] * share)
    return jnp.stack([mean, square, count])


def merge_over(stats, axis):
    count = lax.axis_size(axis)
    stride = 1
    for radix in radices(count):
        got = []
        for step in range(1, radix):
            perm = []
            for i in range(count):
                digit = (i // stride) % radix
                perm.append((i, i + ((digit + step) % radix - digit) * stride))
            got.append(lax.ppermute(stats, axis, perm))
        for other in got:
            stats = merge(stats, other)
        stride *= radix
    return stats


def swap(value, axis, bit):
    return lax.ppermute(value, axis, [(i, i ^ bit) for i in range(lax.axis_size(axis))])


def norm_kernel(before_ref, rows_ref, after_ref, gain_ref, out_ref):
    gain = gain_ref[...]

    def normalize(values):
        values = values.astype(jnp.float32)
        centre = jnp.mean(values, axis=-1, keepdims=True)
        deviate = values - centre
        spread = jnp.mean(deviate * deviate, axis=-1, keepdims=True)
        return (deviate * lax.rsqrt(spread + 1e-05) * gain).astype(jnp.bfloat16)

    row_count = rows_ref.shape[0]
    out_ref[0:HALO, :] = normalize(before_ref[...])
    out_ref[HALO + row_count :, :] = normalize(after_ref[...])
    step = 32

    @pl.loop(0, row_count // step)
    def _(i):
        at = pl.multiple_of(i * step, step)
        out_ref[pl.ds(HALO + at, step), :] = normalize(rows_ref[pl.ds(at, step), :])


def normalize_rows(before, rows, after, ln_gain):
    row_count, width = rows.shape
    return pl.pallas_call(
        norm_kernel,
        out_shape=jax.ShapeDtypeStruct((row_count + 2 * HALO, width), jnp.bfloat16),
        in_specs=[pl.BlockSpec(memory_space=VMEM)] * 4,
        out_specs=pl.BlockSpec(memory_space=VMEM),
        compiler_params=params(12),
        cost_estimate=pl.CostEstimate(
            flops=10 * row_count * width, bytes_accessed=4 * row_count * width, transcendentals=0
        ),
        name="layer_norm",
    )(before, rows, after, ln_gain.reshape(1, width))


def front_kernel(taps, place_ref, normed_ref, *refs):
    *weight_refs, taps_ref, conv_ref, stats_ref, weights, gated = refs
    ext_rows = normed_ref.shape[0]
    row_count, wide = conv_ref.shape
    if len(weight_refs) > 2:
        own = place_ref[0]
        depth = weights.shape[0] // 4
        for i in range(4):
            at = pl.multiple_of(lax.bitwise_xor(own, i) * depth, depth)
            value_ref, gate_ref = weight_refs[2 * i : 2 * i + 2]
            weights[pl.ds(at, depth), 0:wide] = value_ref[...]
            weights[pl.ds(at, depth), wide : 2 * wide] = gate_ref[...]
        value_weights, gate_weights = weights[:, 0:wide], weights[:, wide : 2 * wide]
    else:
        value_weights, gate_weights = weight_refs[0][...], weight_refs[1][...]
    start, length = place_ref[1], place_ref[2]
    normed = normed_ref[...]
    value = jnp.dot(normed, value_weights, preferred_element_type=jnp.float32)
    gate = jnp.dot(normed, gate_weights, preferred_element_type=jnp.float32)
    position = start - HALO + lax.broadcasted_iota(jnp.int32, (ext_rows, 1), 0)
    valid = (position >= 0) & (position < length)
    kept = jnp.where(valid, value * jax.nn.sigmoid(gate), 0.0)
    kept = kept.astype(jnp.bfloat16).astype(jnp.float32)
    units = wide // LANES
    for unit in range(units):
        gated[unit] = kept[:, unit * LANES : (unit + 1) * LANES]
    first = HALO - (taps - 1) // 2
    step = 64
    for unit in range(units):
        lanes = slice(unit * LANES, (unit + 1) * LANES)
        total = jnp.zeros((8, LANES), jnp.float32)
        for at in range(0, row_count, step):
            acc = jnp.zeros((step, LANES), jnp.float32)
            for tap in range(taps):
                acc = acc + gated[unit, at + first + tap : at + first + tap + step, :] * taps_ref[tap : tap + 1, lanes]
            conv_ref[at : at + step, lanes] = acc
    here = start + lax.broadcasted_iota(jnp.int32, (row_count, 1), 0) < length
    count = jnp.clip(length - start, 0, row_count).astype(jnp.float32)
    conv = conv_ref[...]
    mean = jnp.sum(jnp.where(here, conv, 0.0), axis=0, keepdims=True) / jnp.maximum(count, 1.0)
    deviate = jnp.where(here, conv - mean, 0.0)
    square = jnp.sum(deviate * deviate, axis=0, keepdims=True)
    stats_ref[0:1, :] = mean
    stats_ref[1:2, :] = square
    stats_ref[2:3, :] = jnp.full((1, wide), count)


def front_block(block, wide, place, normed, pieces, dw_kernel):
    ext_rows, width = normed.shape
    row_count = ext_rows - 2 * HALO
    taps = dw_kernel.shape[0]
    whole = lambda shape: pl.BlockSpec(shape, lambda i: (0, 0))
    specs = [pl.BlockSpec(memory_space=pltpu.SMEM), whole((ext_rows, width))]
    arrays = [place, normed]
    for array, column in pieces:
        specs.append(pl.BlockSpec((array.shape[0], wide), functools.partial(lambda c, i: (0, c), column)))
        arrays.append(array)
    specs.append(pl.BlockSpec((taps, wide), lambda i: (0, block)))
    arrays.append(dw_kernel)
    return pl.pallas_call(
        functools.partial(front_kernel, taps),
        grid=(1,),
        out_shape=(
            jax.ShapeDtypeStruct((row_count, wide), jnp.float32),
            jax.ShapeDtypeStruct((3, wide), jnp.float32),
        ),
        in_specs=specs,
        out_specs=(whole((row_count, wide)), whole((3, wide))),
        scratch_shapes=[
            VMEM((width, 2 * wide), jnp.bfloat16),
            VMEM((wide // LANES, ext_rows, LANES), jnp.float32),
        ],
        compiler_params=params(24),
        cost_estimate=pl.CostEstimate(
            flops=4 * ext_rows * width * wide,
            bytes_accessed=2 * ext_rows * width + 4 * width * wide + 4 * row_count * wide,
            transcendentals=0,
        ),
        name="front",
    )(*arrays)


def back_kernel(place_ref, mean_ref, scale_ref, shift_ref, *refs):
    *conv_refs, weights_ref, out_ref = refs
    rows = out_ref.shape[0]
    wide = conv_refs[0].shape[1]
    parts = []
    for i, conv_ref in enumerate(conv_refs):
        lanes = slice(i * wide, (i + 1) * wide)
        scaled = (conv_ref[...] - mean_ref[:, lanes]) * scale_ref[:, lanes] + shift_ref[:, lanes]
        parts.append((scaled * jax.nn.sigmoid(scaled)).astype(jnp.bfloat16))
    activated = jnp.concatenate(parts, axis=1)
    result = jnp.dot(activated, weights_ref[...], preferred_element_type=jnp.float32)
    start = place_ref[1] + pl.program_id(0) * rows
    here = start + lax.broadcasted_iota(jnp.int32, (rows, 1), 0) < place_ref[2]
    out_ref[...] = jnp.where(here, result, 0.0).astype(jnp.bfloat16)


def back(place, mean, scale, shift, convs, weights):
    row_count, wide = convs[0].shape
    channels, width = weights.shape
    rows = row_count // 4
    vector = pl.BlockSpec((1, channels), lambda i: (0, 0))
    return pl.pallas_call(
        back_kernel,
        grid=(row_count // rows,),
        out_shape=jax.ShapeDtypeStruct((row_count, width), jnp.bfloat16),
        in_specs=[pl.BlockSpec(memory_space=pltpu.SMEM)]
        + [vector] * 3
        + [pl.BlockSpec((rows, wide), lambda i: (i, 0))] * len(convs)
        + [pl.BlockSpec((channels, width), lambda i: (0, 0))],
        out_specs=pl.BlockSpec((rows, width), lambda i: (i, 0)),
        compiler_params=params(16),
        cost_estimate=pl.CostEstimate(
            flops=2 * row_count * width * channels,
            bytes_accessed=4 * row_count * channels + 2 * channels * width + 2 * row_count * width,
            transcendentals=0,
        ),
        name="back",
    )(place, mean, scale, shift, *convs, weights)


def ordered(even, mine, theirs):
    return jnp.where(even, jnp.concatenate([mine, theirs], 1), jnp.concatenate([theirs, mine], 1))


def body(frames, lengths, ln_gain, w_in, dw_kernel, bn_gain, bn_shift, w_out):
    _, row_count, model_width = frames.shape
    channels = dw_kernel.shape[1]
    wide = channels // 3
    ctx, fsdp = lax.axis_index("ctx"), lax.axis_index("fsdp")
    direct = lax.axis_size("fsdp") == 4 and lax.axis_size("ctx") % 2 == 0
    rows = frames[0]
    if direct:
        even = lax.rem(ctx, 2) == 0
        side = lax.rem(ctx, 2) * channels
        over_x = []
        for block in range(3):
            if block < 2:
                part = lax.dynamic_slice_in_dim(w_in, side + block * wide, wide, axis=1)
            else:
                part = jnp.concatenate(
                    [w_in[:, block * wide : channels], w_in[:, channels + block * wide :]], 1
                )
            over_x.append(swap(part, "fsdp", 2))
        across = swap(w_in, "fsdp", 1)
    else:
        full_in = lax.all_gather(w_in, "fsdp", axis=0, tiled=True)
        full_out = lax.all_gather(w_out, "fsdp", axis=0, tiled=True)
    ends = lax.axis_size("ctx") - 1
    before = lax.ppermute(rows[-HALO:], "ctx", [(i, i + 1) for i in range(ends)])
    after = lax.ppermute(rows[:HALO], "ctx", [(i + 1, i) for i in range(ends)])
    normed = normalize_rows(before, rows, after, ln_gain)
    start = ctx * row_count
    place = jnp.stack([fsdp, start, lengths[0]]).astype(jnp.int32)
    convs, stats = [], []
    for block in range(3):
        if direct:
            if block < 2:
                remote = ordered(even, over_x[block], swap(over_x[block], "ctx", 1))
            else:
                remote = over_x[block]
            beyond = swap(remote, "fsdp", 1)
            pieces = []
            for shard in (w_in, across):
                pieces += [(shard, block), (shard, 3 + block)]
            for shard in (remote, beyond):
                pieces += [(shard, 0), (shard, 1)]
        else:
            pieces = [(full_in, block), (full_in, 3 + block)]
        conv, stat = front_block(block, wide, place, normed, pieces, dw_kernel)
        convs.append(conv)
        stats.append(stat)
    if direct:
        half = model_width // 2
        w_out, over_x = lax.optimization_barrier((w_out, over_x[2]))
        mine = swap(
            lax.dynamic_slice_in_dim(w_out, lax.rem(ctx, 2) * half, half, axis=1), "fsdp", 2
        )
        across = swap(w_out, "fsdp", 1)
        remote = ordered(even, mine, swap(mine, "ctx", 1))
        beyond = swap(remote, "fsdp", 1)
        depth = w_out.shape[0]
        full_out = jnp.zeros((channels, model_width), w_out.dtype)
        for i, shard in enumerate((w_out, across, remote, beyond)):
            full_out = lax.dynamic_update_slice_in_dim(
                full_out, shard, lax.bitwise_xor(fsdp, i) * depth, axis=0
            )
    stats = jnp.concatenate(stats, axis=1)
    stats = merge_over(stats, "fsdp")
    stats = merge_over(stats, "ctx")
    mean = stats[0:1]
    scale = lax.rsqrt(stats[1:2] / stats[2:3] + 1e-05) * bn_gain
    result = back(place, mean, scale, bn_shift[None], convs, full_out)
    return result[None]


def solution(mesh):
    return jax.shard_map(
        body,
        mesh=mesh,
        in_specs=(
            P("fsdp", "ctx", None),
            P("fsdp"),
            P(),
            P("fsdp", None),
            P(),
            P(),
            P(),
            P("fsdp", None),
        ),
        out_specs=P("fsdp", "ctx", None),
        check_vma=False,
    )
```

```python
import functools

import jax
import jax.numpy as jnp
from jax import lax
from jax.experimental import pallas as pl
from jax.experimental.pallas import tpu as pltpu
from jax.sharding import PartitionSpec as P

HALO = 16
LANES = 128
MIB = 1024 * 1024
VMEM = pltpu.VMEM


def cost(flops):
    return pl.CostEstimate(flops=flops, bytes_accessed=0, transcendentals=0)


def params(mib):
    return pltpu.CompilerParams(vmem_limit_bytes=mib * MIB)


def swap(value, axis, bit):
    return lax.ppermute(value, axis, [(i, i ^ bit) for i in range(lax.axis_size(axis))])


def normalize(values, gain):
    values = values.astype(jnp.float32)
    centre = jnp.mean(values, axis=-1, keepdims=True)
    deviate = values - centre
    spread = jnp.mean(deviate * deviate, axis=-1, keepdims=True)
    return (deviate * lax.rsqrt(spread + 1e-05) * gain).astype(jnp.bfloat16)


def norm_kernel(rows_ref, gain_ref, out_ref):
    step = 64

    @pl.loop(0, rows_ref.shape[0] // step)
    def _(i):
        here = pl.ds(pl.multiple_of(i * step, step), step)
        out_ref[here, :] = normalize(rows_ref[here, :], gain_ref[...])


def normalize_rows(rows, gain):
    row_count, width = rows.shape
    return pl.pallas_call(
        norm_kernel,
        out_shape=jax.ShapeDtypeStruct((row_count, width), jnp.bfloat16),
        in_specs=[pl.BlockSpec(memory_space=VMEM)] * 2,
        out_specs=pl.BlockSpec(memory_space=VMEM),
        compiler_params=params(8),
        cost_estimate=cost(10**9),
        name="layer_norm",
    )(rows, gain)


def near_kernel(place_ref, before_ref, rows_ref, after_ref, gain_ref, *refs):
    *weight_refs, ext_ref, first_ref, second_ref, third_ref, weights = refs
    row_count = rows_ref.shape[0]
    gain = gain_ref[...]
    ext_ref[0:HALO, :] = normalize(before_ref[...], gain)
    ext_ref[HALO : HALO + row_count, :] = rows_ref[...]
    ext_ref[HALO + row_count :, :] = normalize(after_ref[...], gain)
    if not weight_refs:
        return
    own = place_ref[0]
    depth, width = weight_refs[0].shape
    for i, weight_ref in enumerate(weight_refs):
        at = pl.multiple_of(lax.bitwise_xor(own % 2, i) * depth, depth)
        weights[pl.ds(at, depth), :] = weight_ref[...]
    near = pl.ds(pl.multiple_of(own // 2 * (2 * depth), 2 * depth), 2 * depth)
    wide = first_ref.shape[1] // 2
    channels = width // 2
    for block, out_ref in enumerate((first_ref, second_ref, third_ref)):
        for i in range(2):
            columns = slice(i * channels + block * wide, i * channels + (block + 1) * wide)
            out_ref[:, i * wide : (i + 1) * wide] = jnp.dot(
                ext_ref[:, near], weights[:, columns], preferred_element_type=jnp.float32
            )


def near_product(place, before, rows, after, gain, shards):
    row_count, width = rows.shape
    ext_rows = row_count + 2 * HALO
    partial = jax.ShapeDtypeStruct((ext_rows, width // 3), jnp.float32)
    depth = 2 * shards[0].shape[0] if shards else 16
    return pl.pallas_call(
        near_kernel,
        out_shape=(jax.ShapeDtypeStruct((ext_rows, width), jnp.bfloat16), partial, partial, partial),
        in_specs=[pl.BlockSpec(memory_space=pltpu.SMEM)]
        + [pl.BlockSpec(memory_space=VMEM)] * (4 + len(shards)),
        out_specs=[pl.BlockSpec(memory_space=VMEM)] * 4,
        scratch_shapes=[VMEM((depth, width), jnp.bfloat16)],
        compiler_params=params(12),
        cost_estimate=cost(10**9),
        name="near",
    )(place, before, rows, after, gain, *shards)


def front_kernel(block, place_ref, normed_ref, *refs):
    *weight_refs, taps_ref, conv_ref, stats_ref, weights, gated = refs
    ext_rows = normed_ref.shape[0]
    row_count, wide = conv_ref.shape
    taps, channels = taps_ref.shape
    if len(weight_refs) == 3:
        near_ref, *far_refs = weight_refs
        own = place_ref[0]
        depth = far_refs[0].shape[0]
        for i, far_ref in enumerate(far_refs):
            at = pl.multiple_of(lax.bitwise_xor(own % 2, i) * depth, depth)
            weights[pl.ds(at, depth), :] = far_ref[...]
        far = pl.ds(pl.multiple_of((1 - own // 2) * (2 * depth), 2 * depth), 2 * depth)
        normed = normed_ref[:, far]
        value = near_ref[:, 0:wide] + jnp.dot(normed, weights[:, 0:wide], preferred_element_type=jnp.float32)
        gate = near_ref[:, wide:] + jnp.dot(normed, weights[:, wide:], preferred_element_type=jnp.float32)
    else:
        columns = slice(block * wide, (block + 1) * wide)
        value = jnp.dot(normed_ref[...], weight_refs[0][:, columns], preferred_element_type=jnp.float32)
        columns = slice(channels + block * wide, channels + (block + 1) * wide)
        gate = jnp.dot(normed_ref[...], weight_refs[0][:, columns], preferred_element_type=jnp.float32)
    start, length = place_ref[1], place_ref[2]
    position = start - HALO + lax.broadcasted_iota(jnp.int32, (ext_rows, 1), 0)
    valid = (position >= 0) & (position < length)
    kept = jnp.where(valid, value * jax.nn.sigmoid(gate), 0.0)
    kept = kept.astype(jnp.bfloat16).astype(jnp.float32)
    units = wide // LANES
    for unit in range(units):
        gated[unit] = kept[:, unit * LANES : (unit + 1) * LANES]
    first = HALO - (taps - 1) // 2
    step = 64
    for unit in range(units):
        lanes = slice(unit * LANES, (unit + 1) * LANES)
        tap_lanes = slice(block * wide + unit * LANES, block * wide + (unit + 1) * LANES)
        for at in range(0, row_count, step):
            acc = jnp.zeros((step, LANES), jnp.float32)
            for tap in range(taps):
                shifted = gated[unit, at + first + tap : at + first + tap + step, :]
                acc = acc + shifted * taps_ref[tap : tap + 1, tap_lanes]
            conv_ref[at : at + step, lanes] = acc
    here = start + lax.broadcasted_iota(jnp.int32, (row_count, 1), 0) < length
    count = jnp.clip(length - start, 0, row_count).astype(jnp.float32)
    conv = conv_ref[...]
    mean = jnp.sum(jnp.where(here, conv, 0.0), axis=0, keepdims=True) / jnp.maximum(count, 1.0)
    deviate = jnp.where(here, conv - mean, 0.0)
    square = jnp.sum(deviate * deviate, axis=0, keepdims=True)
    stats_ref[0:1, :] = mean
    stats_ref[1:2, :] = square
    stats_ref[2:3, :] = jnp.full((1, wide), count)


def front_block(block, wide, place, normed, weights, dw_kernel):
    ext_rows, width = normed.shape
    row_count = ext_rows - 2 * HALO
    depth = 2 * weights[1].shape[0] if len(weights) == 3 else 16
    return pl.pallas_call(
        functools.partial(front_kernel, block),
        out_shape=(
            jax.ShapeDtypeStruct((row_count, wide), jnp.float32),
            jax.ShapeDtypeStruct((3, wide), jnp.float32),
        ),
        in_specs=[pl.BlockSpec(memory_space=pltpu.SMEM)]
        + [pl.BlockSpec(memory_space=VMEM)] * (2 + len(weights)),
        out_specs=[pl.BlockSpec(memory_space=VMEM)] * 2,
        scratch_shapes=[
            VMEM((depth, 2 * wide), jnp.bfloat16),
            VMEM((wide // LANES, ext_rows, LANES), jnp.float32),
        ],
        compiler_params=params(12),
        cost_estimate=cost(4 * 10**9),
        name="front",
    )(place, normed, *weights, dw_kernel)


def back_kernel(place_ref, stats_ref, gain_ref, shift_ref, *refs):
    *conv_refs, out_ref, rows_out, sems, weights = refs
    convs, weight_refs = conv_refs[:3], conv_refs[3:]
    row_count, wide = convs[0].shape
    if len(weight_refs) == 4:
        depth = weight_refs[0].shape[0]
        for i, weight_ref in enumerate(weight_refs):
            at = pl.multiple_of(lax.bitwise_xor(place_ref[0], i) * depth, depth)
            weights[pl.ds(at, depth), :] = weight_ref[...]
    else:
        weights[...] = weight_refs[0][...]
    means, squares, counts = stats_ref[:, 0, :], stats_ref[:, 1, :], stats_ref[:, 2, :]
    count = jnp.sum(counts, axis=0, keepdims=True)
    mean = jnp.sum(counts * means, axis=0, keepdims=True) / count
    between = means - mean
    square = jnp.sum(squares + counts * between * between, axis=0, keepdims=True)
    scale = lax.rsqrt(square / count + 1e-05) * gain_ref[...]
    shift = shift_ref[...]
    pieces = rows_out.shape[0]
    rows = row_count // pieces
    copies = []
    for piece in range(pieces):
        parts = []
        for i, conv_ref in enumerate(convs):
            lanes = slice(i * wide, (i + 1) * wide)
            conv = conv_ref[piece * rows : (piece + 1) * rows, :]
            scaled = (conv - mean[:, lanes]) * scale[:, lanes] + shift[:, lanes]
            parts.append((scaled * jax.nn.sigmoid(scaled)).astype(jnp.bfloat16))
        activated = jnp.concatenate(parts, axis=1)
        result = jnp.dot(activated, weights[...], preferred_element_type=jnp.float32)
        position = place_ref[1] + piece * rows + lax.broadcasted_iota(jnp.int32, (rows, 1), 0)
        rows_out[piece] = jnp.where(position < place_ref[2], result, 0.0).astype(jnp.bfloat16)
        copy = pltpu.make_async_copy(
            rows_out.at[piece], out_ref.at[piece * rows : (piece + 1) * rows], sems.at[piece]
        )
        copy.start()
        copies.append(copy)
    for copy in copies:
        copy.wait()


def back(place, stats, gain, shift, convs, weights):
    row_count = convs[0].shape[0]
    channels, width = gain.shape[1], weights[0].shape[1]
    pieces = 4
    return pl.pallas_call(
        back_kernel,
        out_shape=jax.ShapeDtypeStruct((row_count, width), jnp.bfloat16),
        in_specs=[pl.BlockSpec(memory_space=pltpu.SMEM)]
        + [pl.BlockSpec(memory_space=VMEM)] * (3 + len(convs) + len(weights)),
        out_specs=pl.BlockSpec(memory_space=pl.ANY),
        scratch_shapes=[
            VMEM((pieces, row_count // pieces, width), jnp.bfloat16),
            pltpu.SemaphoreType.DMA((pieces,)),
            VMEM((channels, width), jnp.bfloat16),
        ],
        compiler_params=params(12),
        cost_estimate=cost(10**9),
        name="back",
    )(place, stats, gain, shift, *convs, *weights)


def ordered(even, mine, theirs):
    return jnp.where(even, jnp.concatenate([mine, theirs], 1), jnp.concatenate([theirs, mine], 1))


def combine(first, second):
    count = first[2] + second[2]
    share = second[2] / jnp.maximum(count, 1.0)
    delta = second[0] - first[0]
    mean = first[0] + delta * share
    square = first[1] + second[1] + delta * delta * (first[2] * share)
    return jnp.stack([mean, square, count])


def everyones(stats, axis, groups=None):
    count = len(groups[0]) if groups else lax.axis_size(axis)
    copies = jnp.broadcast_to(stats[None], (count,) + stats.shape)
    return lax.all_to_all(copies, axis, 0, 0, axis_index_groups=groups, tiled=True)


def merged(stats):
    means, squares, counts = stats[:, 0], stats[:, 1], stats[:, 2]
    count = jnp.sum(counts, 0)
    mean = jnp.sum(counts * means, 0) / jnp.maximum(count, 1.0)
    square = jnp.sum(squares + counts * (means - mean) ** 2, 0)
    return jnp.stack([mean, square, count])


def body(frames, lengths, ln_gain, w_in, dw_kernel, bn_gain, bn_shift, w_out):
    _, row_count, model_width = frames.shape
    channels = dw_kernel.shape[1]
    wide = channels // 3
    ctx, fsdp = lax.axis_index("ctx"), lax.axis_index("fsdp")
    ctx_count, fsdp_count = lax.axis_size("ctx"), lax.axis_size("fsdp")
    direct = fsdp_count == 4 and ctx_count % 2 == 0
    rows = frames[0]
    gain = ln_gain[None]
    start = ctx * row_count
    place = jnp.stack([fsdp, start, lengths[0]]).astype(jnp.int32)
    head, tail = rows[:HALO], rows[-HALO:]
    over_x, shards = [], []
    if direct:
        even = lax.rem(ctx, 2) == 0
        side = lax.rem(ctx, 2) * channels
        parts = [lax.dynamic_slice_in_dim(w_in, side + i * wide, wide, axis=1) for i in range(2)]
        parts.append(
            jnp.concatenate([w_in[:, 2 * wide : channels], w_in[:, channels + 2 * wide :]], 1)
        )
        parts, head, tail, rows = lax.optimization_barrier((parts, head, tail, rows))
        over_x = [swap(part, "fsdp", 2) for part in parts]
        shards = [w_in, swap(w_in, "fsdp", 1)]
        across_out = swap(w_out, "fsdp", 1)
    else:
        full_in = lax.all_gather(w_in, "fsdp", axis=0, tiled=True)
        out_weights = [lax.all_gather(w_out, "fsdp", axis=0, tiled=True)]
    ends = ctx_count - 1
    before = lax.ppermute(tail, "ctx", [(i, i + 1) for i in range(ends)])
    after = lax.ppermute(head, "ctx", [(i + 1, i) for i in range(ends)])
    if direct:
        rows, before, after, over_x[0] = lax.optimization_barrier((rows, before, after, over_x[0]))
    normed = normalize_rows(rows, gain)
    if direct:
        over_y = [swap(over_x[0], "ctx", 1)]
        normed, over_x[1], over_y[0] = lax.optimization_barrier((normed, over_x[1], over_y[0]))
        over_y.append(swap(over_x[1], "ctx", 1))
        normed, across_out = lax.optimization_barrier((normed, across_out))
    normed, *partials = near_product(place, before, normed, after, gain, shards)
    convs, stats = [], []
    for block in range(3):
        if direct:
            if block < 2:
                remote = ordered(even, over_x[block], over_y[block])
            else:
                remote = over_x[2]
            weights = [partials[block], remote, swap(remote, "fsdp", 1)]
        else:
            weights = [full_in]
        conv, stat = front_block(block, wide, place, normed, weights, dw_kernel)
        if direct and block == 0:
            conv, over_y[1], over_x[2] = lax.optimization_barrier((conv, over_y[1], over_x[2]))
        convs.append(conv)
        stats.append(stat)
    if direct:
        _, later = lax.optimization_barrier((over_x[1], w_out))
        out_weights = [w_out, across_out, swap(later, "fsdp", 2)]
    stats = jnp.concatenate(stats, axis=1)
    if direct:
        stats = combine(stats, swap(stats, "fsdp", 1))
        stats, out_weights[2] = lax.optimization_barrier((stats, out_weights[2]))
        out_weights.append(swap(out_weights[2], "fsdp", 1))
        groups = [
            [f * ctx_count + p for f in range(core, fsdp_count, 2) for p in range(ctx_count)]
            for core in range(2)
        ]
        stats = everyones(stats, ("fsdp", "ctx"), groups)
    else:
        stats = everyones(merged(everyones(stats, "ctx")), "fsdp")
    result = back(place, stats, bn_gain[None], bn_shift[None], convs, out_weights)
    return result[None]


def solution(mesh):
    return jax.shard_map(
        body,
        mesh=mesh,
        in_specs=(
            P("fsdp", "ctx", None),
            P("fsdp"),
            P(),
            P("fsdp", None),
            P(),
            P(),
            P(),
            P("fsdp", None),
        ),
        out_specs=P("fsdp", "ctx", None),
        check_vma=False,
    )
```

```python
import functools

import jax
import jax.numpy as jnp
from jax import lax
from jax.experimental import pallas as pl
from jax.experimental.pallas import tpu as pltpu
from jax.sharding import PartitionSpec as P

HALO = 16
LANES = 128
MIB = 1024 * 1024
VMEM = pltpu.VMEM


def cost(flops):
    return pl.CostEstimate(flops=flops, bytes_accessed=0, transcendentals=0)


def params(mib):
    return pltpu.CompilerParams(vmem_limit_bytes=mib * MIB)


def swap(value, axis, bit):
    return lax.ppermute(value, axis, [(i, i ^ bit) for i in range(lax.axis_size(axis))])


def cut_kernel(parity_ref, shard_ref, rows_ref, *refs):
    first_ref, second_ref, third_ref, head_ref, tail_ref, sems = refs
    wide = first_ref.shape[1]
    channels = shard_ref.shape[1] // 2
    row_count = rows_ref.shape[0]
    copies = []

    def copy(source, target):
        copies.append(pltpu.make_async_copy(source, target, sems.at[len(copies)]))
        copies[-1].start()

    side = parity_ref[0] * channels
    for block, ref in enumerate((first_ref, second_ref)):
        copy(shard_ref.at[:, pl.ds(pl.multiple_of(side + block * wide, wide), wide)], ref)
    for i in range(2):
        at = i * channels + 2 * wide
        copy(shard_ref.at[:, at : at + wide], third_ref.at[:, i * wide : (i + 1) * wide])
    copy(rows_ref.at[0:HALO, :], head_ref)
    copy(rows_ref.at[row_count - HALO : row_count, :], tail_ref)
    for started in copies:
        started.wait()


def cut(parity, shard, rows, wide):
    depth, width = shard.shape
    shapes = [(depth, wide), (depth, wide), (depth, 2 * wide), (HALO, width), (HALO, width)]
    return pl.pallas_call(
        cut_kernel,
        out_shape=[jax.ShapeDtypeStruct(shape, jnp.bfloat16) for shape in shapes],
        in_specs=[
            pl.BlockSpec(memory_space=pltpu.SMEM),
            pl.BlockSpec(memory_space=pltpu.HBM),
            pl.BlockSpec(memory_space=pltpu.HBM),
        ],
        out_specs=[pl.BlockSpec(memory_space=VMEM)] * 5,
        scratch_shapes=[pltpu.SemaphoreType.DMA((6,))],
        compiler_params=params(56),
        cost_estimate=cost(10**8),
        name="cut",
    )(parity, shard, rows)


def normalize(values, gain):
    values = values.astype(jnp.float32)
    centre = jnp.mean(values, axis=-1, keepdims=True)
    deviate = values - centre
    spread = jnp.mean(deviate * deviate, axis=-1, keepdims=True)
    return (deviate * lax.rsqrt(spread + 1e-05) * gain).astype(jnp.bfloat16)


def norm_kernel(rows_ref, gain_ref, out_ref, held, sems):
    pieces = sems.shape[0]
    step = held.shape[0] // pieces
    parts = [slice(i * step, (i + 1) * step) for i in range(pieces)]
    copies = [
        pltpu.make_async_copy(rows_ref.at[here, :], held.at[here, :], sems.at[i])
        for i, here in enumerate(parts)
    ]
    for copy in copies:
        copy.start()
    for copy, here in zip(copies, parts):
        copy.wait()
        out_ref[here, :] = normalize(held[here, :], gain_ref[...])


def normalize_rows(rows, gain):
    row_count, width = rows.shape
    return pl.pallas_call(
        norm_kernel,
        out_shape=jax.ShapeDtypeStruct((row_count, width), jnp.bfloat16),
        in_specs=[pl.BlockSpec(memory_space=pltpu.HBM), pl.BlockSpec(memory_space=VMEM)],
        out_specs=pl.BlockSpec(memory_space=VMEM),
        scratch_shapes=[VMEM((row_count, width), jnp.bfloat16), pltpu.SemaphoreType.DMA((8,))],
        compiler_params=params(48),
        cost_estimate=cost(10**9),
        name="layer_norm",
    )(rows, gain)


def near_kernel(place_ref, before_ref, rows_ref, after_ref, gain_ref, *refs):
    *weight_refs, ext_ref, first_ref, second_ref, third_ref, weights = refs
    row_count = rows_ref.shape[0]
    gain = gain_ref[...]
    ext_ref[0:HALO, :] = normalize(before_ref[...], gain)
    ext_ref[HALO : HALO + row_count, :] = rows_ref[...]
    ext_ref[HALO + row_count :, :] = normalize(after_ref[...], gain)
    if not weight_refs:
        return
    own = place_ref[0]
    depth, width = weight_refs[0].shape
    for i, weight_ref in enumerate(weight_refs):
        at = pl.multiple_of(lax.bitwise_xor(own % 2, i) * depth, depth)
        weights[pl.ds(at, depth), :] = weight_ref[...]
    near = pl.ds(pl.multiple_of(own // 2 * (2 * depth), 2 * depth), 2 * depth)
    wide = first_ref.shape[1] // 2
    channels = width // 2
    for block, out_ref in enumerate((first_ref, second_ref, third_ref)):
        for i in range(2):
            columns = slice(i * channels + block * wide, i * channels + (block + 1) * wide)
            out_ref[:, i * wide : (i + 1) * wide] = jnp.dot(
                ext_ref[:, near], weights[:, columns], preferred_element_type=jnp.float32
            )


def near_product(place, before, rows, after, gain, shards):
    row_count, width = rows.shape
    ext_rows = row_count + 2 * HALO
    partial = jax.ShapeDtypeStruct((ext_rows, width // 3), jnp.float32)
    depth = 2 * shards[0].shape[0] if shards else 16
    return pl.pallas_call(
        near_kernel,
        out_shape=(jax.ShapeDtypeStruct((ext_rows, width), jnp.bfloat16), partial, partial, partial),
        in_specs=[pl.BlockSpec(memory_space=pltpu.SMEM)]
        + [pl.BlockSpec(memory_space=VMEM)] * (4 + len(shards)),
        out_specs=[pl.BlockSpec(memory_space=VMEM)] * 4,
        scratch_shapes=[VMEM((depth, width), jnp.bfloat16)],
        compiler_params=params(10),
        cost_estimate=cost(10**9),
        name="near",
    )(place, before, rows, after, gain, *shards)


def front_kernel(block, earlier, place_ref, normed_ref, *refs):
    refs, earlier_refs = refs[earlier:], refs[:earlier]
    *weight_refs, taps_ref, conv_ref, stats_ref, weights, gated = refs
    ext_rows = normed_ref.shape[0]
    row_count, wide = conv_ref.shape
    taps, channels = taps_ref.shape
    if len(weight_refs) > 1:
        near_ref, *far_refs = weight_refs
        own = place_ref[0]
        depth = far_refs[0].shape[0]
        halves = len(far_refs) // 2
        for i in range(2):
            at = pl.multiple_of(lax.bitwise_xor(own % 2, i) * depth, depth)
            if halves == 1:
                weights[pl.ds(at, depth), :] = far_refs[i][...]
                continue
            for j in range(2):
                column = pl.multiple_of(lax.bitwise_xor(place_ref[3], j) * wide, wide)
                weights[pl.ds(at, depth), pl.ds(column, wide)] = far_refs[2 * i + j][...]
        far = pl.ds(pl.multiple_of((1 - own // 2) * (2 * depth), 2 * depth), 2 * depth)
        normed = normed_ref[:, far]
        value = near_ref[:, 0:wide] + jnp.dot(normed, weights[:, 0:wide], preferred_element_type=jnp.float32)
        gate = near_ref[:, wide:] + jnp.dot(normed, weights[:, wide:], preferred_element_type=jnp.float32)
    else:
        columns = slice(block * wide, (block + 1) * wide)
        value = jnp.dot(normed_ref[...], weight_refs[0][:, columns], preferred_element_type=jnp.float32)
        columns = slice(channels + block * wide, channels + (block + 1) * wide)
        gate = jnp.dot(normed_ref[...], weight_refs[0][:, columns], preferred_element_type=jnp.float32)
    start, length = place_ref[1], place_ref[2]
    position = start - HALO + lax.broadcasted_iota(jnp.int32, (ext_rows, 1), 0)
    valid = (position >= 0) & (position < length)
    kept = jnp.where(valid, value * jax.nn.sigmoid(gate), 0.0)
    kept = kept.astype(jnp.bfloat16).astype(jnp.float32)
    units = wide // LANES
    for unit in range(units):
        gated[unit] = kept[:, unit * LANES : (unit + 1) * LANES]
    first = HALO - (taps - 1) // 2
    step = 64
    for unit in range(units):
        lanes = slice(unit * LANES, (unit + 1) * LANES)
        tap_lanes = slice(block * wide + unit * LANES, block * wide + (unit + 1) * LANES)
        for at in range(0, row_count, step):
            acc = jnp.zeros((step, LANES), jnp.float32)
            for phase in range(8):
                offsets = [k for k in range(phase, first + taps, 8) if k >= first]
                extent = step + 8 if phase else step
                part = None
                for offset in offsets:
                    base = at + offset - phase
                    tap = offset - first
                    term = gated[unit, base : base + extent, :] * taps_ref[tap : tap + 1, tap_lanes]
                    part = term if part is None else part + term
                if phase:
                    part = pltpu.roll(part, extent - phase, 0)[:step]
                acc = acc + part
            conv_ref[at : at + step, lanes] = acc
    here = start + lax.broadcasted_iota(jnp.int32, (row_count, 1), 0) < length
    count = jnp.clip(length - start, 0, row_count).astype(jnp.float32)
    conv = conv_ref[...]
    mean = jnp.sum(jnp.where(here, conv, 0.0), axis=0, keepdims=True) / jnp.maximum(count, 1.0)
    deviate = jnp.where(here, conv - mean, 0.0)
    square = jnp.sum(deviate * deviate, axis=0, keepdims=True)
    stats = [mean, square, jnp.full((1, wide), count)]
    if not earlier_refs:
        for i, row in enumerate(stats):
            stats_ref[i : i + 1, :] = row
        return
    for copy in range(stats_ref.shape[0]):
        for i, row in enumerate(stats):
            parts = [ref[i : i + 1, :] for ref in earlier_refs] + [row]
            stats_ref[copy, i : i + 1, :] = jnp.concatenate(parts, axis=1)


def front_block(block, wide, place, normed, weights, dw_kernel, earlier=(), copies=1):
    ext_rows, width = normed.shape
    row_count = ext_rows - 2 * HALO
    depth = 2 * weights[1].shape[0] if len(weights) > 1 else 16
    stats_shape = (copies, 3, dw_kernel.shape[1]) if earlier else (3, wide)
    return pl.pallas_call(
        functools.partial(front_kernel, block, len(earlier)),
        out_shape=(
            jax.ShapeDtypeStruct((row_count, wide), jnp.float32),
            jax.ShapeDtypeStruct(stats_shape, jnp.float32),
        ),
        in_specs=[pl.BlockSpec(memory_space=pltpu.SMEM)]
        + [pl.BlockSpec(memory_space=VMEM)] * (2 + len(weights) + len(earlier)),
        out_specs=[pl.BlockSpec(memory_space=VMEM)] * 2,
        scratch_shapes=[
            VMEM((depth, 2 * wide), jnp.bfloat16),
            VMEM((wide // LANES, ext_rows, LANES), jnp.float32),
        ],
        compiler_params=params(10),
        cost_estimate=cost(4 * 10**9),
        name="front",
    )(place, normed, *earlier, *weights, dw_kernel)


def merged(stats_ref):
    means, squares, counts = stats_ref[:, 0, :], stats_ref[:, 1, :], stats_ref[:, 2, :]
    count = jnp.sum(counts, axis=0, keepdims=True)
    mean = jnp.sum(counts * means, axis=0, keepdims=True) / jnp.maximum(count, 1.0)
    between = means - mean
    square = jnp.sum(squares + counts * between * between, axis=0, keepdims=True)
    return mean, square, count


def merge_kernel(stats_ref, out_ref):
    for i, row in enumerate(merged(stats_ref)):
        for copy in range(out_ref.shape[0]):
            out_ref[copy, i : i + 1, :] = row


def merge(stats, copies):
    return pl.pallas_call(
        merge_kernel,
        out_shape=jax.ShapeDtypeStruct((copies,) + stats.shape[1:], jnp.float32),
        in_specs=[pl.BlockSpec(memory_space=VMEM)],
        out_specs=pl.BlockSpec(memory_space=VMEM),
        compiler_params=params(8),
        cost_estimate=cost(10**8),
        name="merge",
    )(stats)


def back_kernel(place_ref, stats_ref, gain_ref, shift_ref, *refs):
    *conv_refs, out_ref, rows_out, sems, weights = refs
    convs, weight_refs = conv_refs[:3], conv_refs[3:]
    row_count, wide = convs[0].shape
    if len(weight_refs) == 4:
        depth = weight_refs[0].shape[0]
        for i, weight_ref in enumerate(weight_refs):
            at = pl.multiple_of(lax.bitwise_xor(place_ref[0], i) * depth, depth)
            weights[pl.ds(at, depth), :] = weight_ref[...]
    else:
        weights[...] = weight_refs[0][...]
    mean, square, count = merged(stats_ref)
    scale = lax.rsqrt(square / count + 1e-05) * gain_ref[...]
    shift = shift_ref[...]
    pieces, rows, columns = rows_out.shape
    across = out_ref.shape[1] // columns
    copies = []
    for piece in range(pieces // across):
        here = slice(piece * rows, (piece + 1) * rows)
        parts = []
        for i, conv_ref in enumerate(convs):
            lanes = slice(i * wide, (i + 1) * wide)
            scaled = (conv_ref[here, :] - mean[:, lanes]) * scale[:, lanes] + shift[:, lanes]
            parts.append((scaled * jax.nn.sigmoid(scaled)).astype(jnp.bfloat16))
        activated = jnp.concatenate(parts, axis=1)
        position = place_ref[1] + piece * rows + lax.broadcasted_iota(jnp.int32, (rows, 1), 0)
        for j in range(across):
            lanes = slice(j * columns, (j + 1) * columns)
            result = jnp.dot(activated, weights[:, lanes], preferred_element_type=jnp.float32)
            slot = piece * across + j
            rows_out[slot] = jnp.where(position < place_ref[2], result, 0.0).astype(jnp.bfloat16)
            copy = pltpu.make_async_copy(rows_out.at[slot], out_ref.at[here, lanes], sems.at[slot])
            copy.start()
            copies.append(copy)
    for copy in copies:
        copy.wait()


def back(place, stats, gain, shift, convs, weights):
    row_count = convs[0].shape[0]
    channels, width = gain.shape[1], weights[0].shape[1]
    pieces, across = 4, 2
    return pl.pallas_call(
        back_kernel,
        out_shape=jax.ShapeDtypeStruct((row_count, width), jnp.bfloat16),
        in_specs=[pl.BlockSpec(memory_space=pltpu.SMEM)]
        + [pl.BlockSpec(memory_space=VMEM)] * (3 + len(convs) + len(weights)),
        out_specs=pl.BlockSpec(memory_space=pl.ANY),
        scratch_shapes=[
            VMEM((pieces, row_count * across // pieces, width // across), jnp.bfloat16),
            pltpu.SemaphoreType.DMA((pieces,)),
            VMEM((channels, width), jnp.bfloat16),
        ],
        compiler_params=params(10),
        cost_estimate=cost(10**9),
        name="back",
    )(place, stats, gain, shift, *convs, *weights)


def everyones(copies, groups):
    return lax.all_to_all(copies, ("fsdp", "ctx"), 0, 0, axis_index_groups=groups, tiled=True)


def tie(*values):
    return lax.optimization_barrier(values)


def body(frames, lengths, ln_gain, w_in, dw_kernel, bn_gain, bn_shift, w_out):
    _, row_count, model_width = frames.shape
    channels = dw_kernel.shape[1]
    wide = channels // 3
    ctx, fsdp = lax.axis_index("ctx"), lax.axis_index("fsdp")
    ctx_count, fsdp_count = lax.axis_size("ctx"), lax.axis_size("fsdp")
    direct = fsdp_count == 4 and ctx_count % 2 == 0
    rows = frames[0]
    gain = ln_gain[None]
    parity = lax.rem(ctx, 2)
    place = jnp.stack([fsdp, ctx * row_count, lengths[0], parity]).astype(jnp.int32)
    ends = ctx_count - 1
    down, up = [(i, i + 1) for i in range(ends)], [(i + 1, i) for i in range(ends)]
    if direct:
        *parts, head, tail = cut(parity[None].astype(jnp.int32), w_in, rows, wide)
        over_x = [swap(part, "fsdp", 2) for part in parts]
        shards = [w_in, swap(w_in, "fsdp", 1)]
        normed = normalize_rows(rows, gain)
        normed, head, tail, over_x[0] = tie(normed, head, tail, over_x[0])
        over_y = [swap(over_x[0], "ctx", 1)]
        before, after = lax.ppermute(tail, "ctx", down), lax.ppermute(head, "ctx", up)
        normed, over_x[1], over_y[0] = tie(normed, over_x[1], over_y[0])
        over_y.append(swap(over_x[1], "ctx", 1))
        normed, *partials = near_product(place, before, normed, after, gain, shards)
        partials[0], over_x[2], over_y[1] = tie(partials[0], over_x[2], over_y[1])
        halves = [(over_x[0], over_y[0]), (over_x[1], over_y[1]), (over_x[2],)]
        weights = [
            [partial, *half, *(swap(part, "fsdp", 1) for part in half)]
            for partial, half in zip(partials, halves)
        ]
        _, later = tie(over_x[2], w_out)
        out_weights = [w_out, swap(later, "fsdp", 1), swap(later, "fsdp", 2)]
    else:
        full_in = lax.all_gather(w_in, "fsdp", axis=0, tiled=True)
        out_weights = [lax.all_gather(w_out, "fsdp", axis=0, tiled=True)]
        before = lax.ppermute(rows[-HALO:], "ctx", down)
        after = lax.ppermute(rows[:HALO], "ctx", up)
        normed = normalize_rows(rows, gain)
        normed, *_ = near_product(place, before, normed, after, gain, [])
        weights = [[full_in]] * 3
    near_by = 2 if ctx_count % 2 == 0 else 1
    member = lambda f, p: f * ctx_count + p
    groups = [
        [member(f, p + i) for f in range(fsdp_count) for i in range(near_by)]
        for p in range(0, ctx_count, near_by)
    ]
    convs, stats = [], []
    for i in range(3):
        extra = (stats, len(groups[0])) if i == 2 else ()
        conv, stat = front_block(i, wide, place, normed, weights[i], dw_kernel, *extra)
        convs.append(conv)
        stats.append(stat)
    stats = merge(everyones(stats[2], groups), len(groups))
    if direct:
        stats, out_weights[2] = tie(stats, out_weights[2])
        out_weights.append(swap(out_weights[2], "fsdp", 1))
    groups = [
        [member(f, p + i) for p in range(0, ctx_count, near_by)]
        for f in range(fsdp_count)
        for i in range(near_by)
    ]
    stats = everyones(stats, groups)
    result = back(place, stats, bn_gain[None], bn_shift[None], convs, out_weights)
    return result[None]


def solution(mesh):
    return jax.shard_map(
        body,
        mesh=mesh,
        in_specs=(
            P("fsdp", "ctx", None),
            P("fsdp"),
            P(),
            P("fsdp", None),
            P(),
            P(),
            P(),
            P("fsdp", None),
        ),
        out_specs=P("fsdp", "ctx", None),
        check_vma=False,
    )
```

```python
import functools

import jax
import jax.numpy as jnp
from jax import lax
from jax.experimental import pallas as pl
from jax.experimental.pallas import tpu as pltpu
from jax.sharding import PartitionSpec as P

HALO = 16
LANES = 128
MIB = 1024 * 1024
VMEM = pltpu.VMEM
ORDER = (0, 1, 2)
SPLIT = (0, 1)


def cost(flops):
    return pl.CostEstimate(flops=flops, bytes_accessed=0, transcendentals=0)


def params(mib):
    return pltpu.CompilerParams(vmem_limit_bytes=mib * MIB)


def swap(value, axis, bit):
    return lax.ppermute(value, axis, [(i, i ^ bit) for i in range(lax.axis_size(axis))])


def cut_kernel(order, split, wide, parity_ref, shard_ref, rows_ref, out_shard_ref, *refs):
    *part_refs, head_ref, tail_ref, upper_ref, lower_ref, sems = refs
    channels = shard_ref.shape[1] // 2
    row_count = rows_ref.shape[0]
    copies = []

    def copy(source, target):
        copies.append(pltpu.make_async_copy(source, target, sems.at[len(copies)]))
        copies[-1].start()

    side = parity_ref[0] * channels
    for block, ref in zip(order, part_refs):
        if block in split:
            copy(shard_ref.at[:, pl.ds(pl.multiple_of(side + block * wide, wide), wide)], ref)
        else:
            for i in range(2):
                at = i * channels + block * wide
                copy(shard_ref.at[:, at : at + wide], ref.at[:, i * wide : (i + 1) * wide])
    copy(rows_ref.at[0:HALO, :], head_ref)
    copy(rows_ref.at[row_count - HALO : row_count, :], tail_ref)
    depth = upper_ref.shape[0]
    copy(out_shard_ref.at[0:depth, :], upper_ref)
    copy(out_shard_ref.at[depth : 2 * depth, :], lower_ref)
    for started in copies:
        started.wait()


def cut(parity, shard, rows, out_shard, wide):
    depth, width = shard.shape
    shapes = [(depth, wide if block in SPLIT else 2 * wide) for block in ORDER]
    shapes += [(HALO, width)] * 2 + [(out_shard.shape[0] // 2, out_shard.shape[1])] * 2
    return pl.pallas_call(
        functools.partial(cut_kernel, ORDER, SPLIT, wide),
        out_shape=[jax.ShapeDtypeStruct(shape, jnp.bfloat16) for shape in shapes],
        in_specs=[
            pl.BlockSpec(memory_space=pltpu.SMEM),
            pl.BlockSpec(memory_space=pltpu.HBM),
            pl.BlockSpec(memory_space=pltpu.HBM),
            pl.BlockSpec(memory_space=pltpu.HBM),
        ],
        out_specs=[pl.BlockSpec(memory_space=VMEM)] * len(shapes),
        scratch_shapes=[pltpu.SemaphoreType.DMA((8,))],
        compiler_params=params(56),
        cost_estimate=cost(10**8),
        name="cut",
    )(parity, shard, rows, out_shard)


def normalize(values, gain):
    values = values.astype(jnp.float32)
    centre = jnp.mean(values, axis=-1, keepdims=True)
    deviate = values - centre
    spread = jnp.mean(deviate * deviate, axis=-1, keepdims=True)
    return (deviate * lax.rsqrt(spread + 1e-05) * gain).astype(jnp.bfloat16)


def norm_kernel(rows_ref, gain_ref, out_ref):
    step = 64

    @pl.loop(0, rows_ref.shape[0] // step)
    def _(i):
        here = pl.ds(pl.multiple_of(i * step, step), step)
        out_ref[here, :] = normalize(rows_ref[here, :], gain_ref[...])


def normalize_rows(rows, gain):
    row_count, width = rows.shape
    return pl.pallas_call(
        norm_kernel,
        out_shape=jax.ShapeDtypeStruct((row_count, width), jnp.bfloat16),
        in_specs=[pl.BlockSpec(memory_space=VMEM)] * 2,
        out_specs=pl.BlockSpec(memory_space=VMEM),
        compiler_params=params(4),
        cost_estimate=cost(4 * 10**9),
        name="layer_norm",
    )(rows, gain)


def near_kernel(place_ref, before_ref, rows_ref, after_ref, gain_ref, *refs):
    *weight_refs, ext_ref, first_ref, second_ref, third_ref, weights = refs
    row_count = rows_ref.shape[0]
    gain = gain_ref[...]
    ext_ref[0:HALO, :] = normalize(before_ref[...], gain)
    ext_ref[HALO : HALO + row_count, :] = rows_ref[...]
    ext_ref[HALO + row_count :, :] = normalize(after_ref[...], gain)
    if not weight_refs:
        return
    own = place_ref[0]
    depth, width = weight_refs[0].shape
    for i, weight_ref in enumerate(weight_refs):
        at = pl.multiple_of(lax.bitwise_xor(own % 2, i) * depth, depth)
        weights[pl.ds(at, depth), :] = weight_ref[...]
    near = pl.ds(pl.multiple_of(own // 2 * (2 * depth), 2 * depth), 2 * depth)
    wide = first_ref.shape[1] // 2
    channels = width // 2
    for block, out_ref in enumerate((first_ref, second_ref, third_ref)):
        for i in range(2):
            columns = slice(i * channels + block * wide, i * channels + (block + 1) * wide)
            out_ref[:, i * wide : (i + 1) * wide] = jnp.dot(
                ext_ref[:, near], weights[:, columns], preferred_element_type=jnp.float32
            )


def near_product(place, before, rows, after, gain, shards):
    row_count, width = rows.shape
    ext_rows = row_count + 2 * HALO
    partial = jax.ShapeDtypeStruct((ext_rows, width // 3), jnp.float32)
    depth = 2 * shards[0].shape[0] if shards else 16
    return pl.pallas_call(
        near_kernel,
        out_shape=(jax.ShapeDtypeStruct((ext_rows, width), jnp.bfloat16), partial, partial, partial),
        in_specs=[pl.BlockSpec(memory_space=pltpu.SMEM)]
        + [pl.BlockSpec(memory_space=VMEM)] * (4 + len(shards)),
        out_specs=[pl.BlockSpec(memory_space=VMEM)] * 4,
        scratch_shapes=[VMEM((depth, width), jnp.bfloat16)],
        compiler_params=params(8),
        cost_estimate=cost(10**8),
        name="near",
    )(place, before, rows, after, gain, *shards)


def front_kernel(block, earlier, place_ref, normed_ref, *refs):
    refs, earlier_refs = refs[earlier:], refs[:earlier]
    *weight_refs, taps_ref, conv_ref, stats_ref, weights, gated = refs
    ext_rows = normed_ref.shape[0]
    row_count, wide = conv_ref.shape
    taps, channels = taps_ref.shape
    if len(weight_refs) > 1:
        near_ref, *far_refs = weight_refs
        own = place_ref[0]
        depth = far_refs[0].shape[0]
        halves = len(far_refs) // 2
        for i in range(2):
            at = pl.multiple_of(lax.bitwise_xor(own % 2, i) * depth, depth)
            if halves == 1:
                weights[pl.ds(at, depth), :] = far_refs[i][...]
                continue
            for j in range(2):
                column = pl.multiple_of(lax.bitwise_xor(place_ref[3], j) * wide, wide)
                weights[pl.ds(at, depth), pl.ds(column, wide)] = far_refs[2 * i + j][...]
        far = pl.ds(pl.multiple_of((1 - own // 2) * (2 * depth), 2 * depth), 2 * depth)
        normed = normed_ref[:, far]
        value = near_ref[:, 0:wide] + jnp.dot(normed, weights[:, 0:wide], preferred_element_type=jnp.float32)
        gate = near_ref[:, wide:] + jnp.dot(normed, weights[:, wide:], preferred_element_type=jnp.float32)
    else:
        columns = slice(block * wide, (block + 1) * wide)
        value = jnp.dot(normed_ref[...], weight_refs[0][:, columns], preferred_element_type=jnp.float32)
        columns = slice(channels + block * wide, channels + (block + 1) * wide)
        gate = jnp.dot(normed_ref[...], weight_refs[0][:, columns], preferred_element_type=jnp.float32)
    start, length = place_ref[1], place_ref[2]
    position = start - HALO + lax.broadcasted_iota(jnp.int32, (ext_rows, 1), 0)
    valid = (position >= 0) & (position < length)
    kept = jnp.where(valid, value * jax.nn.sigmoid(gate), 0.0)
    kept = kept.astype(jnp.bfloat16).astype(jnp.float32)
    first = HALO - (taps - 1) // 2
    step = 64
    for unit in range(wide // LANES):
        lanes = slice(unit * LANES, (unit + 1) * LANES)
        tap_lanes = slice(block * wide + unit * LANES, block * wide + (unit + 1) * LANES)
        column = kept[:, lanes]
        gated[0] = column
        for phase in range(1, 8):
            gated[phase] = pltpu.roll(column, ext_rows - phase, 0)
        for at in range(0, row_count, step):
            acc = None
            for tap in range(taps):
                base = at + (first + tap) // 8 * 8
                term = gated[(first + tap) % 8, base : base + step, :] * taps_ref[tap : tap + 1, tap_lanes]
                acc = term if acc is None else acc + term
            conv_ref[at : at + step, lanes] = acc
    here = start + lax.broadcasted_iota(jnp.int32, (row_count, 1), 0) < length
    count = jnp.clip(length - start, 0, row_count).astype(jnp.float32)
    conv = conv_ref[...]
    mean = jnp.sum(jnp.where(here, conv, 0.0), axis=0, keepdims=True) / jnp.maximum(count, 1.0)
    deviate = jnp.where(here, conv - mean, 0.0)
    square = jnp.sum(deviate * deviate, axis=0, keepdims=True)
    stats = [mean, square, jnp.full((1, wide), count)]
    if not earlier_refs:
        for i, row in enumerate(stats):
            stats_ref[i : i + 1, :] = row
        return
    for i, row in enumerate(stats):
        for copy in range(stats_ref.shape[0]):
            stats_ref[copy, i : i + 1, block * wide : (block + 1) * wide] = row
            for other, ref in zip([j for j in ORDER if j != block], earlier_refs):
                stats_ref[copy, i : i + 1, other * wide : (other + 1) * wide] = ref[i : i + 1, :]


def front_block(block, wide, place, normed, weights, dw_kernel, earlier=(), copies=1):
    ext_rows, width = normed.shape
    row_count = ext_rows - 2 * HALO
    depth = 2 * weights[1].shape[0] if len(weights) > 1 else 16
    stats_shape = (copies, 3, dw_kernel.shape[1]) if earlier else (3, wide)
    return pl.pallas_call(
        functools.partial(front_kernel, block, len(earlier)),
        out_shape=(
            jax.ShapeDtypeStruct((row_count, wide), jnp.float32),
            jax.ShapeDtypeStruct(stats_shape, jnp.float32),
        ),
        in_specs=[pl.BlockSpec(memory_space=pltpu.SMEM)]
        + [pl.BlockSpec(memory_space=VMEM)] * (2 + len(weights) + len(earlier)),
        out_specs=[pl.BlockSpec(memory_space=VMEM)] * 2,
        scratch_shapes=[
            VMEM((depth, 2 * wide), jnp.bfloat16),
            VMEM((8, ext_rows, LANES), jnp.float32),
        ],
        compiler_params=params(10),
        cost_estimate=cost(10**8),
        name="front",
    )(place, normed, *earlier, *weights, dw_kernel)


def merged(parts):
    means, squares, counts = zip(*parts)
    count = sum(counts)
    mean = sum(n * m for n, m in zip(counts, means)) / jnp.maximum(count, 1.0)
    square = sum(squares) + sum(n * (m - mean) * (m - mean) for n, m in zip(counts, means))
    return mean, square, count


def rows_of(refs):
    return [[ref[copy, i : i + 1, :] for i in range(3)] for ref in refs for copy in range(ref.shape[0])]


def merge_kernel(stats_ref, out_ref):
    for i, row in enumerate(merged(rows_of([stats_ref]))):
        for copy in range(out_ref.shape[0]):
            out_ref[copy, i : i + 1, :] = row


def merge(stats, copies):
    return pl.pallas_call(
        merge_kernel,
        out_shape=jax.ShapeDtypeStruct((copies,) + stats.shape[1:], jnp.float32),
        in_specs=[pl.BlockSpec(memory_space=VMEM)],
        out_specs=pl.BlockSpec(memory_space=VMEM),
        compiler_params=params(8),
        cost_estimate=cost(10**8),
        name="merge",
    )(stats)


def back_kernel(stat_count, place_ref, gain_ref, shift_ref, *refs):
    stat_refs, refs = refs[:stat_count], refs[stat_count:]
    *conv_refs, out_ref, rows_out, sems, weights = refs
    convs, weight_refs = conv_refs[:3], conv_refs[3:]
    row_count, wide = convs[0].shape
    if len(weight_refs) > 1:
        depth = weight_refs[0].shape[0]
        for i, weight_ref in enumerate(weight_refs[:2]):
            at = pl.multiple_of(lax.bitwise_xor(place_ref[0], i) * depth, depth)
            weights[pl.ds(at, depth), :] = weight_ref[...]
        half = depth // 2
        for i, weight_ref in enumerate(weight_refs[2:]):
            at = lax.bitwise_xor(place_ref[0], 2 + i // 2) * depth + i % 2 * half
            weights[pl.ds(pl.multiple_of(at, half), half), :] = weight_ref[...]
    else:
        weights[...] = weight_refs[0][...]
    mean, square, count = merged(rows_of(stat_refs))
    scale = lax.rsqrt(square / count + 1e-05) * gain_ref[...]
    shift = shift_ref[...]
    pieces, rows, columns = rows_out.shape
    across = out_ref.shape[1] // columns
    copies = []
    for piece in range(pieces // across):
        here = slice(piece * rows, (piece + 1) * rows)
        parts = []
        for i, conv_ref in enumerate(convs):
            lanes = slice(i * wide, (i + 1) * wide)
            scaled = (conv_ref[here, :] - mean[:, lanes]) * scale[:, lanes] + shift[:, lanes]
            parts.append((scaled * jax.nn.sigmoid(scaled)).astype(jnp.bfloat16))
        activated = jnp.concatenate(parts, axis=1)
        position = place_ref[1] + piece * rows + lax.broadcasted_iota(jnp.int32, (rows, 1), 0)
        for j in range(across):
            lanes = slice(j * columns, (j + 1) * columns)
            result = jnp.dot(activated, weights[:, lanes], preferred_element_type=jnp.float32)
            slot = piece * across + j
            rows_out[slot] = jnp.where(position < place_ref[2], result, 0.0).astype(jnp.bfloat16)
            copy = pltpu.make_async_copy(rows_out.at[slot], out_ref.at[here, lanes], sems.at[slot])
            copy.start()
            copies.append(copy)
    for copy in copies:
        copy.wait()


def back(place, stats, gain, shift, convs, weights):
    row_count = convs[0].shape[0]
    channels, width = gain.shape[1], weights[0].shape[1]
    pieces, across = 4, 2
    return pl.pallas_call(
        functools.partial(back_kernel, len(stats)),
        out_shape=jax.ShapeDtypeStruct((row_count, width), jnp.bfloat16),
        in_specs=[pl.BlockSpec(memory_space=pltpu.SMEM)]
        + [pl.BlockSpec(memory_space=VMEM)] * (2 + len(stats) + len(convs) + len(weights)),
        out_specs=pl.BlockSpec(memory_space=pl.ANY),
        scratch_shapes=[
            VMEM((pieces, row_count * across // pieces, width // across), jnp.bfloat16),
            pltpu.SemaphoreType.DMA((pieces,)),
            VMEM((channels, width), jnp.bfloat16),
        ],
        compiler_params=params(10),
        cost_estimate=cost(10**9),
        name="back",
    )(place, gain, shift, *stats, *convs, *weights)


def everyones(copies, groups):
    return lax.all_to_all(copies, ("fsdp", "ctx"), 0, 0, axis_index_groups=groups, tiled=True)


def tie(*values):
    return lax.optimization_barrier(values)


def body(frames, lengths, ln_gain, w_in, dw_kernel, bn_gain, bn_shift, w_out):
    _, row_count, model_width = frames.shape
    channels = dw_kernel.shape[1]
    wide = channels // 3
    ctx, fsdp = lax.axis_index("ctx"), lax.axis_index("fsdp")
    ctx_count, fsdp_count = lax.axis_size("ctx"), lax.axis_size("fsdp")
    direct = fsdp_count == 4 and ctx_count == 8
    rows = frames[0]
    gain = ln_gain[None]
    parity = lax.rem(ctx, 2)
    place = jnp.stack([fsdp, ctx * row_count, lengths[0], parity]).astype(jnp.int32)
    ends = ctx_count - 1
    down, up = [(i, i + 1) for i in range(ends)], [(i + 1, i) for i in range(ends)]
    both = ("fsdp", "ctx")
    member = lambda f, p: f * ctx_count + p

    def front(block, weights, *extra):
        return front_block(block, wide, place, normed, weights, dw_kernel, *extra)

    if direct:
        *parts, head, tail, upper, lower = cut(parity[None].astype(jnp.int32), w_in, rows, w_out, wide)
        over_x = {block: [swap(part, "fsdp", 2)] for block, part in zip(ORDER, parts)}
        parts[0], shard = tie(parts[0], w_in)
        shards = [w_in, swap(shard, "fsdp", 1)]
        before, after = lax.ppermute(tail, "ctx", down), lax.ppermute(head, "ctx", up)
        normed = normalize_rows(rows, gain)
        normed, before, after, over_x[0][0] = tie(normed, before, after, over_x[0][0])
        over_x[0].append(swap(over_x[0][0], "ctx", 1))
        normed, over_x[1][0] = tie(normed, over_x[1][0])
        over_x[1].append(swap(over_x[1][0], "ctx", 1))
        normed, *partials = near_product(place, before, normed, after, gain, shards)
        partials[0], over_x[0][1], over_x[1][1], w_out, upper = tie(
            partials[0], over_x[0][1], over_x[1][1], w_out, upper
        )
        upper = swap(upper, "fsdp", 2)
        out_weights = [w_out, swap(w_out, "fsdp", 1)]

        def weights_of(block):
            return [partials[block], *over_x[block], *(swap(part, "fsdp", 1) for part in over_x[block])]

        weights = [weights_of(0), weights_of(1)]
        conv_one, stat_one = front(0, weights[0])
        conv_one, weights[1][0], over_x[2][0] = tie(conv_one, weights[1][0], over_x[2][0])
        _, lower = tie(over_x[2][0], lower)
        lower = swap(lower, "fsdp", 2)
        weights.append(weights_of(2))
        conv_two, stat_two = front(1, weights[1])
        conv_three, stats = front(2, weights[2], (stat_one, stat_two), 1)
        convs = [conv_one, conv_two, conv_three]

        def others(flips):
            return [
                lax.ppermute(
                    stats,
                    both,
                    [(member(f, p), member(f ^ df, p ^ dp)) for f in range(4) for p in range(8)],
                )
                for df, dp in flips
            ]

        def union(parts):
            return jnp.stack(merged([[part[:, i] for i in range(3)] for part in parts]), 1)

        stats, upper = tie(stats, upper)
        stats = union([stats] + others([(1, 0)]))
        stats = union([stats] + others([(2, 0), (0, 1), (2, 1)]))
        stats, lower = tie(stats, lower)
        out_weights += [upper, lower, swap(upper, "fsdp", 1), swap(lower, "fsdp", 1)]
        stats = [stats] + others([(0, 2), (0, 4), (0, 6)])
    else:
        full_in = lax.all_gather(w_in, "fsdp", axis=0, tiled=True)
        out_weights = [lax.all_gather(w_out, "fsdp", axis=0, tiled=True)]
        before = lax.ppermute(rows[-HALO:], "ctx", down)
        after = lax.ppermute(rows[:HALO], "ctx", up)
        normed = normalize_rows(rows, gain)
        normed, *_ = near_product(place, before, normed, after, gain, [])
        near_by = 2 if ctx_count % 2 == 0 else 1
        groups = [
            [member(f, p + i) for f in range(fsdp_count) for i in range(near_by)]
            for p in range(0, ctx_count, near_by)
        ]
        convs, stats = [None] * 3, []
        for block in ORDER:
            extra = (stats, len(groups[0])) if block == ORDER[-1] else ()
            convs[block], stat = front(block, [full_in], *extra)
            stats.append(stat)
        stats = merge(everyones(stats[2], groups), len(groups))
        groups = [
            [member(f, p + i) for p in range(0, ctx_count, near_by)]
            for f in range(fsdp_count)
            for i in range(near_by)
        ]
        stats = [everyones(stats, groups)]
    result = back(place, stats, bn_gain[None], bn_shift[None], convs, out_weights)
    return result[None]


def solution(mesh):
    return jax.shard_map(
        body,
        mesh=mesh,
        in_specs=(
            P("fsdp", "ctx", None),
            P("fsdp"),
            P(),
            P("fsdp", None),
            P(),
            P(),
            P(),
            P("fsdp", None),
        ),
        out_specs=P("fsdp", "ctx", None),
        check_vma=False,
    )
```

```python
import functools

import jax
import jax.numpy as jnp
from jax import lax
from jax.experimental import pallas as pl
from jax.experimental.pallas import tpu as pltpu
from jax.sharding import PartitionSpec as P

HALO = 16
LANES = 128
MIB = 1024 * 1024
VMEM = pltpu.VMEM
SPLIT = (0, 1)


def cost(flops):
    return pl.CostEstimate(flops=flops, bytes_accessed=0, transcendentals=0)


def params(mib):
    return pltpu.CompilerParams(vmem_limit_bytes=mib * MIB)


def swap(value, axis, bit):
    return lax.ppermute(value, axis, [(i, i ^ bit) for i in range(lax.axis_size(axis))])


def cut_kernel(wide, parity_ref, shard_ref, out_shard_ref, rows_ref, *refs):
    half_ref, *part_refs, inner_ref, outer_ref, sems = refs
    channels = shard_ref.shape[1] // 2
    parity = parity_ref[0]
    copies = []

    def copy(source, target):
        copies.append(pltpu.make_async_copy(source, target, sems.at[len(copies)]))
        copies[-1].start()

    depth = half_ref.shape[0]
    copy(out_shard_ref.at[pl.ds(pl.multiple_of(parity * depth, depth), depth), :], half_ref)
    for block, ref in enumerate(part_refs):
        if block in SPLIT:
            at = parity * channels + block * wide
            copy(shard_ref.at[:, pl.ds(pl.multiple_of(at, wide), wide)], ref)
        else:
            for i in range(2):
                at = i * channels + block * wide
                copy(shard_ref.at[:, at : at + wide], ref.at[:, i * wide : (i + 1) * wide])
    last = rows_ref.shape[0] - HALO
    copy(rows_ref.at[pl.ds(pl.multiple_of((1 - parity) * last, HALO), HALO), :], inner_ref)
    copy(rows_ref.at[pl.ds(pl.multiple_of(parity * last, HALO), HALO), :], outer_ref)
    for started in copies:
        started.wait()


def cut(parity, shard, out_shard, rows, wide):
    depth, width = shard.shape
    shapes = [(out_shard.shape[0] // 2, out_shard.shape[1])]
    shapes += [(depth, wide if block in SPLIT else 2 * wide) for block in range(3)]
    shapes += [(HALO, width)] * 2
    hbm = pl.BlockSpec(memory_space=pltpu.HBM)
    return pl.pallas_call(
        functools.partial(cut_kernel, wide),
        out_shape=[jax.ShapeDtypeStruct(shape, jnp.bfloat16) for shape in shapes],
        in_specs=[pl.BlockSpec(memory_space=pltpu.SMEM)] + [hbm] * 3,
        out_specs=[hbm] * len(shapes),
        scratch_shapes=[pltpu.SemaphoreType.DMA((8,))],
        compiler_params=params(56),
        cost_estimate=cost(10**8),
        name="cut",
    )(parity, shard, out_shard, rows)


def normalize(values, gain):
    values = values.astype(jnp.float32)
    centre = jnp.mean(values, axis=-1, keepdims=True)
    deviate = values - centre
    spread = jnp.mean(deviate * deviate, axis=-1, keepdims=True)
    return (deviate * lax.rsqrt(spread + 1e-05) * gain).astype(jnp.bfloat16)


def norm_kernel(place_ref, rows_ref, inner_ref, outer_ref, gain_ref, out_ref):
    step = 64
    row_count = rows_ref.shape[0]

    @pl.loop(0, row_count // step)
    def _(i):
        at = pl.multiple_of(i * step, step)
        out_ref[pl.ds(HALO + at, step), :] = normalize(rows_ref[pl.ds(at, step), :], gain_ref[...])

    odd = place_ref[3]
    at = pl.multiple_of((1 - odd) * (HALO + row_count), HALO)
    out_ref[pl.ds(at, HALO), :] = normalize(inner_ref[...], gain_ref[...])
    at = pl.multiple_of(odd * (HALO + row_count), HALO)
    out_ref[pl.ds(at, HALO), :] = normalize(outer_ref[...], gain_ref[...])


def normalize_rows(place, rows, inner, outer, gain):
    row_count, width = rows.shape
    return pl.pallas_call(
        norm_kernel,
        out_shape=jax.ShapeDtypeStruct((row_count + 2 * HALO, width), jnp.bfloat16),
        in_specs=[pl.BlockSpec(memory_space=pltpu.SMEM)] + [pl.BlockSpec(memory_space=VMEM)] * 4,
        out_specs=pl.BlockSpec(memory_space=VMEM),
        compiler_params=params(4),
        cost_estimate=cost(4 * 10**9),
        name="layer_norm",
    )(place, rows, inner, outer, gain)


def near_kernel(place_ref, normed_ref, own_ref, other_ref, *refs):
    *out_refs, weights = refs
    own = place_ref[0]
    depth, width = own_ref.shape
    for i, weight_ref in enumerate((own_ref, other_ref)):
        at = pl.multiple_of(lax.bitwise_xor(own % 2, i) * depth, depth)
        weights[pl.ds(at, depth), :] = weight_ref[...]
    near = pl.ds(pl.multiple_of(own // 2 * (2 * depth), 2 * depth), 2 * depth)
    wide = out_refs[0].shape[1] // 2
    channels = width // 2
    for block, out_ref in enumerate(out_refs):
        for i in range(2):
            columns = slice(i * channels + block * wide, i * channels + (block + 1) * wide)
            out_ref[:, i * wide : (i + 1) * wide] = jnp.dot(
                normed_ref[:, near], weights[:, columns], preferred_element_type=jnp.float32
            )


def near_product(place, normed, own, other):
    ext_rows, width = normed.shape
    partial = jax.ShapeDtypeStruct((ext_rows, width // 3), jnp.float32)
    return pl.pallas_call(
        near_kernel,
        out_shape=[partial] * 3,
        in_specs=[pl.BlockSpec(memory_space=pltpu.SMEM)] + [pl.BlockSpec(memory_space=VMEM)] * 3,
        out_specs=[pl.BlockSpec(memory_space=VMEM)] * 3,
        scratch_shapes=[VMEM((2 * own.shape[0], width), jnp.bfloat16)],
        compiler_params=params(8),
        cost_estimate=cost(10**8),
        name="near",
    )(place, normed, own, other)


def front_kernel(block, earlier, place_ref, normed_ref, *refs):
    refs, earlier_refs = refs[earlier:], refs[:earlier]
    *weight_refs, taps_ref, conv_ref, stats_ref, weights, gated = refs
    ext_rows = normed_ref.shape[0]
    row_count, wide = conv_ref.shape
    taps, channels = taps_ref.shape
    if len(weight_refs) > 1:
        near_ref, *far_refs = weight_refs
        own = place_ref[0]
        depth = far_refs[0].shape[0]
        halves = len(far_refs) // 2
        for i in range(2):
            at = pl.multiple_of(lax.bitwise_xor(own % 2, i) * depth, depth)
            if halves == 1:
                weights[pl.ds(at, depth), :] = far_refs[i][...]
                continue
            for j in range(2):
                column = pl.multiple_of(lax.bitwise_xor(place_ref[3], j) * wide, wide)
                weights[pl.ds(at, depth), pl.ds(column, wide)] = far_refs[2 * i + j][...]
        far = pl.ds(pl.multiple_of((1 - own // 2) * (2 * depth), 2 * depth), 2 * depth)
        normed = normed_ref[:, far]
        value = near_ref[:, 0:wide] + jnp.dot(normed, weights[:, 0:wide], preferred_element_type=jnp.float32)
        gate = near_ref[:, wide:] + jnp.dot(normed, weights[:, wide:], preferred_element_type=jnp.float32)
    else:
        columns = slice(block * wide, (block + 1) * wide)
        value = jnp.dot(normed_ref[...], weight_refs[0][:, columns], preferred_element_type=jnp.float32)
        columns = slice(channels + block * wide, channels + (block + 1) * wide)
        gate = jnp.dot(normed_ref[...], weight_refs[0][:, columns], preferred_element_type=jnp.float32)
    start, length = place_ref[1], place_ref[2]
    position = start - HALO + lax.broadcasted_iota(jnp.int32, (ext_rows, 1), 0)
    valid = (position >= 0) & (position < length)
    kept = jnp.where(valid, value * jax.nn.sigmoid(gate), 0.0)
    kept = kept.astype(jnp.bfloat16).astype(jnp.float32)
    first = HALO - (taps - 1) // 2
    step = 64
    for unit in range(wide // LANES):
        lanes = slice(unit * LANES, (unit + 1) * LANES)
        tap_lanes = slice(block * wide + unit * LANES, block * wide + (unit + 1) * LANES)
        column = kept[:, lanes]
        gated[0] = column
        for phase in range(1, 8):
            gated[phase] = pltpu.roll(column, ext_rows - phase, 0)
        for at in range(0, row_count, step):
            acc = None
            for tap in range(taps):
                base = at + (first + tap) // 8 * 8
                term = gated[(first + tap) % 8, base : base + step, :] * taps_ref[tap : tap + 1, tap_lanes]
                acc = term if acc is None else acc + term
            conv_ref[at : at + step, lanes] = acc
    here = start + lax.broadcasted_iota(jnp.int32, (row_count, 1), 0) < length
    count = jnp.clip(length - start, 0, row_count).astype(jnp.float32)
    conv = conv_ref[...]
    mean = jnp.sum(jnp.where(here, conv, 0.0), axis=0, keepdims=True) / jnp.maximum(count, 1.0)
    deviate = jnp.where(here, conv - mean, 0.0)
    square = jnp.sum(deviate * deviate, axis=0, keepdims=True)
    stats = [mean, square, jnp.full((1, wide), count)]
    if not earlier_refs:
        for i, row in enumerate(stats):
            stats_ref[i : i + 1, :] = row
        return
    for i, row in enumerate(stats):
        for copy in range(stats_ref.shape[0]):
            stats_ref[copy, i : i + 1, block * wide : (block + 1) * wide] = row
            for other, ref in zip([j for j in range(3) if j != block], earlier_refs):
                stats_ref[copy, i : i + 1, other * wide : (other + 1) * wide] = ref[i : i + 1, :]


def front_block(block, wide, place, normed, weights, dw_kernel, earlier=(), copies=1):
    ext_rows, width = normed.shape
    row_count = ext_rows - 2 * HALO
    depth = 2 * weights[1].shape[0] if len(weights) > 1 else 16
    stats_shape = (copies, 3, dw_kernel.shape[1]) if earlier else (3, wide)
    return pl.pallas_call(
        functools.partial(front_kernel, block, len(earlier)),
        out_shape=(
            jax.ShapeDtypeStruct((row_count, wide), jnp.float32),
            jax.ShapeDtypeStruct(stats_shape, jnp.float32),
        ),
        in_specs=[pl.BlockSpec(memory_space=pltpu.SMEM)]
        + [pl.BlockSpec(memory_space=VMEM)] * (2 + len(weights) + len(earlier)),
        out_specs=[pl.BlockSpec(memory_space=VMEM)] * 2,
        scratch_shapes=[
            VMEM((depth, 2 * wide), jnp.bfloat16),
            VMEM((8, ext_rows, LANES), jnp.float32),
        ],
        compiler_params=params(10),
        cost_estimate=cost(10**8),
        name="front",
    )(place, normed, *earlier, *weights, dw_kernel)


def merged(parts):
    means, squares, counts = zip(*parts)
    count = sum(counts)
    mean = sum(n * m for n, m in zip(counts, means)) / jnp.maximum(count, 1.0)
    square = sum(squares) + sum(n * (m - mean) * (m - mean) for n, m in zip(counts, means))
    return mean, square, count


def rows_of(refs):
    return [[ref[copy, i : i + 1, :] for i in range(3)] for ref in refs for copy in range(ref.shape[0])]


def merge_kernel(stats_ref, out_ref):
    for i, row in enumerate(merged(rows_of([stats_ref]))):
        for copy in range(out_ref.shape[0]):
            out_ref[copy, i : i + 1, :] = row


def merge(stats, copies):
    return pl.pallas_call(
        merge_kernel,
        out_shape=jax.ShapeDtypeStruct((copies,) + stats.shape[1:], jnp.float32),
        in_specs=[pl.BlockSpec(memory_space=VMEM)],
        out_specs=pl.BlockSpec(memory_space=VMEM),
        compiler_params=params(8),
        cost_estimate=cost(10**8),
        name="merge",
    )(stats)


def back_kernel(stat_count, place_ref, gain_ref, shift_ref, *refs):
    stat_refs, refs = refs[:stat_count], refs[stat_count:]
    *conv_refs, out_ref, rows_out, sems, weights = refs
    convs, weight_refs = conv_refs[:3], conv_refs[3:]
    row_count, wide = convs[0].shape
    if len(weight_refs) > 1:
        depth = weight_refs[0].shape[0]
        for i, weight_ref in enumerate(weight_refs[:2]):
            at = pl.multiple_of(lax.bitwise_xor(place_ref[0], i) * depth, depth)
            weights[pl.ds(at, depth), :] = weight_ref[...]
        half = depth // 2
        for i, weight_ref in enumerate(weight_refs[2:]):
            at = lax.bitwise_xor(place_ref[0], 2 + i // 2) * depth
            at += lax.bitwise_xor(place_ref[3], i % 2) * half
            weights[pl.ds(pl.multiple_of(at, half), half), :] = weight_ref[...]
    else:
        weights[...] = weight_refs[0][...]
    mean, square, count = merged(rows_of(stat_refs))
    scale = lax.rsqrt(square / count + 1e-05) * gain_ref[...]
    shift = shift_ref[...]
    pieces, rows, columns = rows_out.shape
    across = out_ref.shape[1] // columns
    copies = []
    for piece in range(pieces // across):
        here = slice(piece * rows, (piece + 1) * rows)
        parts = []
        for i, conv_ref in enumerate(convs):
            lanes = slice(i * wide, (i + 1) * wide)
            scaled = (conv_ref[here, :] - mean[:, lanes]) * scale[:, lanes] + shift[:, lanes]
            parts.append((scaled * jax.nn.sigmoid(scaled)).astype(jnp.bfloat16))
        activated = jnp.concatenate(parts, axis=1)
        position = place_ref[1] + piece * rows + lax.broadcasted_iota(jnp.int32, (rows, 1), 0)
        for j in range(across):
            lanes = slice(j * columns, (j + 1) * columns)
            result = jnp.dot(activated, weights[:, lanes], preferred_element_type=jnp.float32)
            slot = piece * across + j
            rows_out[slot] = jnp.where(position < place_ref[2], result, 0.0).astype(jnp.bfloat16)
            copy = pltpu.make_async_copy(rows_out.at[slot], out_ref.at[here, lanes], sems.at[slot])
            copy.start()
            copies.append(copy)
    for copy in copies:
        copy.wait()


def back(place, stats, gain, shift, convs, weights):
    row_count = convs[0].shape[0]
    channels, width = gain.shape[1], weights[0].shape[1]
    pieces, across = 4, 2
    return pl.pallas_call(
        functools.partial(back_kernel, len(stats)),
        out_shape=jax.ShapeDtypeStruct((row_count, width), jnp.bfloat16),
        in_specs=[pl.BlockSpec(memory_space=pltpu.SMEM)]
        + [pl.BlockSpec(memory_space=VMEM)] * (2 + len(stats) + len(convs) + len(weights)),
        out_specs=pl.BlockSpec(memory_space=pl.ANY),
        scratch_shapes=[
            VMEM((pieces, row_count * across // pieces, width // across), jnp.bfloat16),
            pltpu.SemaphoreType.DMA((pieces,)),
            VMEM((channels, width), jnp.bfloat16),
        ],
        compiler_params=params(10),
        cost_estimate=cost(10**9),
        name="back",
    )(place, gain, shift, *stats, *convs, *weights)


def everyones(copies, groups):
    return lax.all_to_all(copies, ("fsdp", "ctx"), 0, 0, axis_index_groups=groups, tiled=True)


def tie(*values):
    return lax.optimization_barrier(values)


def body(frames, lengths, ln_gain, w_in, dw_kernel, bn_gain, bn_shift, w_out):
    _, row_count, model_width = frames.shape
    channels = dw_kernel.shape[1]
    wide = channels // 3
    ctx, fsdp = lax.axis_index("ctx"), lax.axis_index("fsdp")
    ctx_count, fsdp_count = lax.axis_size("ctx"), lax.axis_size("fsdp")
    direct = fsdp_count == 4 and ctx_count == 8
    rows = frames[0]
    gain = ln_gain[None]
    parity = lax.rem(ctx, 2)
    place = jnp.stack([fsdp, ctx * row_count, lengths[0], parity]).astype(jnp.int32)
    ends = ctx_count - 1
    down, up = [(i, i + 1) for i in range(ends)], [(i + 1, i) for i in range(ends)]
    both = ("fsdp", "ctx")
    member = lambda f, p: f * ctx_count + p

    def front(block, weights, *extra):
        return front_block(block, wide, place, normed, weights, dw_kernel, *extra)

    if direct:
        half, *parts, inner, outer = cut(parity[None].astype(jnp.int32), w_in, w_out, rows, wide)
        out_halves = [swap(half, "fsdp", 2)]
        over_x = [[swap(part, "fsdp", 2)] for part in parts]
        inner = swap(inner, "ctx", 1)
        pairs = [(i, i + 1) for i in range(1, ends, 2)]
        outer = lax.ppermute(outer, "ctx", pairs + [(j, i) for i, j in pairs])
        parts[0], shard, w_out = tie(parts[0], w_in, w_out)
        across = swap(shard, "fsdp", 1)
        normed = normalize_rows(place, rows, inner, outer, gain)
        normed, out_halves[0], over_x[0][0] = tie(normed, out_halves[0], over_x[0][0])
        over_x[0].append(swap(over_x[0][0], "ctx", 1))
        out_halves.append(swap(out_halves[0], "ctx", 1))
        partials = list(near_product(place, normed, w_in, across))
        partials[0], *ready = tie(partials[0], over_x[0][1], over_x[1][0], out_halves[1])
        over_x[0][1], over_x[1][0], out_halves[1] = ready
        over_x[1].append(swap(over_x[1][0], "ctx", 1))
        out_weights = [w_out, swap(w_out, "fsdp", 1), *out_halves]
        out_weights += [swap(part, "fsdp", 1) for part in out_halves]

        def weights_of(block):
            return [partials[block], *over_x[block], *(swap(part, "fsdp", 1) for part in over_x[block])]

        conv_one, stat_one = front(0, weights_of(0))
        conv_one, over_x[1][1], over_x[2][0] = tie(conv_one, over_x[1][1], over_x[2][0])
        weights = [weights_of(1), weights_of(2)]
        conv_two, stat_two = front(1, weights[0])
        conv_three, stats = front(2, weights[1], (stat_one, stat_two), 1)
        convs = [conv_one, conv_two, conv_three]

        def others(flips):
            return [
                lax.ppermute(
                    stats,
                    both,
                    [(member(f, p), member(f ^ df, p ^ dp)) for f in range(4) for p in range(8)],
                )
                for df, dp in flips
            ]

        def union(parts):
            return jnp.stack(merged([[part[:, i] for i in range(3)] for part in parts]), 1)

        stats = union([stats] + others([(1, 0)]))
        stats = union([stats] + others([(2, 0), (0, 1), (2, 1)]))
        stats = [stats] + others([(0, 2), (0, 4), (0, 6)])
    else:
        full_in = lax.all_gather(w_in, "fsdp", axis=0, tiled=True)
        out_weights = [lax.all_gather(w_out, "fsdp", axis=0, tiled=True)]
        before = lax.ppermute(rows[-HALO:], "ctx", down)
        after = lax.ppermute(rows[:HALO], "ctx", up)
        inner = jnp.where(parity == 0, after, before)
        outer = jnp.where(parity == 0, before, after)
        normed = normalize_rows(place, rows, inner, outer, gain)
        near_by = 2 if ctx_count % 2 == 0 else 1
        groups = [
            [member(f, p + i) for f in range(fsdp_count) for i in range(near_by)]
            for p in range(0, ctx_count, near_by)
        ]
        convs, stats = [None] * 3, []
        for block in range(3):
            extra = (stats, len(groups[0])) if block == 2 else ()
            convs[block], stat = front(block, [full_in], *extra)
            stats.append(stat)
        stats = merge(everyones(stats[2], groups), len(groups))
        groups = [
            [member(f, p + i) for p in range(0, ctx_count, near_by)]
            for f in range(fsdp_count)
            for i in range(near_by)
        ]
        stats = [everyones(stats, groups)]
    result = back(place, stats, bn_gain[None], bn_shift[None], convs, out_weights)
    return result[None]


def solution(mesh):
    return jax.shard_map(
        body,
        mesh=mesh,
        in_specs=(
            P("fsdp", "ctx", None),
            P("fsdp"),
            P(),
            P("fsdp", None),
            P(),
            P(),
            P(),
            P("fsdp", None),
        ),
        out_specs=P("fsdp", "ctx", None),
        check_vma=False,
    )
```

```python
import functools

import jax
import jax.numpy as jnp
from jax import lax
from jax.experimental import pallas as pl
from jax.experimental.pallas import tpu as pltpu
from jax.sharding import PartitionSpec as P

HALO = 16
LANES = 128
MIB = 1024 * 1024
VMEM = pltpu.VMEM
ORDER = (2, 0, 1)


def cost(flops):
    return pl.CostEstimate(flops=flops, bytes_accessed=0, transcendentals=0)


def params(mib):
    return pltpu.CompilerParams(vmem_limit_bytes=mib * MIB)


def swap(value, axis, bit):
    return lax.ppermute(value, axis, [(i, i ^ bit) for i in range(lax.axis_size(axis))])


def copy_all(pairs, sems):
    copies = [pltpu.make_async_copy(source, target, sems.at[i]) for i, (source, target) in enumerate(pairs)]
    for copy in copies:
        copy.start()
    for copy in copies:
        copy.wait()


def block_columns(shard_ref, block, wide, ref):
    channels = shard_ref.shape[1] // 2
    starts = [i * channels + block * wide for i in range(2)]
    return [
        (shard_ref.at[:, at : at + wide], ref.at[:, i * wide : (i + 1) * wide])
        for i, at in enumerate(starts)
    ]


def first_cut_kernel(wide, place_ref, shard_ref, half_ref, block_ref, sems):
    channels = shard_ref.shape[1] // 2
    side = pl.ds(pl.multiple_of(place_ref[3] * channels + 2 * wide, wide), wide)
    copy_all([(shard_ref.at[:, side], half_ref), *block_columns(shard_ref, 0, wide, block_ref)], sems)


def second_cut_kernel(wide, place_ref, shard_ref, out_shard_ref, rows_ref, *refs):
    block_ref, quarter_ref, inner_ref, outer_ref, sems = refs
    odd = place_ref[3]
    depth, across = quarter_ref.shape
    quarter = out_shard_ref.at[
        pl.ds(pl.multiple_of(odd * depth, depth), depth),
        pl.ds(pl.multiple_of(place_ref[4] * across, across), across),
    ]
    last = rows_ref.shape[0] - HALO
    inner = rows_ref.at[pl.ds(pl.multiple_of((1 - odd) * last, HALO), HALO), :]
    outer = rows_ref.at[pl.ds(pl.multiple_of(odd * last, HALO), HALO), :]
    pairs = [(quarter, quarter_ref), (inner, inner_ref), (outer, outer_ref)]
    copy_all(block_columns(shard_ref, 1, wide, block_ref) + pairs, sems)


def cut(kernel, wide, place, arrays, shapes):
    return pl.pallas_call(
        functools.partial(kernel, wide),
        out_shape=[jax.ShapeDtypeStruct(shape, jnp.bfloat16) for shape in shapes],
        in_specs=[pl.BlockSpec(memory_space=pltpu.SMEM)]
        + [pl.BlockSpec(memory_space=pltpu.HBM)] * len(arrays),
        out_specs=[pl.BlockSpec(memory_space=VMEM)] * len(shapes),
        scratch_shapes=[pltpu.SemaphoreType.DMA((5,))],
        compiler_params=params(40),
        cost_estimate=cost(10**8),
        name="cut",
    )(place, *arrays)


def normalize(values, gain):
    values = values.astype(jnp.float32)
    centre = jnp.mean(values, axis=-1, keepdims=True)
    deviate = values - centre
    spread = jnp.mean(deviate * deviate, axis=-1, keepdims=True)
    return (deviate * lax.rsqrt(spread + 1e-05) * gain).astype(jnp.bfloat16)


def norm_kernel(place_ref, rows_ref, inner_ref, outer_ref, gain_ref, out_ref):
    step = 64
    row_count = rows_ref.shape[0]

    @pl.loop(0, row_count // step)
    def _(i):
        at = pl.multiple_of(i * step, step)
        out_ref[pl.ds(HALO + at, step), :] = normalize(rows_ref[pl.ds(at, step), :], gain_ref[...])

    odd = place_ref[3]
    at = pl.multiple_of((1 - odd) * (HALO + row_count), HALO)
    out_ref[pl.ds(at, HALO), :] = normalize(inner_ref[...], gain_ref[...])
    at = pl.multiple_of(odd * (HALO + row_count), HALO)
    out_ref[pl.ds(at, HALO), :] = normalize(outer_ref[...], gain_ref[...])


def normalize_rows(place, rows, inner, outer, gain):
    row_count, width = rows.shape
    return pl.pallas_call(
        norm_kernel,
        out_shape=jax.ShapeDtypeStruct((row_count + 2 * HALO, width), jnp.bfloat16),
        in_specs=[pl.BlockSpec(memory_space=pltpu.SMEM)] + [pl.BlockSpec(memory_space=VMEM)] * 4,
        out_specs=pl.BlockSpec(memory_space=VMEM),
        compiler_params=params(4),
        cost_estimate=cost(10**8),
        name="layer_norm",
    )(place, rows, inner, outer, gain)


def near_kernel(place_ref, normed_ref, own_ref, other_ref, *refs):
    *out_refs, weights = refs
    own = place_ref[0]
    depth, width = own_ref.shape
    for i, weight_ref in enumerate((own_ref, other_ref)):
        at = pl.multiple_of(lax.bitwise_xor(own % 2, i) * depth, depth)
        weights[pl.ds(at, depth), :] = weight_ref[...]
    near = pl.ds(pl.multiple_of(own // 2 * (2 * depth), 2 * depth), 2 * depth)
    wide = out_refs[0].shape[1] // 2
    channels = width // 2
    for block, out_ref in enumerate(out_refs):
        for i in range(2):
            columns = slice(i * channels + block * wide, i * channels + (block + 1) * wide)
            out_ref[:, i * wide : (i + 1) * wide] = jnp.dot(
                normed_ref[:, near], weights[:, columns], preferred_element_type=jnp.float32
            )


def near_product(place, normed, own, other):
    ext_rows, width = normed.shape
    partial = jax.ShapeDtypeStruct((ext_rows, width // 3), jnp.float32)
    return pl.pallas_call(
        near_kernel,
        out_shape=[partial] * 3,
        in_specs=[pl.BlockSpec(memory_space=pltpu.SMEM)] + [pl.BlockSpec(memory_space=VMEM)] * 3,
        out_specs=[pl.BlockSpec(memory_space=VMEM)] * 3,
        scratch_shapes=[VMEM((2 * own.shape[0], width), jnp.bfloat16)],
        compiler_params=params(8),
        cost_estimate=cost(10**8),
        name="near",
    )(place, normed, own, other)


def front_kernel(block, earlier, place_ref, normed_ref, *refs):
    refs, earlier_refs = refs[earlier:], refs[:earlier]
    *weight_refs, taps_ref, conv_ref, stats_ref, weights, gated = refs
    ext_rows = normed_ref.shape[0]
    row_count, wide = conv_ref.shape
    taps, channels = taps_ref.shape
    if len(weight_refs) > 1:
        near_ref, *far_refs = weight_refs
        own = place_ref[0]
        depth = far_refs[0].shape[0]
        halves = len(far_refs) // 2
        for i in range(2):
            at = pl.multiple_of(lax.bitwise_xor(own % 2, i) * depth, depth)
            if halves == 1:
                weights[pl.ds(at, depth), :] = far_refs[i][...]
                continue
            for j in range(2):
                column = pl.multiple_of(lax.bitwise_xor(place_ref[3], j) * wide, wide)
                weights[pl.ds(at, depth), pl.ds(column, wide)] = far_refs[2 * i + j][...]
        far = pl.ds(pl.multiple_of((1 - own // 2) * (2 * depth), 2 * depth), 2 * depth)
        normed = normed_ref[:, far]
        value = near_ref[:, 0:wide] + jnp.dot(normed, weights[:, 0:wide], preferred_element_type=jnp.float32)
        gate = near_ref[:, wide:] + jnp.dot(normed, weights[:, wide:], preferred_element_type=jnp.float32)
    else:
        columns = slice(block * wide, (block + 1) * wide)
        value = jnp.dot(normed_ref[...], weight_refs[0][:, columns], preferred_element_type=jnp.float32)
        columns = slice(channels + block * wide, channels + (block + 1) * wide)
        gate = jnp.dot(normed_ref[...], weight_refs[0][:, columns], preferred_element_type=jnp.float32)
    start, length = place_ref[1], place_ref[2]
    position = start - HALO + lax.broadcasted_iota(jnp.int32, (ext_rows, 1), 0)
    valid = (position >= 0) & (position < length)
    kept = jnp.where(valid, value * jax.nn.sigmoid(gate), 0.0)
    kept = kept.astype(jnp.bfloat16).astype(jnp.float32)
    first = HALO - (taps - 1) // 2
    step = 64
    for unit in range(wide // LANES):
        lanes = slice(unit * LANES, (unit + 1) * LANES)
        tap_lanes = slice(block * wide + unit * LANES, block * wide + (unit + 1) * LANES)
        column = kept[:, lanes]
        gated[0] = column
        for phase in range(1, 8):
            gated[phase] = pltpu.roll(column, ext_rows - phase, 0)
        for at in range(0, row_count, step):
            acc = None
            for tap in range(taps):
                base = at + (first + tap) // 8 * 8
                term = gated[(first + tap) % 8, base : base + step, :] * taps_ref[tap : tap + 1, tap_lanes]
                acc = term if acc is None else acc + term
            conv_ref[at : at + step, lanes] = acc
    here = start + lax.broadcasted_iota(jnp.int32, (row_count, 1), 0) < length
    count = jnp.clip(length - start, 0, row_count).astype(jnp.float32)
    conv = conv_ref[...]
    mean = jnp.sum(jnp.where(here, conv, 0.0), axis=0, keepdims=True) / jnp.maximum(count, 1.0)
    deviate = jnp.where(here, conv - mean, 0.0)
    square = jnp.sum(deviate * deviate, axis=0, keepdims=True)
    stats = [mean, square, jnp.full((1, wide), count)]
    if not earlier_refs:
        for i, row in enumerate(stats):
            stats_ref[i : i + 1, :] = row
        return
    for i, row in enumerate(stats):
        for copy in range(stats_ref.shape[0]):
            stats_ref[copy, i : i + 1, block * wide : (block + 1) * wide] = row
            for other, ref in zip([j for j in ORDER if j != block], earlier_refs):
                stats_ref[copy, i : i + 1, other * wide : (other + 1) * wide] = ref[i : i + 1, :]


def front_block(block, wide, place, normed, weights, dw_kernel, earlier=(), copies=1):
    ext_rows, width = normed.shape
    row_count = ext_rows - 2 * HALO
    depth = 2 * weights[1].shape[0] if len(weights) > 1 else 16
    stats_shape = (copies, 3, dw_kernel.shape[1]) if earlier else (3, wide)
    return pl.pallas_call(
        functools.partial(front_kernel, block, len(earlier)),
        out_shape=(
            jax.ShapeDtypeStruct((row_count, wide), jnp.float32),
            jax.ShapeDtypeStruct(stats_shape, jnp.float32),
        ),
        in_specs=[pl.BlockSpec(memory_space=pltpu.SMEM)]
        + [pl.BlockSpec(memory_space=VMEM)] * (2 + len(weights) + len(earlier)),
        out_specs=[pl.BlockSpec(memory_space=VMEM)] * 2,
        scratch_shapes=[
            VMEM((depth, 2 * wide), jnp.bfloat16),
            VMEM((8, ext_rows, LANES), jnp.float32),
        ],
        compiler_params=params(10),
        cost_estimate=cost(10**8),
        name="front",
    )(place, normed, *earlier, *weights, dw_kernel)


def merged(parts):
    means, squares, counts = zip(*parts)
    count = sum(counts)
    mean = sum(n * m for n, m in zip(counts, means)) / jnp.maximum(count, 1.0)
    square = sum(squares) + sum(n * (m - mean) * (m - mean) for n, m in zip(counts, means))
    return mean, square, count


def rows_of(refs):
    return [[ref[copy, i : i + 1, :] for i in range(3)] for ref in refs for copy in range(ref.shape[0])]


def merge_kernel(stats_ref, out_ref):
    for i, row in enumerate(merged(rows_of([stats_ref]))):
        for copy in range(out_ref.shape[0]):
            out_ref[copy, i : i + 1, :] = row


def merge(stats, copies):
    return pl.pallas_call(
        merge_kernel,
        out_shape=jax.ShapeDtypeStruct((copies,) + stats.shape[1:], jnp.float32),
        in_specs=[pl.BlockSpec(memory_space=VMEM)],
        out_specs=pl.BlockSpec(memory_space=VMEM),
        compiler_params=params(8),
        cost_estimate=cost(10**8),
        name="merge",
    )(stats)


def back_kernel(stat_count, place_ref, gain_ref, shift_ref, *refs):
    stat_refs, refs = refs[:stat_count], refs[stat_count:]
    *conv_refs, out_ref, rows_out, sems, weights = refs
    convs, weight_refs = conv_refs[:3], conv_refs[3:]
    row_count, wide = convs[0].shape
    if len(weight_refs) > 1:
        depth = weight_refs[0].shape[0]
        for i, weight_ref in enumerate(weight_refs[:2]):
            at = pl.multiple_of(lax.bitwise_xor(place_ref[0], i) * depth, depth)
            weights[pl.ds(at, depth), :] = weight_ref[...]
        half = depth // 2
        for i, weight_ref in enumerate(weight_refs[2:]):
            at = lax.bitwise_xor(place_ref[0], 2 + i // 2) * depth
            at += lax.bitwise_xor(place_ref[3], i % 2) * half
            weights[pl.ds(pl.multiple_of(at, half), half), :] = weight_ref[...]
    else:
        weights[...] = weight_refs[0][...]
    mean, square, count = merged(rows_of(stat_refs))
    scale = lax.rsqrt(square / count + 1e-05) * gain_ref[...]
    shift = shift_ref[...]
    pieces, rows, columns = rows_out.shape
    across = out_ref.shape[1] // columns
    copies = []
    for piece in range(pieces // across):
        here = slice(piece * rows, (piece + 1) * rows)
        parts = []
        for i, conv_ref in enumerate(convs):
            lanes = slice(i * wide, (i + 1) * wide)
            scaled = (conv_ref[here, :] - mean[:, lanes]) * scale[:, lanes] + shift[:, lanes]
            parts.append((scaled * jax.nn.sigmoid(scaled)).astype(jnp.bfloat16))
        activated = jnp.concatenate(parts, axis=1)
        position = place_ref[1] + piece * rows + lax.broadcasted_iota(jnp.int32, (rows, 1), 0)
        for j in range(across):
            lanes = slice(j * columns, (j + 1) * columns)
            result = jnp.dot(activated, weights[:, lanes], preferred_element_type=jnp.float32)
            slot = piece * across + j
            rows_out[slot] = jnp.where(position < place_ref[2], result, 0.0).astype(jnp.bfloat16)
            copy = pltpu.make_async_copy(rows_out.at[slot], out_ref.at[here, lanes], sems.at[slot])
            copy.start()
            copies.append(copy)
    for copy in copies:
        copy.wait()


def back(place, stats, gain, shift, convs, weights):
    row_count = convs[0].shape[0]
    channels, width = gain.shape[1], weights[0].shape[1]
    pieces, across = 4, 2
    return pl.pallas_call(
        functools.partial(back_kernel, len(stats)),
        out_shape=jax.ShapeDtypeStruct((row_count, width), jnp.bfloat16),
        in_specs=[pl.BlockSpec(memory_space=pltpu.SMEM)]
        + [pl.BlockSpec(memory_space=VMEM)] * (2 + len(stats) + len(convs) + len(weights)),
        out_specs=pl.BlockSpec(memory_space=pl.ANY),
        scratch_shapes=[
            VMEM((pieces, row_count * across // pieces, width // across), jnp.bfloat16),
            pltpu.SemaphoreType.DMA((pieces,)),
            VMEM((channels, width), jnp.bfloat16),
        ],
        compiler_params=params(10),
        cost_estimate=cost(10**9),
        name="back",
    )(place, gain, shift, *stats, *convs, *weights)


def everyones(copies, groups):
    return lax.all_to_all(copies, ("fsdp", "ctx"), 0, 0, axis_index_groups=groups, tiled=True)


def tie(*values):
    return lax.optimization_barrier(values)


def body(frames, lengths, ln_gain, w_in, dw_kernel, bn_gain, bn_shift, w_out):
    _, row_count, model_width = frames.shape
    channels = dw_kernel.shape[1]
    wide = channels // 3
    ctx, fsdp = lax.axis_index("ctx"), lax.axis_index("fsdp")
    ctx_count, fsdp_count = lax.axis_size("ctx"), lax.axis_size("fsdp")
    direct = fsdp_count == 4 and ctx_count == 8
    rows = frames[0]
    gain = ln_gain[None]
    parity, pair = lax.rem(ctx, 2), lax.rem(ctx // 2, 2)
    place = jnp.stack([fsdp, ctx * row_count, lengths[0], parity, pair]).astype(jnp.int32)
    ends = ctx_count - 1
    down, up = [(i, i + 1) for i in range(ends)], [(i + 1, i) for i in range(ends)]
    both = ("fsdp", "ctx")
    member = lambda f, p: f * ctx_count + p

    def front(block, weights, *extra):
        return front_block(block, wide, place, normed, weights, dw_kernel, *extra)

    if direct:
        depth, out_depth = w_in.shape[0], w_out.shape[0]
        half, block = cut(first_cut_kernel, wide, place, [w_in], [(depth, wide), (depth, 2 * wide)])
        over_x = {2: [swap(half, "fsdp", 2)], 0: [swap(block, "fsdp", 2)]}
        half, later_in, later_out, later_rows = tie(half, w_in, w_out, rows)
        shapes = [(depth, 2 * wide), (out_depth // 2, model_width // 2)] + [(HALO, model_width)] * 2
        block, quarter, inner, outer = cut(
            second_cut_kernel, wide, place, [later_in, later_out, later_rows], shapes
        )
        over_x[1] = [swap(block, "fsdp", 2)]
        quarter = swap(quarter, "fsdp", 2)
        across = swap(later_in, "fsdp", 1)
        inner = swap(inner, "ctx", 1)
        pairs = [(i, i + 1) for i in range(1, ends, 2)]
        outer = lax.ppermute(outer, "ctx", pairs + [(j, i) for i, j in pairs])
        later_rows, over_x[2][0] = tie(rows, over_x[2][0])
        normed = normalize_rows(place, later_rows, inner, outer, gain)
        normed, quarter = tie(normed, quarter)
        over_x[2].append(swap(over_x[2][0], "ctx", 1))
        beyond_half = swap(over_x[2][0], "fsdp", 1)
        other = swap(quarter, "ctx", 2)
        partials = list(near_product(place, normed, w_in, across))
        partials[2], beyond_half = tie(partials[2], beyond_half)
        partials[2], over_x[2][1], other, w_out = tie(partials[2], over_x[2][1], other, w_out)
        half = jnp.where(
            pair == 0, jnp.concatenate([quarter, other], 1), jnp.concatenate([other, quarter], 1)
        )
        out_halves = [half, swap(half, "ctx", 1)]

        beyond_two = [beyond_half, swap(over_x[2][1], "fsdp", 1)]
        partials[2], over_x[0][0] = tie(partials[2], over_x[0][0])
        beyond_zero = swap(over_x[0][0], "fsdp", 1)
        conv_one, stat_one = front(2, [partials[2], *over_x[2], *beyond_two])
        conv_one, partials[0] = tie(conv_one, partials[0])
        conv_two, stat_two = front(0, [partials[0], *over_x[0], beyond_zero])
        conv_two, over_x[1][0], out_halves[1] = tie(conv_two, over_x[1][0], out_halves[1])
        out_weights = [w_out, swap(w_out, "fsdp", 1), *out_halves]
        out_weights += [swap(part, "fsdp", 1) for part in out_halves]
        beyond_one = swap(over_x[1][0], "fsdp", 1)
        conv_three, stats = front(1, [partials[1], *over_x[1], beyond_one], (stat_one, stat_two), 1)
        stats, *out_weights = tie(stats, *out_weights)
        convs = [conv_two, conv_three, conv_one]

        def others(flips):
            return [
                lax.ppermute(
                    stats,
                    both,
                    [(member(f, p), member(f ^ df, p ^ dp)) for f in range(4) for p in range(8)],
                )
                for df, dp in flips
            ]

        def union(parts):
            return jnp.stack(merged([[part[:, i] for i in range(3)] for part in parts]), 1)

        stats = union([stats] + others([(1, 0)]))
        stats = union([stats] + others([(2, 0), (0, 1), (2, 1)]))
        stats = [stats] + others([(0, 2), (0, 4), (0, 6)])
    else:
        full_in = lax.all_gather(w_in, "fsdp", axis=0, tiled=True)
        out_weights = [lax.all_gather(w_out, "fsdp", axis=0, tiled=True)]
        before = lax.ppermute(rows[-HALO:], "ctx", down)
        after = lax.ppermute(rows[:HALO], "ctx", up)
        inner = jnp.where(parity == 0, after, before)
        outer = jnp.where(parity == 0, before, after)
        normed = normalize_rows(place, rows, inner, outer, gain)
        near_by = 2 if ctx_count % 2 == 0 else 1
        groups = [
            [member(f, p + i) for f in range(fsdp_count) for i in range(near_by)]
            for p in range(0, ctx_count, near_by)
        ]
        convs, stats = [None] * 3, []
        for block in ORDER:
            extra = (stats, len(groups[0])) if block == ORDER[-1] else ()
            convs[block], stat = front(block, [full_in], *extra)
            stats.append(stat)
        stats = merge(everyones(stats[2], groups), len(groups))
        groups = [
            [member(f, p + i) for p in range(0, ctx_count, near_by)]
            for f in range(fsdp_count)
            for i in range(near_by)
        ]
        stats = [everyones(stats, groups)]
    result = back(place, stats, bn_gain[None], bn_shift[None], convs, out_weights)
    return result[None]


def solution(mesh):
    return jax.shard_map(
        body,
        mesh=mesh,
        in_specs=(
            P("fsdp", "ctx", None),
            P("fsdp"),
            P(),
            P("fsdp", None),
            P(),
            P(),
            P(),
            P("fsdp", None),
        ),
        out_specs=P("fsdp", "ctx", None),
        check_vma=False,
    )
```

```python
import functools

import jax
import jax.numpy as jnp
from jax import lax
from jax.experimental import pallas as pl
from jax.experimental.pallas import tpu as pltpu
from jax.sharding import PartitionSpec as P

HALO = 16
LANES = 128
MIB = 1024 * 1024
VMEM = pltpu.VMEM
ORDER = (2, 0, 1)


def cost(flops):
    return pl.CostEstimate(flops=flops, bytes_accessed=0, transcendentals=0)


def params(mib):
    return pltpu.CompilerParams(vmem_limit_bytes=mib * MIB)


def swap(value, axis, bit):
    return lax.ppermute(value, axis, [(i, i ^ bit) for i in range(lax.axis_size(axis))])


def normalize(values, gain):
    values = values.astype(jnp.float32)
    centre = jnp.mean(values, axis=-1, keepdims=True)
    deviate = values - centre
    spread = jnp.mean(deviate * deviate, axis=-1, keepdims=True)
    return (deviate * lax.rsqrt(spread + 1e-05) * gain).astype(jnp.bfloat16)


def norm_kernel(rows_ref, gain_ref, out_ref):
    step = 64

    @pl.loop(0, rows_ref.shape[0] // step)
    def _(i):
        here = pl.ds(pl.multiple_of(i * step, step), step)
        out_ref[here, :] = normalize(rows_ref[here, :], gain_ref[...])


def normalize_rows(rows, gain):
    row_count, width = rows.shape
    return pl.pallas_call(
        norm_kernel,
        out_shape=jax.ShapeDtypeStruct((row_count, width), jnp.bfloat16),
        in_specs=[pl.BlockSpec(memory_space=VMEM)] * 2,
        out_specs=pl.BlockSpec(memory_space=VMEM),
        compiler_params=params(4),
        cost_estimate=cost(10**8),
        name="layer_norm",
    )(rows, gain)


def near_kernel(place_ref, rows_ref, inner_ref, outer_ref, gain_ref, *refs):
    row_count = rows_ref.shape[0]
    gain = gain_ref[...]
    *weight_refs, ext_ref = refs[:3] if len(refs) > 1 else refs
    odd = place_ref[3]
    at = pl.multiple_of((1 - odd) * (HALO + row_count), HALO)
    ext_ref[pl.ds(at, HALO), :] = normalize(inner_ref[...], gain)
    at = pl.multiple_of(odd * (HALO + row_count), HALO)
    ext_ref[pl.ds(at, HALO), :] = normalize(outer_ref[...], gain)
    ext_ref[HALO : HALO + row_count, :] = rows_ref[...]
    if not weight_refs:
        return
    *out_refs, weights = refs[3:]
    own = place_ref[0]
    depth, width = weight_refs[0].shape
    for i, weight_ref in enumerate(weight_refs):
        at = pl.multiple_of(lax.bitwise_xor(own % 2, i) * depth, depth)
        weights[pl.ds(at, depth), :] = weight_ref[...]
    near = pl.ds(pl.multiple_of(own // 2 * (2 * depth), 2 * depth), 2 * depth)
    wide = out_refs[0].shape[1] // 2
    channels = width // 2
    for block, out_ref in enumerate(out_refs):
        for i in range(2):
            columns = slice(i * channels + block * wide, i * channels + (block + 1) * wide)
            out_ref[:, i * wide : (i + 1) * wide] = jnp.dot(
                ext_ref[:, near], weights[:, columns], preferred_element_type=jnp.float32
            )


def near_product(place, rows, inner, outer, gain, *shards):
    row_count, width = rows.shape
    ext_rows = row_count + 2 * HALO
    shapes = [jax.ShapeDtypeStruct((ext_rows, width), jnp.bfloat16)]
    scratch = []
    if shards:
        shapes += [jax.ShapeDtypeStruct((ext_rows, width // 3), jnp.float32)] * 3
        scratch.append(VMEM((2 * shards[0].shape[0], width), jnp.bfloat16))
    return pl.pallas_call(
        near_kernel,
        out_shape=shapes,
        in_specs=[pl.BlockSpec(memory_space=pltpu.SMEM)]
        + [pl.BlockSpec(memory_space=VMEM)] * (4 + len(shards)),
        out_specs=[pl.BlockSpec(memory_space=VMEM)] * len(shapes),
        scratch_shapes=scratch,
        compiler_params=params(8),
        cost_estimate=cost(10**8),
        name="near",
    )(place, rows, inner, outer, gain, *shards)


def front_kernel(block, earlier, place_ref, normed_ref, *refs):
    refs, earlier_refs = refs[earlier:], refs[:earlier]
    *weight_refs, taps_ref, conv_ref, stats_ref, weights, gated = refs
    ext_rows = normed_ref.shape[0]
    row_count, wide = conv_ref.shape
    taps, channels = taps_ref.shape
    if len(weight_refs) > 1:
        near_ref, *far_refs = weight_refs
        own = place_ref[0]
        depth = far_refs[0].shape[0]
        halves = len(far_refs) // 2
        for i in range(2):
            at = pl.multiple_of(lax.bitwise_xor(own % 2, i) * depth, depth)
            if halves == 1:
                weights[pl.ds(at, depth), :] = far_refs[i][...]
                continue
            for j in range(2):
                column = pl.multiple_of(lax.bitwise_xor(place_ref[3], j) * wide, wide)
                weights[pl.ds(at, depth), pl.ds(column, wide)] = far_refs[2 * i + j][...]
        far = pl.ds(pl.multiple_of((1 - own // 2) * (2 * depth), 2 * depth), 2 * depth)
        normed = normed_ref[:, far]
        value = near_ref[:, 0:wide] + jnp.dot(normed, weights[:, 0:wide], preferred_element_type=jnp.float32)
        gate = near_ref[:, wide:] + jnp.dot(normed, weights[:, wide:], preferred_element_type=jnp.float32)
    else:
        columns = slice(block * wide, (block + 1) * wide)
        value = jnp.dot(normed_ref[...], weight_refs[0][:, columns], preferred_element_type=jnp.float32)
        columns = slice(channels + block * wide, channels + (block + 1) * wide)
        gate = jnp.dot(normed_ref[...], weight_refs[0][:, columns], preferred_element_type=jnp.float32)
    start, length = place_ref[1], place_ref[2]
    position = start - HALO + lax.broadcasted_iota(jnp.int32, (ext_rows, 1), 0)
    valid = (position >= 0) & (position < length)
    kept = jnp.where(valid, value * jax.nn.sigmoid(gate), 0.0)
    kept = kept.astype(jnp.bfloat16).astype(jnp.float32)
    first = HALO - (taps - 1) // 2
    step = 64
    for unit in range(wide // LANES):
        lanes = slice(unit * LANES, (unit + 1) * LANES)
        tap_lanes = slice(block * wide + unit * LANES, block * wide + (unit + 1) * LANES)
        column = kept[:, lanes]
        gated[0] = column
        for phase in range(1, 8):
            gated[phase] = pltpu.roll(column, ext_rows - phase, 0)
        for at in range(0, row_count, step):
            acc = None
            for tap in range(taps):
                base = at + (first + tap) // 8 * 8
                term = gated[(first + tap) % 8, base : base + step, :] * taps_ref[tap : tap + 1, tap_lanes]
                acc = term if acc is None else acc + term
            conv_ref[at : at + step, lanes] = acc
    here = start + lax.broadcasted_iota(jnp.int32, (row_count, 1), 0) < length
    count = jnp.clip(length - start, 0, row_count).astype(jnp.float32)
    conv = conv_ref[...]
    mean = jnp.sum(jnp.where(here, conv, 0.0), axis=0, keepdims=True) / jnp.maximum(count, 1.0)
    deviate = jnp.where(here, conv - mean, 0.0)
    square = jnp.sum(deviate * deviate, axis=0, keepdims=True)
    stats = [mean, square, jnp.full((1, wide), count)]
    if not earlier_refs:
        for i, row in enumerate(stats):
            stats_ref[i : i + 1, :] = row
        return
    for i, row in enumerate(stats):
        for copy in range(stats_ref.shape[0]):
            stats_ref[copy, i : i + 1, block * wide : (block + 1) * wide] = row
            for other, ref in zip([j for j in ORDER if j != block], earlier_refs):
                stats_ref[copy, i : i + 1, other * wide : (other + 1) * wide] = ref[i : i + 1, :]


def front_block(block, wide, place, normed, weights, dw_kernel, earlier=(), copies=1):
    ext_rows, width = normed.shape
    row_count = ext_rows - 2 * HALO
    depth = 2 * weights[1].shape[0] if len(weights) > 1 else 16
    stats_shape = (copies, 3, dw_kernel.shape[1]) if earlier else (3, wide)
    return pl.pallas_call(
        functools.partial(front_kernel, block, len(earlier)),
        out_shape=(
            jax.ShapeDtypeStruct((row_count, wide), jnp.float32),
            jax.ShapeDtypeStruct(stats_shape, jnp.float32),
        ),
        in_specs=[pl.BlockSpec(memory_space=pltpu.SMEM)]
        + [pl.BlockSpec(memory_space=VMEM)] * (2 + len(weights) + len(earlier)),
        out_specs=[pl.BlockSpec(memory_space=VMEM)] * 2,
        scratch_shapes=[
            VMEM((depth, 2 * wide), jnp.bfloat16),
            VMEM((8, ext_rows, LANES), jnp.float32),
        ],
        compiler_params=params(10),
        cost_estimate=cost(10**8),
        name="front",
    )(place, normed, *earlier, *weights, dw_kernel)


def merged(parts):
    means, squares, counts = zip(*parts)
    count = sum(counts)
    mean = sum(n * m for n, m in zip(counts, means)) / jnp.maximum(count, 1.0)
    square = sum(squares) + sum(n * (m - mean) * (m - mean) for n, m in zip(counts, means))
    return mean, square, count


def rows_of(refs):
    return [[ref[copy, i : i + 1, :] for i in range(3)] for ref in refs for copy in range(ref.shape[0])]


def merge_kernel(stats_ref, out_ref):
    for i, row in enumerate(merged(rows_of([stats_ref]))):
        for copy in range(out_ref.shape[0]):
            out_ref[copy, i : i + 1, :] = row


def merge(stats, copies):
    return pl.pallas_call(
        merge_kernel,
        out_shape=jax.ShapeDtypeStruct((copies,) + stats.shape[1:], jnp.float32),
        in_specs=[pl.BlockSpec(memory_space=VMEM)],
        out_specs=pl.BlockSpec(memory_space=VMEM),
        compiler_params=params(8),
        cost_estimate=cost(10**8),
        name="merge",
    )(stats)


def back_kernel(stat_count, place_ref, gain_ref, shift_ref, *refs):
    stat_refs, refs = refs[:stat_count], refs[stat_count:]
    *conv_refs, out_ref, rows_out, sems, weights = refs
    convs, weight_refs = conv_refs[:3], conv_refs[3:]
    row_count, wide = convs[0].shape
    if len(weight_refs) > 1:
        depth, width = weight_refs[0].shape
        for i, weight_ref in enumerate(weight_refs[:2]):
            at = pl.multiple_of(lax.bitwise_xor(place_ref[0], i) * depth, depth)
            weights[pl.ds(at, depth), :] = weight_ref[...]
        for i, weight_ref in enumerate(weight_refs[2:]):
            rows, columns = weight_ref.shape
            at = lax.bitwise_xor(place_ref[0], 2 + i // 4) * depth
            at += lax.bitwise_xor(place_ref[3], i // 2 % 2) * rows
            column = lax.bitwise_xor(place_ref[4], i % 2) * columns
            here = pl.ds(pl.multiple_of(at, rows), rows), pl.ds(pl.multiple_of(column, columns), columns)
            weights[here] = weight_ref[...]
    else:
        weights[...] = weight_refs[0][...]
    mean, square, count = merged(rows_of(stat_refs))
    scale = lax.rsqrt(square / count + 1e-05) * gain_ref[...]
    shift = shift_ref[...]
    pieces, rows, columns = rows_out.shape
    across = out_ref.shape[1] // columns
    copies = []
    for piece in range(pieces // across):
        here = slice(piece * rows, (piece + 1) * rows)
        parts = []
        for i, conv_ref in enumerate(convs):
            lanes = slice(i * wide, (i + 1) * wide)
            scaled = (conv_ref[here, :] - mean[:, lanes]) * scale[:, lanes] + shift[:, lanes]
            parts.append((scaled * jax.nn.sigmoid(scaled)).astype(jnp.bfloat16))
        activated = jnp.concatenate(parts, axis=1)
        position = place_ref[1] + piece * rows + lax.broadcasted_iota(jnp.int32, (rows, 1), 0)
        for j in range(across):
            lanes = slice(j * columns, (j + 1) * columns)
            result = jnp.dot(activated, weights[:, lanes], preferred_element_type=jnp.float32)
            slot = piece * across + j
            rows_out[slot] = jnp.where(position < place_ref[2], result, 0.0).astype(jnp.bfloat16)
            copy = pltpu.make_async_copy(rows_out.at[slot], out_ref.at[here, lanes], sems.at[slot])
            copy.start()
            copies.append(copy)
    for copy in copies:
        copy.wait()


def back(place, stats, gain, shift, convs, weights):
    row_count = convs[0].shape[0]
    channels, width = gain.shape[1], weights[0].shape[1]
    pieces, across = 4, 2
    return pl.pallas_call(
        functools.partial(back_kernel, len(stats)),
        out_shape=jax.ShapeDtypeStruct((row_count, width), jnp.bfloat16),
        in_specs=[pl.BlockSpec(memory_space=pltpu.SMEM)]
        + [pl.BlockSpec(memory_space=VMEM)] * (2 + len(stats) + len(convs) + len(weights)),
        out_specs=pl.BlockSpec(memory_space=pl.ANY),
        scratch_shapes=[
            VMEM((pieces, row_count * across // pieces, width // across), jnp.bfloat16),
            pltpu.SemaphoreType.DMA((pieces,)),
            VMEM((channels, width), jnp.bfloat16),
        ],
        compiler_params=params(10),
        cost_estimate=cost(10**9),
        name="back",
    )(place, gain, shift, *stats, *convs, *weights)


def everyones(copies, groups):
    return lax.all_to_all(copies, ("fsdp", "ctx"), 0, 0, axis_index_groups=groups, tiled=True)


def tie(*values):
    return lax.optimization_barrier(values)


def body(frames, lengths, ln_gain, w_in, dw_kernel, bn_gain, bn_shift, w_out):
    _, row_count, model_width = frames.shape
    channels = dw_kernel.shape[1]
    wide = channels // 3
    ctx, fsdp = lax.axis_index("ctx"), lax.axis_index("fsdp")
    ctx_count, fsdp_count = lax.axis_size("ctx"), lax.axis_size("fsdp")
    direct = fsdp_count == 4 and ctx_count == 8
    rows = frames[0]
    gain = ln_gain[None]
    parity, pair = lax.rem(ctx, 2), lax.rem(ctx // 2, 2)
    place = jnp.stack([fsdp, ctx * row_count, lengths[0], parity, pair]).astype(jnp.int32)
    ends = ctx_count - 1
    down, up = [(i, i + 1) for i in range(ends)], [(i + 1, i) for i in range(ends)]
    both = ("fsdp", "ctx")
    member = lambda f, p: f * ctx_count + p

    def front(block, weights, *extra):
        return front_block(block, wide, place, normed, weights, dw_kernel, *extra)

    if direct:
        last = row_count - HALO
        out_depth, out_width = w_out.shape[0] // 2, model_width // 2

        def columns(shard, block):
            at = block * wide
            return jnp.concatenate([shard[:, at : at + wide], shard[:, channels + at : channels + at + wide]], 1)

        half = lax.dynamic_slice_in_dim(w_in, parity * channels + 2 * wide, wide, axis=1)
        over_x = {2: [swap(half, "fsdp", 2)]}
        half, later_in, later_out, later_rows = tie(half, w_in, w_out, rows)
        block = columns(later_in, 0)
        over_x[0] = [swap(block, "fsdp", 2)]
        quarter = lax.dynamic_slice(later_out, (parity * out_depth, pair * out_width), (out_depth, out_width))
        quarter = swap(quarter, "fsdp", 2)
        inner = lax.dynamic_slice_in_dim(later_rows, (1 - parity) * last, HALO, axis=0)
        outer = lax.dynamic_slice_in_dim(later_rows, parity * last, HALO, axis=0)
        inner = swap(inner, "ctx", 1)
        pairs = [(i, i + 1) for i in range(1, ends, 2)]
        outer = lax.ppermute(outer, "ctx", pairs + [(j, i) for i, j in pairs])
        across = swap(later_in, "fsdp", 1)
        normed = normalize_rows(rows, gain)
        normed, over_x[2][0], later_in = tie(normed, over_x[2][0], later_in)
        over_x[2].append(swap(over_x[2][0], "ctx", 1))
        beyond_half = swap(over_x[2][0], "fsdp", 1)
        normed, part = tie(normed, columns(later_in, 1))
        over_x[1] = [swap(part, "fsdp", 2)]
        normed, *partials = near_product(place, normed, inner, outer, gain, w_in, across)
        partials[2], beyond_half, quarter = tie(partials[2], beyond_half, quarter)
        quarters = [quarter, swap(quarter, "ctx", 2), swap(quarter, "ctx", 1)]
        partials[2], over_x[2][1], w_out = tie(partials[2], over_x[2][1], w_out)

        beyond_two = [beyond_half, swap(over_x[2][1], "fsdp", 1)]
        partials[2], over_x[0][0] = tie(partials[2], over_x[0][0])
        beyond_zero = swap(over_x[0][0], "fsdp", 1)
        conv_one, stat_one = front(2, [partials[2], *over_x[2], *beyond_two])
        conv_one, partials[0], *quarters = tie(conv_one, partials[0], *quarters)
        quarters.append(swap(quarters[1], "ctx", 1))
        beyond_quarters = [swap(part, "fsdp", 1) for part in quarters[:3]]
        conv_two, stat_two = front(0, [partials[0], *over_x[0], beyond_zero])
        conv_two, over_x[1][0] = tie(conv_two, over_x[1][0])
        across_out = swap(w_out, "fsdp", 1)
        beyond_one = swap(over_x[1][0], "fsdp", 1)
        conv_three, stats = front(1, [partials[1], *over_x[1], beyond_one], (stat_one, stat_two), 1)
        stats, across_out, quarters[3], *beyond_quarters = tie(
            stats, across_out, quarters[3], *beyond_quarters
        )
        beyond_quarters.append(swap(quarters[3], "fsdp", 1))
        out_weights = [w_out, across_out, *quarters, *beyond_quarters]
        convs = [conv_two, conv_three, conv_one]

        def others(flips):
            return [
                lax.ppermute(
                    stats,
                    both,
                    [(member(f, p), member(f ^ df, p ^ dp)) for f in range(4) for p in range(8)],
                )
                for df, dp in flips
            ]

        def union(parts):
            return jnp.stack(merged([[part[:, i] for i in range(3)] for part in parts]), 1)

        stats = union([stats] + others([(1, 0)]))
        stats = union([stats] + others([(2, 0), (0, 1), (2, 1)]))
        stats = [stats] + others([(0, 2), (0, 4), (0, 6)])
    else:
        full_in = lax.all_gather(w_in, "fsdp", axis=0, tiled=True)
        out_weights = [lax.all_gather(w_out, "fsdp", axis=0, tiled=True)]
        before = lax.ppermute(rows[-HALO:], "ctx", down)
        after = lax.ppermute(rows[:HALO], "ctx", up)
        inner = jnp.where(parity == 0, after, before)
        outer = jnp.where(parity == 0, before, after)
        (normed,) = near_product(place, normalize_rows(rows, gain), inner, outer, gain)
        near_by = 2 if ctx_count % 2 == 0 else 1
        groups = [
            [member(f, p + i) for f in range(fsdp_count) for i in range(near_by)]
            for p in range(0, ctx_count, near_by)
        ]
        convs, stats = [None] * 3, []
        for block in ORDER:
            extra = (stats, len(groups[0])) if block == ORDER[-1] else ()
            convs[block], stat = front(block, [full_in], *extra)
            stats.append(stat)
        stats = merge(everyones(stats[2], groups), len(groups))
        groups = [
            [member(f, p + i) for p in range(0, ctx_count, near_by)]
            for f in range(fsdp_count)
            for i in range(near_by)
        ]
        stats = [everyones(stats, groups)]
    result = back(place, stats, bn_gain[None], bn_shift[None], convs, out_weights)
    return result[None]


def solution(mesh):
    return jax.shard_map(
        body,
        mesh=mesh,
        in_specs=(
            P("fsdp", "ctx", None),
            P("fsdp"),
            P(),
            P("fsdp", None),
            P(),
            P(),
            P(),
            P("fsdp", None),
        ),
        out_specs=P("fsdp", "ctx", None),
        check_vma=False,
    )
```

```python
import functools

import jax
import jax.numpy as jnp
from jax import lax
from jax.experimental import pallas as pl
from jax.experimental.pallas import tpu as pltpu
from jax.sharding import PartitionSpec as P

HALO = 16
LANES = 128
MIB = 1024 * 1024
VMEM = pltpu.VMEM
ORDER = (0, 2, 1)


def cost(flops):
    return pl.CostEstimate(flops=flops, bytes_accessed=0, transcendentals=0)


def params(mib):
    return pltpu.CompilerParams(vmem_limit_bytes=mib * MIB)


def swap(value, axis, bit):
    return lax.ppermute(value, axis, [(i, i ^ bit) for i in range(lax.axis_size(axis))])


def normalize(values, gain):
    values = values.astype(jnp.float32)
    centre = jnp.mean(values, axis=-1, keepdims=True)
    deviate = values - centre
    spread = jnp.mean(deviate * deviate, axis=-1, keepdims=True)
    return (deviate * lax.rsqrt(spread + 1e-05) * gain).astype(jnp.bfloat16)


def norm_kernel(rows_ref, gain_ref, out_ref):
    step = 64

    @pl.loop(0, rows_ref.shape[0] // step)
    def _(i):
        here = pl.ds(pl.multiple_of(i * step, step), step)
        out_ref[here, :] = normalize(rows_ref[here, :], gain_ref[...])


def normalize_rows(rows, gain):
    row_count, width = rows.shape
    return pl.pallas_call(
        norm_kernel,
        out_shape=jax.ShapeDtypeStruct((row_count, width), jnp.bfloat16),
        in_specs=[pl.BlockSpec(memory_space=VMEM)] * 2,
        out_specs=pl.BlockSpec(memory_space=VMEM),
        compiler_params=params(4),
        cost_estimate=cost(10**8),
        name="layer_norm",
    )(rows, gain)


def near_kernel(place_ref, rows_ref, inner_ref, outer_ref, gain_ref, *refs):
    row_count = rows_ref.shape[0]
    gain = gain_ref[...]
    *weight_refs, ext_ref = refs[:3] if len(refs) > 1 else refs
    odd = place_ref[3]
    at = pl.multiple_of((1 - odd) * (HALO + row_count), HALO)
    ext_ref[pl.ds(at, HALO), :] = normalize(inner_ref[...], gain)
    at = pl.multiple_of(odd * (HALO + row_count), HALO)
    ext_ref[pl.ds(at, HALO), :] = normalize(outer_ref[...], gain)
    ext_ref[HALO : HALO + row_count, :] = rows_ref[...]
    if not weight_refs:
        return
    *out_refs, weights = refs[3:]
    own = place_ref[0]
    depth, width = weight_refs[0].shape
    for i, weight_ref in enumerate(weight_refs):
        at = pl.multiple_of(lax.bitwise_xor(own % 2, i) * depth, depth)
        weights[pl.ds(at, depth), :] = weight_ref[...]
    near = pl.ds(pl.multiple_of(own // 2 * (2 * depth), 2 * depth), 2 * depth)
    wide = out_refs[0].shape[1] // 2
    channels = width // 2
    for block, out_ref in enumerate(out_refs):
        for i in range(2):
            columns = slice(i * channels + block * wide, i * channels + (block + 1) * wide)
            out_ref[:, i * wide : (i + 1) * wide] = jnp.dot(
                ext_ref[:, near], weights[:, columns], preferred_element_type=jnp.float32
            )


def near_product(place, rows, inner, outer, gain, *shards):
    row_count, width = rows.shape
    ext_rows = row_count + 2 * HALO
    shapes = [jax.ShapeDtypeStruct((ext_rows, width), jnp.bfloat16)]
    scratch = []
    if shards:
        shapes += [jax.ShapeDtypeStruct((ext_rows, width // 3), jnp.float32)] * 3
        scratch.append(VMEM((2 * shards[0].shape[0], width), jnp.bfloat16))
    return pl.pallas_call(
        near_kernel,
        out_shape=shapes,
        in_specs=[pl.BlockSpec(memory_space=pltpu.SMEM)]
        + [pl.BlockSpec(memory_space=VMEM)] * (4 + len(shards)),
        out_specs=[pl.BlockSpec(memory_space=VMEM)] * len(shapes),
        scratch_shapes=scratch,
        compiler_params=params(8),
        cost_estimate=cost(10**8),
        name="near",
    )(place, rows, inner, outer, gain, *shards)


def front_kernel(block, earlier, place_ref, normed_ref, *refs):
    refs, earlier_refs = refs[earlier:], refs[:earlier]
    *weight_refs, taps_ref, conv_ref, stats_ref, weights, gated = refs
    ext_rows = normed_ref.shape[0]
    row_count, wide = conv_ref.shape
    taps, channels = taps_ref.shape
    if len(weight_refs) > 1:
        near_ref, *far_refs = weight_refs
        own = place_ref[0]
        depth = far_refs[0].shape[0]
        halves = len(far_refs) // 2
        for i in range(2):
            at = pl.multiple_of(lax.bitwise_xor(own % 2, i) * depth, depth)
            if halves == 1:
                weights[pl.ds(at, depth), :] = far_refs[i][...]
                continue
            for j in range(2):
                column = pl.multiple_of(lax.bitwise_xor(place_ref[3], j) * wide, wide)
                weights[pl.ds(at, depth), pl.ds(column, wide)] = far_refs[2 * i + j][...]
        far = pl.ds(pl.multiple_of((1 - own // 2) * (2 * depth), 2 * depth), 2 * depth)
        normed = normed_ref[:, far]
        value = near_ref[:, 0:wide] + jnp.dot(normed, weights[:, 0:wide], preferred_element_type=jnp.float32)
        gate = near_ref[:, wide:] + jnp.dot(normed, weights[:, wide:], preferred_element_type=jnp.float32)
    else:
        columns = slice(block * wide, (block + 1) * wide)
        value = jnp.dot(normed_ref[...], weight_refs[0][:, columns], preferred_element_type=jnp.float32)
        columns = slice(channels + block * wide, channels + (block + 1) * wide)
        gate = jnp.dot(normed_ref[...], weight_refs[0][:, columns], preferred_element_type=jnp.float32)
    start, length = place_ref[1], place_ref[2]
    position = start - HALO + lax.broadcasted_iota(jnp.int32, (ext_rows, 1), 0)
    valid = (position >= 0) & (position < length)
    kept = jnp.where(valid, value * jax.nn.sigmoid(gate), 0.0)
    kept = kept.astype(jnp.bfloat16).astype(jnp.float32)
    first = HALO - (taps - 1) // 2
    step = 64
    for unit in range(wide // LANES):
        lanes = slice(unit * LANES, (unit + 1) * LANES)
        tap_lanes = slice(block * wide + unit * LANES, block * wide + (unit + 1) * LANES)
        column = kept[:, lanes]
        gated[0] = column
        for phase in range(1, 8):
            gated[phase] = pltpu.roll(column, ext_rows - phase, 0)
        for at in range(0, row_count, step):
            acc = None
            for tap in range(taps):
                base = at + (first + tap) // 8 * 8
                term = gated[(first + tap) % 8, base : base + step, :] * taps_ref[tap : tap + 1, tap_lanes]
                acc = term if acc is None else acc + term
            conv_ref[at : at + step, lanes] = acc
    here = start + lax.broadcasted_iota(jnp.int32, (row_count, 1), 0) < length
    count = jnp.clip(length - start, 0, row_count).astype(jnp.float32)
    conv = conv_ref[...]
    mean = jnp.sum(jnp.where(here, conv, 0.0), axis=0, keepdims=True) / jnp.maximum(count, 1.0)
    deviate = jnp.where(here, conv - mean, 0.0)
    square = jnp.sum(deviate * deviate, axis=0, keepdims=True)
    stats = [mean, square, jnp.full((1, wide), count)]
    if not earlier_refs:
        for i, row in enumerate(stats):
            stats_ref[i : i + 1, :] = row
        return
    for i, row in enumerate(stats):
        for copy in range(stats_ref.shape[0]):
            stats_ref[copy, i : i + 1, block * wide : (block + 1) * wide] = row
            for other, ref in zip([j for j in ORDER if j != block], earlier_refs):
                stats_ref[copy, i : i + 1, other * wide : (other + 1) * wide] = ref[i : i + 1, :]


def front_block(block, wide, place, normed, weights, dw_kernel, earlier=(), copies=1):
    ext_rows, width = normed.shape
    row_count = ext_rows - 2 * HALO
    depth = 2 * weights[1].shape[0] if len(weights) > 1 else 16
    stats_shape = (copies, 3, dw_kernel.shape[1]) if earlier else (3, wide)
    return pl.pallas_call(
        functools.partial(front_kernel, block, len(earlier)),
        out_shape=(
            jax.ShapeDtypeStruct((row_count, wide), jnp.float32),
            jax.ShapeDtypeStruct(stats_shape, jnp.float32),
        ),
        in_specs=[pl.BlockSpec(memory_space=pltpu.SMEM)]
        + [pl.BlockSpec(memory_space=VMEM)] * (2 + len(weights) + len(earlier)),
        out_specs=[pl.BlockSpec(memory_space=VMEM)] * 2,
        scratch_shapes=[
            VMEM((depth, 2 * wide), jnp.bfloat16),
            VMEM((8, ext_rows, LANES), jnp.float32),
        ],
        compiler_params=params(10),
        cost_estimate=cost(10**8),
        name="front",
    )(place, normed, *earlier, *weights, dw_kernel)


def merged(parts):
    means, squares, counts = zip(*parts)
    count = sum(counts)
    mean = sum(n * m for n, m in zip(counts, means)) / jnp.maximum(count, 1.0)
    square = sum(squares) + sum(n * (m - mean) * (m - mean) for n, m in zip(counts, means))
    return mean, square, count


def rows_of(refs):
    return [[ref[copy, i : i + 1, :] for i in range(3)] for ref in refs for copy in range(ref.shape[0])]


def merge_kernel(stats_ref, out_ref):
    for i, row in enumerate(merged(rows_of([stats_ref]))):
        for copy in range(out_ref.shape[0]):
            out_ref[copy, i : i + 1, :] = row


def merge(stats, copies):
    return pl.pallas_call(
        merge_kernel,
        out_shape=jax.ShapeDtypeStruct((copies,) + stats.shape[1:], jnp.float32),
        in_specs=[pl.BlockSpec(memory_space=VMEM)],
        out_specs=pl.BlockSpec(memory_space=VMEM),
        compiler_params=params(8),
        cost_estimate=cost(10**8),
        name="merge",
    )(stats)


def back_kernel(stat_count, place_ref, gain_ref, shift_ref, *refs):
    stat_refs, refs = refs[:stat_count], refs[stat_count:]
    *conv_refs, out_ref, rows_out, sems, weights = refs
    convs, weight_refs = conv_refs[:3], conv_refs[3:]
    row_count, wide = convs[0].shape
    if len(weight_refs) > 1:
        depth = weight_refs[0].shape[0]
        for i, weight_ref in enumerate(weight_refs[:2]):
            at = pl.multiple_of(lax.bitwise_xor(place_ref[0], i) * depth, depth)
            weights[pl.ds(at, depth), :] = weight_ref[...]
        for i, weight_ref in enumerate(weight_refs[2:]):
            rows = weight_ref.shape[0]
            at = lax.bitwise_xor(place_ref[0], 2 + i // 4) * depth
            at += lax.bitwise_xor(2 * place_ref[3] + place_ref[4], i % 4) * rows
            weights[pl.ds(pl.multiple_of(at, rows), rows), :] = weight_ref[...]
    else:
        weights[...] = weight_refs[0][...]
    mean, square, count = merged(rows_of(stat_refs))
    scale = lax.rsqrt(square / count + 1e-05) * gain_ref[...]
    shift = shift_ref[...]
    pieces, rows, columns = rows_out.shape
    across = out_ref.shape[1] // columns
    copies = []
    for piece in range(pieces // across):
        here = slice(piece * rows, (piece + 1) * rows)
        parts = []
        for i, conv_ref in enumerate(convs):
            lanes = slice(i * wide, (i + 1) * wide)
            scaled = (conv_ref[here, :] - mean[:, lanes]) * scale[:, lanes] + shift[:, lanes]
            parts.append((scaled * jax.nn.sigmoid(scaled)).astype(jnp.bfloat16))
        activated = jnp.concatenate(parts, axis=1)
        position = place_ref[1] + piece * rows + lax.broadcasted_iota(jnp.int32, (rows, 1), 0)
        for j in range(across):
            lanes = slice(j * columns, (j + 1) * columns)
            result = jnp.dot(activated, weights[:, lanes], preferred_element_type=jnp.float32)
            slot = piece * across + j
            rows_out[slot] = jnp.where(position < place_ref[2], result, 0.0).astype(jnp.bfloat16)
            copy = pltpu.make_async_copy(rows_out.at[slot], out_ref.at[here, lanes], sems.at[slot])
            copy.start()
            copies.append(copy)
    for copy in copies:
        copy.wait()


def back(place, stats, gain, shift, convs, weights):
    row_count = convs[0].shape[0]
    channels, width = gain.shape[1], weights[0].shape[1]
    pieces, across = 4, 2
    return pl.pallas_call(
        functools.partial(back_kernel, len(stats)),
        out_shape=jax.ShapeDtypeStruct((row_count, width), jnp.bfloat16),
        in_specs=[pl.BlockSpec(memory_space=pltpu.SMEM)]
        + [pl.BlockSpec(memory_space=VMEM)] * (2 + len(stats) + len(convs) + len(weights)),
        out_specs=pl.BlockSpec(memory_space=pl.ANY),
        scratch_shapes=[
            VMEM((pieces, row_count * across // pieces, width // across), jnp.bfloat16),
            pltpu.SemaphoreType.DMA((pieces,)),
            VMEM((channels, width), jnp.bfloat16),
        ],
        compiler_params=params(10),
        cost_estimate=cost(10**9),
        name="back",
    )(place, gain, shift, *stats, *convs, *weights)


def everyones(copies, groups):
    return lax.all_to_all(copies, ("fsdp", "ctx"), 0, 0, axis_index_groups=groups, tiled=True)


def tie(*values):
    return lax.optimization_barrier(values)


def body(frames, lengths, ln_gain, w_in, dw_kernel, bn_gain, bn_shift, w_out):
    _, row_count, model_width = frames.shape
    channels = dw_kernel.shape[1]
    wide = channels // 3
    ctx, fsdp = lax.axis_index("ctx"), lax.axis_index("fsdp")
    ctx_count, fsdp_count = lax.axis_size("ctx"), lax.axis_size("fsdp")
    direct = fsdp_count == 4 and ctx_count == 8
    rows = frames[0]
    gain = ln_gain[None]
    parity, pair = lax.rem(ctx, 2), lax.rem(ctx // 2, 2)
    place = jnp.stack([fsdp, ctx * row_count, lengths[0], parity, pair]).astype(jnp.int32)
    ends = ctx_count - 1
    down, up = [(i, i + 1) for i in range(ends)], [(i + 1, i) for i in range(ends)]
    both = ("fsdp", "ctx")
    member = lambda f, p: f * ctx_count + p

    def front(block, weights, *extra):
        return front_block(block, wide, place, normed, weights, dw_kernel, *extra)

    if direct:
        last = row_count - HALO
        depth = w_out.shape[0] // 4

        def columns(shard, block):
            at = block * wide
            return jnp.concatenate([shard[:, at : at + wide], shard[:, channels + at : channels + at + wide]], 1)

        quarter = lax.dynamic_slice_in_dim(w_out, (2 * parity + pair) * depth, depth, axis=0)
        quarter, later_in = tie(quarter, w_in)
        half = lax.dynamic_slice_in_dim(later_in, parity * channels + 2 * wide, wide, axis=1)
        half, later_in = tie(half, later_in)
        block = columns(later_in, 0)
        quarter, half, block = (swap(part, "fsdp", 2) for part in (quarter, half, block))
        across = swap(later_in, "fsdp", 1)
        normed = normalize_rows(rows, gain)
        normed, later_rows, quarter = tie(normed, rows, quarter)
        inner = lax.dynamic_slice_in_dim(later_rows, (1 - parity) * last, HALO, axis=0)
        outer = lax.dynamic_slice_in_dim(later_rows, parity * last, HALO, axis=0)
        inner = swap(inner, "ctx", 1)
        pairs = [(i, i + 1) for i in range(1, ends, 2)]
        outer = lax.ppermute(outer, "ctx", pairs + [(j, i) for i, j in pairs])
        quarters = [quarter, swap(quarter, "ctx", 2), swap(quarter, "ctx", 1)]
        normed, half, later_in = tie(normed, half, later_in)
        over_x = {2: [half, swap(half, "ctx", 1)]}
        beyond_half = swap(half, "fsdp", 1)
        normed, part = tie(normed, columns(later_in, 1))
        over_x[1] = [swap(part, "fsdp", 2)]
        normed, block = tie(normed, block)
        over_x[0] = [block]
        beyond_zero = swap(block, "fsdp", 1)
        normed, *partials = near_product(place, normed, inner, outer, gain, w_in, across)
        partials[0], beyond_half, *quarters = tie(partials[0], beyond_half, *quarters)
        quarters.append(swap(quarters[1], "ctx", 1))
        partials[0], over_x[2][1], w_out = tie(partials[0], over_x[2][1], w_out)

        beyond_two = [beyond_half, swap(over_x[2][1], "fsdp", 1)]
        conv_one, stat_one = front(0, [partials[0], *over_x[0], beyond_zero])
        conv_one, partials[2], quarters[3] = tie(conv_one, partials[2], quarters[3])
        beyond_quarters = [swap(part, "fsdp", 1) for part in quarters]
        conv_two, stat_two = front(2, [partials[2], *over_x[2], *beyond_two])
        conv_two, over_x[1][0] = tie(conv_two, over_x[1][0])
        across_out = swap(w_out, "fsdp", 1)
        beyond_one = swap(over_x[1][0], "fsdp", 1)
        conv_three, stats = front(1, [partials[1], *over_x[1], beyond_one], (stat_one, stat_two), 1)
        stats, across_out, *beyond_quarters = tie(stats, across_out, *beyond_quarters)
        out_weights = [w_out, across_out, *quarters, *beyond_quarters]
        convs = [conv_one, conv_three, conv_two]

        def others(flips):
            return [
                lax.ppermute(
                    stats,
                    both,
                    [(member(f, p), member(f ^ df, p ^ dp)) for f in range(4) for p in range(8)],
                )
                for df, dp in flips
            ]

        def union(parts):
            return jnp.stack(merged([[part[:, i] for i in range(3)] for part in parts]), 1)

        stats = union([stats] + others([(1, 0)]))
        stats = union([stats] + others([(2, 0), (0, 1), (2, 1)]))
        stats = [stats] + others([(0, 2), (0, 4), (0, 6)])
    else:
        full_in = lax.all_gather(w_in, "fsdp", axis=0, tiled=True)
        out_weights = [lax.all_gather(w_out, "fsdp", axis=0, tiled=True)]
        before = lax.ppermute(rows[-HALO:], "ctx", down)
        after = lax.ppermute(rows[:HALO], "ctx", up)
        inner = jnp.where(parity == 0, after, before)
        outer = jnp.where(parity == 0, before, after)
        (normed,) = near_product(place, normalize_rows(rows, gain), inner, outer, gain)
        near_by = 2 if ctx_count % 2 == 0 else 1
        groups = [
            [member(f, p + i) for f in range(fsdp_count) for i in range(near_by)]
            for p in range(0, ctx_count, near_by)
        ]
        convs, stats = [None] * 3, []
        for block in ORDER:
            extra = (stats, len(groups[0])) if block == ORDER[-1] else ()
            convs[block], stat = front(block, [full_in], *extra)
            stats.append(stat)
        stats = merge(everyones(stats[2], groups), len(groups))
        groups = [
            [member(f, p + i) for p in range(0, ctx_count, near_by)]
            for f in range(fsdp_count)
            for i in range(near_by)
        ]
        stats = [everyones(stats, groups)]
    result = back(place, stats, bn_gain[None], bn_shift[None], convs, out_weights)
    return result[None]


def solution(mesh):
    return jax.shard_map(
        body,
        mesh=mesh,
        in_specs=(
            P("fsdp", "ctx", None),
            P("fsdp"),
            P(),
            P("fsdp", None),
            P(),
            P(),
            P(),
            P("fsdp", None),
        ),
        out_specs=P("fsdp", "ctx", None),
        check_vma=False,
    )
```

```python
import functools

import jax
import jax.numpy as jnp
from jax import lax
from jax.experimental import pallas as pl
from jax.experimental.pallas import tpu as pltpu
from jax.sharding import PartitionSpec as P

HALO = 16
LANES = 128
MIB = 1024 * 1024
VMEM = pltpu.VMEM
ORDER = (0, 2, 1)


def cost(flops):
    return pl.CostEstimate(flops=flops, bytes_accessed=0, transcendentals=0)


def params(mib):
    return pltpu.CompilerParams(vmem_limit_bytes=mib * MIB)


def swap(value, axis, bit):
    return lax.ppermute(value, axis, [(i, i ^ bit) for i in range(lax.axis_size(axis))])


def cut_kernel(place_ref, shard_ref, half_ref, zero_ref, one_ref):
    wide = half_ref.shape[1]
    channels = shard_ref.shape[1] // 2
    at = pl.multiple_of(place_ref[3] * channels + 2 * wide, wide)
    half_ref[...] = shard_ref[:, pl.ds(at, wide)]
    for block, ref in enumerate((zero_ref, one_ref)):
        for i in range(2):
            at = i * channels + block * wide
            ref[:, i * wide : (i + 1) * wide] = shard_ref[:, at : at + wide]


def cut(place, shard, wide):
    depth = shard.shape[0]
    shapes = [(depth, wide), (depth, 2 * wide), (depth, 2 * wide)]
    return pl.pallas_call(
        cut_kernel,
        out_shape=[jax.ShapeDtypeStruct(shape, jnp.bfloat16) for shape in shapes],
        in_specs=[pl.BlockSpec(memory_space=pltpu.SMEM), pl.BlockSpec(memory_space=VMEM)],
        out_specs=[pl.BlockSpec(memory_space=VMEM)] * 3,
        compiler_params=params(4),
        cost_estimate=cost(10**8),
        name="cut",
    )(place, shard)


def normalize(values, gain):
    values = values.astype(jnp.float32)
    centre = jnp.mean(values, axis=-1, keepdims=True)
    deviate = values - centre
    spread = jnp.mean(deviate * deviate, axis=-1, keepdims=True)
    return (deviate * lax.rsqrt(spread + 1e-05) * gain).astype(jnp.bfloat16)


def norm_kernel(place_ref, rows_ref, gain_ref, out_ref, inner_ref, outer_ref):
    step = 64
    row_count = rows_ref.shape[0]

    @pl.loop(0, row_count // step)
    def _(i):
        here = pl.ds(pl.multiple_of(i * step, step), step)
        out_ref[here, :] = normalize(rows_ref[here, :], gain_ref[...])

    odd = place_ref[3]
    last = row_count - HALO
    inner_ref[...] = rows_ref[pl.ds(pl.multiple_of((1 - odd) * last, HALO), HALO), :]
    outer_ref[...] = rows_ref[pl.ds(pl.multiple_of(odd * last, HALO), HALO), :]


def normalize_rows(place, rows, gain):
    row_count, width = rows.shape
    shapes = [(row_count, width), (HALO, width), (HALO, width)]
    return pl.pallas_call(
        norm_kernel,
        out_shape=[jax.ShapeDtypeStruct(shape, jnp.bfloat16) for shape in shapes],
        in_specs=[pl.BlockSpec(memory_space=pltpu.SMEM)] + [pl.BlockSpec(memory_space=VMEM)] * 2,
        out_specs=[pl.BlockSpec(memory_space=VMEM)] * 3,
        compiler_params=params(4),
        cost_estimate=cost(10**8),
        name="layer_norm",
    )(place, rows, gain)


def near_kernel(place_ref, rows_ref, inner_ref, outer_ref, gain_ref, *refs):
    row_count = rows_ref.shape[0]
    gain = gain_ref[...]
    *weight_refs, ext_ref = refs[:3] if len(refs) > 1 else refs
    odd = place_ref[3]
    at = pl.multiple_of((1 - odd) * (HALO + row_count), HALO)
    ext_ref[pl.ds(at, HALO), :] = normalize(inner_ref[...], gain)
    at = pl.multiple_of(odd * (HALO + row_count), HALO)
    ext_ref[pl.ds(at, HALO), :] = normalize(outer_ref[...], gain)
    ext_ref[HALO : HALO + row_count, :] = rows_ref[...]
    if not weight_refs:
        return
    *out_refs, weights = refs[3:]
    own = place_ref[0]
    depth, width = weight_refs[0].shape
    for i, weight_ref in enumerate(weight_refs):
        at = pl.multiple_of(lax.bitwise_xor(own % 2, i) * depth, depth)
        weights[pl.ds(at, depth), :] = weight_ref[...]
    near = pl.ds(pl.multiple_of(own // 2 * (2 * depth), 2 * depth), 2 * depth)
    wide = out_refs[0].shape[1] // 2
    channels = width // 2
    for block, out_ref in enumerate(out_refs):
        for i in range(2):
            columns = slice(i * channels + block * wide, i * channels + (block + 1) * wide)
            out_ref[:, i * wide : (i + 1) * wide] = jnp.dot(
                ext_ref[:, near], weights[:, columns], preferred_element_type=jnp.float32
            )


def near_product(place, rows, inner, outer, gain, *shards):
    row_count, width = rows.shape
    ext_rows = row_count + 2 * HALO
    shapes = [jax.ShapeDtypeStruct((ext_rows, width), jnp.bfloat16)]
    scratch = []
    if shards:
        shapes += [jax.ShapeDtypeStruct((ext_rows, width // 3), jnp.float32)] * 3
        scratch.append(VMEM((2 * shards[0].shape[0], width), jnp.bfloat16))
    return pl.pallas_call(
        near_kernel,
        out_shape=shapes,
        in_specs=[pl.BlockSpec(memory_space=pltpu.SMEM)]
        + [pl.BlockSpec(memory_space=VMEM)] * (4 + len(shards)),
        out_specs=[pl.BlockSpec(memory_space=VMEM)] * len(shapes),
        scratch_shapes=scratch,
        compiler_params=params(8),
        cost_estimate=cost(10**8),
        name="near",
    )(place, rows, inner, outer, gain, *shards)


def front_kernel(block, earlier, place_ref, normed_ref, *refs):
    refs, earlier_refs = refs[earlier:], refs[:earlier]
    *weight_refs, taps_ref, conv_ref, stats_ref, weights, gated = refs
    ext_rows = normed_ref.shape[0]
    row_count, wide = conv_ref.shape
    taps, channels = taps_ref.shape
    if len(weight_refs) > 1:
        near_ref, *far_refs = weight_refs
        own = place_ref[0]
        depth = far_refs[0].shape[0]
        halves = len(far_refs) // 2
        for i in range(2):
            at = pl.multiple_of(lax.bitwise_xor(own % 2, i) * depth, depth)
            if halves == 1:
                weights[pl.ds(at, depth), :] = far_refs[i][...]
                continue
            for j in range(2):
                column = pl.multiple_of(lax.bitwise_xor(place_ref[3], j) * wide, wide)
                weights[pl.ds(at, depth), pl.ds(column, wide)] = far_refs[2 * i + j][...]
        far = pl.ds(pl.multiple_of((1 - own // 2) * (2 * depth), 2 * depth), 2 * depth)
        normed = normed_ref[:, far]
        value = near_ref[:, 0:wide] + jnp.dot(normed, weights[:, 0:wide], preferred_element_type=jnp.float32)
        gate = near_ref[:, wide:] + jnp.dot(normed, weights[:, wide:], preferred_element_type=jnp.float32)
    else:
        columns = slice(block * wide, (block + 1) * wide)
        value = jnp.dot(normed_ref[...], weight_refs[0][:, columns], preferred_element_type=jnp.float32)
        columns = slice(channels + block * wide, channels + (block + 1) * wide)
        gate = jnp.dot(normed_ref[...], weight_refs[0][:, columns], preferred_element_type=jnp.float32)
    start, length = place_ref[1], place_ref[2]
    position = start - HALO + lax.broadcasted_iota(jnp.int32, (ext_rows, 1), 0)
    valid = (position >= 0) & (position < length)
    kept = jnp.where(valid, value * jax.nn.sigmoid(gate), 0.0)
    kept = kept.astype(jnp.bfloat16).astype(jnp.float32)
    first = HALO - (taps - 1) // 2
    step = 64
    for unit in range(wide // LANES):
        lanes = slice(unit * LANES, (unit + 1) * LANES)
        tap_lanes = slice(block * wide + unit * LANES, block * wide + (unit + 1) * LANES)
        column = kept[:, lanes]
        gated[0] = column
        for phase in range(1, 8):
            gated[phase] = pltpu.roll(column, ext_rows - phase, 0)
        for at in range(0, row_count, step):
            acc = None
            for tap in range(taps):
                base = at + (first + tap) // 8 * 8
                term = gated[(first + tap) % 8, base : base + step, :] * taps_ref[tap : tap + 1, tap_lanes]
                acc = term if acc is None else acc + term
            conv_ref[at : at + step, lanes] = acc
    here = start + lax.broadcasted_iota(jnp.int32, (row_count, 1), 0) < length
    count = jnp.clip(length - start, 0, row_count).astype(jnp.float32)
    conv = conv_ref[...]
    mean = jnp.sum(jnp.where(here, conv, 0.0), axis=0, keepdims=True) / jnp.maximum(count, 1.0)
    deviate = jnp.where(here, conv - mean, 0.0)
    square = jnp.sum(deviate * deviate, axis=0, keepdims=True)
    stats = [mean, square, jnp.full((1, wide), count)]
    if not earlier_refs:
        for i, row in enumerate(stats):
            stats_ref[i : i + 1, :] = row
        return
    for i, row in enumerate(stats):
        for copy in range(stats_ref.shape[0]):
            stats_ref[copy, i : i + 1, block * wide : (block + 1) * wide] = row
            for other, ref in zip([j for j in ORDER if j != block], earlier_refs):
                stats_ref[copy, i : i + 1, other * wide : (other + 1) * wide] = ref[i : i + 1, :]


def front_block(block, wide, place, normed, weights, dw_kernel, earlier=(), copies=1):
    ext_rows, width = normed.shape
    row_count = ext_rows - 2 * HALO
    depth = 2 * weights[1].shape[0] if len(weights) > 1 else 16
    stats_shape = (copies, 3, dw_kernel.shape[1]) if earlier else (3, wide)
    return pl.pallas_call(
        functools.partial(front_kernel, block, len(earlier)),
        out_shape=(
            jax.ShapeDtypeStruct((row_count, wide), jnp.float32),
            jax.ShapeDtypeStruct(stats_shape, jnp.float32),
        ),
        in_specs=[pl.BlockSpec(memory_space=pltpu.SMEM)]
        + [pl.BlockSpec(memory_space=VMEM)] * (2 + len(weights) + len(earlier)),
        out_specs=[pl.BlockSpec(memory_space=VMEM)] * 2,
        scratch_shapes=[
            VMEM((depth, 2 * wide), jnp.bfloat16),
            VMEM((8, ext_rows, LANES), jnp.float32),
        ],
        compiler_params=params(10),
        cost_estimate=cost(10**8),
        name="front",
    )(place, normed, *earlier, *weights, dw_kernel)


def merged(parts):
    means, squares, counts = zip(*parts)
    count = sum(counts)
    mean = sum(n * m for n, m in zip(counts, means)) / jnp.maximum(count, 1.0)
    square = sum(squares) + sum(n * (m - mean) * (m - mean) for n, m in zip(counts, means))
    return mean, square, count


def rows_of(refs):
    return [[ref[copy, i : i + 1, :] for i in range(3)] for ref in refs for copy in range(ref.shape[0])]


def merge_kernel(stats_ref, out_ref):
    for i, row in enumerate(merged(rows_of([stats_ref]))):
        for copy in range(out_ref.shape[0]):
            out_ref[copy, i : i + 1, :] = row


def merge(stats, copies):
    return pl.pallas_call(
        merge_kernel,
        out_shape=jax.ShapeDtypeStruct((copies,) + stats.shape[1:], jnp.float32),
        in_specs=[pl.BlockSpec(memory_space=VMEM)],
        out_specs=pl.BlockSpec(memory_space=VMEM),
        compiler_params=params(8),
        cost_estimate=cost(10**8),
        name="merge",
    )(stats)


def back_kernel(stat_count, place_ref, gain_ref, shift_ref, *refs):
    stat_refs, refs = refs[:stat_count], refs[stat_count:]
    *conv_refs, out_ref, rows_out, sems, weights = refs
    convs, weight_refs = conv_refs[:3], conv_refs[3:]
    row_count, wide = convs[0].shape
    if len(weight_refs) > 1:
        depth = weight_refs[0].shape[0]
        for i, weight_ref in enumerate(weight_refs):
            at = pl.multiple_of(lax.bitwise_xor(place_ref[0], i) * depth, depth)
            weights[pl.ds(at, depth), :] = weight_ref[...]
    else:
        weights[...] = weight_refs[0][...]
    mean, square, count = merged(rows_of(stat_refs))
    scale = lax.rsqrt(square / count + 1e-05) * gain_ref[...]
    shift = shift_ref[...]
    pieces, rows, columns = rows_out.shape
    across = out_ref.shape[1] // columns
    copies = []
    for piece in range(pieces // across):
        here = slice(piece * rows, (piece + 1) * rows)
        parts = []
        for i, conv_ref in enumerate(convs):
            lanes = slice(i * wide, (i + 1) * wide)
            scaled = (conv_ref[here, :] - mean[:, lanes]) * scale[:, lanes] + shift[:, lanes]
            parts.append((scaled * jax.nn.sigmoid(scaled)).astype(jnp.bfloat16))
        activated = jnp.concatenate(parts, axis=1)
        position = place_ref[1] + piece * rows + lax.broadcasted_iota(jnp.int32, (rows, 1), 0)
        for j in range(across):
            lanes = slice(j * columns, (j + 1) * columns)
            result = jnp.dot(activated, weights[:, lanes], preferred_element_type=jnp.float32)
            slot = piece * across + j
            rows_out[slot] = jnp.where(position < place_ref[2], result, 0.0).astype(jnp.bfloat16)
            copy = pltpu.make_async_copy(rows_out.at[slot], out_ref.at[here, lanes], sems.at[slot])
            copy.start()
            copies.append(copy)
    for copy in copies:
        copy.wait()


def back(place, stats, gain, shift, convs, weights):
    row_count = convs[0].shape[0]
    channels, width = gain.shape[1], weights[0].shape[1]
    pieces, across = 4, 2
    return pl.pallas_call(
        functools.partial(back_kernel, len(stats)),
        out_shape=jax.ShapeDtypeStruct((row_count, width), jnp.bfloat16),
        in_specs=[pl.BlockSpec(memory_space=pltpu.SMEM)]
        + [pl.BlockSpec(memory_space=VMEM)] * (2 + len(stats) + len(convs) + len(weights)),
        out_specs=pl.BlockSpec(memory_space=pl.ANY),
        scratch_shapes=[
            VMEM((pieces, row_count * across // pieces, width // across), jnp.bfloat16),
            pltpu.SemaphoreType.DMA((pieces,)),
            VMEM((channels, width), jnp.bfloat16),
        ],
        compiler_params=params(10),
        cost_estimate=cost(10**9),
        name="back",
    )(place, gain, shift, *stats, *convs, *weights)


def everyones(copies, groups):
    return lax.all_to_all(copies, ("fsdp", "ctx"), 0, 0, axis_index_groups=groups, tiled=True)


def tie(*values):
    return lax.optimization_barrier(values)


def body(frames, lengths, ln_gain, w_in, dw_kernel, bn_gain, bn_shift, w_out):
    _, row_count, model_width = frames.shape
    channels = dw_kernel.shape[1]
    wide = channels // 3
    ctx, fsdp = lax.axis_index("ctx"), lax.axis_index("fsdp")
    ctx_count, fsdp_count = lax.axis_size("ctx"), lax.axis_size("fsdp")
    direct = fsdp_count == 4 and ctx_count == 8
    rows = frames[0]
    gain = ln_gain[None]
    parity = lax.rem(ctx, 2)
    place = jnp.stack([fsdp, ctx * row_count, lengths[0], parity]).astype(jnp.int32)
    ends = ctx_count - 1
    down, up = [(i, i + 1) for i in range(ends)], [(i + 1, i) for i in range(ends)]
    both = ("fsdp", "ctx")
    member = lambda f, p: f * ctx_count + p

    def front(block, weights, *extra):
        return front_block(block, wide, place, normed, weights, dw_kernel, *extra)

    if direct:
        half, zero, one = (swap(part, "fsdp", 2) for part in cut(place, w_in, wide))
        across = swap(w_in, "fsdp", 1)
        normed, inner, outer = normalize_rows(place, rows, gain)
        normed, half = tie(normed, half)
        rest = swap(half, "ctx", 1)
        inner = swap(inner, "ctx", 1)
        pairs = [(i, i + 1) for i in range(1, ends, 2)]
        outer = lax.ppermute(outer, "ctx", pairs + [(j, i) for i, j in pairs])
        beyond_half = swap(half, "fsdp", 1)
        normed, zero, rest = tie(normed, zero, rest)
        beyond_zero, beyond_rest = swap(zero, "fsdp", 1), swap(rest, "fsdp", 1)
        normed, *partials = near_product(place, normed, inner, outer, gain, w_in, across)
        partials[0], beyond_half, w_out = tie(partials[0], beyond_half, w_out)
        conv_zero, stat_zero = front(0, [partials[0], zero, beyond_zero])
        conv_zero, partials[2] = tie(conv_zero, partials[2])
        conv_two, stat_two = front(2, [partials[2], half, rest, beyond_half, beyond_rest])
        conv_two, one, w_out = tie(conv_two, one, w_out)
        remote_out, across_out = swap(w_out, "fsdp", 2), swap(w_out, "fsdp", 1)
        conv_one, stats = front(1, [partials[1], one, swap(one, "fsdp", 1)], (stat_zero, stat_two), 1)
        convs = [conv_zero, conv_one, conv_two]

        def others(flips):
            return [
                lax.ppermute(
                    stats,
                    both,
                    [(member(f, p), member(f ^ df, p ^ dp)) for f in range(4) for p in range(8)],
                )
                for df, dp in flips
            ]

        def union(parts):
            return jnp.stack(merged([[part[:, i] for i in range(3)] for part in parts]), 1)

        stats = union([stats] + others([(1, 0)]))
        stats = union([stats] + others([(2, 0), (0, 1), (2, 1)]))
        stats = [stats] + others([(0, 2), (0, 4), (0, 6)])
        *stats, remote_out = tie(*stats, remote_out)
        out_weights = [w_out, across_out, remote_out, swap(remote_out, "fsdp", 1)]
    else:
        full_in = lax.all_gather(w_in, "fsdp", axis=0, tiled=True)
        out_weights = [lax.all_gather(w_out, "fsdp", axis=0, tiled=True)]
        before = lax.ppermute(rows[-HALO:], "ctx", down)
        after = lax.ppermute(rows[:HALO], "ctx", up)
        inner = jnp.where(parity == 0, after, before)
        outer = jnp.where(parity == 0, before, after)
        normed, _, _ = normalize_rows(place, rows, gain)
        (normed,) = near_product(place, normed, inner, outer, gain)
        near_by = 2 if ctx_count % 2 == 0 else 1
        groups = [
            [member(f, p + i) for f in range(fsdp_count) for i in range(near_by)]
            for p in range(0, ctx_count, near_by)
        ]
        convs, stats = [None] * 3, []
        for block in ORDER:
            extra = (stats, len(groups[0])) if block == ORDER[-1] else ()
            convs[block], stat = front(block, [full_in], *extra)
            stats.append(stat)
        stats = merge(everyones(stats[2], groups), len(groups))
        groups = [
            [member(f, p + i) for p in range(0, ctx_count, near_by)]
            for f in range(fsdp_count)
            for i in range(near_by)
        ]
        stats = [everyones(stats, groups)]
    result = back(place, stats, bn_gain[None], bn_shift[None], convs, out_weights)
    return result[None]


def solution(mesh):
    return jax.shard_map(
        body,
        mesh=mesh,
        in_specs=(
            P("fsdp", "ctx", None),
            P("fsdp"),
            P(),
            P("fsdp", None),
            P(),
            P(),
            P(),
            P("fsdp", None),
        ),
        out_specs=P("fsdp", "ctx", None),
        check_vma=False,
    )
```

```python
import functools

import jax
import jax.numpy as jnp
from jax import lax
from jax.experimental import pallas as pl
from jax.experimental.pallas import tpu as pltpu
from jax.sharding import PartitionSpec as P

HALO = 16
LANES = 128
MIB = 1024 * 1024
VMEM = pltpu.VMEM
ORDER = (2, 0, 1)


def cost(flops):
    return pl.CostEstimate(flops=flops, bytes_accessed=0, transcendentals=0)


def params(mib):
    return pltpu.CompilerParams(vmem_limit_bytes=mib * MIB)


def swap(value, axis, bit):
    return lax.ppermute(value, axis, [(i, i ^ bit) for i in range(lax.axis_size(axis))])


def cut_kernel(place_ref, shard_ref, two_ref, zero_ref, one_ref):
    wide = two_ref.shape[1]
    channels = shard_ref.shape[1] // 2
    for block, ref in ((2, two_ref), (0, zero_ref)):
        at = pl.multiple_of(place_ref[3] * channels + block * wide, wide)
        ref[...] = shard_ref[:, pl.ds(at, wide)]
    for i in range(2):
        at = i * channels + wide
        one_ref[:, i * wide : (i + 1) * wide] = shard_ref[:, at : at + wide]


def cut(place, shard, wide):
    depth = shard.shape[0]
    shapes = [(depth, wide), (depth, wide), (depth, 2 * wide)]
    return pl.pallas_call(
        cut_kernel,
        out_shape=[jax.ShapeDtypeStruct(shape, jnp.bfloat16) for shape in shapes],
        in_specs=[pl.BlockSpec(memory_space=pltpu.SMEM), pl.BlockSpec(memory_space=VMEM)],
        out_specs=[pl.BlockSpec(memory_space=VMEM)] * 3,
        compiler_params=params(4),
        cost_estimate=cost(10**8),
        name="cut",
    )(place, shard)


def normalize(values, gain):
    values = values.astype(jnp.float32)
    centre = jnp.mean(values, axis=-1, keepdims=True)
    deviate = values - centre
    spread = jnp.mean(deviate * deviate, axis=-1, keepdims=True)
    return (deviate * lax.rsqrt(spread + 1e-05) * gain).astype(jnp.bfloat16)


def norm_kernel(place_ref, rows_ref, gain_ref, out_ref, inner_ref, outer_ref):
    step = 64
    row_count = rows_ref.shape[0]

    @pl.loop(0, row_count // step)
    def _(i):
        here = pl.ds(pl.multiple_of(i * step, step), step)
        out_ref[here, :] = normalize(rows_ref[here, :], gain_ref[...])

    odd = place_ref[3]
    last = row_count - HALO
    inner_ref[...] = rows_ref[pl.ds(pl.multiple_of((1 - odd) * last, HALO), HALO), :]
    outer_ref[...] = rows_ref[pl.ds(pl.multiple_of(odd * last, HALO), HALO), :]


def normalize_rows(place, rows, gain):
    row_count, width = rows.shape
    shapes = [(row_count, width), (HALO, width), (HALO, width)]
    return pl.pallas_call(
        norm_kernel,
        out_shape=[jax.ShapeDtypeStruct(shape, jnp.bfloat16) for shape in shapes],
        in_specs=[pl.BlockSpec(memory_space=pltpu.SMEM)] + [pl.BlockSpec(memory_space=VMEM)] * 2,
        out_specs=[pl.BlockSpec(memory_space=VMEM)] * 3,
        compiler_params=params(4),
        cost_estimate=cost(10**8),
        name="layer_norm",
    )(place, rows, gain)


def near_kernel(place_ref, rows_ref, inner_ref, outer_ref, gain_ref, *refs):
    row_count = rows_ref.shape[0]
    gain = gain_ref[...]
    *weight_refs, ext_ref = refs[:3] if len(refs) > 1 else refs
    odd = place_ref[3]
    at = pl.multiple_of((1 - odd) * (HALO + row_count), HALO)
    ext_ref[pl.ds(at, HALO), :] = normalize(inner_ref[...], gain)
    at = pl.multiple_of(odd * (HALO + row_count), HALO)
    ext_ref[pl.ds(at, HALO), :] = normalize(outer_ref[...], gain)
    ext_ref[HALO : HALO + row_count, :] = rows_ref[...]
    if not weight_refs:
        return
    *out_refs, weights = refs[3:]
    own = place_ref[0]
    depth, width = weight_refs[0].shape
    for i, weight_ref in enumerate(weight_refs):
        at = pl.multiple_of(lax.bitwise_xor(own % 2, i) * depth, depth)
        weights[pl.ds(at, depth), :] = weight_ref[...]
    near = pl.ds(pl.multiple_of(own // 2 * (2 * depth), 2 * depth), 2 * depth)
    wide = out_refs[0].shape[1] // 2
    channels = width // 2
    for block, out_ref in enumerate(out_refs):
        for i in range(2):
            columns = slice(i * channels + block * wide, i * channels + (block + 1) * wide)
            out_ref[:, i * wide : (i + 1) * wide] = jnp.dot(
                ext_ref[:, near], weights[:, columns], preferred_element_type=jnp.float32
            )


def near_product(place, rows, inner, outer, gain, *shards):
    row_count, width = rows.shape
    ext_rows = row_count + 2 * HALO
    shapes = [jax.ShapeDtypeStruct((ext_rows, width), jnp.bfloat16)]
    scratch = []
    if shards:
        shapes += [jax.ShapeDtypeStruct((ext_rows, width // 3), jnp.float32)] * 3
        scratch.append(VMEM((2 * shards[0].shape[0], width), jnp.bfloat16))
    return pl.pallas_call(
        near_kernel,
        out_shape=shapes,
        in_specs=[pl.BlockSpec(memory_space=pltpu.SMEM)]
        + [pl.BlockSpec(memory_space=VMEM)] * (4 + len(shards)),
        out_specs=[pl.BlockSpec(memory_space=VMEM)] * len(shapes),
        scratch_shapes=scratch,
        compiler_params=params(8),
        cost_estimate=cost(10**8),
        name="near",
    )(place, rows, inner, outer, gain, *shards)


def front_kernel(block, earlier, place_ref, normed_ref, *refs):
    refs, earlier_refs = refs[earlier:], refs[:earlier]
    *weight_refs, taps_ref, conv_ref, stats_ref, weights, gated = refs
    ext_rows = normed_ref.shape[0]
    row_count, wide = conv_ref.shape
    taps, channels = taps_ref.shape
    if len(weight_refs) > 1:
        near_ref, *far_refs = weight_refs
        own = place_ref[0]
        depth = far_refs[0].shape[0]
        halves = len(far_refs) // 2
        for i in range(2):
            at = pl.multiple_of(lax.bitwise_xor(own % 2, i) * depth, depth)
            if halves == 1:
                weights[pl.ds(at, depth), :] = far_refs[i][...]
                continue
            for j in range(2):
                column = pl.multiple_of(lax.bitwise_xor(place_ref[3], j) * wide, wide)
                weights[pl.ds(at, depth), pl.ds(column, wide)] = far_refs[2 * i + j][...]
        far = pl.ds(pl.multiple_of((1 - own // 2) * (2 * depth), 2 * depth), 2 * depth)
        normed = normed_ref[:, far]
        value = near_ref[:, 0:wide] + jnp.dot(normed, weights[:, 0:wide], preferred_element_type=jnp.float32)
        gate = near_ref[:, wide:] + jnp.dot(normed, weights[:, wide:], preferred_element_type=jnp.float32)
    else:
        columns = slice(block * wide, (block + 1) * wide)
        value = jnp.dot(normed_ref[...], weight_refs[0][:, columns], preferred_element_type=jnp.float32)
        columns = slice(channels + block * wide, channels + (block + 1) * wide)
        gate = jnp.dot(normed_ref[...], weight_refs[0][:, columns], preferred_element_type=jnp.float32)
    start, length = place_ref[1], place_ref[2]
    position = start - HALO + lax.broadcasted_iota(jnp.int32, (ext_rows, 1), 0)
    valid = (position >= 0) & (position < length)
    kept = jnp.where(valid, value * jax.nn.sigmoid(gate), 0.0)
    kept = kept.astype(jnp.bfloat16).astype(jnp.float32)
    first = HALO - (taps - 1) // 2
    step = 64
    for unit in range(wide // LANES):
        lanes = slice(unit * LANES, (unit + 1) * LANES)
        tap_lanes = slice(block * wide + unit * LANES, block * wide + (unit + 1) * LANES)
        column = kept[:, lanes]
        gated[0] = column
        for phase in range(1, 8):
            gated[phase] = pltpu.roll(column, ext_rows - phase, 0)
        for at in range(0, row_count, step):
            acc = None
            for tap in range(taps):
                base = at + (first + tap) // 8 * 8
                term = gated[(first + tap) % 8, base : base + step, :] * taps_ref[tap : tap + 1, tap_lanes]
                acc = term if acc is None else acc + term
            conv_ref[at : at + step, lanes] = acc
    here = start + lax.broadcasted_iota(jnp.int32, (row_count, 1), 0) < length
    count = jnp.clip(length - start, 0, row_count).astype(jnp.float32)
    conv = conv_ref[...]
    mean = jnp.sum(jnp.where(here, conv, 0.0), axis=0, keepdims=True) / jnp.maximum(count, 1.0)
    deviate = jnp.where(here, conv - mean, 0.0)
    square = jnp.sum(deviate * deviate, axis=0, keepdims=True)
    stats = [mean, square, jnp.full((1, wide), count)]
    if not earlier_refs:
        for i, row in enumerate(stats):
            stats_ref[i : i + 1, :] = row
        return
    for i, row in enumerate(stats):
        for copy in range(stats_ref.shape[0]):
            stats_ref[copy, i : i + 1, block * wide : (block + 1) * wide] = row
            for other, ref in zip([j for j in ORDER if j != block], earlier_refs):
                stats_ref[copy, i : i + 1, other * wide : (other + 1) * wide] = ref[i : i + 1, :]


def front_block(block, wide, place, normed, weights, dw_kernel, earlier=(), copies=1):
    ext_rows, width = normed.shape
    row_count = ext_rows - 2 * HALO
    depth = 2 * weights[1].shape[0] if len(weights) > 1 else 16
    stats_shape = (copies, 3, dw_kernel.shape[1]) if earlier else (3, wide)
    return pl.pallas_call(
        functools.partial(front_kernel, block, len(earlier)),
        out_shape=(
            jax.ShapeDtypeStruct((row_count, wide), jnp.float32),
            jax.ShapeDtypeStruct(stats_shape, jnp.float32),
        ),
        in_specs=[pl.BlockSpec(memory_space=pltpu.SMEM)]
        + [pl.BlockSpec(memory_space=VMEM)] * (2 + len(weights) + len(earlier)),
        out_specs=[pl.BlockSpec(memory_space=VMEM)] * 2,
        scratch_shapes=[
            VMEM((depth, 2 * wide), jnp.bfloat16),
            VMEM((8, ext_rows, LANES), jnp.float32),
        ],
        compiler_params=params(10),
        cost_estimate=cost(10**8),
        name="front",
    )(place, normed, *earlier, *weights, dw_kernel)


def merged(parts):
    means, squares, counts = zip(*parts)
    count = sum(counts)
    mean = sum(n * m for n, m in zip(counts, means)) / jnp.maximum(count, 1.0)
    square = sum(squares) + sum(n * (m - mean) * (m - mean) for n, m in zip(counts, means))
    return mean, square, count


def rows_of(refs):
    return [[ref[copy, i : i + 1, :] for i in range(3)] for ref in refs for copy in range(ref.shape[0])]


def merge_kernel(stats_ref, out_ref):
    for i, row in enumerate(merged(rows_of([stats_ref]))):
        for copy in range(out_ref.shape[0]):
            out_ref[copy, i : i + 1, :] = row


def merge(stats, copies):
    return pl.pallas_call(
        merge_kernel,
        out_shape=jax.ShapeDtypeStruct((copies,) + stats.shape[1:], jnp.float32),
        in_specs=[pl.BlockSpec(memory_space=VMEM)],
        out_specs=pl.BlockSpec(memory_space=VMEM),
        compiler_params=params(8),
        cost_estimate=cost(10**8),
        name="merge",
    )(stats)


def back_kernel(stat_count, place_ref, gain_ref, shift_ref, *refs):
    stat_refs, refs = refs[:stat_count], refs[stat_count:]
    *conv_refs, out_ref, rows_out, sems, weights = refs
    convs, weight_refs = conv_refs[:3], conv_refs[3:]
    row_count, wide = convs[0].shape
    if len(weight_refs) > 1:
        depth = weight_refs[0].shape[0]
        for i, weight_ref in enumerate(weight_refs):
            at = pl.multiple_of(lax.bitwise_xor(place_ref[0], i) * depth, depth)
            weights[pl.ds(at, depth), :] = weight_ref[...]
    else:
        weights[...] = weight_refs[0][...]
    mean, square, count = merged(rows_of(stat_refs))
    scale = lax.rsqrt(square / count + 1e-05) * gain_ref[...]
    shift = shift_ref[...]
    pieces, rows, columns = rows_out.shape
    across = out_ref.shape[1] // columns
    copies = []
    for piece in range(pieces // across):
        here = slice(piece * rows, (piece + 1) * rows)
        parts = []
        for i, conv_ref in enumerate(convs):
            lanes = slice(i * wide, (i + 1) * wide)
            scaled = (conv_ref[here, :] - mean[:, lanes]) * scale[:, lanes] + shift[:, lanes]
            parts.append((scaled * jax.nn.sigmoid(scaled)).astype(jnp.bfloat16))
        activated = jnp.concatenate(parts, axis=1)
        position = place_ref[1] + piece * rows + lax.broadcasted_iota(jnp.int32, (rows, 1), 0)
        for j in range(across):
            lanes = slice(j * columns, (j + 1) * columns)
            result = jnp.dot(activated, weights[:, lanes], preferred_element_type=jnp.float32)
            slot = piece * across + j
            rows_out[slot] = jnp.where(position < place_ref[2], result, 0.0).astype(jnp.bfloat16)
            copy = pltpu.make_async_copy(rows_out.at[slot], out_ref.at[here, lanes], sems.at[slot])
            copy.start()
            copies.append(copy)
    for copy in copies:
        copy.wait()


def back(place, stats, gain, shift, convs, weights):
    row_count = convs[0].shape[0]
    channels, width = gain.shape[1], weights[0].shape[1]
    pieces, across = 4, 2
    return pl.pallas_call(
        functools.partial(back_kernel, len(stats)),
        out_shape=jax.ShapeDtypeStruct((row_count, width), jnp.bfloat16),
        in_specs=[pl.BlockSpec(memory_space=pltpu.SMEM)]
        + [pl.BlockSpec(memory_space=VMEM)] * (2 + len(stats) + len(convs) + len(weights)),
        out_specs=pl.BlockSpec(memory_space=pl.ANY),
        scratch_shapes=[
            VMEM((pieces, row_count * across // pieces, width // across), jnp.bfloat16),
            pltpu.SemaphoreType.DMA((pieces,)),
            VMEM((channels, width), jnp.bfloat16),
        ],
        compiler_params=params(10),
        cost_estimate=cost(10**9),
        name="back",
    )(place, gain, shift, *stats, *convs, *weights)


def everyones(copies, groups):
    return lax.all_to_all(copies, ("fsdp", "ctx"), 0, 0, axis_index_groups=groups, tiled=True)


def tie(*values):
    return lax.optimization_barrier(values)


def body(frames, lengths, ln_gain, w_in, dw_kernel, bn_gain, bn_shift, w_out):
    _, row_count, model_width = frames.shape
    channels = dw_kernel.shape[1]
    wide = channels // 3
    ctx, fsdp = lax.axis_index("ctx"), lax.axis_index("fsdp")
    ctx_count, fsdp_count = lax.axis_size("ctx"), lax.axis_size("fsdp")
    direct = fsdp_count == 4 and ctx_count == 8
    rows = frames[0]
    gain = ln_gain[None]
    parity = lax.rem(ctx, 2)
    place = jnp.stack([fsdp, ctx * row_count, lengths[0], parity]).astype(jnp.int32)
    ends = ctx_count - 1
    down, up = [(i, i + 1) for i in range(ends)], [(i + 1, i) for i in range(ends)]
    both = ("fsdp", "ctx")
    member = lambda f, p: f * ctx_count + p

    def front(block, weights, *extra):
        return front_block(block, wide, place, normed, weights, dw_kernel, *extra)

    if direct:
        two, zero, one = (swap(part, "fsdp", 2) for part in cut(place, w_in, wide))
        across = swap(w_in, "fsdp", 1)
        normed, inner, outer = normalize_rows(place, rows, gain)
        normed, two = tie(normed, two)
        two = [two, swap(two, "ctx", 1)]
        inner = swap(inner, "ctx", 1)
        pairs = [(i, i + 1) for i in range(1, ends, 2)]
        outer = lax.ppermute(outer, "ctx", pairs + [(j, i) for i, j in pairs])
        normed, inner, outer, zero = tie(normed, inner, outer, zero)
        zero = [zero, swap(zero, "ctx", 1)]
        two.append(swap(two[0], "fsdp", 1))
        zero.append(swap(zero[0], "fsdp", 1))
        normed, *partials = near_product(place, normed, inner, outer, gain, w_in, across)
        partials[2], *parts = tie(partials[2], *two, *zero, w_out)
        two, zero, w_out = parts[:3], parts[3:6], parts[6]
        two.append(swap(two[1], "fsdp", 1))
        zero.append(swap(zero[1], "fsdp", 1))
        conv_two, stat_two = front(2, [partials[2], *two])
        conv_two, partials[0], one = tie(conv_two, partials[0], one)
        beyond_one = swap(one, "fsdp", 1)
        conv_zero, stat_zero = front(0, [partials[0], *zero])
        conv_zero, w_out = tie(conv_zero, w_out)
        remote_out, across_out = swap(w_out, "fsdp", 2), swap(w_out, "fsdp", 1)
        conv_one, stats = front(1, [partials[1], one, beyond_one], (stat_two, stat_zero), 1)
        convs = [conv_zero, conv_one, conv_two]

        def others(flips):
            return [
                lax.ppermute(
                    stats,
                    both,
                    [(member(f, p), member(f ^ df, p ^ dp)) for f in range(4) for p in range(8)],
                )
                for df, dp in flips
            ]

        def union(parts):
            return jnp.stack(merged([[part[:, i] for i in range(3)] for part in parts]), 1)

        stats = union([stats] + others([(1, 0)]))
        stats = union([stats] + others([(0, 2), (0, 4), (0, 6)]))
        stats = [stats] + others([(2, 0), (0, 1), (2, 1)])
        out_weights = [w_out, across_out, remote_out, swap(remote_out, "fsdp", 1)]
    else:
        full_in = lax.all_gather(w_in, "fsdp", axis=0, tiled=True)
        out_weights = [lax.all_gather(w_out, "fsdp", axis=0, tiled=True)]
        before = lax.ppermute(rows[-HALO:], "ctx", down)
        after = lax.ppermute(rows[:HALO], "ctx", up)
        inner = jnp.where(parity == 0, after, before)
        outer = jnp.where(parity == 0, before, after)
        normed, _, _ = normalize_rows(place, rows, gain)
        (normed,) = near_product(place, normed, inner, outer, gain)
        near_by = 2 if ctx_count % 2 == 0 else 1
        groups = [
            [member(f, p + i) for f in range(fsdp_count) for i in range(near_by)]
            for p in range(0, ctx_count, near_by)
        ]
        convs, stats = [None] * 3, []
        for block in ORDER:
            extra = (stats, len(groups[0])) if block == ORDER[-1] else ()
            convs[block], stat = front(block, [full_in], *extra)
            stats.append(stat)
        stats = merge(everyones(stats[2], groups), len(groups))
        groups = [
            [member(f, p + i) for p in range(0, ctx_count, near_by)]
            for f in range(fsdp_count)
            for i in range(near_by)
        ]
        stats = [everyones(stats, groups)]
    result = back(place, stats, bn_gain[None], bn_shift[None], convs, out_weights)
    return result[None]


def solution(mesh):
    return jax.shard_map(
        body,
        mesh=mesh,
        in_specs=(
            P("fsdp", "ctx", None),
            P("fsdp"),
            P(),
            P("fsdp", None),
            P(),
            P(),
            P(),
            P("fsdp", None),
        ),
        out_specs=P("fsdp", "ctx", None),
        check_vma=False,
    )
```

```python
import functools

import jax
import jax.numpy as jnp
from jax import lax
from jax.experimental import pallas as pl
from jax.experimental.pallas import tpu as pltpu
from jax.sharding import PartitionSpec as P

HALO = 16
LANES = 128
MIB = 1024 * 1024
VMEM = pltpu.VMEM
ORDER = (2, 0, 1)


def cost(flops):
    return pl.CostEstimate(flops=flops, bytes_accessed=0, transcendentals=0)


def params(mib):
    return pltpu.CompilerParams(vmem_limit_bytes=mib * MIB)


def swap(value, axis, bit):
    return lax.ppermute(value, axis, [(i, i ^ bit) for i in range(lax.axis_size(axis))])


def cut_kernel(place_ref, shard_ref, out_shard_ref, two_ref, zero_ref, one_ref, half_ref):
    wide = two_ref.shape[1]
    channels = shard_ref.shape[1] // 2
    odd = place_ref[3]
    for block, ref in ((2, two_ref), (0, zero_ref)):
        at = pl.multiple_of(odd * channels + block * wide, wide)
        ref[...] = shard_ref[:, pl.ds(at, wide)]
    for i in range(2):
        at = i * channels + wide
        one_ref[:, i * wide : (i + 1) * wide] = shard_ref[:, at : at + wide]
    rows = half_ref.shape[0]
    half_ref[...] = out_shard_ref[pl.ds(pl.multiple_of(odd * rows, rows), rows), :]


def cut(place, shard, out_shard, wide):
    depth = shard.shape[0]
    shapes = [(depth, wide), (depth, wide), (depth, 2 * wide)]
    shapes.append((out_shard.shape[0] // 2, out_shard.shape[1]))
    return pl.pallas_call(
        cut_kernel,
        out_shape=[jax.ShapeDtypeStruct(shape, jnp.bfloat16) for shape in shapes],
        in_specs=[pl.BlockSpec(memory_space=pltpu.SMEM)] + [pl.BlockSpec(memory_space=VMEM)] * 2,
        out_specs=[pl.BlockSpec(memory_space=VMEM)] * len(shapes),
        compiler_params=params(4),
        cost_estimate=cost(10**8),
        name="cut",
    )(place, shard, out_shard)


def normalize(values, gain):
    values = values.astype(jnp.float32)
    centre = jnp.mean(values, axis=-1, keepdims=True)
    deviate = values - centre
    spread = jnp.mean(deviate * deviate, axis=-1, keepdims=True)
    return (deviate * lax.rsqrt(spread + 1e-05) * gain).astype(jnp.bfloat16)


def norm_kernel(place_ref, rows_ref, gain_ref, out_ref, inner_ref, outer_ref):
    step = 64
    row_count = rows_ref.shape[0]

    @pl.loop(0, row_count // step)
    def _(i):
        here = pl.ds(pl.multiple_of(i * step, step), step)
        out_ref[here, :] = normalize(rows_ref[here, :], gain_ref[...])

    odd = place_ref[3]
    last = row_count - HALO
    inner_ref[...] = rows_ref[pl.ds(pl.multiple_of((1 - odd) * last, HALO), HALO), :]
    outer_ref[...] = rows_ref[pl.ds(pl.multiple_of(odd * last, HALO), HALO), :]


def normalize_rows(place, rows, gain):
    row_count, width = rows.shape
    shapes = [(row_count, width), (HALO, width), (HALO, width)]
    return pl.pallas_call(
        norm_kernel,
        out_shape=[jax.ShapeDtypeStruct(shape, jnp.bfloat16) for shape in shapes],
        in_specs=[pl.BlockSpec(memory_space=pltpu.SMEM)] + [pl.BlockSpec(memory_space=VMEM)] * 2,
        out_specs=[pl.BlockSpec(memory_space=VMEM)] * 3,
        compiler_params=params(4),
        cost_estimate=cost(10**8),
        name="layer_norm",
    )(place, rows, gain)


def near_kernel(place_ref, rows_ref, inner_ref, outer_ref, gain_ref, *refs):
    row_count = rows_ref.shape[0]
    gain = gain_ref[...]
    *weight_refs, ext_ref = refs[:3] if len(refs) > 1 else refs
    odd = place_ref[3]
    at = pl.multiple_of((1 - odd) * (HALO + row_count), HALO)
    ext_ref[pl.ds(at, HALO), :] = normalize(inner_ref[...], gain)
    at = pl.multiple_of(odd * (HALO + row_count), HALO)
    ext_ref[pl.ds(at, HALO), :] = normalize(outer_ref[...], gain)
    ext_ref[HALO : HALO + row_count, :] = rows_ref[...]
    if not weight_refs:
        return
    *out_refs, weights = refs[3:]
    own = place_ref[0]
    depth, width = weight_refs[0].shape
    for i, weight_ref in enumerate(weight_refs):
        at = pl.multiple_of(lax.bitwise_xor(own % 2, i) * depth, depth)
        weights[pl.ds(at, depth), :] = weight_ref[...]
    near = pl.ds(pl.multiple_of(own // 2 * (2 * depth), 2 * depth), 2 * depth)
    wide = out_refs[0].shape[1] // 2
    channels = width // 2
    for block, out_ref in enumerate(out_refs):
        for i in range(2):
            columns = slice(i * channels + block * wide, i * channels + (block + 1) * wide)
            out_ref[:, i * wide : (i + 1) * wide] = jnp.dot(
                ext_ref[:, near], weights[:, columns], preferred_element_type=jnp.float32
            )


def near_product(place, rows, inner, outer, gain, *shards):
    row_count, width = rows.shape
    ext_rows = row_count + 2 * HALO
    shapes = [jax.ShapeDtypeStruct((ext_rows, width), jnp.bfloat16)]
    scratch = []
    if shards:
        shapes += [jax.ShapeDtypeStruct((ext_rows, width // 3), jnp.float32)] * 3
        scratch.append(VMEM((2 * shards[0].shape[0], width), jnp.bfloat16))
    return pl.pallas_call(
        near_kernel,
        out_shape=shapes,
        in_specs=[pl.BlockSpec(memory_space=pltpu.SMEM)]
        + [pl.BlockSpec(memory_space=VMEM)] * (4 + len(shards)),
        out_specs=[pl.BlockSpec(memory_space=VMEM)] * len(shapes),
        scratch_shapes=scratch,
        compiler_params=params(8),
        cost_estimate=cost(10**8),
        name="near",
    )(place, rows, inner, outer, gain, *shards)


def front_kernel(block, earlier, place_ref, normed_ref, *refs):
    refs, earlier_refs = refs[earlier:], refs[:earlier]
    *weight_refs, taps_ref, conv_ref, stats_ref, weights, gated = refs
    ext_rows = normed_ref.shape[0]
    row_count, wide = conv_ref.shape
    taps, channels = taps_ref.shape
    if len(weight_refs) > 1:
        near_ref, *far_refs = weight_refs
        own = place_ref[0]
        depth = far_refs[0].shape[0]
        halves = len(far_refs) // 2
        for i in range(2):
            at = pl.multiple_of(lax.bitwise_xor(own % 2, i) * depth, depth)
            if halves == 1:
                weights[pl.ds(at, depth), :] = far_refs[i][...]
                continue
            for j in range(2):
                column = pl.multiple_of(lax.bitwise_xor(place_ref[3], j) * wide, wide)
                weights[pl.ds(at, depth), pl.ds(column, wide)] = far_refs[2 * i + j][...]
        far = pl.ds(pl.multiple_of((1 - own // 2) * (2 * depth), 2 * depth), 2 * depth)
        normed = normed_ref[:, far]
        value = near_ref[:, 0:wide] + jnp.dot(normed, weights[:, 0:wide], preferred_element_type=jnp.float32)
        gate = near_ref[:, wide:] + jnp.dot(normed, weights[:, wide:], preferred_element_type=jnp.float32)
    else:
        columns = slice(block * wide, (block + 1) * wide)
        value = jnp.dot(normed_ref[...], weight_refs[0][:, columns], preferred_element_type=jnp.float32)
        columns = slice(channels + block * wide, channels + (block + 1) * wide)
        gate = jnp.dot(normed_ref[...], weight_refs[0][:, columns], preferred_element_type=jnp.float32)
    start, length = place_ref[1], place_ref[2]
    position = start - HALO + lax.broadcasted_iota(jnp.int32, (ext_rows, 1), 0)
    valid = (position >= 0) & (position < length)
    kept = jnp.where(valid, value * jax.nn.sigmoid(gate), 0.0)
    kept = kept.astype(jnp.bfloat16).astype(jnp.float32)
    first = HALO - (taps - 1) // 2
    step = 128
    for unit in range(wide // LANES):
        lanes = slice(unit * LANES, (unit + 1) * LANES)
        tap_lanes = slice(block * wide + unit * LANES, block * wide + (unit + 1) * LANES)
        column = kept[:, lanes]
        gated[0] = column
        for phase in range(1, 8):
            gated[phase] = pltpu.roll(column, ext_rows - phase, 0)
        for at in range(0, row_count, step):
            acc = None
            for phase in range(8):
                offsets = [k for k in range(phase, first + taps, 8) if k >= first]
                low = offsets[0] - phase
                tiles = gated[phase, at + low : at + offsets[-1] - phase + step, :]
                for offset in offsets:
                    base = offset - phase - low
                    tap = offset - first
                    term = tiles[base : base + step] * taps_ref[tap : tap + 1, tap_lanes]
                    acc = term if acc is None else acc + term
            conv_ref[at : at + step, lanes] = acc
    here = start + lax.broadcasted_iota(jnp.int32, (row_count, 1), 0) < length
    count = jnp.clip(length - start, 0, row_count).astype(jnp.float32)
    conv = conv_ref[...]
    mean = jnp.sum(jnp.where(here, conv, 0.0), axis=0, keepdims=True) / jnp.maximum(count, 1.0)
    deviate = jnp.where(here, conv - mean, 0.0)
    square = jnp.sum(deviate * deviate, axis=0, keepdims=True)
    stats = [mean, square, jnp.full((1, wide), count)]
    if not earlier_refs:
        for i, row in enumerate(stats):
            stats_ref[i : i + 1, :] = row
        return
    for i, row in enumerate(stats):
        for copy in range(stats_ref.shape[0]):
            stats_ref[copy, i : i + 1, block * wide : (block + 1) * wide] = row
            for other, ref in zip([j for j in ORDER if j != block], earlier_refs):
                stats_ref[copy, i : i + 1, other * wide : (other + 1) * wide] = ref[i : i + 1, :]


def front_block(block, wide, place, normed, weights, dw_kernel, earlier=(), copies=1):
    ext_rows, width = normed.shape
    row_count = ext_rows - 2 * HALO
    depth = 2 * weights[1].shape[0] if len(weights) > 1 else 16
    stats_shape = (copies, 3, dw_kernel.shape[1]) if earlier else (3, wide)
    return pl.pallas_call(
        functools.partial(front_kernel, block, len(earlier)),
        out_shape=(
            jax.ShapeDtypeStruct((row_count, wide), jnp.float32),
            jax.ShapeDtypeStruct(stats_shape, jnp.float32),
        ),
        in_specs=[pl.BlockSpec(memory_space=pltpu.SMEM)]
        + [pl.BlockSpec(memory_space=VMEM)] * (2 + len(weights) + len(earlier)),
        out_specs=[pl.BlockSpec(memory_space=VMEM)] * 2,
        scratch_shapes=[
            VMEM((depth, 2 * wide), jnp.bfloat16),
            VMEM((8, ext_rows, LANES), jnp.float32),
        ],
        compiler_params=params(10),
        cost_estimate=cost(4 * 10**9 if block == ORDER[1] else 10**8),
        name="front",
    )(place, normed, *earlier, *weights, dw_kernel)


def merged(parts):
    means, squares, counts = zip(*parts)
    count = sum(counts)
    mean = sum(n * m for n, m in zip(counts, means)) / jnp.maximum(count, 1.0)
    square = sum(squares) + sum(n * (m - mean) * (m - mean) for n, m in zip(counts, means))
    return mean, square, count


def rows_of(refs):
    return [[ref[copy, i : i + 1, :] for i in range(3)] for ref in refs for copy in range(ref.shape[0])]


def merge_kernel(stats_ref, out_ref):
    for i, row in enumerate(merged(rows_of([stats_ref]))):
        for copy in range(out_ref.shape[0]):
            out_ref[copy, i : i + 1, :] = row


def merge(stats, copies):
    return pl.pallas_call(
        merge_kernel,
        out_shape=jax.ShapeDtypeStruct((copies,) + stats.shape[1:], jnp.float32),
        in_specs=[pl.BlockSpec(memory_space=VMEM)],
        out_specs=pl.BlockSpec(memory_space=VMEM),
        compiler_params=params(8),
        cost_estimate=cost(10**8),
        name="merge",
    )(stats)


def back_kernel(stat_count, place_ref, gain_ref, shift_ref, *refs):
    stat_refs, refs = refs[:stat_count], refs[stat_count:]
    *conv_refs, out_ref, rows_out, sems, weights = refs
    convs, weight_refs = conv_refs[:3], conv_refs[3:]
    row_count, wide = convs[0].shape
    if len(weight_refs) > 1:
        depth = weight_refs[0].shape[0]
        for i, weight_ref in enumerate(weight_refs[:2]):
            at = pl.multiple_of(lax.bitwise_xor(place_ref[0], i) * depth, depth)
            weights[pl.ds(at, depth), :] = weight_ref[...]
        half = depth // 2
        for i, weight_ref in enumerate(weight_refs[2:]):
            at = lax.bitwise_xor(place_ref[0], 2 + i // 2) * depth
            at += lax.bitwise_xor(place_ref[3], i % 2) * half
            weights[pl.ds(pl.multiple_of(at, half), half), :] = weight_ref[...]
    else:
        weights[...] = weight_refs[0][...]
    mean, square, count = merged(rows_of(stat_refs))
    scale = lax.rsqrt(square / count + 1e-05) * gain_ref[...]
    shift = shift_ref[...]
    pieces, rows, columns = rows_out.shape
    across = out_ref.shape[1] // columns
    copies = []
    for piece in range(pieces // across):
        here = slice(piece * rows, (piece + 1) * rows)
        parts = []
        for i, conv_ref in enumerate(convs):
            lanes = slice(i * wide, (i + 1) * wide)
            scaled = (conv_ref[here, :] - mean[:, lanes]) * scale[:, lanes] + shift[:, lanes]
            parts.append((scaled * jax.nn.sigmoid(scaled)).astype(jnp.bfloat16))
        activated = jnp.concatenate(parts, axis=1)
        position = place_ref[1] + piece * rows + lax.broadcasted_iota(jnp.int32, (rows, 1), 0)
        for j in range(across):
            lanes = slice(j * columns, (j + 1) * columns)
            result = jnp.dot(activated, weights[:, lanes], preferred_element_type=jnp.float32)
            slot = piece * across + j
            rows_out[slot] = jnp.where(position < place_ref[2], result, 0.0).astype(jnp.bfloat16)
            copy = pltpu.make_async_copy(rows_out.at[slot], out_ref.at[here, lanes], sems.at[slot])
            copy.start()
            copies.append(copy)
    for copy in copies:
        copy.wait()


def back(place, stats, gain, shift, convs, weights):
    row_count = convs[0].shape[0]
    channels, width = gain.shape[1], weights[0].shape[1]
    pieces, across = 4, 2
    return pl.pallas_call(
        functools.partial(back_kernel, len(stats)),
        out_shape=jax.ShapeDtypeStruct((row_count, width), jnp.bfloat16),
        in_specs=[pl.BlockSpec(memory_space=pltpu.SMEM)]
        + [pl.BlockSpec(memory_space=VMEM)] * (2 + len(stats) + len(convs) + len(weights)),
        out_specs=pl.BlockSpec(memory_space=pl.ANY),
        scratch_shapes=[
            VMEM((pieces, row_count * across // pieces, width // across), jnp.bfloat16),
            pltpu.SemaphoreType.DMA((pieces,)),
            VMEM((channels, width), jnp.bfloat16),
        ],
        compiler_params=params(10),
        cost_estimate=cost(10**9),
        name="back",
    )(place, gain, shift, *stats, *convs, *weights)


def everyones(copies, groups):
    return lax.all_to_all(copies, ("fsdp", "ctx"), 0, 0, axis_index_groups=groups, tiled=True)


def tie(*values):
    return lax.optimization_barrier(values)


def body(frames, lengths, ln_gain, w_in, dw_kernel, bn_gain, bn_shift, w_out):
    _, row_count, model_width = frames.shape
    channels = dw_kernel.shape[1]
    wide = channels // 3
    ctx, fsdp = lax.axis_index("ctx"), lax.axis_index("fsdp")
    ctx_count, fsdp_count = lax.axis_size("ctx"), lax.axis_size("fsdp")
    direct = fsdp_count == 4 and ctx_count == 8
    rows = frames[0]
    gain = ln_gain[None]
    parity = lax.rem(ctx, 2)
    place = jnp.stack([fsdp, ctx * row_count, lengths[0], parity]).astype(jnp.int32)
    ends = ctx_count - 1
    down, up = [(i, i + 1) for i in range(ends)], [(i + 1, i) for i in range(ends)]
    both = ("fsdp", "ctx")
    member = lambda f, p: f * ctx_count + p

    def front(block, weights, *extra):
        return front_block(block, wide, place, normed, weights, dw_kernel, *extra)

    if direct:
        two, zero, one, half = (swap(part, "fsdp", 2) for part in cut(place, w_in, w_out, wide))
        across = swap(w_in, "fsdp", 1)
        normed, inner, outer = normalize_rows(place, rows, gain)
        normed, two = tie(normed, two)
        two = [two, swap(two, "ctx", 1)]
        inner = swap(inner, "ctx", 1)
        pairs = [(i, i + 1) for i in range(1, ends, 2)]
        outer = lax.ppermute(outer, "ctx", pairs + [(j, i) for i, j in pairs])
        normed, inner, outer, two[1], zero = tie(normed, inner, outer, two[1], zero)
        zero = [zero, swap(zero, "ctx", 1)]
        two.append(swap(two[0], "fsdp", 1))
        zero.append(swap(zero[0], "fsdp", 1))
        normed, *partials = near_product(place, normed, inner, outer, gain, w_in, across)
        partials[2], *parts = tie(partials[2], *two, *zero, half, w_out)
        two, zero, half, w_out = parts[:3], parts[3:6], *parts[6:]
        halves = [half, swap(half, "ctx", 1)]
        two.append(swap(two[1], "fsdp", 1))
        zero.append(swap(zero[1], "fsdp", 1))
        conv_two, stat_two = front(2, [partials[2], *two])
        conv_two, partials[0], one = tie(conv_two, partials[0], one)
        beyond_one = swap(one, "fsdp", 1)
        conv_zero, stat_zero = front(0, [partials[0], *zero])
        across_out, beyond_half = swap(w_out, "fsdp", 1), swap(half, "fsdp", 1)
        conv_one, stats = front(1, [partials[1], one, beyond_one], (stat_two, stat_zero), 1)
        convs = [conv_zero, conv_one, conv_two]

        def others(flips):
            return [
                lax.ppermute(
                    stats,
                    both,
                    [(member(f, p), member(f ^ df, p ^ dp)) for f in range(4) for p in range(8)],
                )
                for df, dp in flips
            ]

        def union(parts):
            return jnp.stack(merged([[part[:, i] for i in range(3)] for part in parts]), 1)

        stats, halves[1], across_out, beyond_half = tie(stats, halves[1], across_out, beyond_half)
        beyond_rest = swap(halves[1], "fsdp", 1)
        stats = union([stats] + others([(1, 0)]))
        stats, beyond_rest = tie(stats, beyond_rest)
        out_weights = [w_out, across_out, *halves, beyond_half, beyond_rest]
        stats = union([stats] + others([(0, 2)]))
        stats = union([stats] + others([(0, 4)]))
        stats = [stats] + others([(0, 1), (2, 0), (2, 1)])
    else:
        full_in = lax.all_gather(w_in, "fsdp", axis=0, tiled=True)
        out_weights = [lax.all_gather(w_out, "fsdp", axis=0, tiled=True)]
        before = lax.ppermute(rows[-HALO:], "ctx", down)
        after = lax.ppermute(rows[:HALO], "ctx", up)
        inner = jnp.where(parity == 0, after, before)
        outer = jnp.where(parity == 0, before, after)
        normed, _, _ = normalize_rows(place, rows, gain)
        (normed,) = near_product(place, normed, inner, outer, gain)
        near_by = 2 if ctx_count % 2 == 0 else 1
        groups = [
            [member(f, p + i) for f in range(fsdp_count) for i in range(near_by)]
            for p in range(0, ctx_count, near_by)
        ]
        convs, stats = [None] * 3, []
        for block in ORDER:
            extra = (stats, len(groups[0])) if block == ORDER[-1] else ()
            convs[block], stat = front(block, [full_in], *extra)
            stats.append(stat)
        stats = merge(everyones(stats[2], groups), len(groups))
        groups = [
            [member(f, p + i) for p in range(0, ctx_count, near_by)]
            for f in range(fsdp_count)
            for i in range(near_by)
        ]
        stats = [everyones(stats, groups)]
    result = back(place, stats, bn_gain[None], bn_shift[None], convs, out_weights)
    return result[None]


def solution(mesh):
    return jax.shard_map(
        body,
        mesh=mesh,
        in_specs=(
            P("fsdp", "ctx", None),
            P("fsdp"),
            P(),
            P("fsdp", None),
            P(),
            P(),
            P(),
            P("fsdp", None),
        ),
        out_specs=P("fsdp", "ctx", None),
        check_vma=False,
    )
```

```python
import functools

import jax
import jax.numpy as jnp
from jax import lax
from jax.experimental import pallas as pl
from jax.experimental.pallas import tpu as pltpu
from jax.sharding import PartitionSpec as P

HALO = 16
LANES = 128
MIB = 1024 * 1024
VMEM = pltpu.VMEM
ORDER = (2, 0, 1)


def cost(flops):
    return pl.CostEstimate(flops=flops, bytes_accessed=0, transcendentals=0)


def params(mib):
    return pltpu.CompilerParams(vmem_limit_bytes=mib * MIB)


def swap(value, axis, bit):
    return lax.ppermute(value, axis, [(i, i ^ bit) for i in range(lax.axis_size(axis))])


def cut_kernel(place_ref, shard_ref, two_ref, zero_ref, one_ref):
    wide = two_ref.shape[1]
    channels = shard_ref.shape[1] // 2
    for block, ref in ((2, two_ref), (0, zero_ref)):
        at = pl.multiple_of(place_ref[3] * channels + block * wide, wide)
        ref[...] = shard_ref[:, pl.ds(at, wide)]
    for i in range(2):
        at = i * channels + wide
        one_ref[:, i * wide : (i + 1) * wide] = shard_ref[:, at : at + wide]


def cut(place, shard, wide):
    depth = shard.shape[0]
    shapes = [(depth, wide), (depth, wide), (depth, 2 * wide)]
    return pl.pallas_call(
        cut_kernel,
        out_shape=[jax.ShapeDtypeStruct(shape, jnp.bfloat16) for shape in shapes],
        in_specs=[pl.BlockSpec(memory_space=pltpu.SMEM), pl.BlockSpec(memory_space=VMEM)],
        out_specs=[pl.BlockSpec(memory_space=VMEM)] * 3,
        compiler_params=params(4),
        cost_estimate=cost(10**8),
        name="cut",
    )(place, shard)


def normalize(values, gain):
    values = values.astype(jnp.float32)
    centre = jnp.mean(values, axis=-1, keepdims=True)
    deviate = values - centre
    spread = jnp.mean(deviate * deviate, axis=-1, keepdims=True)
    return (deviate * lax.rsqrt(spread + 1e-05) * gain).astype(jnp.bfloat16)


def norm_kernel(place_ref, rows_ref, gain_ref, out_ref, inner_ref, outer_ref):
    step = 64
    row_count = rows_ref.shape[0]

    @pl.loop(0, row_count // step)
    def _(i):
        here = pl.ds(pl.multiple_of(i * step, step), step)
        out_ref[here, :] = normalize(rows_ref[here, :], gain_ref[...])

    odd = place_ref[3]
    last = row_count - HALO
    inner_ref[...] = rows_ref[pl.ds(pl.multiple_of((1 - odd) * last, HALO), HALO), :]
    outer_ref[...] = rows_ref[pl.ds(pl.multiple_of(odd * last, HALO), HALO), :]


def normalize_rows(place, rows, gain):
    row_count, width = rows.shape
    shapes = [(row_count, width), (HALO, width), (HALO, width)]
    return pl.pallas_call(
        norm_kernel,
        out_shape=[jax.ShapeDtypeStruct(shape, jnp.bfloat16) for shape in shapes],
        in_specs=[pl.BlockSpec(memory_space=pltpu.SMEM)] + [pl.BlockSpec(memory_space=VMEM)] * 2,
        out_specs=[pl.BlockSpec(memory_space=VMEM)] * 3,
        compiler_params=params(4),
        cost_estimate=cost(10**8),
        name="layer_norm",
    )(place, rows, gain)


def near_kernel(place_ref, rows_ref, inner_ref, outer_ref, gain_ref, *refs):
    row_count = rows_ref.shape[0]
    gain = gain_ref[...]
    *weight_refs, ext_ref = refs[:3] if len(refs) > 1 else refs
    odd = place_ref[3]
    at = pl.multiple_of((1 - odd) * (HALO + row_count), HALO)
    ext_ref[pl.ds(at, HALO), :] = normalize(inner_ref[...], gain)
    at = pl.multiple_of(odd * (HALO + row_count), HALO)
    ext_ref[pl.ds(at, HALO), :] = normalize(outer_ref[...], gain)
    ext_ref[HALO : HALO + row_count, :] = rows_ref[...]
    if not weight_refs:
        return
    *out_refs, weights = refs[3:]
    own = place_ref[0]
    depth, width = weight_refs[0].shape
    for i, weight_ref in enumerate(weight_refs):
        at = pl.multiple_of(lax.bitwise_xor(own % 2, i) * depth, depth)
        weights[pl.ds(at, depth), :] = weight_ref[...]
    near = pl.ds(pl.multiple_of(own // 2 * (2 * depth), 2 * depth), 2 * depth)
    wide = out_refs[0].shape[1] // 2
    channels = width // 2
    for block, out_ref in enumerate(out_refs):
        for i in range(2):
            columns = slice(i * channels + block * wide, i * channels + (block + 1) * wide)
            out_ref[:, i * wide : (i + 1) * wide] = jnp.dot(
                ext_ref[:, near], weights[:, columns], preferred_element_type=jnp.float32
            )


def near_product(place, rows, inner, outer, gain, *shards):
    row_count, width = rows.shape
    ext_rows = row_count + 2 * HALO
    shapes = [jax.ShapeDtypeStruct((ext_rows, width), jnp.bfloat16)]
    scratch = []
    if shards:
        shapes += [jax.ShapeDtypeStruct((ext_rows, width // 3), jnp.float32)] * 3
        scratch.append(VMEM((2 * shards[0].shape[0], width), jnp.bfloat16))
    return pl.pallas_call(
        near_kernel,
        out_shape=shapes,
        in_specs=[pl.BlockSpec(memory_space=pltpu.SMEM)]
        + [pl.BlockSpec(memory_space=VMEM)] * (4 + len(shards)),
        out_specs=[pl.BlockSpec(memory_space=VMEM)] * len(shapes),
        scratch_shapes=scratch,
        compiler_params=params(8),
        cost_estimate=cost(10**8),
        name="near",
    )(place, rows, inner, outer, gain, *shards)


def front_kernel(block, earlier, place_ref, normed_ref, *refs):
    refs, earlier_refs = refs[earlier:], refs[:earlier]
    *weight_refs, taps_ref, conv_ref, stats_ref, weights, gated = refs
    ext_rows = normed_ref.shape[0]
    row_count, wide = conv_ref.shape
    taps, channels = taps_ref.shape
    if len(weight_refs) > 1:
        near_ref, *far_refs = weight_refs
        own = place_ref[0]
        depth = far_refs[0].shape[0]
        halves = len(far_refs) // 2
        for i in range(2):
            at = pl.multiple_of(lax.bitwise_xor(own % 2, i) * depth, depth)
            if halves == 1:
                weights[pl.ds(at, depth), :] = far_refs[i][...]
                continue
            for j in range(2):
                column = pl.multiple_of(lax.bitwise_xor(place_ref[3], j) * wide, wide)
                weights[pl.ds(at, depth), pl.ds(column, wide)] = far_refs[2 * i + j][...]
        far = pl.ds(pl.multiple_of((1 - own // 2) * (2 * depth), 2 * depth), 2 * depth)
        normed = normed_ref[:, far]
        value = near_ref[:, 0:wide] + jnp.dot(normed, weights[:, 0:wide], preferred_element_type=jnp.float32)
        gate = near_ref[:, wide:] + jnp.dot(normed, weights[:, wide:], preferred_element_type=jnp.float32)
    else:
        columns = slice(block * wide, (block + 1) * wide)
        value = jnp.dot(normed_ref[...], weight_refs[0][:, columns], preferred_element_type=jnp.float32)
        columns = slice(channels + block * wide, channels + (block + 1) * wide)
        gate = jnp.dot(normed_ref[...], weight_refs[0][:, columns], preferred_element_type=jnp.float32)
    start, length = place_ref[1], place_ref[2]
    position = start - HALO + lax.broadcasted_iota(jnp.int32, (ext_rows, 1), 0)
    valid = (position >= 0) & (position < length)
    kept = jnp.where(valid, value * jax.nn.sigmoid(gate), 0.0)
    kept = kept.astype(jnp.bfloat16).astype(jnp.float32)
    first = HALO - (taps - 1) // 2
    step = 64
    for unit in range(wide // LANES):
        lanes = slice(unit * LANES, (unit + 1) * LANES)
        tap_lanes = slice(block * wide + unit * LANES, block * wide + (unit + 1) * LANES)
        column = kept[:, lanes]
        gated[0] = column
        for phase in range(1, 8):
            gated[phase] = pltpu.roll(column, ext_rows - phase, 0)
        for at in range(0, row_count, step):
            acc = None
            for tap in range(taps):
                base = at + (first + tap) // 8 * 8
                term = gated[(first + tap) % 8, base : base + step, :] * taps_ref[tap : tap + 1, tap_lanes]
                acc = term if acc is None else acc + term
            conv_ref[at : at + step, lanes] = acc
    here = start + lax.broadcasted_iota(jnp.int32, (row_count, 1), 0) < length
    count = jnp.clip(length - start, 0, row_count).astype(jnp.float32)
    conv = conv_ref[...]
    mean = jnp.sum(jnp.where(here, conv, 0.0), axis=0, keepdims=True) / jnp.maximum(count, 1.0)
    deviate = jnp.where(here, conv - mean, 0.0)
    square = jnp.sum(deviate * deviate, axis=0, keepdims=True)
    stats = [mean, square, jnp.full((1, wide), count)]
    if not earlier_refs:
        for i, row in enumerate(stats):
            stats_ref[i : i + 1, :] = row
        return
    for i, row in enumerate(stats):
        for copy in range(stats_ref.shape[0]):
            stats_ref[copy, i : i + 1, block * wide : (block + 1) * wide] = row
            for other, ref in zip([j for j in ORDER if j != block], earlier_refs):
                stats_ref[copy, i : i + 1, other * wide : (other + 1) * wide] = ref[i : i + 1, :]


def front_block(block, wide, place, normed, weights, dw_kernel, earlier=(), copies=1):
    ext_rows, width = normed.shape
    row_count = ext_rows - 2 * HALO
    depth = 2 * weights[1].shape[0] if len(weights) > 1 else 16
    stats_shape = (copies, 3, dw_kernel.shape[1]) if earlier else (3, wide)
    return pl.pallas_call(
        functools.partial(front_kernel, block, len(earlier)),
        out_shape=(
            jax.ShapeDtypeStruct((row_count, wide), jnp.float32),
            jax.ShapeDtypeStruct(stats_shape, jnp.float32),
        ),
        in_specs=[pl.BlockSpec(memory_space=pltpu.SMEM)]
        + [pl.BlockSpec(memory_space=VMEM)] * (2 + len(weights) + len(earlier)),
        out_specs=[pl.BlockSpec(memory_space=VMEM)] * 2,
        scratch_shapes=[
            VMEM((depth, 2 * wide), jnp.bfloat16),
            VMEM((8, ext_rows, LANES), jnp.float32),
        ],
        compiler_params=params(10),
        cost_estimate=cost(4 * 10**9 if block == ORDER[0] else 10**8),
        name="front",
    )(place, normed, *earlier, *weights, dw_kernel)


def merged(parts):
    means, squares, counts = zip(*parts)
    count = sum(counts)
    mean = sum(n * m for n, m in zip(counts, means)) / jnp.maximum(count, 1.0)
    square = sum(squares) + sum(n * (m - mean) * (m - mean) for n, m in zip(counts, means))
    return mean, square, count


def rows_of(refs):
    return [[ref[copy, i : i + 1, :] for i in range(3)] for ref in refs for copy in range(ref.shape[0])]


def merge_kernel(stats_ref, out_ref):
    for i, row in enumerate(merged(rows_of([stats_ref]))):
        for copy in range(out_ref.shape[0]):
            out_ref[copy, i : i + 1, :] = row


def merge(stats, copies):
    return pl.pallas_call(
        merge_kernel,
        out_shape=jax.ShapeDtypeStruct((copies,) + stats.shape[1:], jnp.float32),
        in_specs=[pl.BlockSpec(memory_space=VMEM)],
        out_specs=pl.BlockSpec(memory_space=VMEM),
        compiler_params=params(8),
        cost_estimate=cost(10**8),
        name="merge",
    )(stats)


def back_kernel(stat_count, place_ref, gain_ref, shift_ref, *refs):
    stat_refs, refs = refs[:stat_count], refs[stat_count:]
    *conv_refs, out_ref, rows_out, sems, weights = refs
    convs, weight_refs = conv_refs[:3], conv_refs[3:]
    row_count, wide = convs[0].shape
    if len(weight_refs) > 1:
        depth = weight_refs[0].shape[0]
        for i, weight_ref in enumerate(weight_refs):
            at = pl.multiple_of(lax.bitwise_xor(place_ref[0], i) * depth, depth)
            weights[pl.ds(at, depth), :] = weight_ref[...]
    else:
        weights[...] = weight_refs[0][...]
    mean, square, count = merged(rows_of(stat_refs))
    scale = lax.rsqrt(square / count + 1e-05) * gain_ref[...]
    shift = shift_ref[...]
    pieces, rows, columns = rows_out.shape
    across = out_ref.shape[1] // columns
    copies = []
    for piece in range(pieces // across):
        here = slice(piece * rows, (piece + 1) * rows)
        parts = []
        for i, conv_ref in enumerate(convs):
            lanes = slice(i * wide, (i + 1) * wide)
            scaled = (conv_ref[here, :] - mean[:, lanes]) * scale[:, lanes] + shift[:, lanes]
            parts.append((scaled * jax.nn.sigmoid(scaled)).astype(jnp.bfloat16))
        activated = jnp.concatenate(parts, axis=1)
        position = place_ref[1] + piece * rows + lax.broadcasted_iota(jnp.int32, (rows, 1), 0)
        for j in range(across):
            lanes = slice(j * columns, (j + 1) * columns)
            result = jnp.dot(activated, weights[:, lanes], preferred_element_type=jnp.float32)
            slot = piece * across + j
            rows_out[slot] = jnp.where(position < place_ref[2], result, 0.0).astype(jnp.bfloat16)
            copy = pltpu.make_async_copy(rows_out.at[slot], out_ref.at[here, lanes], sems.at[slot])
            copy.start()
            copies.append(copy)
    for copy in copies:
        copy.wait()


def back(place, stats, gain, shift, convs, weights):
    row_count = convs[0].shape[0]
    channels, width = gain.shape[1], weights[0].shape[1]
    pieces, across = 4, 2
    return pl.pallas_call(
        functools.partial(back_kernel, len(stats)),
        out_shape=jax.ShapeDtypeStruct((row_count, width), jnp.bfloat16),
        in_specs=[pl.BlockSpec(memory_space=pltpu.SMEM)]
        + [pl.BlockSpec(memory_space=VMEM)] * (2 + len(stats) + len(convs) + len(weights)),
        out_specs=pl.BlockSpec(memory_space=pl.ANY),
        scratch_shapes=[
            VMEM((pieces, row_count * across // pieces, width // across), jnp.bfloat16),
            pltpu.SemaphoreType.DMA((pieces,)),
            VMEM((channels, width), jnp.bfloat16),
        ],
        compiler_params=params(10),
        cost_estimate=cost(10**9),
        name="back",
    )(place, gain, shift, *stats, *convs, *weights)


def everyones(copies, groups):
    return lax.all_to_all(copies, ("fsdp", "ctx"), 0, 0, axis_index_groups=groups, tiled=True)


def tie(*values):
    return lax.optimization_barrier(values)


def body(frames, lengths, ln_gain, w_in, dw_kernel, bn_gain, bn_shift, w_out):
    _, row_count, model_width = frames.shape
    channels = dw_kernel.shape[1]
    wide = channels // 3
    ctx, fsdp = lax.axis_index("ctx"), lax.axis_index("fsdp")
    ctx_count, fsdp_count = lax.axis_size("ctx"), lax.axis_size("fsdp")
    direct = fsdp_count == 4 and ctx_count == 8
    rows = frames[0]
    gain = ln_gain[None]
    parity = lax.rem(ctx, 2)
    place = jnp.stack([fsdp, ctx * row_count, lengths[0], parity]).astype(jnp.int32)
    ends = ctx_count - 1
    down, up = [(i, i + 1) for i in range(ends)], [(i + 1, i) for i in range(ends)]
    both = ("fsdp", "ctx")
    member = lambda f, p: f * ctx_count + p

    def front(block, weights, *extra):
        return front_block(block, wide, place, normed, weights, dw_kernel, *extra)

    if direct:
        two, zero, one = (swap(part, "fsdp", 2) for part in cut(place, w_in, wide))
        across = swap(w_in, "fsdp", 1)
        normed, inner, outer = normalize_rows(place, rows, gain)
        inner = swap(inner, "ctx", 1)
        pairs = [(i, i + 1) for i in range(1, ends, 2)]
        outer = lax.ppermute(outer, "ctx", pairs + [(j, i) for i, j in pairs])
        normed, inner, outer, two, zero = tie(normed, inner, outer, two, zero)
        two, zero = [two, swap(two, "ctx", 1)], [zero, swap(zero, "ctx", 1)]
        two.append(swap(two[0], "fsdp", 1))
        zero.append(swap(zero[0], "fsdp", 1))
        normed, *partials = near_product(place, normed, inner, outer, gain, w_in, across)
        partials[2], two[1], two[2], zero[2], w_out = tie(partials[2], two[1], two[2], zero[2], w_out)
        two.append(swap(two[1], "fsdp", 1))
        partials[2], one, zero[1] = tie(partials[2], one, zero[1])
        beyond_one = swap(one, "fsdp", 1)
        zero.append(swap(zero[1], "fsdp", 1))
        conv_two, stat_two = front(2, [partials[2], *two])
        conv_two, partials[0] = tie(conv_two, partials[0])
        conv_zero, stat_zero = front(0, [partials[0], *zero])
        conv_zero, partials[1] = tie(conv_zero, partials[1])
        conv_one, stats = front(1, [partials[1], one, beyond_one], (stat_two, stat_zero), 1)
        remote_out, across_out = swap(w_out, "fsdp", 2), swap(w_out, "fsdp", 1)
        convs = [conv_zero, conv_one, conv_two]

        def others(flips):
            return [
                lax.ppermute(
                    stats,
                    both,
                    [(member(f, p), member(f ^ df, p ^ dp)) for f in range(4) for p in range(8)],
                )
                for df, dp in flips
            ]

        def union(parts):
            return jnp.stack(merged([[part[:, i] for i in range(3)] for part in parts]), 1)

        stats = union([stats] + others([(1, 0)]))
        stats = union([stats] + others([(0, 2)]))
        stats = union([stats] + others([(0, 4)]))
        stats = [stats] + others([(0, 1), (2, 0), (2, 1)])
        stats[1], remote_out = tie(stats[1], remote_out)
        out_weights = [w_out, across_out, remote_out, swap(remote_out, "fsdp", 1)]
    else:
        full_in = lax.all_gather(w_in, "fsdp", axis=0, tiled=True)
        out_weights = [lax.all_gather(w_out, "fsdp", axis=0, tiled=True)]
        before = lax.ppermute(rows[-HALO:], "ctx", down)
        after = lax.ppermute(rows[:HALO], "ctx", up)
        inner = jnp.where(parity == 0, after, before)
        outer = jnp.where(parity == 0, before, after)
        normed, _, _ = normalize_rows(place, rows, gain)
        (normed,) = near_product(place, normed, inner, outer, gain)
        near_by = 2 if ctx_count % 2 == 0 else 1
        groups = [
            [member(f, p + i) for f in range(fsdp_count) for i in range(near_by)]
            for p in range(0, ctx_count, near_by)
        ]
        convs, stats = [None] * 3, []
        for block in ORDER:
            extra = (stats, len(groups[0])) if block == ORDER[-1] else ()
            convs[block], stat = front(block, [full_in], *extra)
            stats.append(stat)
        stats = merge(everyones(stats[2], groups), len(groups))
        groups = [
            [member(f, p + i) for p in range(0, ctx_count, near_by)]
            for f in range(fsdp_count)
            for i in range(near_by)
        ]
        stats = [everyones(stats, groups)]
    result = back(place, stats, bn_gain[None], bn_shift[None], convs, out_weights)
    return result[None]


def solution(mesh):
    return jax.shard_map(
        body,
        mesh=mesh,
        in_specs=(
            P("fsdp", "ctx", None),
            P("fsdp"),
            P(),
            P("fsdp", None),
            P(),
            P(),
            P(),
            P("fsdp", None),
        ),
        out_specs=P("fsdp", "ctx", None),
        check_vma=False,
    )
```

```python
import functools

import jax
import jax.numpy as jnp
from jax import lax
from jax.experimental import pallas as pl
from jax.experimental.pallas import tpu as pltpu
from jax.sharding import PartitionSpec as P

HALO = 16
LANES = 128
MIB = 1024 * 1024
VMEM = pltpu.VMEM
ORDER = (2, 0, 1)


def cost(flops):
    return pl.CostEstimate(flops=flops, bytes_accessed=0, transcendentals=0)


def params(mib):
    return pltpu.CompilerParams(vmem_limit_bytes=mib * MIB)


def swap(value, axis, bit):
    return lax.ppermute(value, axis, [(i, i ^ bit) for i in range(lax.axis_size(axis))])


def cut_kernel(place_ref, shard_ref, two_ref, zero_ref, one_ref):
    wide = two_ref.shape[1]
    channels = shard_ref.shape[1] // 2
    for block, ref in ((2, two_ref), (0, zero_ref)):
        at = pl.multiple_of(place_ref[3] * channels + block * wide, wide)
        ref[...] = shard_ref[:, pl.ds(at, wide)]
    for i in range(2):
        at = i * channels + wide
        one_ref[:, i * wide : (i + 1) * wide] = shard_ref[:, at : at + wide]


def cut(place, shard, wide):
    depth = shard.shape[0]
    shapes = [(depth, wide), (depth, wide), (depth, 2 * wide)]
    return pl.pallas_call(
        cut_kernel,
        out_shape=[jax.ShapeDtypeStruct(shape, jnp.bfloat16) for shape in shapes],
        in_specs=[pl.BlockSpec(memory_space=pltpu.SMEM), pl.BlockSpec(memory_space=VMEM)],
        out_specs=[pl.BlockSpec(memory_space=VMEM)] * 3,
        compiler_params=params(4),
        cost_estimate=cost(10**8),
        name="cut",
    )(place, shard)


def normalize(values, gain):
    values = values.astype(jnp.float32)
    centre = jnp.mean(values, axis=-1, keepdims=True)
    deviate = values - centre
    spread = jnp.mean(deviate * deviate, axis=-1, keepdims=True)
    return (deviate * lax.rsqrt(spread + 1e-05) * gain).astype(jnp.bfloat16)


def norm_kernel(place_ref, rows_ref, gain_ref, shard_ref, out_ref, inner_ref, outer_ref, *piece_refs):
    step = 64
    row_count = rows_ref.shape[0]

    @pl.loop(0, row_count // step)
    def _(i):
        here = pl.ds(pl.multiple_of(i * step, step), step)
        out_ref[here, :] = normalize(rows_ref[here, :], gain_ref[...])

    odd = place_ref[3]
    last = row_count - HALO
    inner_ref[...] = rows_ref[pl.ds(pl.multiple_of((1 - odd) * last, HALO), HALO), :]
    outer_ref[...] = rows_ref[pl.ds(pl.multiple_of(odd * last, HALO), HALO), :]
    for i, ref in enumerate(piece_refs):
        ref[...] = shard_ref[i * ref.shape[0] : (i + 1) * ref.shape[0], :]


def normalize_rows(place, rows, gain, shard, pieces):
    row_count, width = rows.shape
    shapes = [(row_count, width), (HALO, width), (HALO, width)]
    shapes += [(shard.shape[0] // max(pieces, 1), width)] * pieces
    return pl.pallas_call(
        norm_kernel,
        out_shape=[jax.ShapeDtypeStruct(shape, jnp.bfloat16) for shape in shapes],
        in_specs=[pl.BlockSpec(memory_space=pltpu.SMEM)] + [pl.BlockSpec(memory_space=VMEM)] * 3,
        out_specs=[pl.BlockSpec(memory_space=VMEM)] * len(shapes),
        compiler_params=params(4),
        cost_estimate=cost(10**8),
        name="layer_norm",
    )(place, rows, gain, shard)


def near_kernel(place_ref, rows_ref, inner_ref, outer_ref, gain_ref, *refs):
    row_count = rows_ref.shape[0]
    gain = gain_ref[...]
    *weight_refs, ext_ref = refs[:3] if len(refs) > 1 else refs
    odd = place_ref[3]
    at = pl.multiple_of((1 - odd) * (HALO + row_count), HALO)
    ext_ref[pl.ds(at, HALO), :] = normalize(inner_ref[...], gain)
    at = pl.multiple_of(odd * (HALO + row_count), HALO)
    ext_ref[pl.ds(at, HALO), :] = normalize(outer_ref[...], gain)
    ext_ref[HALO : HALO + row_count, :] = rows_ref[...]
    if not weight_refs:
        return
    *out_refs, weights = refs[3:]
    own = place_ref[0]
    depth, width = weight_refs[0].shape
    for i, weight_ref in enumerate(weight_refs):
        at = pl.multiple_of(lax.bitwise_xor(own % 2, i) * depth, depth)
        weights[pl.ds(at, depth), :] = weight_ref[...]
    near = pl.ds(pl.multiple_of(own // 2 * (2 * depth), 2 * depth), 2 * depth)
    wide = out_refs[0].shape[1] // 2
    channels = width // 2
    for block, out_ref in enumerate(out_refs):
        for i in range(2):
            columns = slice(i * channels + block * wide, i * channels + (block + 1) * wide)
            out_ref[:, i * wide : (i + 1) * wide] = jnp.dot(
                ext_ref[:, near], weights[:, columns], preferred_element_type=jnp.float32
            )


def near_product(place, rows, inner, outer, gain, *shards):
    row_count, width = rows.shape
    ext_rows = row_count + 2 * HALO
    shapes = [jax.ShapeDtypeStruct((ext_rows, width), jnp.bfloat16)]
    scratch = []
    if shards:
        shapes += [jax.ShapeDtypeStruct((ext_rows, width // 3), jnp.float32)] * 3
        scratch.append(VMEM((2 * shards[0].shape[0], width), jnp.bfloat16))
    return pl.pallas_call(
        near_kernel,
        out_shape=shapes,
        in_specs=[pl.BlockSpec(memory_space=pltpu.SMEM)]
        + [pl.BlockSpec(memory_space=VMEM)] * (4 + len(shards)),
        out_specs=[pl.BlockSpec(memory_space=VMEM)] * len(shapes),
        scratch_shapes=scratch,
        compiler_params=params(8),
        cost_estimate=cost(10**8),
        name="near",
    )(place, rows, inner, outer, gain, *shards)


def front_kernel(block, earlier, place_ref, normed_ref, *refs):
    refs, earlier_refs = refs[earlier:], refs[:earlier]
    *weight_refs, taps_ref, conv_ref, stats_ref, weights, gated = refs
    ext_rows = normed_ref.shape[0]
    row_count, wide = conv_ref.shape
    taps, channels = taps_ref.shape
    if len(weight_refs) > 1:
        near_ref, *far_refs = weight_refs
        own = place_ref[0]
        depth = far_refs[0].shape[0]
        halves = len(far_refs) // 2
        for i in range(2):
            at = pl.multiple_of(lax.bitwise_xor(own % 2, i) * depth, depth)
            if halves == 1:
                weights[pl.ds(at, depth), :] = far_refs[i][...]
                continue
            for j in range(2):
                column = pl.multiple_of(lax.bitwise_xor(place_ref[3], j) * wide, wide)
                weights[pl.ds(at, depth), pl.ds(column, wide)] = far_refs[2 * i + j][...]
        far = pl.ds(pl.multiple_of((1 - own // 2) * (2 * depth), 2 * depth), 2 * depth)
        normed = normed_ref[:, far]
        value = near_ref[:, 0:wide] + jnp.dot(normed, weights[:, 0:wide], preferred_element_type=jnp.float32)
        gate = near_ref[:, wide:] + jnp.dot(normed, weights[:, wide:], preferred_element_type=jnp.float32)
    else:
        columns = slice(block * wide, (block + 1) * wide)
        value = jnp.dot(normed_ref[...], weight_refs[0][:, columns], preferred_element_type=jnp.float32)
        columns = slice(channels + block * wide, channels + (block + 1) * wide)
        gate = jnp.dot(normed_ref[...], weight_refs[0][:, columns], preferred_element_type=jnp.float32)
    start, length = place_ref[1], place_ref[2]
    position = start - HALO + lax.broadcasted_iota(jnp.int32, (ext_rows, 1), 0)
    valid = (position >= 0) & (position < length)
    kept = jnp.where(valid, value * jax.nn.sigmoid(gate), 0.0)
    kept = kept.astype(jnp.bfloat16).astype(jnp.float32)
    first = HALO - (taps - 1) // 2
    step = 64
    for unit in range(wide // LANES):
        lanes = slice(unit * LANES, (unit + 1) * LANES)
        tap_lanes = slice(block * wide + unit * LANES, block * wide + (unit + 1) * LANES)
        column = kept[:, lanes]
        gated[0] = column
        for phase in range(1, 8):
            gated[phase] = pltpu.roll(column, ext_rows - phase, 0)
        for at in range(0, row_count, step):
            acc = None
            for tap in range(taps):
                base = at + (first + tap) // 8 * 8
                term = gated[(first + tap) % 8, base : base + step, :] * taps_ref[tap : tap + 1, tap_lanes]
                acc = term if acc is None else acc + term
            conv_ref[at : at + step, lanes] = acc
    here = start + lax.broadcasted_iota(jnp.int32, (row_count, 1), 0) < length
    count = jnp.clip(length - start, 0, row_count).astype(jnp.float32)
    conv = conv_ref[...]
    mean = jnp.sum(jnp.where(here, conv, 0.0), axis=0, keepdims=True) / jnp.maximum(count, 1.0)
    deviate = jnp.where(here, conv - mean, 0.0)
    square = jnp.sum(deviate * deviate, axis=0, keepdims=True)
    stats = [mean, square, jnp.full((1, wide), count)]
    if not earlier_refs:
        for i, row in enumerate(stats):
            stats_ref[i : i + 1, :] = row
        return
    for i, row in enumerate(stats):
        for copy in range(stats_ref.shape[0]):
            stats_ref[copy, i : i + 1, block * wide : (block + 1) * wide] = row
            for other, ref in zip([j for j in ORDER if j != block], earlier_refs):
                stats_ref[copy, i : i + 1, other * wide : (other + 1) * wide] = ref[i : i + 1, :]


def front_block(block, wide, place, normed, weights, dw_kernel, earlier=(), copies=1):
    ext_rows, width = normed.shape
    row_count = ext_rows - 2 * HALO
    depth = 2 * weights[1].shape[0] if len(weights) > 1 else 16
    stats_shape = (copies, 3, dw_kernel.shape[1]) if earlier else (3, wide)
    return pl.pallas_call(
        functools.partial(front_kernel, block, len(earlier)),
        out_shape=(
            jax.ShapeDtypeStruct((row_count, wide), jnp.float32),
            jax.ShapeDtypeStruct(stats_shape, jnp.float32),
        ),
        in_specs=[pl.BlockSpec(memory_space=pltpu.SMEM)]
        + [pl.BlockSpec(memory_space=VMEM)] * (2 + len(weights) + len(earlier)),
        out_specs=[pl.BlockSpec(memory_space=VMEM)] * 2,
        scratch_shapes=[
            VMEM((depth, 2 * wide), jnp.bfloat16),
            VMEM((8, ext_rows, LANES), jnp.float32),
        ],
        compiler_params=params(10),
        cost_estimate=cost(4 * 10**9 if block == ORDER[1] else 10**8),
        name="front",
    )(place, normed, *earlier, *weights, dw_kernel)


def merged(parts):
    means, squares, counts = zip(*parts)
    count = sum(counts)
    mean = sum(n * m for n, m in zip(counts, means)) / jnp.maximum(count, 1.0)
    square = sum(squares) + sum(n * (m - mean) * (m - mean) for n, m in zip(counts, means))
    return mean, square, count


def rows_of(refs):
    return [[ref[copy, i : i + 1, :] for i in range(3)] for ref in refs for copy in range(ref.shape[0])]


def merge_kernel(stats_ref, out_ref):
    for i, row in enumerate(merged(rows_of([stats_ref]))):
        for copy in range(out_ref.shape[0]):
            out_ref[copy, i : i + 1, :] = row


def merge(stats, copies):
    return pl.pallas_call(
        merge_kernel,
        out_shape=jax.ShapeDtypeStruct((copies,) + stats.shape[1:], jnp.float32),
        in_specs=[pl.BlockSpec(memory_space=VMEM)],
        out_specs=pl.BlockSpec(memory_space=VMEM),
        compiler_params=params(8),
        cost_estimate=cost(10**8),
        name="merge",
    )(stats)


def back_kernel(stat_count, place_ref, gain_ref, shift_ref, *refs):
    stat_refs, refs = refs[:stat_count], refs[stat_count:]
    *conv_refs, out_ref, rows_out, sems, weights = refs
    convs, weight_refs = conv_refs[:3], conv_refs[3:]
    row_count, wide = convs[0].shape
    if len(weight_refs) > 1:
        depth = weight_refs[0].shape[0]
        for i, weight_ref in enumerate(weight_refs[:2]):
            at = pl.multiple_of(lax.bitwise_xor(place_ref[0], i) * depth, depth)
            weights[pl.ds(at, depth), :] = weight_ref[...]
        rows = weight_refs[2].shape[0]
        pieces = depth // rows
        for i, weight_ref in enumerate(weight_refs[2:]):
            at = lax.bitwise_xor(place_ref[0], 2 + i // pieces) * depth + i % pieces * rows
            weights[pl.ds(pl.multiple_of(at, rows), rows), :] = weight_ref[...]
    else:
        weights[...] = weight_refs[0][...]
    mean, square, count = merged(rows_of(stat_refs))
    scale = lax.rsqrt(square / count + 1e-05) * gain_ref[...]
    shift = shift_ref[...]
    pieces, rows, columns = rows_out.shape
    across = out_ref.shape[1] // columns
    copies = []
    for piece in range(pieces // across):
        here = slice(piece * rows, (piece + 1) * rows)
        parts = []
        for i, conv_ref in enumerate(convs):
            lanes = slice(i * wide, (i + 1) * wide)
            scaled = (conv_ref[here, :] - mean[:, lanes]) * scale[:, lanes] + shift[:, lanes]
            parts.append((scaled * jax.nn.sigmoid(scaled)).astype(jnp.bfloat16))
        activated = jnp.concatenate(parts, axis=1)
        position = place_ref[1] + piece * rows + lax.broadcasted_iota(jnp.int32, (rows, 1), 0)
        for j in range(across):
            lanes = slice(j * columns, (j + 1) * columns)
            result = jnp.dot(activated, weights[:, lanes], preferred_element_type=jnp.float32)
            slot = piece * across + j
            rows_out[slot] = jnp.where(position < place_ref[2], result, 0.0).astype(jnp.bfloat16)
            copy = pltpu.make_async_copy(rows_out.at[slot], out_ref.at[here, lanes], sems.at[slot])
            copy.start()
            copies.append(copy)
    for copy in copies:
        copy.wait()


def back(place, stats, gain, shift, convs, weights):
    row_count = convs[0].shape[0]
    channels, width = gain.shape[1], weights[0].shape[1]
    pieces, across = 4, 2
    return pl.pallas_call(
        functools.partial(back_kernel, len(stats)),
        out_shape=jax.ShapeDtypeStruct((row_count, width), jnp.bfloat16),
        in_specs=[pl.BlockSpec(memory_space=pltpu.SMEM)]
        + [pl.BlockSpec(memory_space=VMEM)] * (2 + len(stats) + len(convs) + len(weights)),
        out_specs=pl.BlockSpec(memory_space=pl.ANY),
        scratch_shapes=[
            VMEM((pieces, row_count * across // pieces, width // across), jnp.bfloat16),
            pltpu.SemaphoreType.DMA((pieces,)),
            VMEM((channels, width), jnp.bfloat16),
        ],
        compiler_params=params(10),
        cost_estimate=cost(10**9),
        name="back",
    )(place, gain, shift, *stats, *convs, *weights)


def everyones(copies, groups):
    return lax.all_to_all(copies, ("fsdp", "ctx"), 0, 0, axis_index_groups=groups, tiled=True)


def tie(*values):
    return lax.optimization_barrier(values)


def body(frames, lengths, ln_gain, w_in, dw_kernel, bn_gain, bn_shift, w_out):
    _, row_count, model_width = frames.shape
    channels = dw_kernel.shape[1]
    wide = channels // 3
    ctx, fsdp = lax.axis_index("ctx"), lax.axis_index("fsdp")
    ctx_count, fsdp_count = lax.axis_size("ctx"), lax.axis_size("fsdp")
    direct = fsdp_count == 4 and ctx_count == 8
    rows = frames[0]
    gain = ln_gain[None]
    parity = lax.rem(ctx, 2)
    place = jnp.stack([fsdp, ctx * row_count, lengths[0], parity]).astype(jnp.int32)
    ends = ctx_count - 1
    down, up = [(i, i + 1) for i in range(ends)], [(i + 1, i) for i in range(ends)]
    both = ("fsdp", "ctx")
    member = lambda f, p: f * ctx_count + p

    def front(block, weights, *extra):
        return front_block(block, wide, place, normed, weights, dw_kernel, *extra)

    if direct:
        two, zero, one = (swap(part, "fsdp", 2) for part in cut(place, w_in, wide))
        across = swap(w_in, "fsdp", 1)
        normed, inner, outer, *pieces = normalize_rows(place, rows, gain, w_out, 3)
        inner = swap(inner, "ctx", 1)
        pairs = [(i, i + 1) for i in range(1, ends, 2)]
        outer = lax.ppermute(outer, "ctx", pairs + [(j, i) for i, j in pairs])
        normed, inner, outer, two, zero = tie(normed, inner, outer, two, zero)
        two, zero = [two, swap(two, "ctx", 1)], [zero, swap(zero, "ctx", 1)]
        two.append(swap(two[0], "fsdp", 1))
        zero.append(swap(zero[0], "fsdp", 1))
        normed, *partials = near_product(place, normed, inner, outer, gain, w_in, across)
        partials[2], two[1], two[2], zero[2], w_out = tie(partials[2], two[1], two[2], zero[2], w_out)
        two.append(swap(two[1], "fsdp", 1))
        partials[2], one, zero[1] = tie(partials[2], one, zero[1])
        beyond_one = swap(one, "fsdp", 1)
        zero.append(swap(zero[1], "fsdp", 1))
        conv_two, stat_two = front(2, [partials[2], *two])
        pieces = [swap(piece, "fsdp", 2) for piece in pieces]
        conv_two, partials[0], pieces[0] = tie(conv_two, partials[0], pieces[0])
        beyond = [swap(pieces[0], "fsdp", 1)]
        conv_zero, stat_zero = front(0, [partials[0], *zero])
        conv_zero, partials[1] = tie(conv_zero, partials[1])
        conv_one, stats = front(1, [partials[1], one, beyond_one], (stat_two, stat_zero), 1)
        across_out = swap(w_out, "fsdp", 1)
        stats, pieces[1], beyond[0] = tie(stats, pieces[1], beyond[0])
        beyond.append(swap(pieces[1], "fsdp", 1))
        convs = [conv_zero, conv_one, conv_two]

        def others(flips):
            return [
                lax.ppermute(
                    stats,
                    both,
                    [(member(f, p), member(f ^ df, p ^ dp)) for f in range(4) for p in range(8)],
                )
                for df, dp in flips
            ]

        def union(parts):
            return jnp.stack(merged([[part[:, i] for i in range(3)] for part in parts]), 1)

        stats = union([stats] + others([(1, 0)]))
        stats = union([stats] + others([(0, 2)]))
        stats, pieces[2], beyond[1] = tie(stats, pieces[2], beyond[1])
        beyond.append(swap(pieces[2], "fsdp", 1))
        stats = union([stats] + others([(0, 4)]))
        stats = [stats] + others([(0, 1), (2, 0), (2, 1)])
        out_weights = [w_out, across_out, *pieces, *beyond]
    else:
        full_in = lax.all_gather(w_in, "fsdp", axis=0, tiled=True)
        out_weights = [lax.all_gather(w_out, "fsdp", axis=0, tiled=True)]
        before = lax.ppermute(rows[-HALO:], "ctx", down)
        after = lax.ppermute(rows[:HALO], "ctx", up)
        inner = jnp.where(parity == 0, after, before)
        outer = jnp.where(parity == 0, before, after)
        normed, _, _ = normalize_rows(place, rows, gain, w_out, 0)
        (normed,) = near_product(place, normed, inner, outer, gain)
        near_by = 2 if ctx_count % 2 == 0 else 1
        groups = [
            [member(f, p + i) for f in range(fsdp_count) for i in range(near_by)]
            for p in range(0, ctx_count, near_by)
        ]
        convs, stats = [None] * 3, []
        for block in ORDER:
            extra = (stats, len(groups[0])) if block == ORDER[-1] else ()
            convs[block], stat = front(block, [full_in], *extra)
            stats.append(stat)
        stats = merge(everyones(stats[2], groups), len(groups))
        groups = [
            [member(f, p + i) for p in range(0, ctx_count, near_by)]
            for f in range(fsdp_count)
            for i in range(near_by)
        ]
        stats = [everyones(stats, groups)]
    result = back(place, stats, bn_gain[None], bn_shift[None], convs, out_weights)
    return result[None]


def solution(mesh):
    return jax.shard_map(
        body,
        mesh=mesh,
        in_specs=(
            P("fsdp", "ctx", None),
            P("fsdp"),
            P(),
            P("fsdp", None),
            P(),
            P(),
            P(),
            P("fsdp", None),
        ),
        out_specs=P("fsdp", "ctx", None),
        check_vma=False,
    )
```

```python
import functools

import jax
import jax.numpy as jnp
from jax import lax
from jax.experimental import pallas as pl
from jax.experimental.pallas import tpu as pltpu
from jax.sharding import PartitionSpec as P

HALO = 16
LANES = 128
MIB = 1024 * 1024
VMEM = pltpu.VMEM
ORDER = (2, 0, 1)


def cost(flops):
    return pl.CostEstimate(flops=flops, bytes_accessed=0, transcendentals=0)


def params(mib):
    return pltpu.CompilerParams(vmem_limit_bytes=mib * MIB)


def swap(value, axis, bit):
    return lax.ppermute(value, axis, [(i, i ^ bit) for i in range(lax.axis_size(axis))])


def cut_kernel(place_ref, shard_ref, two_ref, zero_ref, one_ref):
    wide = two_ref.shape[1]
    channels = shard_ref.shape[1] // 2
    for block, ref in ((2, two_ref), (0, zero_ref)):
        at = pl.multiple_of(place_ref[3] * channels + block * wide, wide)
        ref[...] = shard_ref[:, pl.ds(at, wide)]
    for i in range(2):
        at = i * channels + wide
        one_ref[:, i * wide : (i + 1) * wide] = shard_ref[:, at : at + wide]


def cut(place, shard, wide):
    depth = shard.shape[0]
    shapes = [(depth, wide), (depth, wide), (depth, 2 * wide)]
    return pl.pallas_call(
        cut_kernel,
        out_shape=[jax.ShapeDtypeStruct(shape, jnp.bfloat16) for shape in shapes],
        in_specs=[pl.BlockSpec(memory_space=pltpu.SMEM), pl.BlockSpec(memory_space=VMEM)],
        out_specs=[pl.BlockSpec(memory_space=VMEM)] * 3,
        compiler_params=params(4),
        cost_estimate=cost(10**8),
        name="cut",
    )(place, shard)


def normalize(values, gain):
    values = values.astype(jnp.float32)
    centre = jnp.mean(values, axis=-1, keepdims=True)
    deviate = values - centre
    spread = jnp.mean(deviate * deviate, axis=-1, keepdims=True)
    return (deviate * lax.rsqrt(spread + 1e-05) * gain).astype(jnp.bfloat16)


def edge_kernel(place_ref, rows_ref, inner_ref, outer_ref):
    odd = place_ref[3]
    last = rows_ref.shape[0] - HALO
    inner_ref[...] = rows_ref[pl.ds(pl.multiple_of((1 - odd) * last, HALO), HALO), :]
    outer_ref[...] = rows_ref[pl.ds(pl.multiple_of(odd * last, HALO), HALO), :]


def edge_rows(place, rows):
    shape = jax.ShapeDtypeStruct((HALO, rows.shape[1]), rows.dtype)
    return pl.pallas_call(
        edge_kernel,
        out_shape=[shape, shape],
        in_specs=[pl.BlockSpec(memory_space=pltpu.SMEM), pl.BlockSpec(memory_space=VMEM)],
        out_specs=[pl.BlockSpec(memory_space=VMEM)] * 2,
        compiler_params=params(2),
        cost_estimate=cost(10**8),
        name="edges",
    )(place, rows)


def norm_kernel(rows_ref, gain_ref, shard_ref, out_ref, *piece_refs):
    step = 64

    @pl.loop(0, rows_ref.shape[0] // step)
    def _(i):
        here = pl.ds(pl.multiple_of(i * step, step), step)
        out_ref[here, :] = normalize(rows_ref[here, :], gain_ref[...])

    at = 0
    for ref in piece_refs:
        ref[...] = shard_ref[at : at + ref.shape[0], :]
        at += ref.shape[0]


def normalize_rows(rows, gain, shard, pieces):
    row_count, width = rows.shape
    shapes = [(row_count, width)] + [(piece, width) for piece in pieces]
    return pl.pallas_call(
        norm_kernel,
        out_shape=[jax.ShapeDtypeStruct(shape, jnp.bfloat16) for shape in shapes],
        in_specs=[pl.BlockSpec(memory_space=VMEM)] * 3,
        out_specs=[pl.BlockSpec(memory_space=VMEM)] * len(shapes),
        compiler_params=params(4),
        cost_estimate=cost(10**8),
        name="layer_norm",
    )(rows, gain, shard)


def near_kernel(place_ref, rows_ref, inner_ref, outer_ref, gain_ref, *refs):
    row_count = rows_ref.shape[0]
    gain = gain_ref[...]
    *weight_refs, ext_ref = refs[:3] if len(refs) > 1 else refs
    odd = place_ref[3]
    at = pl.multiple_of((1 - odd) * (HALO + row_count), HALO)
    ext_ref[pl.ds(at, HALO), :] = normalize(inner_ref[...], gain)
    at = pl.multiple_of(odd * (HALO + row_count), HALO)
    ext_ref[pl.ds(at, HALO), :] = normalize(outer_ref[...], gain)
    ext_ref[HALO : HALO + row_count, :] = rows_ref[...]
    if not weight_refs:
        return
    *out_refs, weights = refs[3:]
    own = place_ref[0]
    depth, width = weight_refs[0].shape
    for i, weight_ref in enumerate(weight_refs):
        at = pl.multiple_of(lax.bitwise_xor(own % 2, i) * depth, depth)
        weights[pl.ds(at, depth), :] = weight_ref[...]
    near = pl.ds(pl.multiple_of(own // 2 * (2 * depth), 2 * depth), 2 * depth)
    wide = out_refs[0].shape[1] // 2
    channels = width // 2
    for block, out_ref in enumerate(out_refs):
        for i in range(2):
            columns = slice(i * channels + block * wide, i * channels + (block + 1) * wide)
            out_ref[:, i * wide : (i + 1) * wide] = jnp.dot(
                ext_ref[:, near], weights[:, columns], preferred_element_type=jnp.float32
            )


def near_product(place, rows, inner, outer, gain, *shards):
    row_count, width = rows.shape
    ext_rows = row_count + 2 * HALO
    shapes = [jax.ShapeDtypeStruct((ext_rows, width), jnp.bfloat16)]
    scratch = []
    if shards:
        shapes += [jax.ShapeDtypeStruct((ext_rows, width // 3), jnp.float32)] * 3
        scratch.append(VMEM((2 * shards[0].shape[0], width), jnp.bfloat16))
    return pl.pallas_call(
        near_kernel,
        out_shape=shapes,
        in_specs=[pl.BlockSpec(memory_space=pltpu.SMEM)]
        + [pl.BlockSpec(memory_space=VMEM)] * (4 + len(shards)),
        out_specs=[pl.BlockSpec(memory_space=VMEM)] * len(shapes),
        scratch_shapes=scratch,
        compiler_params=params(8),
        cost_estimate=cost(10**8),
        name="near",
    )(place, rows, inner, outer, gain, *shards)


def front_kernel(block, earlier, place_ref, normed_ref, *refs):
    refs, earlier_refs = refs[earlier:], refs[:earlier]
    *weight_refs, taps_ref, conv_ref, stats_ref, weights, gated = refs
    ext_rows = normed_ref.shape[0]
    row_count, wide = conv_ref.shape
    taps, channels = taps_ref.shape
    if len(weight_refs) > 1:
        near_ref, *far_refs = weight_refs
        own = place_ref[0]
        depth = far_refs[0].shape[0]
        halves = len(far_refs) // 2
        for i in range(2):
            at = pl.multiple_of(lax.bitwise_xor(own % 2, i) * depth, depth)
            if halves == 1:
                weights[pl.ds(at, depth), :] = far_refs[i][...]
                continue
            for j in range(2):
                column = pl.multiple_of(lax.bitwise_xor(place_ref[3], j) * wide, wide)
                weights[pl.ds(at, depth), pl.ds(column, wide)] = far_refs[2 * i + j][...]
        far = pl.ds(pl.multiple_of((1 - own // 2) * (2 * depth), 2 * depth), 2 * depth)
        normed = normed_ref[:, far]
        value = near_ref[:, 0:wide] + jnp.dot(normed, weights[:, 0:wide], preferred_element_type=jnp.float32)
        gate = near_ref[:, wide:] + jnp.dot(normed, weights[:, wide:], preferred_element_type=jnp.float32)
    else:
        columns = slice(block * wide, (block + 1) * wide)
        value = jnp.dot(normed_ref[...], weight_refs[0][:, columns], preferred_element_type=jnp.float32)
        columns = slice(channels + block * wide, channels + (block + 1) * wide)
        gate = jnp.dot(normed_ref[...], weight_refs[0][:, columns], preferred_element_type=jnp.float32)
    start, length = place_ref[1], place_ref[2]
    position = start - HALO + lax.broadcasted_iota(jnp.int32, (ext_rows, 1), 0)
    valid = (position >= 0) & (position < length)
    kept = jnp.where(valid, value * jax.nn.sigmoid(gate), 0.0)
    kept = kept.astype(jnp.bfloat16).astype(jnp.float32)
    first = HALO - (taps - 1) // 2
    step = 64
    for unit in range(wide // LANES):
        lanes = slice(unit * LANES, (unit + 1) * LANES)
        tap_lanes = slice(block * wide + unit * LANES, block * wide + (unit + 1) * LANES)
        column = kept[:, lanes]
        gated[0] = column
        for phase in range(1, 8):
            gated[phase] = pltpu.roll(column, ext_rows - phase, 0)
        for at in range(0, row_count, step):
            acc = None
            for tap in range(taps):
                base = at + (first + tap) // 8 * 8
                term = gated[(first + tap) % 8, base : base + step, :] * taps_ref[tap : tap + 1, tap_lanes]
                acc = term if acc is None else acc + term
            conv_ref[at : at + step, lanes] = acc
    here = start + lax.broadcasted_iota(jnp.int32, (row_count, 1), 0) < length
    count = jnp.clip(length - start, 0, row_count).astype(jnp.float32)
    conv = conv_ref[...]
    mean = jnp.sum(jnp.where(here, conv, 0.0), axis=0, keepdims=True) / jnp.maximum(count, 1.0)
    deviate = jnp.where(here, conv - mean, 0.0)
    square = jnp.sum(deviate * deviate, axis=0, keepdims=True)
    stats = [mean, square, jnp.full((1, wide), count)]
    if not earlier_refs:
        for i, row in enumerate(stats):
            stats_ref[i : i + 1, :] = row
        return
    for i, row in enumerate(stats):
        for copy in range(stats_ref.shape[0]):
            stats_ref[copy, i : i + 1, block * wide : (block + 1) * wide] = row
            for other, ref in zip([j for j in ORDER if j != block], earlier_refs):
                stats_ref[copy, i : i + 1, other * wide : (other + 1) * wide] = ref[i : i + 1, :]


def front_block(block, wide, place, normed, weights, dw_kernel, earlier=(), copies=1):
    ext_rows, width = normed.shape
    row_count = ext_rows - 2 * HALO
    depth = 2 * weights[1].shape[0] if len(weights) > 1 else 16
    stats_shape = (copies, 3, dw_kernel.shape[1]) if earlier else (3, wide)
    return pl.pallas_call(
        functools.partial(front_kernel, block, len(earlier)),
        out_shape=(
            jax.ShapeDtypeStruct((row_count, wide), jnp.float32),
            jax.ShapeDtypeStruct(stats_shape, jnp.float32),
        ),
        in_specs=[pl.BlockSpec(memory_space=pltpu.SMEM)]
        + [pl.BlockSpec(memory_space=VMEM)] * (2 + len(weights) + len(earlier)),
        out_specs=[pl.BlockSpec(memory_space=VMEM)] * 2,
        scratch_shapes=[
            VMEM((depth, 2 * wide), jnp.bfloat16),
            VMEM((8, ext_rows, LANES), jnp.float32),
        ],
        compiler_params=params(10),
        cost_estimate=cost(4 * 10**9 if block == ORDER[1] else 10**8),
        name="front",
    )(place, normed, *earlier, *weights, dw_kernel)


def merged(parts):
    means, squares, counts = zip(*parts)
    count = sum(counts)
    mean = sum(n * m for n, m in zip(counts, means)) / jnp.maximum(count, 1.0)
    square = sum(squares) + sum(n * (m - mean) * (m - mean) for n, m in zip(counts, means))
    return mean, square, count


def rows_of(refs):
    return [[ref[copy, i : i + 1, :] for i in range(3)] for ref in refs for copy in range(ref.shape[0])]


def merge_kernel(stats_ref, out_ref):
    for i, row in enumerate(merged(rows_of([stats_ref]))):
        for copy in range(out_ref.shape[0]):
            out_ref[copy, i : i + 1, :] = row


def merge(stats, copies):
    return pl.pallas_call(
        merge_kernel,
        out_shape=jax.ShapeDtypeStruct((copies,) + stats.shape[1:], jnp.float32),
        in_specs=[pl.BlockSpec(memory_space=VMEM)],
        out_specs=pl.BlockSpec(memory_space=VMEM),
        compiler_params=params(8),
        cost_estimate=cost(10**8),
        name="merge",
    )(stats)


def back_kernel(stat_count, place_ref, gain_ref, shift_ref, *refs):
    stat_refs, refs = refs[:stat_count], refs[stat_count:]
    *conv_refs, out_ref, rows_out, sems, weights = refs
    convs, weight_refs = conv_refs[:3], conv_refs[3:]
    row_count, wide = convs[0].shape
    if len(weight_refs) > 1:
        depth = weight_refs[0].shape[0]
        for i, weight_ref in enumerate(weight_refs[:2]):
            at = pl.multiple_of(lax.bitwise_xor(place_ref[0], i) * depth, depth)
            weights[pl.ds(at, depth), :] = weight_ref[...]
        at, unit = 0, 16
        for weight_ref in weight_refs[2:]:
            rows = weight_ref.shape[0]
            start = lax.bitwise_xor(place_ref[0], 2 + at // depth) * depth + at % depth
            weights[pl.ds(pl.multiple_of(start, unit), rows), :] = weight_ref[...]
            at += rows
    else:
        weights[...] = weight_refs[0][...]
    mean, square, count = merged(rows_of(stat_refs))
    scale = lax.rsqrt(square / count + 1e-05) * gain_ref[...]
    shift = shift_ref[...]
    pieces, rows, columns = rows_out.shape
    across = out_ref.shape[1] // columns
    copies = []
    for piece in range(pieces // across):
        here = slice(piece * rows, (piece + 1) * rows)
        parts = []
        for i, conv_ref in enumerate(convs):
            lanes = slice(i * wide, (i + 1) * wide)
            scaled = (conv_ref[here, :] - mean[:, lanes]) * scale[:, lanes] + shift[:, lanes]
            parts.append((scaled * jax.nn.sigmoid(scaled)).astype(jnp.bfloat16))
        activated = jnp.concatenate(parts, axis=1)
        position = place_ref[1] + piece * rows + lax.broadcasted_iota(jnp.int32, (rows, 1), 0)
        for j in range(across):
            lanes = slice(j * columns, (j + 1) * columns)
            result = jnp.dot(activated, weights[:, lanes], preferred_element_type=jnp.float32)
            slot = piece * across + j
            rows_out[slot] = jnp.where(position < place_ref[2], result, 0.0).astype(jnp.bfloat16)
            copy = pltpu.make_async_copy(rows_out.at[slot], out_ref.at[here, lanes], sems.at[slot])
            copy.start()
            copies.append(copy)
    for copy in copies:
        copy.wait()


def back(place, stats, gain, shift, convs, weights):
    row_count = convs[0].shape[0]
    channels, width = gain.shape[1], weights[0].shape[1]
    pieces, across = 4, 2
    return pl.pallas_call(
        functools.partial(back_kernel, len(stats)),
        out_shape=jax.ShapeDtypeStruct((row_count, width), jnp.bfloat16),
        in_specs=[pl.BlockSpec(memory_space=pltpu.SMEM)]
        + [pl.BlockSpec(memory_space=VMEM)] * (2 + len(stats) + len(convs) + len(weights)),
        out_specs=pl.BlockSpec(memory_space=pl.ANY),
        scratch_shapes=[
            VMEM((pieces, row_count * across // pieces, width // across), jnp.bfloat16),
            pltpu.SemaphoreType.DMA((pieces,)),
            VMEM((channels, width), jnp.bfloat16),
        ],
        compiler_params=params(10),
        cost_estimate=cost(10**9),
        name="back",
    )(place, gain, shift, *stats, *convs, *weights)


def everyones(copies, groups):
    return lax.all_to_all(copies, ("fsdp", "ctx"), 0, 0, axis_index_groups=groups, tiled=True)


def tie(*values):
    return lax.optimization_barrier(values)


def body(frames, lengths, ln_gain, w_in, dw_kernel, bn_gain, bn_shift, w_out):
    _, row_count, model_width = frames.shape
    channels = dw_kernel.shape[1]
    wide = channels // 3
    ctx, fsdp = lax.axis_index("ctx"), lax.axis_index("fsdp")
    ctx_count, fsdp_count = lax.axis_size("ctx"), lax.axis_size("fsdp")
    direct = fsdp_count == 4 and ctx_count == 8
    rows = frames[0]
    gain = ln_gain[None]
    parity = lax.rem(ctx, 2)
    place = jnp.stack([fsdp, ctx * row_count, lengths[0], parity]).astype(jnp.int32)
    ends = ctx_count - 1
    down, up = [(i, i + 1) for i in range(ends)], [(i + 1, i) for i in range(ends)]
    both = ("fsdp", "ctx")
    member = lambda f, p: f * ctx_count + p

    def front(block, weights, *extra):
        return front_block(block, wide, place, normed, weights, dw_kernel, *extra)

    if direct:
        two, zero, one = (swap(part, "fsdp", 2) for part in cut(place, w_in, wide))
        across = swap(w_in, "fsdp", 1)
        inner, outer = edge_rows(place, rows)
        part_rows = w_out.shape[0] // 12
        normed, *pieces = normalize_rows(rows, gain, w_out, [5 * part_rows, 5 * part_rows, 2 * part_rows])
        inner = swap(inner, "ctx", 1)
        pairs = [(i, i + 1) for i in range(1, ends, 2)]
        outer = lax.ppermute(outer, "ctx", pairs + [(j, i) for i, j in pairs])
        normed, inner, outer, two, zero = tie(normed, inner, outer, two, zero)
        two, zero = [two, swap(two, "ctx", 1)], [zero, swap(zero, "ctx", 1)]
        two.append(swap(two[0], "fsdp", 1))
        zero.append(swap(zero[0], "fsdp", 1))
        normed, two[1] = tie(normed, two[1])
        two.append(swap(two[1], "fsdp", 1))
        normed, *partials = near_product(place, normed, inner, outer, gain, w_in, across)
        partials[2], zero[1], *late = tie(partials[2], zero[1], two[2], two[3], zero[2], w_out)
        two[2], two[3], zero[2], w_out = late
        partials[2], one = tie(partials[2], one)
        beyond_one = swap(one, "fsdp", 1)
        zero.append(swap(zero[1], "fsdp", 1))
        conv_two, stat_two = front(2, [partials[2], *two])
        pieces = [swap(piece, "fsdp", 2) for piece in pieces]
        conv_two, partials[0], pieces[0] = tie(conv_two, partials[0], pieces[0])
        beyond = [swap(pieces[0], "fsdp", 1)]
        conv_zero, stat_zero = front(0, [partials[0], *zero])
        conv_zero, partials[1] = tie(conv_zero, partials[1])
        conv_one, stats = front(1, [partials[1], one, beyond_one], (stat_two, stat_zero), 1)
        across_out = swap(w_out, "fsdp", 1)
        stats, pieces[1], beyond[0] = tie(stats, pieces[1], beyond[0])
        beyond.append(swap(pieces[1], "fsdp", 1))
        convs = [conv_zero, conv_one, conv_two]

        def others(flips):
            return [
                lax.ppermute(
                    stats,
                    both,
                    [(member(f, p), member(f ^ df, p ^ dp)) for f in range(4) for p in range(8)],
                )
                for df, dp in flips
            ]

        def union(parts):
            return jnp.stack(merged([[part[:, i] for i in range(3)] for part in parts]), 1)

        stats = union([stats] + others([(1, 0)]))
        stats = union([stats] + others([(0, 2)]))
        stats, pieces[2], beyond[1] = tie(stats, pieces[2], beyond[1])
        beyond.append(swap(pieces[2], "fsdp", 1))
        stats = union([stats] + others([(0, 4)]))
        stats = [stats] + others([(0, 1), (2, 0), (2, 1)])
        out_weights = [w_out, across_out, *pieces, *beyond]
    else:
        full_in = lax.all_gather(w_in, "fsdp", axis=0, tiled=True)
        out_weights = [lax.all_gather(w_out, "fsdp", axis=0, tiled=True)]
        before = lax.ppermute(rows[-HALO:], "ctx", down)
        after = lax.ppermute(rows[:HALO], "ctx", up)
        inner = jnp.where(parity == 0, after, before)
        outer = jnp.where(parity == 0, before, after)
        (normed,) = normalize_rows(rows, gain, w_out, ())
        (normed,) = near_product(place, normed, inner, outer, gain)
        near_by = 2 if ctx_count % 2 == 0 else 1
        groups = [
            [member(f, p + i) for f in range(fsdp_count) for i in range(near_by)]
            for p in range(0, ctx_count, near_by)
        ]
        convs, stats = [None] * 3, []
        for block in ORDER:
            extra = (stats, len(groups[0])) if block == ORDER[-1] else ()
            convs[block], stat = front(block, [full_in], *extra)
            stats.append(stat)
        stats = merge(everyones(stats[2], groups), len(groups))
        groups = [
            [member(f, p + i) for p in range(0, ctx_count, near_by)]
            for f in range(fsdp_count)
            for i in range(near_by)
        ]
        stats = [everyones(stats, groups)]
    result = back(place, stats, bn_gain[None], bn_shift[None], convs, out_weights)
    return result[None]


def solution(mesh):
    return jax.shard_map(
        body,
        mesh=mesh,
        in_specs=(
            P("fsdp", "ctx", None),
            P("fsdp"),
            P(),
            P("fsdp", None),
            P(),
            P(),
            P(),
            P("fsdp", None),
        ),
        out_specs=P("fsdp", "ctx", None),
        check_vma=False,
    )
```

```python
import functools

import jax
import jax.numpy as jnp
from jax import lax
from jax.experimental import pallas as pl
from jax.experimental.pallas import tpu as pltpu
from jax.sharding import PartitionSpec as P

HALO = 16
LANES = 128
MIB = 1024 * 1024
VMEM = pltpu.VMEM
ORDER = (2, 0, 1)


def cost(flops):
    return pl.CostEstimate(flops=flops, bytes_accessed=0, transcendentals=0)


def params(mib):
    return pltpu.CompilerParams(vmem_limit_bytes=mib * MIB)


def swap(value, axis, bit):
    return lax.ppermute(value, axis, [(i, i ^ bit) for i in range(lax.axis_size(axis))])


def cut_kernel(place_ref, shard_ref, two_ref, zero_ref, one_ref):
    wide = two_ref.shape[1]
    channels = shard_ref.shape[1] // 2
    for block, ref in ((2, two_ref), (0, zero_ref)):
        at = pl.multiple_of(place_ref[3] * channels + block * wide, wide)
        ref[...] = shard_ref[:, pl.ds(at, wide)]
    for i in range(2):
        at = i * channels + wide
        one_ref[:, i * wide : (i + 1) * wide] = shard_ref[:, at : at + wide]


def cut(place, shard, wide):
    depth = shard.shape[0]
    shapes = [(depth, wide), (depth, wide), (depth, 2 * wide)]
    return pl.pallas_call(
        cut_kernel,
        out_shape=[jax.ShapeDtypeStruct(shape, jnp.bfloat16) for shape in shapes],
        in_specs=[pl.BlockSpec(memory_space=pltpu.SMEM), pl.BlockSpec(memory_space=VMEM)],
        out_specs=[pl.BlockSpec(memory_space=VMEM)] * 3,
        compiler_params=params(4),
        cost_estimate=cost(10**8),
        name="cut",
    )(place, shard)


def normalize(values, gain):
    values = values.astype(jnp.float32)
    centre = jnp.mean(values, axis=-1, keepdims=True)
    deviate = values - centre
    spread = jnp.mean(deviate * deviate, axis=-1, keepdims=True)
    return (deviate * lax.rsqrt(spread + 1e-05) * gain).astype(jnp.bfloat16)


def edge_kernel(place_ref, rows_ref, inner_ref, outer_ref):
    odd = place_ref[3]
    last = rows_ref.shape[0] - HALO
    inner_ref[...] = rows_ref[pl.ds(pl.multiple_of((1 - odd) * last, HALO), HALO), :]
    outer_ref[...] = rows_ref[pl.ds(pl.multiple_of(odd * last, HALO), HALO), :]


def edge_rows(place, rows):
    shape = jax.ShapeDtypeStruct((HALO, rows.shape[1]), rows.dtype)
    return pl.pallas_call(
        edge_kernel,
        out_shape=[shape, shape],
        in_specs=[pl.BlockSpec(memory_space=pltpu.SMEM), pl.BlockSpec(memory_space=VMEM)],
        out_specs=[pl.BlockSpec(memory_space=VMEM)] * 2,
        compiler_params=params(2),
        cost_estimate=cost(10**8),
        name="edges",
    )(place, rows)


def norm_kernel(rows_ref, gain_ref, shard_ref, out_ref, *piece_refs):
    step = 64

    @pl.loop(0, rows_ref.shape[0] // step)
    def _(i):
        here = pl.ds(pl.multiple_of(i * step, step), step)
        out_ref[here, :] = normalize(rows_ref[here, :], gain_ref[...])

    at = 0
    for ref in piece_refs:
        ref[...] = shard_ref[at : at + ref.shape[0], :]
        at += ref.shape[0]


def normalize_rows(rows, gain, shard, pieces):
    row_count, width = rows.shape
    shapes = [(row_count, width)] + [(piece, width) for piece in pieces]
    return pl.pallas_call(
        norm_kernel,
        out_shape=[jax.ShapeDtypeStruct(shape, jnp.bfloat16) for shape in shapes],
        in_specs=[pl.BlockSpec(memory_space=VMEM)] * 3,
        out_specs=[pl.BlockSpec(memory_space=VMEM)] * len(shapes),
        compiler_params=params(4),
        cost_estimate=cost(10**8),
        name="layer_norm",
    )(rows, gain, shard)


def near_kernel(place_ref, rows_ref, inner_ref, outer_ref, gain_ref, *refs):
    row_count = rows_ref.shape[0]
    gain = gain_ref[...]
    *weight_refs, ext_ref = refs[:3] if len(refs) > 1 else refs
    odd = place_ref[3]
    at = pl.multiple_of((1 - odd) * (HALO + row_count), HALO)
    ext_ref[pl.ds(at, HALO), :] = normalize(inner_ref[...], gain)
    at = pl.multiple_of(odd * (HALO + row_count), HALO)
    ext_ref[pl.ds(at, HALO), :] = normalize(outer_ref[...], gain)
    ext_ref[HALO : HALO + row_count, :] = rows_ref[...]
    if not weight_refs:
        return
    *out_refs, weights = refs[3:]
    own = place_ref[0]
    depth, width = weight_refs[0].shape
    for i, weight_ref in enumerate(weight_refs):
        at = pl.multiple_of(lax.bitwise_xor(own % 2, i) * depth, depth)
        weights[pl.ds(at, depth), :] = weight_ref[...]
    near = pl.ds(pl.multiple_of(own // 2 * (2 * depth), 2 * depth), 2 * depth)
    wide = out_refs[0].shape[1] // 2
    channels = width // 2
    for block, out_ref in enumerate(out_refs):
        for i in range(2):
            columns = slice(i * channels + block * wide, i * channels + (block + 1) * wide)
            out_ref[:, i * wide : (i + 1) * wide] = jnp.dot(
                ext_ref[:, near], weights[:, columns], preferred_element_type=jnp.float32
            )


def near_product(place, rows, inner, outer, gain, *shards):
    row_count, width = rows.shape
    ext_rows = row_count + 2 * HALO
    shapes = [jax.ShapeDtypeStruct((ext_rows, width), jnp.bfloat16)]
    scratch = []
    if shards:
        shapes += [jax.ShapeDtypeStruct((ext_rows, width // 3), jnp.float32)] * 3
        scratch.append(VMEM((2 * shards[0].shape[0], width), jnp.bfloat16))
    return pl.pallas_call(
        near_kernel,
        out_shape=shapes,
        in_specs=[pl.BlockSpec(memory_space=pltpu.SMEM)]
        + [pl.BlockSpec(memory_space=VMEM)] * (4 + len(shards)),
        out_specs=[pl.BlockSpec(memory_space=VMEM)] * len(shapes),
        scratch_shapes=scratch,
        compiler_params=params(8),
        cost_estimate=cost(10**8),
        name="near",
    )(place, rows, inner, outer, gain, *shards)


def front_kernel(block, earlier, place_ref, normed_ref, *refs):
    refs, earlier_refs = refs[earlier:], refs[:earlier]
    *weight_refs, taps_ref, conv_ref, stats_ref, weights, gated = refs
    ext_rows = normed_ref.shape[0]
    row_count, wide = conv_ref.shape
    taps, channels = taps_ref.shape
    if len(weight_refs) > 1:
        near_ref, *far_refs = weight_refs
        own = place_ref[0]
        depth = far_refs[0].shape[0]
        halves = len(far_refs) // 2
        for i in range(2):
            at = pl.multiple_of(lax.bitwise_xor(own % 2, i) * depth, depth)
            if halves == 1:
                weights[pl.ds(at, depth), :] = far_refs[i][...]
                continue
            for j in range(2):
                column = pl.multiple_of(lax.bitwise_xor(place_ref[3], j) * wide, wide)
                weights[pl.ds(at, depth), pl.ds(column, wide)] = far_refs[2 * i + j][...]
        far = pl.ds(pl.multiple_of((1 - own // 2) * (2 * depth), 2 * depth), 2 * depth)
        normed = normed_ref[:, far]
        value = near_ref[:, 0:wide] + jnp.dot(normed, weights[:, 0:wide], preferred_element_type=jnp.float32)
        gate = near_ref[:, wide:] + jnp.dot(normed, weights[:, wide:], preferred_element_type=jnp.float32)
    else:
        columns = slice(block * wide, (block + 1) * wide)
        value = jnp.dot(normed_ref[...], weight_refs[0][:, columns], preferred_element_type=jnp.float32)
        columns = slice(channels + block * wide, channels + (block + 1) * wide)
        gate = jnp.dot(normed_ref[...], weight_refs[0][:, columns], preferred_element_type=jnp.float32)
    start, length = place_ref[1], place_ref[2]
    position = start - HALO + lax.broadcasted_iota(jnp.int32, (ext_rows, 1), 0)
    valid = (position >= 0) & (position < length)
    kept = jnp.where(valid, value * jax.nn.sigmoid(gate), 0.0)
    kept = kept.astype(jnp.bfloat16).astype(jnp.float32)
    first = HALO - (taps - 1) // 2
    step = 64
    for unit in range(wide // LANES):
        lanes = slice(unit * LANES, (unit + 1) * LANES)
        tap_lanes = slice(block * wide + unit * LANES, block * wide + (unit + 1) * LANES)
        column = kept[:, lanes]
        gated[0] = column
        for phase in range(1, 8):
            gated[phase] = pltpu.roll(column, ext_rows - phase, 0)
        for at in range(0, row_count, step):
            acc = None
            for tap in range(taps):
                base = at + (first + tap) // 8 * 8
                term = gated[(first + tap) % 8, base : base + step, :] * taps_ref[tap : tap + 1, tap_lanes]
                acc = term if acc is None else acc + term
            conv_ref[at : at + step, lanes] = acc
    here = start + lax.broadcasted_iota(jnp.int32, (row_count, 1), 0) < length
    count = jnp.clip(length - start, 0, row_count).astype(jnp.float32)
    conv = conv_ref[...]
    mean = jnp.sum(jnp.where(here, conv, 0.0), axis=0, keepdims=True) / jnp.maximum(count, 1.0)
    deviate = jnp.where(here, conv - mean, 0.0)
    square = jnp.sum(deviate * deviate, axis=0, keepdims=True)
    stats = [mean, square, jnp.full((1, wide), count)]
    if not earlier_refs:
        for i, row in enumerate(stats):
            stats_ref[i : i + 1, :] = row
        return
    for i, row in enumerate(stats):
        for copy in range(stats_ref.shape[0]):
            stats_ref[copy, i : i + 1, block * wide : (block + 1) * wide] = row
            for other, ref in zip([j for j in ORDER if j != block], earlier_refs):
                stats_ref[copy, i : i + 1, other * wide : (other + 1) * wide] = ref[i : i + 1, :]


def front_block(block, wide, place, normed, weights, dw_kernel, earlier=(), copies=1):
    ext_rows, width = normed.shape
    row_count = ext_rows - 2 * HALO
    depth = 2 * weights[1].shape[0] if len(weights) > 1 else 16
    stats_shape = (copies, 3, dw_kernel.shape[1]) if earlier else (3, wide)
    return pl.pallas_call(
        functools.partial(front_kernel, block, len(earlier)),
        out_shape=(
            jax.ShapeDtypeStruct((row_count, wide), jnp.float32),
            jax.ShapeDtypeStruct(stats_shape, jnp.float32),
        ),
        in_specs=[pl.BlockSpec(memory_space=pltpu.SMEM)]
        + [pl.BlockSpec(memory_space=VMEM)] * (2 + len(weights) + len(earlier)),
        out_specs=[pl.BlockSpec(memory_space=VMEM)] * 2,
        scratch_shapes=[
            VMEM((depth, 2 * wide), jnp.bfloat16),
            VMEM((8, ext_rows, LANES), jnp.float32),
        ],
        compiler_params=params(10),
        cost_estimate=cost(4 * 10**9 if block == ORDER[1] else 10**8),
        name="front",
    )(place, normed, *earlier, *weights, dw_kernel)


def merged(parts):
    means, squares, counts = zip(*parts)
    count = sum(counts)
    mean = sum(n * m for n, m in zip(counts, means)) / jnp.maximum(count, 1.0)
    square = sum(squares) + sum(n * (m - mean) * (m - mean) for n, m in zip(counts, means))
    return mean, square, count


def rows_of(refs):
    return [[ref[copy, i : i + 1, :] for i in range(3)] for ref in refs for copy in range(ref.shape[0])]


def merge_kernel(stats_ref, out_ref):
    for i, row in enumerate(merged(rows_of([stats_ref]))):
        for copy in range(out_ref.shape[0]):
            out_ref[copy, i : i + 1, :] = row


def merge(stats, copies):
    return pl.pallas_call(
        merge_kernel,
        out_shape=jax.ShapeDtypeStruct((copies,) + stats.shape[1:], jnp.float32),
        in_specs=[pl.BlockSpec(memory_space=VMEM)],
        out_specs=pl.BlockSpec(memory_space=VMEM),
        compiler_params=params(8),
        cost_estimate=cost(10**8),
        name="merge",
    )(stats)


def back_kernel(stat_count, place_ref, gain_ref, shift_ref, *refs):
    stat_refs, refs = refs[:stat_count], refs[stat_count:]
    *conv_refs, out_ref, rows_out, sems, weights = refs
    convs, weight_refs = conv_refs[:3], conv_refs[3:]
    row_count, wide = convs[0].shape
    if len(weight_refs) > 1:
        depth = weight_refs[0].shape[0]
        for i, weight_ref in enumerate(weight_refs[:2]):
            at = pl.multiple_of(lax.bitwise_xor(place_ref[0], i) * depth, depth)
            weights[pl.ds(at, depth), :] = weight_ref[...]
        at, unit = 0, 16
        for weight_ref in weight_refs[2:]:
            rows = weight_ref.shape[0]
            start = lax.bitwise_xor(place_ref[0], 2 + at // depth) * depth + at % depth
            weights[pl.ds(pl.multiple_of(start, unit), rows), :] = weight_ref[...]
            at += rows
    else:
        weights[...] = weight_refs[0][...]
    mean, square, count = merged(rows_of(stat_refs))
    scale = lax.rsqrt(square / count + 1e-05) * gain_ref[...]
    shift = shift_ref[...]
    pieces, rows, columns = rows_out.shape
    across = out_ref.shape[1] // columns
    copies = []
    for piece in range(pieces // across):
        here = slice(piece * rows, (piece + 1) * rows)
        parts = []
        for i, conv_ref in enumerate(convs):
            lanes = slice(i * wide, (i + 1) * wide)
            scaled = (conv_ref[here, :] - mean[:, lanes]) * scale[:, lanes] + shift[:, lanes]
            parts.append((scaled * jax.nn.sigmoid(scaled)).astype(jnp.bfloat16))
        activated = jnp.concatenate(parts, axis=1)
        position = place_ref[1] + piece * rows + lax.broadcasted_iota(jnp.int32, (rows, 1), 0)
        for j in range(across):
            lanes = slice(j * columns, (j + 1) * columns)
            result = jnp.dot(activated, weights[:, lanes], preferred_element_type=jnp.float32)
            slot = piece * across + j
            rows_out[slot] = jnp.where(position < place_ref[2], result, 0.0).astype(jnp.bfloat16)
            copy = pltpu.make_async_copy(rows_out.at[slot], out_ref.at[here, lanes], sems.at[slot])
            copy.start()
            copies.append(copy)
    for copy in copies:
        copy.wait()


def back(place, stats, gain, shift, convs, weights):
    row_count = convs[0].shape[0]
    channels, width = gain.shape[1], weights[0].shape[1]
    pieces, across = 4, 2
    return pl.pallas_call(
        functools.partial(back_kernel, len(stats)),
        out_shape=jax.ShapeDtypeStruct((row_count, width), jnp.bfloat16),
        in_specs=[pl.BlockSpec(memory_space=pltpu.SMEM)]
        + [pl.BlockSpec(memory_space=VMEM)] * (2 + len(stats) + len(convs) + len(weights)),
        out_specs=pl.BlockSpec(memory_space=pl.ANY),
        scratch_shapes=[
            VMEM((pieces, row_count * across // pieces, width // across), jnp.bfloat16),
            pltpu.SemaphoreType.DMA((pieces,)),
            VMEM((channels, width), jnp.bfloat16),
        ],
        compiler_params=params(10),
        cost_estimate=cost(10**9),
        name="back",
    )(place, gain, shift, *stats, *convs, *weights)


def everyones(copies, groups):
    return lax.all_to_all(copies, ("fsdp", "ctx"), 0, 0, axis_index_groups=groups, tiled=True)


def tie(*values):
    return lax.optimization_barrier(values)


def body(frames, lengths, ln_gain, w_in, dw_kernel, bn_gain, bn_shift, w_out):
    _, row_count, model_width = frames.shape
    channels = dw_kernel.shape[1]
    wide = channels // 3
    ctx, fsdp = lax.axis_index("ctx"), lax.axis_index("fsdp")
    ctx_count, fsdp_count = lax.axis_size("ctx"), lax.axis_size("fsdp")
    direct = fsdp_count == 4 and ctx_count == 8
    rows = frames[0]
    gain = ln_gain[None]
    parity = lax.rem(ctx, 2)
    place = jnp.stack([fsdp, ctx * row_count, lengths[0], parity]).astype(jnp.int32)
    ends = ctx_count - 1
    down, up = [(i, i + 1) for i in range(ends)], [(i + 1, i) for i in range(ends)]
    both = ("fsdp", "ctx")
    member = lambda f, p: f * ctx_count + p

    def front(block, weights, *extra):
        return front_block(block, wide, place, normed, weights, dw_kernel, *extra)

    if direct:
        two, zero, one = cut(place, w_in, wide)
        two, zero = swap(two, "fsdp", 2), swap(zero, "fsdp", 2)
        across = swap(w_in, "fsdp", 1)
        inner, outer = edge_rows(place, rows)
        part_rows = w_out.shape[0] // 12
        normed, *pieces = normalize_rows(rows, gain, w_out, [3 * part_rows, 9 * part_rows])
        inner = swap(inner, "ctx", 1)
        pairs = [(i, i + 1) for i in range(1, ends, 2)]
        outer = lax.ppermute(outer, "ctx", pairs + [(j, i) for i, j in pairs])
        normed, inner, outer, two, zero = tie(normed, inner, outer, two, zero)
        two, zero = [two, swap(two, "ctx", 1)], [zero, swap(zero, "ctx", 1)]
        normed, *partials = near_product(place, normed, inner, outer, gain, w_in, across)
        partials[2], one, two[0], zero[0] = tie(partials[2], one, two[0], zero[0])
        one = swap(one, "fsdp", 2)
        two.append(swap(two[0], "fsdp", 1))
        zero.append(swap(zero[0], "fsdp", 1))
        partials[2], *parts = tie(partials[2], *two, *zero, w_out)
        two, zero, w_out = parts[:3], parts[3:6], parts[6]
        two.append(swap(two[1], "fsdp", 1))
        zero.append(swap(zero[1], "fsdp", 1))
        conv_two, stat_two = front(2, [partials[2], *two])
        conv_two, partials[0], one = tie(conv_two, partials[0], one)
        beyond_one = swap(one, "fsdp", 1)
        pieces = [swap(piece, "fsdp", 2) for piece in pieces]
        conv_zero, stat_zero = front(0, [partials[0], *zero])
        conv_zero, partials[1] = tie(conv_zero, partials[1])
        conv_one, stats = front(1, [partials[1], one, beyond_one], (stat_two, stat_zero), 1)
        across_out = swap(w_out, "fsdp", 1)
        stats, pieces[0] = tie(stats, pieces[0])
        beyond = [swap(pieces[0], "fsdp", 1)]
        convs = [conv_zero, conv_one, conv_two]

        def others(flips):
            return [
                lax.ppermute(
                    stats,
                    both,
                    [(member(f, p), member(f ^ df, p ^ dp)) for f in range(4) for p in range(8)],
                )
                for df, dp in flips
            ]

        def union(parts):
            return jnp.stack(merged([[part[:, i] for i in range(3)] for part in parts]), 1)

        stats = union([stats] + others([(1, 0)]))
        stats = union([stats] + others([(0, 2)]))
        stats = union([stats] + others([(0, 4)]))
        stats = [stats] + others([(0, 1), (2, 0), (2, 1)])
        *stats, pieces[1] = tie(*stats, pieces[1])
        beyond.append(swap(pieces[1], "fsdp", 1))
        out_weights = [w_out, across_out, *pieces, *beyond]
    else:
        full_in = lax.all_gather(w_in, "fsdp", axis=0, tiled=True)
        out_weights = [lax.all_gather(w_out, "fsdp", axis=0, tiled=True)]
        before = lax.ppermute(rows[-HALO:], "ctx", down)
        after = lax.ppermute(rows[:HALO], "ctx", up)
        inner = jnp.where(parity == 0, after, before)
        outer = jnp.where(parity == 0, before, after)
        (normed,) = normalize_rows(rows, gain, w_out, ())
        (normed,) = near_product(place, normed, inner, outer, gain)
        near_by = 2 if ctx_count % 2 == 0 else 1
        groups = [
            [member(f, p + i) for f in range(fsdp_count) for i in range(near_by)]
            for p in range(0, ctx_count, near_by)
        ]
        convs, stats = [None] * 3, []
        for block in ORDER:
            extra = (stats, len(groups[0])) if block == ORDER[-1] else ()
            convs[block], stat = front(block, [full_in], *extra)
            stats.append(stat)
        stats = merge(everyones(stats[2], groups), len(groups))
        groups = [
            [member(f, p + i) for p in range(0, ctx_count, near_by)]
            for f in range(fsdp_count)
            for i in range(near_by)
        ]
        stats = [everyones(stats, groups)]
    result = back(place, stats, bn_gain[None], bn_shift[None], convs, out_weights)
    return result[None]


def solution(mesh):
    return jax.shard_map(
        body,
        mesh=mesh,
        in_specs=(
            P("fsdp", "ctx", None),
            P("fsdp"),
            P(),
            P("fsdp", None),
            P(),
            P(),
            P(),
            P("fsdp", None),
        ),
        out_specs=P("fsdp", "ctx", None),
        check_vma=False,
    )
```

```python
import functools

import jax
import jax.numpy as jnp
from jax import lax
from jax.experimental import pallas as pl
from jax.experimental.pallas import tpu as pltpu
from jax.sharding import PartitionSpec as P

HALO = 16
LANES = 128
MIB = 1024 * 1024
VMEM = pltpu.VMEM
ORDER = (2, 0, 1)
SHARED = {2: 3, 0: 4}


def cost(flops):
    return pl.CostEstimate(flops=flops, bytes_accessed=0, transcendentals=0)


def params(mib):
    return pltpu.CompilerParams(vmem_limit_bytes=mib * MIB)


def swap(value, axis, bit):
    return lax.ppermute(value, axis, [(i, i ^ bit) for i in range(lax.axis_size(axis))])


def cut_kernel(place_ref, shard_ref, two_ref, zero_ref, one_ref):
    wide = two_ref.shape[1]
    channels = shard_ref.shape[1] // 2
    for block, ref in ((2, two_ref), (0, zero_ref)):
        at = pl.multiple_of(place_ref[SHARED[block]] * channels + block * wide, wide)
        ref[...] = shard_ref[:, pl.ds(at, wide)]
    for i in range(2):
        at = i * channels + wide
        one_ref[:, i * wide : (i + 1) * wide] = shard_ref[:, at : at + wide]


def cut(place, shard, wide):
    depth = shard.shape[0]
    shapes = [(depth, wide), (depth, wide), (depth, 2 * wide)]
    return pl.pallas_call(
        cut_kernel,
        out_shape=[jax.ShapeDtypeStruct(shape, jnp.bfloat16) for shape in shapes],
        in_specs=[pl.BlockSpec(memory_space=pltpu.SMEM), pl.BlockSpec(memory_space=VMEM)],
        out_specs=[pl.BlockSpec(memory_space=VMEM)] * 3,
        compiler_params=params(4),
        cost_estimate=cost(10**8),
        name="cut",
    )(place, shard)


def normalize(values, gain):
    values = values.astype(jnp.float32)
    centre = jnp.mean(values, axis=-1, keepdims=True)
    deviate = values - centre
    spread = jnp.mean(deviate * deviate, axis=-1, keepdims=True)
    return (deviate * lax.rsqrt(spread + 1e-05) * gain).astype(jnp.bfloat16)


def edge_kernel(place_ref, rows_ref, inner_ref, outer_ref):
    odd = place_ref[3]
    last = rows_ref.shape[0] - HALO
    inner_ref[...] = rows_ref[pl.ds(pl.multiple_of((1 - odd) * last, HALO), HALO), :]
    outer_ref[...] = rows_ref[pl.ds(pl.multiple_of(odd * last, HALO), HALO), :]


def edge_rows(place, rows):
    shape = jax.ShapeDtypeStruct((HALO, rows.shape[1]), rows.dtype)
    return pl.pallas_call(
        edge_kernel,
        out_shape=[shape, shape],
        in_specs=[pl.BlockSpec(memory_space=pltpu.SMEM), pl.BlockSpec(memory_space=VMEM)],
        out_specs=[pl.BlockSpec(memory_space=VMEM)] * 2,
        compiler_params=params(2),
        cost_estimate=cost(10**8),
        name="edges",
    )(place, rows)


def norm_kernel(rows_ref, gain_ref, shard_ref, out_ref, *piece_refs):
    step = 64

    @pl.loop(0, rows_ref.shape[0] // step)
    def _(i):
        here = pl.ds(pl.multiple_of(i * step, step), step)
        out_ref[here, :] = normalize(rows_ref[here, :], gain_ref[...])

    at = 0
    for ref in piece_refs:
        ref[...] = shard_ref[at : at + ref.shape[0], :]
        at += ref.shape[0]


def normalize_rows(rows, gain, shard, pieces):
    row_count, width = rows.shape
    shapes = [(row_count, width)] + [(piece, width) for piece in pieces]
    return pl.pallas_call(
        norm_kernel,
        out_shape=[jax.ShapeDtypeStruct(shape, jnp.bfloat16) for shape in shapes],
        in_specs=[pl.BlockSpec(memory_space=VMEM)] * 3,
        out_specs=[pl.BlockSpec(memory_space=VMEM)] * len(shapes),
        compiler_params=params(4),
        cost_estimate=cost(10**8),
        name="layer_norm",
    )(rows, gain, shard)


def near_kernel(place_ref, rows_ref, inner_ref, outer_ref, gain_ref, *refs):
    row_count = rows_ref.shape[0]
    gain = gain_ref[...]
    *weight_refs, ext_ref = refs[:3] if len(refs) > 1 else refs
    odd = place_ref[3]
    at = pl.multiple_of((1 - odd) * (HALO + row_count), HALO)
    ext_ref[pl.ds(at, HALO), :] = normalize(inner_ref[...], gain)
    at = pl.multiple_of(odd * (HALO + row_count), HALO)
    ext_ref[pl.ds(at, HALO), :] = normalize(outer_ref[...], gain)
    ext_ref[HALO : HALO + row_count, :] = rows_ref[...]
    if not weight_refs:
        return
    *out_refs, weights = refs[3:]
    own = place_ref[0]
    depth, width = weight_refs[0].shape
    for i, weight_ref in enumerate(weight_refs):
        at = pl.multiple_of(lax.bitwise_xor(own % 2, i) * depth, depth)
        weights[pl.ds(at, depth), :] = weight_ref[...]
    near = pl.ds(pl.multiple_of(own // 2 * (2 * depth), 2 * depth), 2 * depth)
    wide = out_refs[0].shape[1] // 2
    channels = width // 2
    for block, out_ref in enumerate(out_refs):
        for i in range(2):
            columns = slice(i * channels + block * wide, i * channels + (block + 1) * wide)
            out_ref[:, i * wide : (i + 1) * wide] = jnp.dot(
                ext_ref[:, near], weights[:, columns], preferred_element_type=jnp.float32
            )


def near_product(place, rows, inner, outer, gain, *shards):
    row_count, width = rows.shape
    ext_rows = row_count + 2 * HALO
    shapes = [jax.ShapeDtypeStruct((ext_rows, width), jnp.bfloat16)]
    scratch = []
    if shards:
        shapes += [jax.ShapeDtypeStruct((ext_rows, width // 3), jnp.float32)] * 3
        scratch.append(VMEM((2 * shards[0].shape[0], width), jnp.bfloat16))
    return pl.pallas_call(
        near_kernel,
        out_shape=shapes,
        in_specs=[pl.BlockSpec(memory_space=pltpu.SMEM)]
        + [pl.BlockSpec(memory_space=VMEM)] * (4 + len(shards)),
        out_specs=[pl.BlockSpec(memory_space=VMEM)] * len(shapes),
        scratch_shapes=scratch,
        compiler_params=params(8),
        cost_estimate=cost(10**8),
        name="near",
    )(place, rows, inner, outer, gain, *shards)


def front_kernel(block, earlier, place_ref, normed_ref, *refs):
    refs, earlier_refs = refs[earlier:], refs[:earlier]
    *weight_refs, taps_ref, conv_ref, stats_ref, weights, gated = refs
    ext_rows = normed_ref.shape[0]
    row_count, wide = conv_ref.shape
    taps, channels = taps_ref.shape
    if len(weight_refs) > 1:
        near_ref, *far_refs = weight_refs
        own = place_ref[0]
        depth = far_refs[0].shape[0]
        halves = len(far_refs) // 2
        for i in range(2):
            at = pl.multiple_of(lax.bitwise_xor(own % 2, i) * depth, depth)
            if halves == 1:
                weights[pl.ds(at, depth), :] = far_refs[i][...]
                continue
            for j in range(2):
                column = pl.multiple_of(lax.bitwise_xor(place_ref[SHARED[block]], j) * wide, wide)
                weights[pl.ds(at, depth), pl.ds(column, wide)] = far_refs[2 * i + j][...]
        far = pl.ds(pl.multiple_of((1 - own // 2) * (2 * depth), 2 * depth), 2 * depth)
        normed = normed_ref[:, far]
        value = near_ref[:, 0:wide] + jnp.dot(normed, weights[:, 0:wide], preferred_element_type=jnp.float32)
        gate = near_ref[:, wide:] + jnp.dot(normed, weights[:, wide:], preferred_element_type=jnp.float32)
    else:
        columns = slice(block * wide, (block + 1) * wide)
        value = jnp.dot(normed_ref[...], weight_refs[0][:, columns], preferred_element_type=jnp.float32)
        columns = slice(channels + block * wide, channels + (block + 1) * wide)
        gate = jnp.dot(normed_ref[...], weight_refs[0][:, columns], preferred_element_type=jnp.float32)
    start, length = place_ref[1], place_ref[2]
    position = start - HALO + lax.broadcasted_iota(jnp.int32, (ext_rows, 1), 0)
    valid = (position >= 0) & (position < length)
    kept = jnp.where(valid, value * jax.nn.sigmoid(gate), 0.0)
    kept = kept.astype(jnp.bfloat16).astype(jnp.float32)
    first = HALO - (taps - 1) // 2
    step = 64
    for unit in range(wide // LANES):
        lanes = slice(unit * LANES, (unit + 1) * LANES)
        tap_lanes = slice(block * wide + unit * LANES, block * wide + (unit + 1) * LANES)
        column = kept[:, lanes]
        gated[0] = column
        for phase in range(1, 8):
            gated[phase] = pltpu.roll(column, ext_rows - phase, 0)
        for at in range(0, row_count, step):
            acc = None
            for tap in range(taps):
                base = at + (first + tap) // 8 * 8
                term = gated[(first + tap) % 8, base : base + step, :] * taps_ref[tap : tap + 1, tap_lanes]
                acc = term if acc is None else acc + term
            conv_ref[at : at + step, lanes] = acc
    here = start + lax.broadcasted_iota(jnp.int32, (row_count, 1), 0) < length
    count = jnp.clip(length - start, 0, row_count).astype(jnp.float32)
    conv = conv_ref[...]
    mean = jnp.sum(jnp.where(here, conv, 0.0), axis=0, keepdims=True) / jnp.maximum(count, 1.0)
    deviate = jnp.where(here, conv - mean, 0.0)
    square = jnp.sum(deviate * deviate, axis=0, keepdims=True)
    stats = [mean, square, jnp.full((1, wide), count)]
    if not earlier_refs:
        for i, row in enumerate(stats):
            stats_ref[i : i + 1, :] = row
        return
    for i, row in enumerate(stats):
        for copy in range(stats_ref.shape[0]):
            stats_ref[copy, i : i + 1, block * wide : (block + 1) * wide] = row
            for other, ref in zip([j for j in ORDER if j != block], earlier_refs):
                stats_ref[copy, i : i + 1, other * wide : (other + 1) * wide] = ref[i : i + 1, :]


def front_block(block, wide, place, normed, weights, dw_kernel, earlier=(), copies=1):
    ext_rows, width = normed.shape
    row_count = ext_rows - 2 * HALO
    depth = 2 * weights[1].shape[0] if len(weights) > 1 else 16
    stats_shape = (copies, 3, dw_kernel.shape[1]) if earlier else (3, wide)
    return pl.pallas_call(
        functools.partial(front_kernel, block, len(earlier)),
        out_shape=(
            jax.ShapeDtypeStruct((row_count, wide), jnp.float32),
            jax.ShapeDtypeStruct(stats_shape, jnp.float32),
        ),
        in_specs=[pl.BlockSpec(memory_space=pltpu.SMEM)]
        + [pl.BlockSpec(memory_space=VMEM)] * (2 + len(weights) + len(earlier)),
        out_specs=[pl.BlockSpec(memory_space=VMEM)] * 2,
        scratch_shapes=[
            VMEM((depth, 2 * wide), jnp.bfloat16),
            VMEM((8, ext_rows, LANES), jnp.float32),
        ],
        compiler_params=params(10),
        cost_estimate=cost(4 * 10**9 if block == ORDER[1] else 10**8),
        name="front",
    )(place, normed, *earlier, *weights, dw_kernel)


def merged(parts):
    means, squares, counts = zip(*parts)
    count = sum(counts)
    mean = sum(n * m for n, m in zip(counts, means)) / jnp.maximum(count, 1.0)
    square = sum(squares) + sum(n * (m - mean) * (m - mean) for n, m in zip(counts, means))
    return mean, square, count


def rows_of(refs):
    return [[ref[copy, i : i + 1, :] for i in range(3)] for ref in refs for copy in range(ref.shape[0])]


def merge_kernel(stats_ref, out_ref):
    for i, row in enumerate(merged(rows_of([stats_ref]))):
        for copy in range(out_ref.shape[0]):
            out_ref[copy, i : i + 1, :] = row


def merge(stats, copies):
    return pl.pallas_call(
        merge_kernel,
        out_shape=jax.ShapeDtypeStruct((copies,) + stats.shape[1:], jnp.float32),
        in_specs=[pl.BlockSpec(memory_space=VMEM)],
        out_specs=pl.BlockSpec(memory_space=VMEM),
        compiler_params=params(8),
        cost_estimate=cost(10**8),
        name="merge",
    )(stats)


def back_kernel(stat_count, place_ref, gain_ref, shift_ref, *refs):
    stat_refs, refs = refs[:stat_count], refs[stat_count:]
    *conv_refs, out_ref, rows_out, sems, weights = refs
    convs, weight_refs = conv_refs[:3], conv_refs[3:]
    row_count, wide = convs[0].shape
    if len(weight_refs) > 1:
        depth = weight_refs[0].shape[0]
        for i, weight_ref in enumerate(weight_refs[:2]):
            at = pl.multiple_of(lax.bitwise_xor(place_ref[0], i) * depth, depth)
            weights[pl.ds(at, depth), :] = weight_ref[...]
        at, unit = 0, 16
        for weight_ref in weight_refs[2:]:
            rows = weight_ref.shape[0]
            start = lax.bitwise_xor(place_ref[0], 2 + at // depth) * depth + at % depth
            weights[pl.ds(pl.multiple_of(start, unit), rows), :] = weight_ref[...]
            at += rows
    else:
        weights[...] = weight_refs[0][...]
    mean, square, count = merged(rows_of(stat_refs))
    scale = lax.rsqrt(square / count + 1e-05) * gain_ref[...]
    shift = shift_ref[...]
    pieces, rows, columns = rows_out.shape
    across = out_ref.shape[1] // columns
    copies = []
    for piece in range(pieces // across):
        here = slice(piece * rows, (piece + 1) * rows)
        parts = []
        for i, conv_ref in enumerate(convs):
            lanes = slice(i * wide, (i + 1) * wide)
            scaled = (conv_ref[here, :] - mean[:, lanes]) * scale[:, lanes] + shift[:, lanes]
            parts.append((scaled * jax.nn.sigmoid(scaled)).astype(jnp.bfloat16))
        activated = jnp.concatenate(parts, axis=1)
        position = place_ref[1] + piece * rows + lax.broadcasted_iota(jnp.int32, (rows, 1), 0)
        for j in range(across):
            lanes = slice(j * columns, (j + 1) * columns)
            result = jnp.dot(activated, weights[:, lanes], preferred_element_type=jnp.float32)
            slot = piece * across + j
            rows_out[slot] = jnp.where(position < place_ref[2], result, 0.0).astype(jnp.bfloat16)
            copy = pltpu.make_async_copy(rows_out.at[slot], out_ref.at[here, lanes], sems.at[slot])
            copy.start()
            copies.append(copy)
    for copy in copies:
        copy.wait()


def back(place, stats, gain, shift, convs, weights):
    row_count = convs[0].shape[0]
    channels, width = gain.shape[1], weights[0].shape[1]
    pieces, across = 4, 2
    return pl.pallas_call(
        functools.partial(back_kernel, len(stats)),
        out_shape=jax.ShapeDtypeStruct((row_count, width), jnp.bfloat16),
        in_specs=[pl.BlockSpec(memory_space=pltpu.SMEM)]
        + [pl.BlockSpec(memory_space=VMEM)] * (2 + len(stats) + len(convs) + len(weights)),
        out_specs=pl.BlockSpec(memory_space=pl.ANY),
        scratch_shapes=[
            VMEM((pieces, row_count * across // pieces, width // across), jnp.bfloat16),
            pltpu.SemaphoreType.DMA((pieces,)),
            VMEM((channels, width), jnp.bfloat16),
        ],
        compiler_params=params(10),
        cost_estimate=cost(10**9),
        name="back",
    )(place, gain, shift, *stats, *convs, *weights)


def everyones(copies, groups):
    return lax.all_to_all(copies, ("fsdp", "ctx"), 0, 0, axis_index_groups=groups, tiled=True)


def tie(*values):
    return lax.optimization_barrier(values)


def body(frames, lengths, ln_gain, w_in, dw_kernel, bn_gain, bn_shift, w_out):
    _, row_count, model_width = frames.shape
    channels = dw_kernel.shape[1]
    wide = channels // 3
    ctx, fsdp = lax.axis_index("ctx"), lax.axis_index("fsdp")
    ctx_count, fsdp_count = lax.axis_size("ctx"), lax.axis_size("fsdp")
    direct = fsdp_count == 4 and ctx_count == 8
    rows = frames[0]
    gain = ln_gain[None]
    parity, pair = lax.rem(ctx, 2), lax.rem(ctx // 2, 2)
    place = jnp.stack([fsdp, ctx * row_count, lengths[0], parity, pair]).astype(jnp.int32)
    ends = ctx_count - 1
    down, up = [(i, i + 1) for i in range(ends)], [(i + 1, i) for i in range(ends)]
    both = ("fsdp", "ctx")
    member = lambda f, p: f * ctx_count + p

    def front(block, weights, *extra):
        return front_block(block, wide, place, normed, weights, dw_kernel, *extra)

    if direct:
        two, zero, one = cut(place, w_in, wide)
        two, zero = swap(two, "fsdp", 2), swap(zero, "fsdp", 2)
        across = swap(w_in, "fsdp", 1)
        inner, outer = edge_rows(place, rows)
        part_rows = w_out.shape[0] // 12
        normed, *pieces = normalize_rows(rows, gain, w_out, [4 * part_rows, 8 * part_rows])
        inner = swap(inner, "ctx", 1)
        pairs = [(i, i + 1) for i in range(1, ends, 2)]
        outer = lax.ppermute(outer, "ctx", pairs + [(j, i) for i, j in pairs])
        normed, inner, outer, two, zero = tie(normed, inner, outer, two, zero)
        two, zero = [two, swap(two, "ctx", 1)], [zero, swap(zero, "ctx", 2)]
        normed, *partials = near_product(place, normed, inner, outer, gain, w_in, across)
        partials[2], one, two[0], zero[0] = tie(partials[2], one, two[0], zero[0])
        one = swap(one, "fsdp", 2)
        two.append(swap(two[0], "fsdp", 1))
        zero.append(swap(zero[0], "fsdp", 1))
        partials[2], *parts = tie(partials[2], *two, *zero, w_out)
        two, zero, w_out = parts[:3], parts[3:6], parts[6]
        two.append(swap(two[1], "fsdp", 1))
        zero.append(swap(zero[1], "fsdp", 1))
        conv_two, stat_two = front(2, [partials[2], *two])
        conv_two, partials[0], one = tie(conv_two, partials[0], one)
        beyond_one = swap(one, "fsdp", 1)
        pieces = [swap(piece, "fsdp", 2) for piece in pieces]
        conv_zero, stat_zero = front(0, [partials[0], *zero])
        conv_zero, partials[1] = tie(conv_zero, partials[1])
        conv_one, stats = front(1, [partials[1], one, beyond_one], (stat_two, stat_zero), 1)
        across_out = swap(w_out, "fsdp", 1)
        stats, pieces[0] = tie(stats, pieces[0])
        beyond = [swap(pieces[0], "fsdp", 1)]
        convs = [conv_zero, conv_one, conv_two]

        def others(flips):
            return [
                lax.ppermute(
                    stats,
                    both,
                    [(member(f, p), member(f ^ df, p ^ dp)) for f in range(4) for p in range(8)],
                )
                for df, dp in flips
            ]

        def union(parts):
            return jnp.stack(merged([[part[:, i] for i in range(3)] for part in parts]), 1)

        stats = union([stats] + others([(1, 0)]))
        stats = union([stats] + others([(0, 2)]))
        stats = union([stats] + others([(0, 4)]))
        stats = [stats] + others([(0, 1), (2, 0), (2, 1)])
        *stats, pieces[1] = tie(*stats, pieces[1])
        beyond.append(swap(pieces[1], "fsdp", 1))
        out_weights = [w_out, across_out, *pieces, *beyond]
    else:
        full_in = lax.all_gather(w_in, "fsdp", axis=0, tiled=True)
        out_weights = [lax.all_gather(w_out, "fsdp", axis=0, tiled=True)]
        before = lax.ppermute(rows[-HALO:], "ctx", down)
        after = lax.ppermute(rows[:HALO], "ctx", up)
        inner = jnp.where(parity == 0, after, before)
        outer = jnp.where(parity == 0, before, after)
        (normed,) = normalize_rows(rows, gain, w_out, ())
        (normed,) = near_product(place, normed, inner, outer, gain)
        near_by = 2 if ctx_count % 2 == 0 else 1
        groups = [
            [member(f, p + i) for f in range(fsdp_count) for i in range(near_by)]
            for p in range(0, ctx_count, near_by)
        ]
        convs, stats = [None] * 3, []
        for block in ORDER:
            extra = (stats, len(groups[0])) if block == ORDER[-1] else ()
            convs[block], stat = front(block, [full_in], *extra)
            stats.append(stat)
        stats = merge(everyones(stats[2], groups), len(groups))
        groups = [
            [member(f, p + i) for p in range(0, ctx_count, near_by)]
            for f in range(fsdp_count)
            for i in range(near_by)
        ]
        stats = [everyones(stats, groups)]
    result = back(place, stats, bn_gain[None], bn_shift[None], convs, out_weights)
    return result[None]


def solution(mesh):
    return jax.shard_map(
        body,
        mesh=mesh,
        in_specs=(
            P("fsdp", "ctx", None),
            P("fsdp"),
            P(),
            P("fsdp", None),
            P(),
            P(),
            P(),
            P("fsdp", None),
        ),
        out_specs=P("fsdp", "ctx", None),
        check_vma=False,
    )
```

```python
import functools

import jax
import jax.numpy as jnp
from jax import lax
from jax.experimental import pallas as pl
from jax.experimental.pallas import tpu as pltpu
from jax.sharding import PartitionSpec as P

HALO = 16
LANES = 128
MIB = 1024 * 1024
VMEM = pltpu.VMEM
ORDER = (2, 0, 1)
SHARED = {2: 3, 0: 4}


def cost(flops):
    return pl.CostEstimate(flops=flops, bytes_accessed=0, transcendentals=0)


def params(mib):
    return pltpu.CompilerParams(vmem_limit_bytes=mib * MIB)


def swap(value, axis, bit):
    return lax.ppermute(value, axis, [(i, i ^ bit) for i in range(lax.axis_size(axis))])


def cut_kernel(place_ref, shard_ref, two_ref, zero_ref, one_ref):
    wide = two_ref.shape[1]
    channels = shard_ref.shape[1] // 2
    for block, ref in ((2, two_ref), (0, zero_ref)):
        at = pl.multiple_of(place_ref[SHARED[block]] * channels + block * wide, wide)
        ref[...] = shard_ref[:, pl.ds(at, wide)]
    for i in range(2):
        at = i * channels + wide
        one_ref[:, i * wide : (i + 1) * wide] = shard_ref[:, at : at + wide]


def cut(place, shard, wide):
    depth = shard.shape[0]
    shapes = [(depth, wide), (depth, wide), (depth, 2 * wide)]
    return pl.pallas_call(
        cut_kernel,
        out_shape=[jax.ShapeDtypeStruct(shape, jnp.bfloat16) for shape in shapes],
        in_specs=[pl.BlockSpec(memory_space=pltpu.SMEM), pl.BlockSpec(memory_space=VMEM)],
        out_specs=[pl.BlockSpec(memory_space=VMEM)] * 3,
        compiler_params=params(4),
        cost_estimate=cost(10**8),
        name="cut",
    )(place, shard)


def normalize(values, gain):
    values = values.astype(jnp.float32)
    centre = jnp.mean(values, axis=-1, keepdims=True)
    deviate = values - centre
    spread = jnp.mean(deviate * deviate, axis=-1, keepdims=True)
    return (deviate * lax.rsqrt(spread + 1e-05) * gain).astype(jnp.bfloat16)


def edge_kernel(place_ref, rows_ref, inner_ref, outer_ref):
    odd = place_ref[3]
    last = rows_ref.shape[0] - HALO
    inner_ref[...] = rows_ref[pl.ds(pl.multiple_of((1 - odd) * last, HALO), HALO), :]
    outer_ref[...] = rows_ref[pl.ds(pl.multiple_of(odd * last, HALO), HALO), :]


def edge_rows(place, rows):
    shape = jax.ShapeDtypeStruct((HALO, rows.shape[1]), rows.dtype)
    return pl.pallas_call(
        edge_kernel,
        out_shape=[shape, shape],
        in_specs=[pl.BlockSpec(memory_space=pltpu.SMEM), pl.BlockSpec(memory_space=VMEM)],
        out_specs=[pl.BlockSpec(memory_space=VMEM)] * 2,
        compiler_params=params(2),
        cost_estimate=cost(10**8),
        name="edges",
    )(place, rows)


def norm_kernel(rows_ref, gain_ref, shard_ref, out_ref, *piece_refs):
    step = 64

    @pl.loop(0, rows_ref.shape[0] // step)
    def _(i):
        here = pl.ds(pl.multiple_of(i * step, step), step)
        out_ref[here, :] = normalize(rows_ref[here, :], gain_ref[...])

    at = 0
    for ref in piece_refs:
        ref[...] = shard_ref[at : at + ref.shape[0], :]
        at += ref.shape[0]


def normalize_rows(rows, gain, shard, pieces):
    row_count, width = rows.shape
    shapes = [(row_count, width)] + [(piece, width) for piece in pieces]
    return pl.pallas_call(
        norm_kernel,
        out_shape=[jax.ShapeDtypeStruct(shape, jnp.bfloat16) for shape in shapes],
        in_specs=[pl.BlockSpec(memory_space=VMEM)] * 3,
        out_specs=[pl.BlockSpec(memory_space=VMEM)] * len(shapes),
        compiler_params=params(4),
        cost_estimate=cost(10**8),
        name="layer_norm",
    )(rows, gain, shard)


def near_kernel(place_ref, rows_ref, inner_ref, outer_ref, gain_ref, *refs):
    row_count = rows_ref.shape[0]
    gain = gain_ref[...]
    *weight_refs, ext_ref = refs[:3] if len(refs) > 1 else refs
    odd = place_ref[3]
    at = pl.multiple_of((1 - odd) * (HALO + row_count), HALO)
    ext_ref[pl.ds(at, HALO), :] = normalize(inner_ref[...], gain)
    at = pl.multiple_of(odd * (HALO + row_count), HALO)
    ext_ref[pl.ds(at, HALO), :] = normalize(outer_ref[...], gain)
    ext_ref[HALO : HALO + row_count, :] = rows_ref[...]
    if not weight_refs:
        return
    *out_refs, weights = refs[3:]
    own = place_ref[0]
    depth, width = weight_refs[0].shape
    for i, weight_ref in enumerate(weight_refs):
        at = pl.multiple_of(lax.bitwise_xor(own % 2, i) * depth, depth)
        weights[pl.ds(at, depth), :] = weight_ref[...]
    near = pl.ds(pl.multiple_of(own // 2 * (2 * depth), 2 * depth), 2 * depth)
    wide = out_refs[0].shape[1] // 2
    channels = width // 2
    for block, out_ref in enumerate(out_refs):
        for i in range(2):
            columns = slice(i * channels + block * wide, i * channels + (block + 1) * wide)
            out_ref[:, i * wide : (i + 1) * wide] = jnp.dot(
                ext_ref[:, near], weights[:, columns], preferred_element_type=jnp.float32
            )


def near_product(place, rows, inner, outer, gain, *shards):
    row_count, width = rows.shape
    ext_rows = row_count + 2 * HALO
    shapes = [jax.ShapeDtypeStruct((ext_rows, width), jnp.bfloat16)]
    scratch = []
    if shards:
        shapes += [jax.ShapeDtypeStruct((ext_rows, width // 3), jnp.float32)] * 3
        scratch.append(VMEM((2 * shards[0].shape[0], width), jnp.bfloat16))
    return pl.pallas_call(
        near_kernel,
        out_shape=shapes,
        in_specs=[pl.BlockSpec(memory_space=pltpu.SMEM)]
        + [pl.BlockSpec(memory_space=VMEM)] * (4 + len(shards)),
        out_specs=[pl.BlockSpec(memory_space=VMEM)] * len(shapes),
        scratch_shapes=scratch,
        compiler_params=params(8),
        cost_estimate=cost(10**8),
        name="near",
    )(place, rows, inner, outer, gain, *shards)


def front_kernel(block, earlier, place_ref, normed_ref, *refs):
    refs, earlier_refs = refs[earlier:], refs[:earlier]
    *weight_refs, taps_ref, conv_ref, stats_ref, weights, gated = refs
    ext_rows = normed_ref.shape[0]
    row_count, wide = conv_ref.shape
    taps, channels = taps_ref.shape
    if len(weight_refs) > 1:
        near_ref, *far_refs = weight_refs
        own = place_ref[0]
        depth = far_refs[0].shape[0]
        halves = len(far_refs) // 2
        for i in range(2):
            at = pl.multiple_of(lax.bitwise_xor(own % 2, i) * depth, depth)
            if halves == 1:
                weights[pl.ds(at, depth), :] = far_refs[i][...]
                continue
            for j in range(2):
                column = pl.multiple_of(lax.bitwise_xor(place_ref[SHARED[block]], j) * wide, wide)
                weights[pl.ds(at, depth), pl.ds(column, wide)] = far_refs[2 * i + j][...]
        far = pl.ds(pl.multiple_of((1 - own // 2) * (2 * depth), 2 * depth), 2 * depth)
        normed = normed_ref[:, far]
        value = near_ref[:, 0:wide] + jnp.dot(normed, weights[:, 0:wide], preferred_element_type=jnp.float32)
        gate = near_ref[:, wide:] + jnp.dot(normed, weights[:, wide:], preferred_element_type=jnp.float32)
    else:
        columns = slice(block * wide, (block + 1) * wide)
        value = jnp.dot(normed_ref[...], weight_refs[0][:, columns], preferred_element_type=jnp.float32)
        columns = slice(channels + block * wide, channels + (block + 1) * wide)
        gate = jnp.dot(normed_ref[...], weight_refs[0][:, columns], preferred_element_type=jnp.float32)
    start, length = place_ref[1], place_ref[2]
    position = start - HALO + lax.broadcasted_iota(jnp.int32, (ext_rows, 1), 0)
    valid = (position >= 0) & (position < length)
    kept = jnp.where(valid, value * jax.nn.sigmoid(gate), 0.0)
    kept = kept.astype(jnp.bfloat16).astype(jnp.float32)
    first = HALO - (taps - 1) // 2
    step = 64
    for unit in range(wide // LANES):
        lanes = slice(unit * LANES, (unit + 1) * LANES)
        tap_lanes = slice(block * wide + unit * LANES, block * wide + (unit + 1) * LANES)
        column = kept[:, lanes]
        gated[0] = column
        for phase in range(1, 8):
            gated[phase] = pltpu.roll(column, ext_rows - phase, 0)
        for at in range(0, row_count, step):
            acc = None
            for tap in range(taps):
                base = at + (first + tap) // 8 * 8
                term = gated[(first + tap) % 8, base : base + step, :] * taps_ref[tap : tap + 1, tap_lanes]
                acc = term if acc is None else acc + term
            conv_ref[at : at + step, lanes] = acc
    here = start + lax.broadcasted_iota(jnp.int32, (row_count, 1), 0) < length
    count = jnp.clip(length - start, 0, row_count).astype(jnp.float32)
    conv = conv_ref[...]
    mean = jnp.sum(jnp.where(here, conv, 0.0), axis=0, keepdims=True) / jnp.maximum(count, 1.0)
    deviate = jnp.where(here, conv - mean, 0.0)
    square = jnp.sum(deviate * deviate, axis=0, keepdims=True)
    stats = [mean, square, jnp.full((1, wide), count)]
    if not earlier_refs:
        for i, row in enumerate(stats):
            stats_ref[i : i + 1, :] = row
        return
    for i, row in enumerate(stats):
        for copy in range(stats_ref.shape[0]):
            stats_ref[copy, i : i + 1, block * wide : (block + 1) * wide] = row
            for other, ref in zip([j for j in ORDER if j != block], earlier_refs):
                stats_ref[copy, i : i + 1, other * wide : (other + 1) * wide] = ref[i : i + 1, :]


def front_block(block, wide, place, normed, weights, dw_kernel, earlier=(), copies=1):
    ext_rows, width = normed.shape
    row_count = ext_rows - 2 * HALO
    depth = 2 * weights[1].shape[0] if len(weights) > 1 else 16
    stats_shape = (copies, 3, dw_kernel.shape[1]) if earlier else (3, wide)
    return pl.pallas_call(
        functools.partial(front_kernel, block, len(earlier)),
        out_shape=(
            jax.ShapeDtypeStruct((row_count, wide), jnp.float32),
            jax.ShapeDtypeStruct(stats_shape, jnp.float32),
        ),
        in_specs=[pl.BlockSpec(memory_space=pltpu.SMEM)]
        + [pl.BlockSpec(memory_space=VMEM)] * (2 + len(weights) + len(earlier)),
        out_specs=[pl.BlockSpec(memory_space=VMEM)] * 2,
        scratch_shapes=[
            VMEM((depth, 2 * wide), jnp.bfloat16),
            VMEM((8, ext_rows, LANES), jnp.float32),
        ],
        compiler_params=params(10),
        cost_estimate=cost(4 * 10**9 if block == ORDER[1] else 10**8),
        name="front",
    )(place, normed, *earlier, *weights, dw_kernel)


def merged(parts):
    means, squares, counts = zip(*parts)
    count = sum(counts)
    mean = sum(n * m for n, m in zip(counts, means)) / jnp.maximum(count, 1.0)
    square = sum(squares) + sum(n * (m - mean) * (m - mean) for n, m in zip(counts, means))
    return mean, square, count


def rows_of(refs):
    return [[ref[copy, i : i + 1, :] for i in range(3)] for ref in refs for copy in range(ref.shape[0])]


def merge_kernel(stats_ref, out_ref):
    for i, row in enumerate(merged(rows_of([stats_ref]))):
        for copy in range(out_ref.shape[0]):
            out_ref[copy, i : i + 1, :] = row


def merge(stats, copies):
    return pl.pallas_call(
        merge_kernel,
        out_shape=jax.ShapeDtypeStruct((copies,) + stats.shape[1:], jnp.float32),
        in_specs=[pl.BlockSpec(memory_space=VMEM)],
        out_specs=pl.BlockSpec(memory_space=VMEM),
        compiler_params=params(8),
        cost_estimate=cost(10**8),
        name="merge",
    )(stats)


def back_kernel(stat_count, place_ref, gain_ref, shift_ref, *refs):
    stat_refs, refs = refs[:stat_count], refs[stat_count:]
    *conv_refs, out_ref, rows_out, sems, weights = refs
    convs, weight_refs = conv_refs[:3], conv_refs[3:]
    row_count, wide = convs[0].shape
    if len(weight_refs) > 1:
        depth = weight_refs[0].shape[0]
        for i, weight_ref in enumerate(weight_refs[:2]):
            at = pl.multiple_of(lax.bitwise_xor(place_ref[0], i) * depth, depth)
            weights[pl.ds(at, depth), :] = weight_ref[...]
        at, unit = 0, 16
        for weight_ref in weight_refs[2:]:
            rows = weight_ref.shape[0]
            start = lax.bitwise_xor(place_ref[0], 2 + at // depth) * depth + at % depth
            weights[pl.ds(pl.multiple_of(start, unit), rows), :] = weight_ref[...]
            at += rows
    else:
        weights[...] = weight_refs[0][...]
    mean, square, count = merged(rows_of(stat_refs))
    scale = lax.rsqrt(square / count + 1e-05) * gain_ref[...]
    shift = shift_ref[...]
    pieces, rows, columns = rows_out.shape
    across = out_ref.shape[1] // columns
    copies = []
    for piece in range(pieces // across):
        here = slice(piece * rows, (piece + 1) * rows)
        parts = []
        for i, conv_ref in enumerate(convs):
            lanes = slice(i * wide, (i + 1) * wide)
            scaled = (conv_ref[here, :] - mean[:, lanes]) * scale[:, lanes] + shift[:, lanes]
            parts.append((scaled * jax.nn.sigmoid(scaled)).astype(jnp.bfloat16))
        activated = jnp.concatenate(parts, axis=1)
        position = place_ref[1] + piece * rows + lax.broadcasted_iota(jnp.int32, (rows, 1), 0)
        for j in range(across):
            lanes = slice(j * columns, (j + 1) * columns)
            result = jnp.dot(activated, weights[:, lanes], preferred_element_type=jnp.float32)
            slot = piece * across + j
            rows_out[slot] = jnp.where(position < place_ref[2], result, 0.0).astype(jnp.bfloat16)
            copy = pltpu.make_async_copy(rows_out.at[slot], out_ref.at[here, lanes], sems.at[slot])
            copy.start()
            copies.append(copy)
    for copy in copies:
        copy.wait()


def back(place, stats, gain, shift, convs, weights):
    row_count = convs[0].shape[0]
    channels, width = gain.shape[1], weights[0].shape[1]
    pieces, across = 4, 2
    return pl.pallas_call(
        functools.partial(back_kernel, len(stats)),
        out_shape=jax.ShapeDtypeStruct((row_count, width), jnp.bfloat16),
        in_specs=[pl.BlockSpec(memory_space=pltpu.SMEM)]
        + [pl.BlockSpec(memory_space=VMEM)] * (2 + len(stats) + len(convs) + len(weights)),
        out_specs=pl.BlockSpec(memory_space=pl.ANY),
        scratch_shapes=[
            VMEM((pieces, row_count * across // pieces, width // across), jnp.bfloat16),
            pltpu.SemaphoreType.DMA((pieces,)),
            VMEM((channels, width), jnp.bfloat16),
        ],
        compiler_params=params(10),
        cost_estimate=cost(10**9),
        name="back",
    )(place, gain, shift, *stats, *convs, *weights)


def everyones(copies, groups):
    return lax.all_to_all(copies, ("fsdp", "ctx"), 0, 0, axis_index_groups=groups, tiled=True)


def tie(*values):
    return lax.optimization_barrier(values)


def body(frames, lengths, ln_gain, w_in, dw_kernel, bn_gain, bn_shift, w_out):
    _, row_count, model_width = frames.shape
    channels = dw_kernel.shape[1]
    wide = channels // 3
    ctx, fsdp = lax.axis_index("ctx"), lax.axis_index("fsdp")
    ctx_count, fsdp_count = lax.axis_size("ctx"), lax.axis_size("fsdp")
    direct = fsdp_count == 4 and ctx_count == 8
    rows = frames[0]
    gain = ln_gain[None]
    parity, pair = lax.rem(ctx, 2), lax.rem(ctx // 2, 2)
    place = jnp.stack([fsdp, ctx * row_count, lengths[0], parity, pair]).astype(jnp.int32)
    ends = ctx_count - 1
    down, up = [(i, i + 1) for i in range(ends)], [(i + 1, i) for i in range(ends)]
    both = ("fsdp", "ctx")
    member = lambda f, p: f * ctx_count + p

    def front(block, weights, *extra):
        return front_block(block, wide, place, normed, weights, dw_kernel, *extra)

    if direct:
        two, zero, one = cut(place, w_in, wide)
        two, zero, one = (swap(part, "fsdp", 2) for part in (two, zero, one))
        across = swap(w_in, "fsdp", 1)
        inner, outer = edge_rows(place, rows)
        part_rows = w_out.shape[0] // 12
        normed, *pieces = normalize_rows(rows, gain, w_out, [4 * part_rows, 8 * part_rows])
        inner = swap(inner, "ctx", 1)
        pairs = [(i, i + 1) for i in range(1, ends, 2)]
        outer = lax.ppermute(outer, "ctx", pairs + [(j, i) for i, j in pairs])
        normed, inner, outer, two, zero = tie(normed, inner, outer, two, zero)
        two, zero = [two, swap(two, "ctx", 1)], [zero, swap(zero, "ctx", 2)]
        normed, *partials = near_product(place, normed, inner, outer, gain, w_in, across)
        partials[2], two[0], zero[0] = tie(partials[2], two[0], zero[0])
        two.append(swap(two[0], "fsdp", 1))
        zero.append(swap(zero[0], "fsdp", 1))
        partials[2], *parts = tie(partials[2], *two, *zero, w_out)
        two, zero, w_out = parts[:3], parts[3:6], parts[6]
        two.append(swap(two[1], "fsdp", 1))
        zero.append(swap(zero[1], "fsdp", 1))
        partials[2], one = tie(partials[2], one)
        beyond_one = swap(one, "fsdp", 1)
        conv_two, stat_two = front(2, [partials[2], *two])
        conv_two, partials[0] = tie(conv_two, partials[0])
        pieces = [swap(piece, "fsdp", 2) for piece in pieces]
        conv_zero, stat_zero = front(0, [partials[0], *zero])
        conv_zero, partials[1] = tie(conv_zero, partials[1])
        conv_one, stats = front(1, [partials[1], one, beyond_one], (stat_two, stat_zero), 1)
        across_out = swap(w_out, "fsdp", 1)
        stats, pieces[0] = tie(stats, pieces[0])
        beyond = [swap(pieces[0], "fsdp", 1)]
        convs = [conv_zero, conv_one, conv_two]

        def others(flips):
            return [
                lax.ppermute(
                    stats,
                    both,
                    [(member(f, p), member(f ^ df, p ^ dp)) for f in range(4) for p in range(8)],
                )
                for df, dp in flips
            ]

        def union(parts):
            return jnp.stack(merged([[part[:, i] for i in range(3)] for part in parts]), 1)

        stats = union([stats] + others([(1, 0)]))
        stats = union([stats] + others([(0, 2)]))
        stats = union([stats] + others([(0, 4)]))
        stats = [stats] + others([(0, 1), (2, 0), (2, 1)])
        *stats, pieces[1] = tie(*stats, pieces[1])
        beyond.append(swap(pieces[1], "fsdp", 1))
        out_weights = [w_out, across_out, *pieces, *beyond]
    else:
        full_in = lax.all_gather(w_in, "fsdp", axis=0, tiled=True)
        out_weights = [lax.all_gather(w_out, "fsdp", axis=0, tiled=True)]
        before = lax.ppermute(rows[-HALO:], "ctx", down)
        after = lax.ppermute(rows[:HALO], "ctx", up)
        inner = jnp.where(parity == 0, after, before)
        outer = jnp.where(parity == 0, before, after)
        (normed,) = normalize_rows(rows, gain, w_out, ())
        (normed,) = near_product(place, normed, inner, outer, gain)
        near_by = 2 if ctx_count % 2 == 0 else 1
        groups = [
            [member(f, p + i) for f in range(fsdp_count) for i in range(near_by)]
            for p in range(0, ctx_count, near_by)
        ]
        convs, stats = [None] * 3, []
        for block in ORDER:
            extra = (stats, len(groups[0])) if block == ORDER[-1] else ()
            convs[block], stat = front(block, [full_in], *extra)
            stats.append(stat)
        stats = merge(everyones(stats[2], groups), len(groups))
        groups = [
            [member(f, p + i) for p in range(0, ctx_count, near_by)]
            for f in range(fsdp_count)
            for i in range(near_by)
        ]
        stats = [everyones(stats, groups)]
    result = back(place, stats, bn_gain[None], bn_shift[None], convs, out_weights)
    return result[None]


def solution(mesh):
    return jax.shard_map(
        body,
        mesh=mesh,
        in_specs=(
            P("fsdp", "ctx", None),
            P("fsdp"),
            P(),
            P("fsdp", None),
            P(),
            P(),
            P(),
            P("fsdp", None),
        ),
        out_specs=P("fsdp", "ctx", None),
        check_vma=False,
    )
```

```python
import functools

import jax
import jax.numpy as jnp
from jax import lax
from jax.experimental import pallas as pl
from jax.experimental.pallas import tpu as pltpu
from jax.sharding import PartitionSpec as P

HALO = 16
LANES = 128
MIB = 1024 * 1024
VMEM = pltpu.VMEM
ORDER = (2, 0, 1)
SHARED = {2: 3, 0: 4}


def cost(flops):
    return pl.CostEstimate(flops=flops, bytes_accessed=0, transcendentals=0)


def params(mib):
    return pltpu.CompilerParams(vmem_limit_bytes=mib * MIB)


def swap(value, axis, bit):
    return lax.ppermute(value, axis, [(i, i ^ bit) for i in range(lax.axis_size(axis))])


def cut_kernel(pairs_ref, shard_ref, two_ref, zero_ref, one_ref):
    wide = two_ref.shape[1]
    channels = shard_ref.shape[1] // 2
    for block, ref in ((2, two_ref), (0, zero_ref)):
        at = pl.multiple_of(pairs_ref[SHARED[block] - 3] * channels + block * wide, wide)
        ref[...] = shard_ref[:, pl.ds(at, wide)]
    for i in range(2):
        at = i * channels + wide
        one_ref[:, i * wide : (i + 1) * wide] = shard_ref[:, at : at + wide]


def cut(place, shard, wide):
    depth = shard.shape[0]
    shapes = [(depth, wide), (depth, wide), (depth, 2 * wide)]
    return pl.pallas_call(
        cut_kernel,
        out_shape=[jax.ShapeDtypeStruct(shape, jnp.bfloat16) for shape in shapes],
        in_specs=[pl.BlockSpec(memory_space=pltpu.SMEM), pl.BlockSpec(memory_space=VMEM)],
        out_specs=[pl.BlockSpec(memory_space=VMEM)] * 3,
        compiler_params=params(4),
        cost_estimate=cost(10**8),
        name="cut",
    )(place, shard)


def normalize(values, gain):
    values = values.astype(jnp.float32)
    centre = jnp.mean(values, axis=-1, keepdims=True)
    deviate = values - centre
    spread = jnp.mean(deviate * deviate, axis=-1, keepdims=True)
    return (deviate * lax.rsqrt(spread + 1e-05) * gain).astype(jnp.bfloat16)


def edge_kernel(pairs_ref, rows_ref, inner_ref, outer_ref):
    odd = pairs_ref[0]
    last = rows_ref.shape[0] - HALO
    inner_ref[...] = rows_ref[pl.ds(pl.multiple_of((1 - odd) * last, HALO), HALO), :]
    outer_ref[...] = rows_ref[pl.ds(pl.multiple_of(odd * last, HALO), HALO), :]


def edge_rows(place, rows):
    shape = jax.ShapeDtypeStruct((HALO, rows.shape[1]), rows.dtype)
    return pl.pallas_call(
        edge_kernel,
        out_shape=[shape, shape],
        in_specs=[pl.BlockSpec(memory_space=pltpu.SMEM), pl.BlockSpec(memory_space=VMEM)],
        out_specs=[pl.BlockSpec(memory_space=VMEM)] * 2,
        compiler_params=params(2),
        cost_estimate=cost(10**8),
        name="edges",
    )(place, rows)


def norm_kernel(rows_ref, gain_ref, shard_ref, out_ref, *piece_refs):
    step = 64

    @pl.loop(0, rows_ref.shape[0] // step)
    def _(i):
        here = pl.ds(pl.multiple_of(i * step, step), step)
        out_ref[here, :] = normalize(rows_ref[here, :], gain_ref[...])

    at = 0
    for ref in piece_refs:
        ref[...] = shard_ref[at : at + ref.shape[0], :]
        at += ref.shape[0]


def normalize_rows(rows, gain, shard, pieces):
    row_count, width = rows.shape
    shapes = [(row_count, width)] + [(piece, width) for piece in pieces]
    return pl.pallas_call(
        norm_kernel,
        out_shape=[jax.ShapeDtypeStruct(shape, jnp.bfloat16) for shape in shapes],
        in_specs=[pl.BlockSpec(memory_space=VMEM)] * 3,
        out_specs=[pl.BlockSpec(memory_space=VMEM)] * len(shapes),
        compiler_params=params(4),
        cost_estimate=cost(10**8),
        name="layer_norm",
    )(rows, gain, shard)


def near_kernel(place_ref, rows_ref, inner_ref, outer_ref, gain_ref, *refs):
    row_count = rows_ref.shape[0]
    gain = gain_ref[...]
    *weight_refs, ext_ref = refs[:3] if len(refs) > 1 else refs
    odd = place_ref[3]
    at = pl.multiple_of((1 - odd) * (HALO + row_count), HALO)
    ext_ref[pl.ds(at, HALO), :] = normalize(inner_ref[...], gain)
    at = pl.multiple_of(odd * (HALO + row_count), HALO)
    ext_ref[pl.ds(at, HALO), :] = normalize(outer_ref[...], gain)
    ext_ref[HALO : HALO + row_count, :] = rows_ref[...]
    if not weight_refs:
        return
    *out_refs, weights = refs[3:]
    own = place_ref[0]
    depth, width = weight_refs[0].shape
    for i, weight_ref in enumerate(weight_refs):
        at = pl.multiple_of(lax.bitwise_xor(own % 2, i) * depth, depth)
        weights[pl.ds(at, depth), :] = weight_ref[...]
    near = pl.ds(pl.multiple_of(own // 2 * (2 * depth), 2 * depth), 2 * depth)
    wide = out_refs[0].shape[1] // 2
    channels = width // 2
    for block, out_ref in enumerate(out_refs):
        for i in range(2):
            columns = slice(i * channels + block * wide, i * channels + (block + 1) * wide)
            out_ref[:, i * wide : (i + 1) * wide] = jnp.dot(
                ext_ref[:, near], weights[:, columns], preferred_element_type=jnp.float32
            )


def near_product(place, rows, inner, outer, gain, *shards):
    row_count, width = rows.shape
    ext_rows = row_count + 2 * HALO
    shapes = [jax.ShapeDtypeStruct((ext_rows, width), jnp.bfloat16)]
    scratch = []
    if shards:
        shapes += [jax.ShapeDtypeStruct((ext_rows, width // 3), jnp.float32)] * 3
        scratch.append(VMEM((2 * shards[0].shape[0], width), jnp.bfloat16))
    return pl.pallas_call(
        near_kernel,
        out_shape=shapes,
        in_specs=[pl.BlockSpec(memory_space=pltpu.SMEM)]
        + [pl.BlockSpec(memory_space=VMEM)] * (4 + len(shards)),
        out_specs=[pl.BlockSpec(memory_space=VMEM)] * len(shapes),
        scratch_shapes=scratch,
        compiler_params=params(8),
        cost_estimate=cost(10**8),
        name="near",
    )(place, rows, inner, outer, gain, *shards)


def front_kernel(block, earlier, place_ref, normed_ref, *refs):
    refs, earlier_refs = refs[earlier:], refs[:earlier]
    *weight_refs, taps_ref, conv_ref, stats_ref, weights, gated = refs
    ext_rows = normed_ref.shape[0]
    row_count, wide = conv_ref.shape
    taps, channels = taps_ref.shape
    if len(weight_refs) > 1:
        near_ref, *far_refs = weight_refs
        own = place_ref[0]
        depth = far_refs[0].shape[0]
        halves = len(far_refs) // 2
        for i in range(2):
            at = pl.multiple_of(lax.bitwise_xor(own % 2, i) * depth, depth)
            if halves == 1:
                weights[pl.ds(at, depth), :] = far_refs[i][...]
                continue
            for j in range(2):
                column = pl.multiple_of(lax.bitwise_xor(place_ref[SHARED[block]], j) * wide, wide)
                weights[pl.ds(at, depth), pl.ds(column, wide)] = far_refs[2 * i + j][...]
        far = pl.ds(pl.multiple_of((1 - own // 2) * (2 * depth), 2 * depth), 2 * depth)
        normed = normed_ref[:, far]
        value = near_ref[:, 0:wide] + jnp.dot(normed, weights[:, 0:wide], preferred_element_type=jnp.float32)
        gate = near_ref[:, wide:] + jnp.dot(normed, weights[:, wide:], preferred_element_type=jnp.float32)
    else:
        columns = slice(block * wide, (block + 1) * wide)
        value = jnp.dot(normed_ref[...], weight_refs[0][:, columns], preferred_element_type=jnp.float32)
        columns = slice(channels + block * wide, channels + (block + 1) * wide)
        gate = jnp.dot(normed_ref[...], weight_refs[0][:, columns], preferred_element_type=jnp.float32)
    start, length = place_ref[1], place_ref[2]
    position = start - HALO + lax.broadcasted_iota(jnp.int32, (ext_rows, 1), 0)
    valid = (position >= 0) & (position < length)
    kept = jnp.where(valid, value * jax.nn.sigmoid(gate), 0.0)
    kept = kept.astype(jnp.bfloat16).astype(jnp.float32)
    first = HALO - (taps - 1) // 2
    step = 64
    for unit in range(wide // LANES):
        lanes = slice(unit * LANES, (unit + 1) * LANES)
        tap_lanes = slice(block * wide + unit * LANES, block * wide + (unit + 1) * LANES)
        column = kept[:, lanes]
        gated[0] = column
        for phase in range(1, 8):
            gated[phase] = pltpu.roll(column, ext_rows - phase, 0)
        for at in range(0, row_count, step):
            acc = None
            for tap in range(taps):
                base = at + (first + tap) // 8 * 8
                term = gated[(first + tap) % 8, base : base + step, :] * taps_ref[tap : tap + 1, tap_lanes]
                acc = term if acc is None else acc + term
            conv_ref[at : at + step, lanes] = acc
    here = start + lax.broadcasted_iota(jnp.int32, (row_count, 1), 0) < length
    count = jnp.clip(length - start, 0, row_count).astype(jnp.float32)
    conv = conv_ref[...]
    mean = jnp.sum(jnp.where(here, conv, 0.0), axis=0, keepdims=True) / jnp.maximum(count, 1.0)
    deviate = jnp.where(here, conv - mean, 0.0)
    square = jnp.sum(deviate * deviate, axis=0, keepdims=True)
    stats = [mean, square, jnp.full((1, wide), count)]
    if not earlier_refs:
        for i, row in enumerate(stats):
            stats_ref[i : i + 1, :] = row
        return
    for i, row in enumerate(stats):
        for copy in range(stats_ref.shape[0]):
            stats_ref[copy, i : i + 1, block * wide : (block + 1) * wide] = row
            for other, ref in zip([j for j in ORDER if j != block], earlier_refs):
                stats_ref[copy, i : i + 1, other * wide : (other + 1) * wide] = ref[i : i + 1, :]


def front_block(block, wide, place, normed, weights, dw_kernel, earlier=(), copies=1):
    ext_rows, width = normed.shape
    row_count = ext_rows - 2 * HALO
    depth = 2 * weights[1].shape[0] if len(weights) > 1 else 16
    stats_shape = (copies, 3, dw_kernel.shape[1]) if earlier else (3, wide)
    return pl.pallas_call(
        functools.partial(front_kernel, block, len(earlier)),
        out_shape=(
            jax.ShapeDtypeStruct((row_count, wide), jnp.float32),
            jax.ShapeDtypeStruct(stats_shape, jnp.float32),
        ),
        in_specs=[pl.BlockSpec(memory_space=pltpu.SMEM)]
        + [pl.BlockSpec(memory_space=VMEM)] * (2 + len(weights) + len(earlier)),
        out_specs=[pl.BlockSpec(memory_space=VMEM)] * 2,
        scratch_shapes=[
            VMEM((depth, 2 * wide), jnp.bfloat16),
            VMEM((8, ext_rows, LANES), jnp.float32),
        ],
        compiler_params=params(10),
        cost_estimate=cost(4 * 10**9 if block == ORDER[1] else 10**8),
        name="front",
    )(place, normed, *earlier, *weights, dw_kernel)


def merged(parts):
    means, squares, counts = zip(*parts)
    count = sum(counts)
    mean = sum(n * m for n, m in zip(counts, means)) / jnp.maximum(count, 1.0)
    square = sum(squares) + sum(n * (m - mean) * (m - mean) for n, m in zip(counts, means))
    return mean, square, count


def rows_of(refs):
    return [[ref[copy, i : i + 1, :] for i in range(3)] for ref in refs for copy in range(ref.shape[0])]


def merge_kernel(stats_ref, out_ref):
    for i, row in enumerate(merged(rows_of([stats_ref]))):
        for copy in range(out_ref.shape[0]):
            out_ref[copy, i : i + 1, :] = row


def merge(stats, copies):
    return pl.pallas_call(
        merge_kernel,
        out_shape=jax.ShapeDtypeStruct((copies,) + stats.shape[1:], jnp.float32),
        in_specs=[pl.BlockSpec(memory_space=VMEM)],
        out_specs=pl.BlockSpec(memory_space=VMEM),
        compiler_params=params(8),
        cost_estimate=cost(10**8),
        name="merge",
    )(stats)


def back_kernel(stat_count, place_ref, gain_ref, shift_ref, *refs):
    stat_refs, refs = refs[:stat_count], refs[stat_count:]
    *conv_refs, out_ref, rows_out, sems, weights = refs
    convs, weight_refs = conv_refs[:3], conv_refs[3:]
    row_count, wide = convs[0].shape
    if len(weight_refs) > 1:
        depth = weight_refs[0].shape[0]
        for i, weight_ref in enumerate(weight_refs[:2]):
            at = pl.multiple_of(lax.bitwise_xor(place_ref[0], i) * depth, depth)
            weights[pl.ds(at, depth), :] = weight_ref[...]
        at, unit = 0, 16
        for weight_ref in weight_refs[2:]:
            rows = weight_ref.shape[0]
            start = lax.bitwise_xor(place_ref[0], 2 + at // depth) * depth + at % depth
            weights[pl.ds(pl.multiple_of(start, unit), rows), :] = weight_ref[...]
            at += rows
    else:
        weights[...] = weight_refs[0][...]
    mean, square, count = merged(rows_of(stat_refs))
    scale = lax.rsqrt(square / count + 1e-05) * gain_ref[...]
    shift = shift_ref[...]
    pieces, rows, columns = rows_out.shape
    across = out_ref.shape[1] // columns
    copies = []
    for piece in range(pieces // across):
        here = slice(piece * rows, (piece + 1) * rows)
        parts = []
        for i, conv_ref in enumerate(convs):
            lanes = slice(i * wide, (i + 1) * wide)
            scaled = (conv_ref[here, :] - mean[:, lanes]) * scale[:, lanes] + shift[:, lanes]
            parts.append((scaled * jax.nn.sigmoid(scaled)).astype(jnp.bfloat16))
        activated = jnp.concatenate(parts, axis=1)
        position = place_ref[1] + piece * rows + lax.broadcasted_iota(jnp.int32, (rows, 1), 0)
        for j in range(across):
            lanes = slice(j * columns, (j + 1) * columns)
            result = jnp.dot(activated, weights[:, lanes], preferred_element_type=jnp.float32)
            slot = piece * across + j
            rows_out[slot] = jnp.where(position < place_ref[2], result, 0.0).astype(jnp.bfloat16)
            copy = pltpu.make_async_copy(rows_out.at[slot], out_ref.at[here, lanes], sems.at[slot])
            copy.start()
            copies.append(copy)
    for copy in copies:
        copy.wait()


def back(place, stats, gain, shift, convs, weights):
    row_count = convs[0].shape[0]
    channels, width = gain.shape[1], weights[0].shape[1]
    pieces, across = 4, 2
    return pl.pallas_call(
        functools.partial(back_kernel, len(stats)),
        out_shape=jax.ShapeDtypeStruct((row_count, width), jnp.bfloat16),
        in_specs=[pl.BlockSpec(memory_space=pltpu.SMEM)]
        + [pl.BlockSpec(memory_space=VMEM)] * (2 + len(stats) + len(convs) + len(weights)),
        out_specs=pl.BlockSpec(memory_space=pl.ANY),
        scratch_shapes=[
            VMEM((pieces, row_count * across // pieces, width // across), jnp.bfloat16),
            pltpu.SemaphoreType.DMA((pieces,)),
            VMEM((channels, width), jnp.bfloat16),
        ],
        compiler_params=params(10),
        cost_estimate=cost(10**9),
        name="back",
    )(place, gain, shift, *stats, *convs, *weights)


def everyones(copies, groups):
    return lax.all_to_all(copies, ("fsdp", "ctx"), 0, 0, axis_index_groups=groups, tiled=True)


def tie(*values):
    return lax.optimization_barrier(values)


def body(frames, lengths, ln_gain, w_in, dw_kernel, bn_gain, bn_shift, w_out):
    _, row_count, model_width = frames.shape
    channels = dw_kernel.shape[1]
    wide = channels // 3
    ctx, fsdp = lax.axis_index("ctx"), lax.axis_index("fsdp")
    ctx_count, fsdp_count = lax.axis_size("ctx"), lax.axis_size("fsdp")
    direct = fsdp_count == 4 and ctx_count == 8
    rows = frames[0]
    gain = ln_gain[None]
    parity, pair = lax.rem(ctx, 2), lax.rem(ctx // 2, 2)
    place = jnp.stack([fsdp, ctx * row_count, lengths[0], parity, pair]).astype(jnp.int32)
    ends = ctx_count - 1
    down, up = [(i, i + 1) for i in range(ends)], [(i + 1, i) for i in range(ends)]
    both = ("fsdp", "ctx")
    member = lambda f, p: f * ctx_count + p

    def front(block, weights, *extra):
        return front_block(block, wide, place, normed, weights, dw_kernel, *extra)

    if direct:
        positions = jnp.stack([parity, pair]).astype(jnp.int32)
        two, zero, one = cut(positions, w_in, wide)
        one, later_in = tie(one, w_in)
        two, zero, one = (swap(part, "fsdp", 2) for part in (two, zero, one))
        across = swap(later_in, "fsdp", 1)
        inner, outer = edge_rows(positions, rows)
        part_rows = w_out.shape[0] // 12
        normed, *pieces = normalize_rows(rows, gain, w_out, [4 * part_rows, 8 * part_rows])
        inner = swap(inner, "ctx", 1)
        pairs = [(i, i + 1) for i in range(1, ends, 2)]
        outer = lax.ppermute(outer, "ctx", pairs + [(j, i) for i, j in pairs])
        normed, inner, outer, two, zero = tie(normed, inner, outer, two, zero)
        two, zero = [two, swap(two, "ctx", 1)], [zero, swap(zero, "ctx", 2)]
        normed, *partials = near_product(place, normed, inner, outer, gain, w_in, across)
        partials[2], two[0], zero[0] = tie(partials[2], two[0], zero[0])
        two.append(swap(two[0], "fsdp", 1))
        zero.append(swap(zero[0], "fsdp", 1))
        partials[2], *parts = tie(partials[2], *two, *zero, w_out)
        two, zero, w_out = parts[:3], parts[3:6], parts[6]
        two.append(swap(two[1], "fsdp", 1))
        zero.append(swap(zero[1], "fsdp", 1))
        partials[2], one = tie(partials[2], one)
        beyond_one = swap(one, "fsdp", 1)
        conv_two, stat_two = front(2, [partials[2], *two])
        conv_two, partials[0] = tie(conv_two, partials[0])
        pieces = [swap(piece, "fsdp", 2) for piece in pieces]
        conv_zero, stat_zero = front(0, [partials[0], *zero])
        conv_zero, partials[1] = tie(conv_zero, partials[1])
        conv_one, stats = front(1, [partials[1], one, beyond_one], (stat_two, stat_zero), 1)
        across_out = swap(w_out, "fsdp", 1)
        stats, pieces[0] = tie(stats, pieces[0])
        beyond = [swap(pieces[0], "fsdp", 1)]
        convs = [conv_zero, conv_one, conv_two]

        def others(flips):
            return [
                lax.ppermute(
                    stats,
                    both,
                    [(member(f, p), member(f ^ df, p ^ dp)) for f in range(4) for p in range(8)],
                )
                for df, dp in flips
            ]

        def union(parts):
            return jnp.stack(merged([[part[:, i] for i in range(3)] for part in parts]), 1)

        stats = union([stats] + others([(1, 0)]))
        stats, beyond[0] = tie(stats, beyond[0])
        stats = union([stats] + others([(0, 2)]))
        stats = union([stats] + others([(0, 4)]))
        stats = [stats] + others([(0, 1), (2, 0), (2, 1)])
        *stats, pieces[1] = tie(*stats, pieces[1])
        beyond.append(swap(pieces[1], "fsdp", 1))
        out_weights = [w_out, across_out, *pieces, *beyond]
    else:
        full_in = lax.all_gather(w_in, "fsdp", axis=0, tiled=True)
        out_weights = [lax.all_gather(w_out, "fsdp", axis=0, tiled=True)]
        before = lax.ppermute(rows[-HALO:], "ctx", down)
        after = lax.ppermute(rows[:HALO], "ctx", up)
        inner = jnp.where(parity == 0, after, before)
        outer = jnp.where(parity == 0, before, after)
        (normed,) = normalize_rows(rows, gain, w_out, ())
        (normed,) = near_product(place, normed, inner, outer, gain)
        near_by = 2 if ctx_count % 2 == 0 else 1
        groups = [
            [member(f, p + i) for f in range(fsdp_count) for i in range(near_by)]
            for p in range(0, ctx_count, near_by)
        ]
        convs, stats = [None] * 3, []
        for block in ORDER:
            extra = (stats, len(groups[0])) if block == ORDER[-1] else ()
            convs[block], stat = front(block, [full_in], *extra)
            stats.append(stat)
        stats = merge(everyones(stats[2], groups), len(groups))
        groups = [
            [member(f, p + i) for p in range(0, ctx_count, near_by)]
            for f in range(fsdp_count)
            for i in range(near_by)
        ]
        stats = [everyones(stats, groups)]
    result = back(place, stats, bn_gain[None], bn_shift[None], convs, out_weights)
    return result[None]


def solution(mesh):
    return jax.shard_map(
        body,
        mesh=mesh,
        in_specs=(
            P("fsdp", "ctx", None),
            P("fsdp"),
            P(),
            P("fsdp", None),
            P(),
            P(),
            P(),
            P("fsdp", None),
        ),
        out_specs=P("fsdp", "ctx", None),
        check_vma=False,
    )
```

```python
import functools

import jax
import jax.numpy as jnp
from jax import lax
from jax.experimental import pallas as pl
from jax.experimental.pallas import tpu as pltpu
from jax.sharding import PartitionSpec as P

HALO = 16
LANES = 128
MIB = 1024 * 1024
VMEM = pltpu.VMEM
ORDER = (2, 0, 1)
SHARED = {2: 3, 0: 4}


def cost(flops):
    return pl.CostEstimate(flops=flops, bytes_accessed=0, transcendentals=0)


def params(mib):
    return pltpu.CompilerParams(vmem_limit_bytes=mib * MIB)


def swap(value, axis, bit):
    return lax.ppermute(value, axis, [(i, i ^ bit) for i in range(lax.axis_size(axis))])


def cut_kernel(place_ref, shard_ref, two_ref, zero_ref, one_ref):
    wide = two_ref.shape[1]
    channels = shard_ref.shape[1] // 2
    for block, ref in ((2, two_ref), (0, zero_ref)):
        at = pl.multiple_of(place_ref[SHARED[block]] * channels + block * wide, wide)
        ref[...] = shard_ref[:, pl.ds(at, wide)]
    for i in range(2):
        at = i * channels + wide
        one_ref[:, i * wide : (i + 1) * wide] = shard_ref[:, at : at + wide]


def cut(place, shard, wide):
    depth = shard.shape[0]
    shapes = [(depth, wide), (depth, wide), (depth, 2 * wide)]
    return pl.pallas_call(
        cut_kernel,
        out_shape=[jax.ShapeDtypeStruct(shape, jnp.bfloat16) for shape in shapes],
        in_specs=[pl.BlockSpec(memory_space=pltpu.SMEM), pl.BlockSpec(memory_space=VMEM)],
        out_specs=[pl.BlockSpec(memory_space=VMEM)] * 3,
        compiler_params=params(4),
        cost_estimate=cost(10**8),
        name="cut",
    )(place, shard)


def normalize(values, gain):
    values = values.astype(jnp.float32)
    centre = jnp.mean(values, axis=-1, keepdims=True)
    deviate = values - centre
    spread = jnp.mean(deviate * deviate, axis=-1, keepdims=True)
    return (deviate * lax.rsqrt(spread + 1e-05) * gain).astype(jnp.bfloat16)


def edge_kernel(place_ref, rows_ref, inner_ref, outer_ref):
    odd = place_ref[3]
    last = rows_ref.shape[0] - HALO
    inner_ref[...] = rows_ref[pl.ds(pl.multiple_of((1 - odd) * last, HALO), HALO), :]
    outer_ref[...] = rows_ref[pl.ds(pl.multiple_of(odd * last, HALO), HALO), :]


def edge_rows(place, rows):
    shape = jax.ShapeDtypeStruct((HALO, rows.shape[1]), rows.dtype)
    return pl.pallas_call(
        edge_kernel,
        out_shape=[shape, shape],
        in_specs=[pl.BlockSpec(memory_space=pltpu.SMEM), pl.BlockSpec(memory_space=VMEM)],
        out_specs=[pl.BlockSpec(memory_space=VMEM)] * 2,
        compiler_params=params(2),
        cost_estimate=cost(10**8),
        name="edges",
    )(place, rows)


def norm_kernel(rows_ref, gain_ref, shard_ref, out_ref, *piece_refs):
    step = 64

    @pl.loop(0, rows_ref.shape[0] // step)
    def _(i):
        here = pl.ds(pl.multiple_of(i * step, step), step)
        out_ref[here, :] = normalize(rows_ref[here, :], gain_ref[...])

    at = 0
    for ref in piece_refs:
        ref[...] = shard_ref[at : at + ref.shape[0], :]
        at += ref.shape[0]


def normalize_rows(rows, gain, shard, pieces):
    row_count, width = rows.shape
    shapes = [(row_count, width)] + [(piece, width) for piece in pieces]
    return pl.pallas_call(
        norm_kernel,
        out_shape=[jax.ShapeDtypeStruct(shape, jnp.bfloat16) for shape in shapes],
        in_specs=[pl.BlockSpec(memory_space=VMEM)] * 3,
        out_specs=[pl.BlockSpec(memory_space=VMEM)] * len(shapes),
        compiler_params=params(4),
        cost_estimate=cost(10**8),
        name="layer_norm",
    )(rows, gain, shard)


def near_kernel(place_ref, rows_ref, inner_ref, outer_ref, gain_ref, *refs):
    row_count = rows_ref.shape[0]
    gain = gain_ref[...]
    *weight_refs, ext_ref = refs[:3] if len(refs) > 1 else refs
    odd = place_ref[3]
    at = pl.multiple_of((1 - odd) * (HALO + row_count), HALO)
    ext_ref[pl.ds(at, HALO), :] = normalize(inner_ref[...], gain)
    at = pl.multiple_of(odd * (HALO + row_count), HALO)
    ext_ref[pl.ds(at, HALO), :] = normalize(outer_ref[...], gain)
    ext_ref[HALO : HALO + row_count, :] = rows_ref[...]
    if not weight_refs:
        return
    *out_refs, weights = refs[3:]
    own = place_ref[0]
    depth, width = weight_refs[0].shape
    for i, weight_ref in enumerate(weight_refs):
        at = pl.multiple_of(lax.bitwise_xor(own % 2, i) * depth, depth)
        weights[pl.ds(at, depth), :] = weight_ref[...]
    near = pl.ds(pl.multiple_of(own // 2 * (2 * depth), 2 * depth), 2 * depth)
    wide = out_refs[0].shape[1] // 2
    channels = width // 2
    for block, out_ref in enumerate(out_refs):
        for i in range(2):
            columns = slice(i * channels + block * wide, i * channels + (block + 1) * wide)
            out_ref[:, i * wide : (i + 1) * wide] = jnp.dot(
                ext_ref[:, near], weights[:, columns], preferred_element_type=jnp.float32
            )


def near_product(place, rows, inner, outer, gain, *shards):
    row_count, width = rows.shape
    ext_rows = row_count + 2 * HALO
    shapes = [jax.ShapeDtypeStruct((ext_rows, width), jnp.bfloat16)]
    scratch = []
    if shards:
        shapes += [jax.ShapeDtypeStruct((ext_rows, width // 3), jnp.float32)] * 3
        scratch.append(VMEM((2 * shards[0].shape[0], width), jnp.bfloat16))
    return pl.pallas_call(
        near_kernel,
        out_shape=shapes,
        in_specs=[pl.BlockSpec(memory_space=pltpu.SMEM)]
        + [pl.BlockSpec(memory_space=VMEM)] * (4 + len(shards)),
        out_specs=[pl.BlockSpec(memory_space=VMEM)] * len(shapes),
        scratch_shapes=scratch,
        compiler_params=params(8),
        cost_estimate=cost(10**8),
        name="near",
    )(place, rows, inner, outer, gain, *shards)


def front_kernel(block, earlier, place_ref, normed_ref, *refs):
    refs, earlier_refs = refs[earlier:], refs[:earlier]
    *weight_refs, taps_ref, conv_ref, stats_ref, weights, gated = refs
    ext_rows = normed_ref.shape[0]
    row_count, wide = conv_ref.shape
    taps, channels = taps_ref.shape
    if len(weight_refs) > 1:
        near_ref, *far_refs = weight_refs
        own = place_ref[0]
        depth = far_refs[0].shape[0]
        halves = len(far_refs) // 2
        for i in range(2):
            at = pl.multiple_of(lax.bitwise_xor(own % 2, i) * depth, depth)
            if halves == 1:
                weights[pl.ds(at, depth), :] = far_refs[i][...]
                continue
            for j in range(2):
                column = pl.multiple_of(lax.bitwise_xor(place_ref[SHARED[block]], j) * wide, wide)
                weights[pl.ds(at, depth), pl.ds(column, wide)] = far_refs[2 * i + j][...]
        far = pl.ds(pl.multiple_of((1 - own // 2) * (2 * depth), 2 * depth), 2 * depth)
        normed = normed_ref[:, far]
        value = near_ref[:, 0:wide] + jnp.dot(normed, weights[:, 0:wide], preferred_element_type=jnp.float32)
        gate = near_ref[:, wide:] + jnp.dot(normed, weights[:, wide:], preferred_element_type=jnp.float32)
    else:
        columns = slice(block * wide, (block + 1) * wide)
        value = jnp.dot(normed_ref[...], weight_refs[0][:, columns], preferred_element_type=jnp.float32)
        columns = slice(channels + block * wide, channels + (block + 1) * wide)
        gate = jnp.dot(normed_ref[...], weight_refs[0][:, columns], preferred_element_type=jnp.float32)
    start, length = place_ref[1], place_ref[2]
    position = start - HALO + lax.broadcasted_iota(jnp.int32, (ext_rows, 1), 0)
    valid = (position >= 0) & (position < length)
    kept = jnp.where(valid, value * jax.nn.sigmoid(gate), 0.0)
    kept = kept.astype(jnp.bfloat16).astype(jnp.float32)
    first = HALO - (taps - 1) // 2
    step = 64
    for unit in range(wide // LANES):
        lanes = slice(unit * LANES, (unit + 1) * LANES)
        tap_lanes = slice(block * wide + unit * LANES, block * wide + (unit + 1) * LANES)
        column = kept[:, lanes]
        gated[0] = column
        for phase in range(1, 8):
            gated[phase] = pltpu.roll(column, ext_rows - phase, 0)
        for at in range(0, row_count, step):
            acc = None
            for tap in range(taps):
                base = at + (first + tap) // 8 * 8
                term = gated[(first + tap) % 8, base : base + step, :] * taps_ref[tap : tap + 1, tap_lanes]
                acc = term if acc is None else acc + term
            conv_ref[at : at + step, lanes] = acc
    here = start + lax.broadcasted_iota(jnp.int32, (row_count, 1), 0) < length
    count = jnp.clip(length - start, 0, row_count).astype(jnp.float32)
    conv = conv_ref[...]
    mean = jnp.sum(jnp.where(here, conv, 0.0), axis=0, keepdims=True) / jnp.maximum(count, 1.0)
    deviate = jnp.where(here, conv - mean, 0.0)
    square = jnp.sum(deviate * deviate, axis=0, keepdims=True)
    stats = [mean, square, jnp.full((1, wide), count)]
    if not earlier_refs:
        for i, row in enumerate(stats):
            stats_ref[i : i + 1, :] = row
        return
    for i, row in enumerate(stats):
        for copy in range(stats_ref.shape[0]):
            stats_ref[copy, i : i + 1, block * wide : (block + 1) * wide] = row
            for other, ref in zip([j for j in ORDER if j != block], earlier_refs):
                stats_ref[copy, i : i + 1, other * wide : (other + 1) * wide] = ref[i : i + 1, :]


def front_block(block, wide, place, normed, weights, dw_kernel, earlier=(), copies=1):
    ext_rows, width = normed.shape
    row_count = ext_rows - 2 * HALO
    depth = 2 * weights[1].shape[0] if len(weights) > 1 else 16
    stats_shape = (copies, 3, dw_kernel.shape[1]) if earlier else (3, wide)
    return pl.pallas_call(
        functools.partial(front_kernel, block, len(earlier)),
        out_shape=(
            jax.ShapeDtypeStruct((row_count, wide), jnp.float32),
            jax.ShapeDtypeStruct(stats_shape, jnp.float32),
        ),
        in_specs=[pl.BlockSpec(memory_space=pltpu.SMEM)]
        + [pl.BlockSpec(memory_space=VMEM)] * (2 + len(weights) + len(earlier)),
        out_specs=[pl.BlockSpec(memory_space=VMEM)] * 2,
        scratch_shapes=[
            VMEM((depth, 2 * wide), jnp.bfloat16),
            VMEM((8, ext_rows, LANES), jnp.float32),
        ],
        compiler_params=params(10),
        cost_estimate=cost(4 * 10**9 if block == ORDER[1] else 10**8),
        name="front",
    )(place, normed, *earlier, *weights, dw_kernel)


def merged(parts):
    means, squares, counts = zip(*parts)
    count = sum(counts)
    mean = sum(n * m for n, m in zip(counts, means)) / jnp.maximum(count, 1.0)
    square = sum(squares) + sum(n * (m - mean) * (m - mean) for n, m in zip(counts, means))
    return mean, square, count


def rows_of(refs):
    return [[ref[copy, i : i + 1, :] for i in range(3)] for ref in refs for copy in range(ref.shape[0])]


def merge_kernel(stats_ref, out_ref):
    for i, row in enumerate(merged(rows_of([stats_ref]))):
        for copy in range(out_ref.shape[0]):
            out_ref[copy, i : i + 1, :] = row


def merge(stats, copies):
    return pl.pallas_call(
        merge_kernel,
        out_shape=jax.ShapeDtypeStruct((copies,) + stats.shape[1:], jnp.float32),
        in_specs=[pl.BlockSpec(memory_space=VMEM)],
        out_specs=pl.BlockSpec(memory_space=VMEM),
        compiler_params=params(8),
        cost_estimate=cost(10**8),
        name="merge",
    )(stats)


def back_kernel(stat_count, place_ref, gain_ref, shift_ref, *refs):
    stat_refs, refs = refs[:stat_count], refs[stat_count:]
    *conv_refs, out_ref, rows_out, sems, weights = refs
    convs, weight_refs = conv_refs[:3], conv_refs[3:]
    row_count, wide = convs[0].shape
    if len(weight_refs) > 1:
        depth = weight_refs[0].shape[0]
        for i, weight_ref in enumerate(weight_refs[:2]):
            at = pl.multiple_of(lax.bitwise_xor(place_ref[0], i) * depth, depth)
            weights[pl.ds(at, depth), :] = weight_ref[...]
        at, unit = 0, 16
        for weight_ref in weight_refs[2:]:
            rows = weight_ref.shape[0]
            start = lax.bitwise_xor(place_ref[0], 2 + at // depth) * depth + at % depth
            weights[pl.ds(pl.multiple_of(start, unit), rows), :] = weight_ref[...]
            at += rows
    else:
        weights[...] = weight_refs[0][...]
    mean, square, count = merged(rows_of(stat_refs))
    scale = lax.rsqrt(square / count + 1e-05) * gain_ref[...]
    shift = shift_ref[...]
    pieces, rows, columns = rows_out.shape
    across = out_ref.shape[1] // columns
    copies = []
    for piece in range(pieces // across):
        here = slice(piece * rows, (piece + 1) * rows)
        parts = []
        for i, conv_ref in enumerate(convs):
            lanes = slice(i * wide, (i + 1) * wide)
            scaled = (conv_ref[here, :] - mean[:, lanes]) * scale[:, lanes] + shift[:, lanes]
            parts.append((scaled * jax.nn.sigmoid(scaled)).astype(jnp.bfloat16))
        activated = jnp.concatenate(parts, axis=1)
        position = place_ref[1] + piece * rows + lax.broadcasted_iota(jnp.int32, (rows, 1), 0)
        for j in range(across):
            lanes = slice(j * columns, (j + 1) * columns)
            result = jnp.dot(activated, weights[:, lanes], preferred_element_type=jnp.float32)
            slot = piece * across + j
            rows_out[slot] = jnp.where(position < place_ref[2], result, 0.0).astype(jnp.bfloat16)
            copy = pltpu.make_async_copy(rows_out.at[slot], out_ref.at[here, lanes], sems.at[slot])
            copy.start()
            copies.append(copy)
    for copy in copies:
        copy.wait()


def back(place, stats, gain, shift, convs, weights):
    row_count = convs[0].shape[0]
    channels, width = gain.shape[1], weights[0].shape[1]
    pieces, across = 4, 2
    return pl.pallas_call(
        functools.partial(back_kernel, len(stats)),
        out_shape=jax.ShapeDtypeStruct((row_count, width), jnp.bfloat16),
        in_specs=[pl.BlockSpec(memory_space=pltpu.SMEM)]
        + [pl.BlockSpec(memory_space=VMEM)] * (2 + len(stats) + len(convs) + len(weights)),
        out_specs=pl.BlockSpec(memory_space=pl.ANY),
        scratch_shapes=[
            VMEM((pieces, row_count * across // pieces, width // across), jnp.bfloat16),
            pltpu.SemaphoreType.DMA((pieces,)),
            VMEM((channels, width), jnp.bfloat16),
        ],
        compiler_params=params(10),
        cost_estimate=cost(10**9),
        name="back",
    )(place, gain, shift, *stats, *convs, *weights)


def everyones(copies, groups):
    return lax.all_to_all(copies, ("fsdp", "ctx"), 0, 0, axis_index_groups=groups, tiled=True)


def tie(*values):
    return lax.optimization_barrier(values)


def body(frames, lengths, ln_gain, w_in, dw_kernel, bn_gain, bn_shift, w_out):
    _, row_count, model_width = frames.shape
    channels = dw_kernel.shape[1]
    wide = channels // 3
    ctx, fsdp = lax.axis_index("ctx"), lax.axis_index("fsdp")
    ctx_count, fsdp_count = lax.axis_size("ctx"), lax.axis_size("fsdp")
    direct = fsdp_count == 4 and ctx_count == 8
    rows = frames[0]
    gain = ln_gain[None]
    parity, pair = lax.rem(ctx, 2), lax.rem(ctx // 2, 2)
    place = jnp.stack([fsdp, ctx * row_count, lengths[0], parity, pair]).astype(jnp.int32)
    ends = ctx_count - 1
    down, up = [(i, i + 1) for i in range(ends)], [(i + 1, i) for i in range(ends)]
    both = ("fsdp", "ctx")
    member = lambda f, p: f * ctx_count + p

    def front(block, weights, *extra):
        return front_block(block, wide, place, normed, weights, dw_kernel, *extra)

    if direct:
        two, zero, one = cut(place, w_in, wide)
        two, zero, one = (swap(part, "fsdp", 2) for part in (two, zero, one))
        across = swap(w_in, "fsdp", 1)
        inner, outer = edge_rows(place, rows)
        normed, *pieces = normalize_rows(rows, gain, w_out, [w_out.shape[0]])
        inner = swap(inner, "ctx", 1)
        pairs = [(i, i + 1) for i in range(1, ends, 2)]
        outer = lax.ppermute(outer, "ctx", pairs + [(j, i) for i, j in pairs])
        normed, inner, outer, two, zero = tie(normed, inner, outer, two, zero)
        two, zero = [two, swap(two, "ctx", 1)], [zero, swap(zero, "ctx", 2)]
        normed, *partials = near_product(place, normed, inner, outer, gain, w_in, across)
        partials[2], two[0], zero[0] = tie(partials[2], two[0], zero[0])
        two.append(swap(two[0], "fsdp", 1))
        zero.append(swap(zero[0], "fsdp", 1))
        partials[2], *parts = tie(partials[2], *two, *zero, w_out)
        two, zero, w_out = parts[:3], parts[3:6], parts[6]
        two.append(swap(two[1], "fsdp", 1))
        zero.append(swap(zero[1], "fsdp", 1))
        partials[2], one = tie(partials[2], one)
        beyond_one = swap(one, "fsdp", 1)
        conv_two, stat_two = front(2, [partials[2], *two])
        conv_two, partials[0] = tie(conv_two, partials[0])
        pieces = [swap(piece, "fsdp", 2) for piece in pieces]
        conv_zero, stat_zero = front(0, [partials[0], *zero])
        conv_zero, partials[1] = tie(conv_zero, partials[1])
        conv_one, stats = front(1, [partials[1], one, beyond_one], (stat_two, stat_zero), 1)
        across_out = swap(w_out, "fsdp", 1)
        convs = [conv_zero, conv_one, conv_two]

        def others(flips):
            return [
                lax.ppermute(
                    stats,
                    both,
                    [(member(f, p), member(f ^ df, p ^ dp)) for f in range(4) for p in range(8)],
                )
                for df, dp in flips
            ]

        def union(parts):
            return jnp.stack(merged([[part[:, i] for i in range(3)] for part in parts]), 1)

        stats = union([stats] + others([(1, 0)]))
        stats = union([stats] + others([(0, 2)]))
        stats = union([stats] + others([(0, 4)]))
        stats = [stats] + others([(0, 1), (2, 0), (2, 1)])
        *stats, pieces[0] = tie(*stats, pieces[0])
        beyond = [swap(pieces[0], "fsdp", 1)]
        out_weights = [w_out, across_out, *pieces, *beyond]
    else:
        full_in = lax.all_gather(w_in, "fsdp", axis=0, tiled=True)
        out_weights = [lax.all_gather(w_out, "fsdp", axis=0, tiled=True)]
        before = lax.ppermute(rows[-HALO:], "ctx", down)
        after = lax.ppermute(rows[:HALO], "ctx", up)
        inner = jnp.where(parity == 0, after, before)
        outer = jnp.where(parity == 0, before, after)
        (normed,) = normalize_rows(rows, gain, w_out, ())
        (normed,) = near_product(place, normed, inner, outer, gain)
        near_by = 2 if ctx_count % 2 == 0 else 1
        groups = [
            [member(f, p + i) for f in range(fsdp_count) for i in range(near_by)]
            for p in range(0, ctx_count, near_by)
        ]
        convs, stats = [None] * 3, []
        for block in ORDER:
            extra = (stats, len(groups[0])) if block == ORDER[-1] else ()
            convs[block], stat = front(block, [full_in], *extra)
            stats.append(stat)
        stats = merge(everyones(stats[2], groups), len(groups))
        groups = [
            [member(f, p + i) for p in range(0, ctx_count, near_by)]
            for f in range(fsdp_count)
            for i in range(near_by)
        ]
        stats = [everyones(stats, groups)]
    result = back(place, stats, bn_gain[None], bn_shift[None], convs, out_weights)
    return result[None]


def solution(mesh):
    return jax.shard_map(
        body,
        mesh=mesh,
        in_specs=(
            P("fsdp", "ctx", None),
            P("fsdp"),
            P(),
            P("fsdp", None),
            P(),
            P(),
            P(),
            P("fsdp", None),
        ),
        out_specs=P("fsdp", "ctx", None),
        check_vma=False,
    )
```

```python
import functools

import jax
import jax.numpy as jnp
from jax import lax
from jax.experimental import pallas as pl
from jax.experimental.pallas import tpu as pltpu
from jax.sharding import PartitionSpec as P

HALO = 16
LANES = 128
MIB = 1024 * 1024
VMEM = pltpu.VMEM
ORDER = (2, 0, 1)
SHARED = {2: 3, 0: 4}


def cost(flops):
    return pl.CostEstimate(flops=flops, bytes_accessed=0, transcendentals=0)


def params(mib):
    return pltpu.CompilerParams(vmem_limit_bytes=mib * MIB)


def swap(value, axis, bit):
    return lax.ppermute(value, axis, [(i, i ^ bit) for i in range(lax.axis_size(axis))])


def cut_kernel(place_ref, shard_ref, two_ref, zero_ref, one_ref):
    wide = two_ref.shape[1]
    channels = shard_ref.shape[1] // 2
    for block, ref in ((2, two_ref), (0, zero_ref)):
        at = pl.multiple_of(place_ref[SHARED[block]] * channels + block * wide, wide)
        ref[...] = shard_ref[:, pl.ds(at, wide)]
    for i in range(2):
        at = i * channels + wide
        one_ref[:, i * wide : (i + 1) * wide] = shard_ref[:, at : at + wide]


def cut(place, shard, wide):
    depth = shard.shape[0]
    shapes = [(depth, wide), (depth, wide), (depth, 2 * wide)]
    return pl.pallas_call(
        cut_kernel,
        out_shape=[jax.ShapeDtypeStruct(shape, jnp.bfloat16) for shape in shapes],
        in_specs=[pl.BlockSpec(memory_space=pltpu.SMEM), pl.BlockSpec(memory_space=VMEM)],
        out_specs=[pl.BlockSpec(memory_space=VMEM)] * 3,
        compiler_params=params(4),
        cost_estimate=cost(10**8),
        name="cut",
    )(place, shard)


def normalize(values, gain):
    values = values.astype(jnp.float32)
    centre = jnp.mean(values, axis=-1, keepdims=True)
    deviate = values - centre
    spread = jnp.mean(deviate * deviate, axis=-1, keepdims=True)
    return (deviate * lax.rsqrt(spread + 1e-05) * gain).astype(jnp.bfloat16)


def edge_kernel(place_ref, rows_ref, inner_ref, outer_ref):
    odd = place_ref[3]
    last = rows_ref.shape[0] - HALO
    inner_ref[...] = rows_ref[pl.ds(pl.multiple_of((1 - odd) * last, HALO), HALO), :]
    outer_ref[...] = rows_ref[pl.ds(pl.multiple_of(odd * last, HALO), HALO), :]


def edge_rows(place, rows):
    shape = jax.ShapeDtypeStruct((HALO, rows.shape[1]), rows.dtype)
    return pl.pallas_call(
        edge_kernel,
        out_shape=[shape, shape],
        in_specs=[pl.BlockSpec(memory_space=pltpu.SMEM), pl.BlockSpec(memory_space=VMEM)],
        out_specs=[pl.BlockSpec(memory_space=VMEM)] * 2,
        compiler_params=params(2),
        cost_estimate=cost(10**8),
        name="edges",
    )(place, rows)


def norm_kernel(rows_ref, gain_ref, shard_ref, out_ref, *piece_refs):
    step = 64

    @pl.loop(0, rows_ref.shape[0] // step)
    def _(i):
        here = pl.ds(pl.multiple_of(i * step, step), step)
        out_ref[here, :] = normalize(rows_ref[here, :], gain_ref[...])

    at = 0
    for ref in piece_refs:
        ref[...] = shard_ref[at : at + ref.shape[0], :]
        at += ref.shape[0]


def normalize_rows(rows, gain, shard, pieces):
    row_count, width = rows.shape
    shapes = [(row_count, width)] + [(piece, width) for piece in pieces]
    return pl.pallas_call(
        norm_kernel,
        out_shape=[jax.ShapeDtypeStruct(shape, jnp.bfloat16) for shape in shapes],
        in_specs=[pl.BlockSpec(memory_space=VMEM)] * 3,
        out_specs=[pl.BlockSpec(memory_space=VMEM)] * len(shapes),
        compiler_params=params(4),
        cost_estimate=cost(10**8),
        name="layer_norm",
    )(rows, gain, shard)


def near_kernel(place_ref, rows_ref, inner_ref, outer_ref, gain_ref, *refs):
    row_count = rows_ref.shape[0]
    gain = gain_ref[...]
    *weight_refs, ext_ref = refs[:3] if len(refs) > 1 else refs
    odd = place_ref[3]
    at = pl.multiple_of((1 - odd) * (HALO + row_count), HALO)
    ext_ref[pl.ds(at, HALO), :] = normalize(inner_ref[...], gain)
    at = pl.multiple_of(odd * (HALO + row_count), HALO)
    ext_ref[pl.ds(at, HALO), :] = normalize(outer_ref[...], gain)
    ext_ref[HALO : HALO + row_count, :] = rows_ref[...]
    if not weight_refs:
        return
    *out_refs, weights = refs[3:]
    own = place_ref[0]
    depth, width = weight_refs[0].shape
    for i, weight_ref in enumerate(weight_refs):
        at = pl.multiple_of(lax.bitwise_xor(own % 2, i) * depth, depth)
        weights[pl.ds(at, depth), :] = weight_ref[...]
    near = pl.ds(pl.multiple_of(own // 2 * (2 * depth), 2 * depth), 2 * depth)
    wide = out_refs[0].shape[1] // 2
    channels = width // 2
    for block, out_ref in enumerate(out_refs):
        for i in range(2):
            columns = slice(i * channels + block * wide, i * channels + (block + 1) * wide)
            out_ref[:, i * wide : (i + 1) * wide] = jnp.dot(
                ext_ref[:, near], weights[:, columns], preferred_element_type=jnp.float32
            )


def near_product(place, rows, inner, outer, gain, *shards):
    row_count, width = rows.shape
    ext_rows = row_count + 2 * HALO
    shapes = [jax.ShapeDtypeStruct((ext_rows, width), jnp.bfloat16)]
    scratch = []
    if shards:
        shapes += [jax.ShapeDtypeStruct((ext_rows, width // 3), jnp.float32)] * 3
        scratch.append(VMEM((2 * shards[0].shape[0], width), jnp.bfloat16))
    return pl.pallas_call(
        near_kernel,
        out_shape=shapes,
        in_specs=[pl.BlockSpec(memory_space=pltpu.SMEM)]
        + [pl.BlockSpec(memory_space=VMEM)] * (4 + len(shards)),
        out_specs=[pl.BlockSpec(memory_space=VMEM)] * len(shapes),
        scratch_shapes=scratch,
        compiler_params=params(8),
        cost_estimate=cost(10**8),
        name="near",
    )(place, rows, inner, outer, gain, *shards)


def front_kernel(block, earlier, place_ref, normed_ref, *refs):
    refs, earlier_refs = refs[earlier:], refs[:earlier]
    *weight_refs, taps_ref, conv_ref, stats_ref, weights, gated = refs
    ext_rows = normed_ref.shape[0]
    row_count, wide = conv_ref.shape
    taps, channels = taps_ref.shape
    if len(weight_refs) > 1:
        near_ref, *far_refs = weight_refs
        own = place_ref[0]
        depth = far_refs[0].shape[0]
        halves = len(far_refs) // 2
        for i in range(2):
            at = pl.multiple_of(lax.bitwise_xor(own % 2, i) * depth, depth)
            if halves == 1:
                weights[pl.ds(at, depth), :] = far_refs[i][...]
                continue
            for j in range(2):
                column = pl.multiple_of(lax.bitwise_xor(place_ref[SHARED[block]], j) * wide, wide)
                weights[pl.ds(at, depth), pl.ds(column, wide)] = far_refs[2 * i + j][...]
        far = pl.ds(pl.multiple_of((1 - own // 2) * (2 * depth), 2 * depth), 2 * depth)
        normed = normed_ref[:, far]
        value = near_ref[:, 0:wide] + jnp.dot(normed, weights[:, 0:wide], preferred_element_type=jnp.float32)
        gate = near_ref[:, wide:] + jnp.dot(normed, weights[:, wide:], preferred_element_type=jnp.float32)
    else:
        columns = slice(block * wide, (block + 1) * wide)
        value = jnp.dot(normed_ref[...], weight_refs[0][:, columns], preferred_element_type=jnp.float32)
        columns = slice(channels + block * wide, channels + (block + 1) * wide)
        gate = jnp.dot(normed_ref[...], weight_refs[0][:, columns], preferred_element_type=jnp.float32)
    start, length = place_ref[1], place_ref[2]
    position = start - HALO + lax.broadcasted_iota(jnp.int32, (ext_rows, 1), 0)
    valid = (position >= 0) & (position < length)
    kept = jnp.where(valid, value * jax.nn.sigmoid(gate), 0.0)
    kept = kept.astype(jnp.bfloat16).astype(jnp.float32)
    first = HALO - (taps - 1) // 2
    step = 64
    for unit in range(wide // LANES):
        lanes = slice(unit * LANES, (unit + 1) * LANES)
        tap_lanes = slice(block * wide + unit * LANES, block * wide + (unit + 1) * LANES)
        column = kept[:, lanes]
        gated[0] = column
        for phase in range(1, 8):
            gated[phase] = pltpu.roll(column, ext_rows - phase, 0)
        for at in range(0, row_count, step):
            acc = None
            for tap in range(taps):
                base = at + (first + tap) // 8 * 8
                term = gated[(first + tap) % 8, base : base + step, :] * taps_ref[tap : tap + 1, tap_lanes]
                acc = term if acc is None else acc + term
            conv_ref[at : at + step, lanes] = acc
    here = start + lax.broadcasted_iota(jnp.int32, (row_count, 1), 0) < length
    count = jnp.clip(length - start, 0, row_count).astype(jnp.float32)
    conv = conv_ref[...]
    mean = jnp.sum(jnp.where(here, conv, 0.0), axis=0, keepdims=True) / jnp.maximum(count, 1.0)
    deviate = jnp.where(here, conv - mean, 0.0)
    square = jnp.sum(deviate * deviate, axis=0, keepdims=True)
    stats = [mean, square, jnp.full((1, wide), count)]
    if not earlier_refs:
        for i, row in enumerate(stats):
            stats_ref[i : i + 1, :] = row
        return
    for i, row in enumerate(stats):
        for copy in range(stats_ref.shape[0]):
            stats_ref[copy, i : i + 1, block * wide : (block + 1) * wide] = row
            for other, ref in zip([j for j in ORDER if j != block], earlier_refs):
                stats_ref[copy, i : i + 1, other * wide : (other + 1) * wide] = ref[i : i + 1, :]


def front_block(block, wide, place, normed, weights, dw_kernel, earlier=(), copies=1):
    ext_rows, width = normed.shape
    row_count = ext_rows - 2 * HALO
    depth = 2 * weights[1].shape[0] if len(weights) > 1 else 16
    stats_shape = (copies, 3, dw_kernel.shape[1]) if earlier else (3, wide)
    return pl.pallas_call(
        functools.partial(front_kernel, block, len(earlier)),
        out_shape=(
            jax.ShapeDtypeStruct((row_count, wide), jnp.float32),
            jax.ShapeDtypeStruct(stats_shape, jnp.float32),
        ),
        in_specs=[pl.BlockSpec(memory_space=pltpu.SMEM)]
        + [pl.BlockSpec(memory_space=VMEM)] * (2 + len(weights) + len(earlier)),
        out_specs=[pl.BlockSpec(memory_space=VMEM)] * 2,
        scratch_shapes=[
            VMEM((depth, 2 * wide), jnp.bfloat16),
            VMEM((8, ext_rows, LANES), jnp.float32),
        ],
        compiler_params=params(10),
        cost_estimate=cost(4 * 10**9 if block == ORDER[1] else 10**8),
        name="front",
    )(place, normed, *earlier, *weights, dw_kernel)


def merged(parts):
    means, squares, counts = zip(*parts)
    count = sum(counts)
    mean = sum(n * m for n, m in zip(counts, means)) / jnp.maximum(count, 1.0)
    square = sum(squares) + sum(n * (m - mean) * (m - mean) for n, m in zip(counts, means))
    return mean, square, count


def rows_of(refs):
    return [[ref[copy, i : i + 1, :] for i in range(3)] for ref in refs for copy in range(ref.shape[0])]


def merge_kernel(stats_ref, out_ref):
    for i, row in enumerate(merged(rows_of([stats_ref]))):
        for copy in range(out_ref.shape[0]):
            out_ref[copy, i : i + 1, :] = row


def merge(stats, copies):
    return pl.pallas_call(
        merge_kernel,
        out_shape=jax.ShapeDtypeStruct((copies,) + stats.shape[1:], jnp.float32),
        in_specs=[pl.BlockSpec(memory_space=VMEM)],
        out_specs=pl.BlockSpec(memory_space=VMEM),
        compiler_params=params(8),
        cost_estimate=cost(10**8),
        name="merge",
    )(stats)


def back_kernel(stat_count, place_ref, gain_ref, shift_ref, *refs):
    stat_refs, refs = refs[:stat_count], refs[stat_count:]
    *conv_refs, out_ref, rows_out, sems, weights = refs
    convs, weight_refs = conv_refs[:3], conv_refs[3:]
    row_count, wide = convs[0].shape
    if len(weight_refs) > 1:
        depth = weight_refs[0].shape[0]
        for i, weight_ref in enumerate(weight_refs[:2]):
            at = pl.multiple_of(lax.bitwise_xor(place_ref[0], i) * depth, depth)
            weights[pl.ds(at, depth), :] = weight_ref[...]
        at, unit = 0, 16
        for weight_ref in weight_refs[2:]:
            rows = weight_ref.shape[0]
            start = lax.bitwise_xor(place_ref[0], 2 + at // depth) * depth + at % depth
            weights[pl.ds(pl.multiple_of(start, unit), rows), :] = weight_ref[...]
            at += rows
    else:
        weights[...] = weight_refs[0][...]
    mean, square, count = merged(rows_of(stat_refs))
    scale = lax.rsqrt(square / count + 1e-05) * gain_ref[...]
    shift = shift_ref[...]
    pieces, rows, columns = rows_out.shape
    across = out_ref.shape[1] // columns
    copies = []
    for piece in range(pieces // across):
        here = slice(piece * rows, (piece + 1) * rows)
        parts = []
        for i, conv_ref in enumerate(convs):
            lanes = slice(i * wide, (i + 1) * wide)
            scaled = (conv_ref[here, :] - mean[:, lanes]) * scale[:, lanes] + shift[:, lanes]
            parts.append((scaled * jax.nn.sigmoid(scaled)).astype(jnp.bfloat16))
        activated = jnp.concatenate(parts, axis=1)
        position = place_ref[1] + piece * rows + lax.broadcasted_iota(jnp.int32, (rows, 1), 0)
        for j in range(across):
            lanes = slice(j * columns, (j + 1) * columns)
            result = jnp.dot(activated, weights[:, lanes], preferred_element_type=jnp.float32)
            slot = piece * across + j
            rows_out[slot] = jnp.where(position < place_ref[2], result, 0.0).astype(jnp.bfloat16)
            copy = pltpu.make_async_copy(rows_out.at[slot], out_ref.at[here, lanes], sems.at[slot])
            copy.start()
            copies.append(copy)
    for copy in copies:
        copy.wait()


def back(place, stats, gain, shift, convs, weights):
    row_count = convs[0].shape[0]
    channels, width = gain.shape[1], weights[0].shape[1]
    pieces, across = 4, 2
    return pl.pallas_call(
        functools.partial(back_kernel, len(stats)),
        out_shape=jax.ShapeDtypeStruct((row_count, width), jnp.bfloat16),
        in_specs=[pl.BlockSpec(memory_space=pltpu.SMEM)]
        + [pl.BlockSpec(memory_space=VMEM)] * (2 + len(stats) + len(convs) + len(weights)),
        out_specs=pl.BlockSpec(memory_space=pl.ANY),
        scratch_shapes=[
            VMEM((pieces, row_count * across // pieces, width // across), jnp.bfloat16),
            pltpu.SemaphoreType.DMA((pieces,)),
            VMEM((channels, width), jnp.bfloat16),
        ],
        compiler_params=params(10),
        cost_estimate=cost(10**9),
        name="back",
    )(place, gain, shift, *stats, *convs, *weights)


def everyones(copies, groups):
    return lax.all_to_all(copies, ("fsdp", "ctx"), 0, 0, axis_index_groups=groups, tiled=True)


def tie(*values):
    return lax.optimization_barrier(values)


def body(frames, lengths, ln_gain, w_in, dw_kernel, bn_gain, bn_shift, w_out):
    _, row_count, model_width = frames.shape
    channels = dw_kernel.shape[1]
    wide = channels // 3
    ctx, fsdp = lax.axis_index("ctx"), lax.axis_index("fsdp")
    ctx_count, fsdp_count = lax.axis_size("ctx"), lax.axis_size("fsdp")
    direct = fsdp_count == 4 and ctx_count == 8
    rows = frames[0]
    gain = ln_gain[None]
    parity, pair = lax.rem(ctx, 2), lax.rem(ctx // 2, 2)
    place = jnp.stack([fsdp, ctx * row_count, lengths[0], parity, pair]).astype(jnp.int32)
    ends = ctx_count - 1
    down, up = [(i, i + 1) for i in range(ends)], [(i + 1, i) for i in range(ends)]
    both = ("fsdp", "ctx")
    member = lambda f, p: f * ctx_count + p

    def front(block, weights, *extra):
        return front_block(block, wide, place, normed, weights, dw_kernel, *extra)

    if direct:
        two, zero, one = cut(place, w_in, wide)
        two, zero, one = (swap(part, "fsdp", 2) for part in (two, zero, one))
        across = swap(w_in, "fsdp", 1)
        inner, outer = edge_rows(place, rows)
        part_rows = w_out.shape[0] // 12
        normed, *pieces = normalize_rows(rows, gain, w_out, [4 * part_rows, 8 * part_rows])
        inner = swap(inner, "ctx", 1)
        pairs = [(i, i + 1) for i in range(1, ends, 2)]
        outer = lax.ppermute(outer, "ctx", pairs + [(j, i) for i, j in pairs])
        normed, inner, outer, two, zero = tie(normed, inner, outer, two, zero)
        two, zero = [two, swap(two, "ctx", 1)], [zero, swap(zero, "ctx", 2)]
        normed, *partials = near_product(place, normed, inner, outer, gain, w_in, across)
        partials[2], two[0], zero[0] = tie(partials[2], two[0], zero[0])
        two.append(swap(two[0], "fsdp", 1))
        zero.append(swap(zero[0], "fsdp", 1))
        partials[2], *parts = tie(partials[2], *two, *zero, w_out)
        two, zero, w_out = parts[:3], parts[3:6], parts[6]
        two.append(swap(two[1], "fsdp", 1))
        zero.append(swap(zero[1], "fsdp", 1))
        partials[2], one = tie(partials[2], one)
        beyond_one = swap(one, "fsdp", 1)
        conv_two, stat_two = front(2, [partials[2], *two])
        conv_two, partials[0] = tie(conv_two, partials[0])
        pieces = [swap(piece, "fsdp", 2) for piece in pieces]
        conv_zero, stat_zero = front(0, [partials[0], *zero])
        conv_zero, partials[1] = tie(conv_zero, partials[1])
        conv_one, stats = front(1, [partials[1], one, beyond_one], (stat_two, stat_zero), 1)
        across_out = swap(w_out, "fsdp", 1)
        stats, pieces[0] = tie(stats, pieces[0])
        beyond = [swap(pieces[0], "fsdp", 1)]
        convs = [conv_zero, conv_one, conv_two]

        def others(flips):
            return [
                lax.ppermute(
                    stats,
                    both,
                    [(member(f, p), member(f ^ df, p ^ dp)) for f in range(4) for p in range(8)],
                )
                for df, dp in flips
            ]

        def union(parts):
            return jnp.stack(merged([[part[:, i] for i in range(3)] for part in parts]), 1)

        stats = union([stats] + others([(1, 0)]))
        stats, beyond[0] = tie(stats, beyond[0])
        stats = union([stats] + others([(0, 2)]))
        stats = union([stats] + others([(0, 4)]))
        stats = [stats] + others([(0, 1), (2, 0), (2, 1)])
        *stats, pieces[1] = tie(*stats, pieces[1])
        beyond.append(swap(pieces[1], "fsdp", 1))
        out_weights = [w_out, across_out, *pieces, *beyond]
    else:
        full_in = lax.all_gather(w_in, "fsdp", axis=0, tiled=True)
        out_weights = [lax.all_gather(w_out, "fsdp", axis=0, tiled=True)]
        before = lax.ppermute(rows[-HALO:], "ctx", down)
        after = lax.ppermute(rows[:HALO], "ctx", up)
        inner = jnp.where(parity == 0, after, before)
        outer = jnp.where(parity == 0, before, after)
        (normed,) = normalize_rows(rows, gain, w_out, ())
        (normed,) = near_product(place, normed, inner, outer, gain)
        near_by = 2 if ctx_count % 2 == 0 else 1
        groups = [
            [member(f, p + i) for f in range(fsdp_count) for i in range(near_by)]
            for p in range(0, ctx_count, near_by)
        ]
        convs, stats = [None] * 3, []
        for block in ORDER:
            extra = (stats, len(groups[0])) if block == ORDER[-1] else ()
            convs[block], stat = front(block, [full_in], *extra)
            stats.append(stat)
        stats = merge(everyones(stats[2], groups), len(groups))
        groups = [
            [member(f, p + i) for p in range(0, ctx_count, near_by)]
            for f in range(fsdp_count)
            for i in range(near_by)
        ]
        stats = [everyones(stats, groups)]
    result = back(place, stats, bn_gain[None], bn_shift[None], convs, out_weights)
    return result[None]


def solution(mesh):
    return jax.shard_map(
        body,
        mesh=mesh,
        in_specs=(
            P("fsdp", "ctx", None),
            P("fsdp"),
            P(),
            P("fsdp", None),
            P(),
            P(),
            P(),
            P("fsdp", None),
        ),
        out_specs=P("fsdp", "ctx", None),
        check_vma=False,
    )
```

```python
import functools

import jax
import jax.numpy as jnp
from jax import lax
from jax.experimental import pallas as pl
from jax.experimental.pallas import tpu as pltpu
from jax.sharding import PartitionSpec as P

HALO = 16
LANES = 128
MIB = 1024 * 1024
VMEM = pltpu.VMEM
ORDER = (2, 0, 1)
SHARED = {2: 3, 0: 4}


def cost(flops):
    return pl.CostEstimate(flops=flops, bytes_accessed=0, transcendentals=0)


def params(mib):
    return pltpu.CompilerParams(vmem_limit_bytes=mib * MIB)


def swap(value, axis, bit):
    return lax.ppermute(value, axis, [(i, i ^ bit) for i in range(lax.axis_size(axis))])


def cut_kernel(place_ref, shard_ref, two_ref, zero_ref, one_ref):
    wide = two_ref.shape[1]
    channels = shard_ref.shape[1] // 2
    for block, ref in ((2, two_ref), (0, zero_ref)):
        at = pl.multiple_of(place_ref[SHARED[block]] * channels + block * wide, wide)
        ref[...] = shard_ref[:, pl.ds(at, wide)]
    for i in range(2):
        at = i * channels + wide
        one_ref[:, i * wide : (i + 1) * wide] = shard_ref[:, at : at + wide]


def cut(place, shard, wide):
    depth = shard.shape[0]
    shapes = [(depth, wide), (depth, wide), (depth, 2 * wide)]
    return pl.pallas_call(
        cut_kernel,
        out_shape=[jax.ShapeDtypeStruct(shape, jnp.bfloat16) for shape in shapes],
        in_specs=[pl.BlockSpec(memory_space=pltpu.SMEM), pl.BlockSpec(memory_space=VMEM)],
        out_specs=[pl.BlockSpec(memory_space=VMEM)] * 3,
        compiler_params=params(4),
        cost_estimate=cost(10**8),
        name="cut",
    )(place, shard)


def normalize(values, gain):
    values = values.astype(jnp.float32)
    centre = jnp.mean(values, axis=-1, keepdims=True)
    deviate = values - centre
    spread = jnp.mean(deviate * deviate, axis=-1, keepdims=True)
    return (deviate * lax.rsqrt(spread + 1e-05) * gain).astype(jnp.bfloat16)


def edge_kernel(place_ref, rows_ref, inner_ref, outer_ref):
    odd = place_ref[3]
    last = rows_ref.shape[0] - HALO
    inner_ref[...] = rows_ref[pl.ds(pl.multiple_of((1 - odd) * last, HALO), HALO), :]
    outer_ref[...] = rows_ref[pl.ds(pl.multiple_of(odd * last, HALO), HALO), :]


def edge_rows(place, rows):
    shape = jax.ShapeDtypeStruct((HALO, rows.shape[1]), rows.dtype)
    return pl.pallas_call(
        edge_kernel,
        out_shape=[shape, shape],
        in_specs=[pl.BlockSpec(memory_space=pltpu.SMEM), pl.BlockSpec(memory_space=VMEM)],
        out_specs=[pl.BlockSpec(memory_space=VMEM)] * 2,
        compiler_params=params(2),
        cost_estimate=cost(10**8),
        name="edges",
    )(place, rows)


def norm_kernel(rows_ref, gain_ref, shard_ref, out_ref, *piece_refs):
    step = 64

    @pl.loop(0, rows_ref.shape[0] // step)
    def _(i):
        here = pl.ds(pl.multiple_of(i * step, step), step)
        out_ref[here, :] = normalize(rows_ref[here, :], gain_ref[...])

    at = 0
    for ref in piece_refs:
        ref[...] = shard_ref[at : at + ref.shape[0], :]
        at += ref.shape[0]


def normalize_rows(rows, gain, shard, pieces):
    row_count, width = rows.shape
    shapes = [(row_count, width)] + [(piece, width) for piece in pieces]
    return pl.pallas_call(
        norm_kernel,
        out_shape=[jax.ShapeDtypeStruct(shape, jnp.bfloat16) for shape in shapes],
        in_specs=[pl.BlockSpec(memory_space=VMEM)] * 3,
        out_specs=[pl.BlockSpec(memory_space=VMEM)] * len(shapes),
        compiler_params=params(4),
        cost_estimate=cost(10**8),
        name="layer_norm",
    )(rows, gain, shard)


def near_kernel(place_ref, rows_ref, inner_ref, outer_ref, gain_ref, *refs):
    row_count = rows_ref.shape[0]
    gain = gain_ref[...]
    *weight_refs, ext_ref = refs[:3] if len(refs) > 1 else refs
    odd = place_ref[3]
    at = pl.multiple_of((1 - odd) * (HALO + row_count), HALO)
    ext_ref[pl.ds(at, HALO), :] = normalize(inner_ref[...], gain)
    at = pl.multiple_of(odd * (HALO + row_count), HALO)
    ext_ref[pl.ds(at, HALO), :] = normalize(outer_ref[...], gain)
    ext_ref[HALO : HALO + row_count, :] = rows_ref[...]
    if not weight_refs:
        return
    *out_refs, weights = refs[3:]
    own = place_ref[0]
    depth, width = weight_refs[0].shape
    for i, weight_ref in enumerate(weight_refs):
        at = pl.multiple_of(lax.bitwise_xor(own % 2, i) * depth, depth)
        weights[pl.ds(at, depth), :] = weight_ref[...]
    near = pl.ds(pl.multiple_of(own // 2 * (2 * depth), 2 * depth), 2 * depth)
    wide = out_refs[0].shape[1] // 2
    channels = width // 2
    for block, out_ref in enumerate(out_refs):
        for i in range(2):
            columns = slice(i * channels + block * wide, i * channels + (block + 1) * wide)
            out_ref[:, i * wide : (i + 1) * wide] = jnp.dot(
                ext_ref[:, near], weights[:, columns], preferred_element_type=jnp.float32
            )


def near_product(place, rows, inner, outer, gain, *shards):
    row_count, width = rows.shape
    ext_rows = row_count + 2 * HALO
    shapes = [jax.ShapeDtypeStruct((ext_rows, width), jnp.bfloat16)]
    scratch = []
    if shards:
        shapes += [jax.ShapeDtypeStruct((ext_rows, width // 3), jnp.float32)] * 3
        scratch.append(VMEM((2 * shards[0].shape[0], width), jnp.bfloat16))
    return pl.pallas_call(
        near_kernel,
        out_shape=shapes,
        in_specs=[pl.BlockSpec(memory_space=pltpu.SMEM)]
        + [pl.BlockSpec(memory_space=VMEM)] * (4 + len(shards)),
        out_specs=[pl.BlockSpec(memory_space=VMEM)] * len(shapes),
        scratch_shapes=scratch,
        compiler_params=params(8),
        cost_estimate=cost(10**8),
        name="near",
    )(place, rows, inner, outer, gain, *shards)


def front_kernel(block, earlier, place_ref, normed_ref, *refs):
    refs, earlier_refs = refs[earlier:], refs[:earlier]
    *weight_refs, taps_ref, conv_ref, stats_ref, weights, gated = refs
    ext_rows = normed_ref.shape[0]
    row_count, wide = conv_ref.shape
    taps, channels = taps_ref.shape
    if len(weight_refs) > 1:
        near_ref, *far_refs = weight_refs
        own = place_ref[0]
        depth = far_refs[0].shape[0]
        halves = len(far_refs) // 2
        for i in range(2):
            at = pl.multiple_of(lax.bitwise_xor(own % 2, i) * depth, depth)
            if halves == 1:
                weights[pl.ds(at, depth), :] = far_refs[i][...]
                continue
            for j in range(2):
                column = pl.multiple_of(lax.bitwise_xor(place_ref[SHARED[block]], j) * wide, wide)
                weights[pl.ds(at, depth), pl.ds(column, wide)] = far_refs[2 * i + j][...]
        far = pl.ds(pl.multiple_of((1 - own // 2) * (2 * depth), 2 * depth), 2 * depth)
        normed = normed_ref[:, far]
        value = near_ref[:, 0:wide] + jnp.dot(normed, weights[:, 0:wide], preferred_element_type=jnp.float32)
        gate = near_ref[:, wide:] + jnp.dot(normed, weights[:, wide:], preferred_element_type=jnp.float32)
    else:
        columns = slice(block * wide, (block + 1) * wide)
        value = jnp.dot(normed_ref[...], weight_refs[0][:, columns], preferred_element_type=jnp.float32)
        columns = slice(channels + block * wide, channels + (block + 1) * wide)
        gate = jnp.dot(normed_ref[...], weight_refs[0][:, columns], preferred_element_type=jnp.float32)
    start, length = place_ref[1], place_ref[2]
    position = start - HALO + lax.broadcasted_iota(jnp.int32, (ext_rows, 1), 0)
    valid = (position >= 0) & (position < length)
    kept = jnp.where(valid, value * jax.nn.sigmoid(gate), 0.0)
    kept = kept.astype(jnp.bfloat16).astype(jnp.float32)
    first = HALO - (taps - 1) // 2
    step = 64
    for unit in range(wide // LANES):
        lanes = slice(unit * LANES, (unit + 1) * LANES)
        tap_lanes = slice(block * wide + unit * LANES, block * wide + (unit + 1) * LANES)
        column = kept[:, lanes]
        gated[0] = column
        for phase in range(1, 8):
            gated[phase] = pltpu.roll(column, ext_rows - phase, 0)
        for at in range(0, row_count, step):
            acc = None
            for tap in range(taps):
                base = at + (first + tap) // 8 * 8
                term = gated[(first + tap) % 8, base : base + step, :] * taps_ref[tap : tap + 1, tap_lanes]
                acc = term if acc is None else acc + term
            conv_ref[at : at + step, lanes] = acc
    here = start + lax.broadcasted_iota(jnp.int32, (row_count, 1), 0) < length
    count = jnp.clip(length - start, 0, row_count).astype(jnp.float32)
    conv = conv_ref[...]
    mean = jnp.sum(jnp.where(here, conv, 0.0), axis=0, keepdims=True) / jnp.maximum(count, 1.0)
    deviate = jnp.where(here, conv - mean, 0.0)
    square = jnp.sum(deviate * deviate, axis=0, keepdims=True)
    stats = [mean, square, jnp.full((1, wide), count)]
    if not earlier_refs:
        for i, row in enumerate(stats):
            stats_ref[i : i + 1, :] = row
        return
    for i, row in enumerate(stats):
        for copy in range(stats_ref.shape[0]):
            stats_ref[copy, i : i + 1, block * wide : (block + 1) * wide] = row
            for other, ref in zip([j for j in ORDER if j != block], earlier_refs):
                stats_ref[copy, i : i + 1, other * wide : (other + 1) * wide] = ref[i : i + 1, :]


def front_block(block, wide, place, normed, weights, dw_kernel, earlier=(), copies=1):
    ext_rows, width = normed.shape
    row_count = ext_rows - 2 * HALO
    depth = 2 * weights[1].shape[0] if len(weights) > 1 else 16
    stats_shape = (copies, 3, dw_kernel.shape[1]) if earlier else (3, wide)
    return pl.pallas_call(
        functools.partial(front_kernel, block, len(earlier)),
        out_shape=(
            jax.ShapeDtypeStruct((row_count, wide), jnp.float32),
            jax.ShapeDtypeStruct(stats_shape, jnp.float32),
        ),
        in_specs=[pl.BlockSpec(memory_space=pltpu.SMEM)]
        + [pl.BlockSpec(memory_space=VMEM)] * (2 + len(weights) + len(earlier)),
        out_specs=[pl.BlockSpec(memory_space=VMEM)] * 2,
        scratch_shapes=[
            VMEM((depth, 2 * wide), jnp.bfloat16),
            VMEM((8, ext_rows, LANES), jnp.float32),
        ],
        compiler_params=params(10),
        cost_estimate=cost(4 * 10**9 if block == ORDER[1] else 10**8),
        name="front",
    )(place, normed, *earlier, *weights, dw_kernel)


def merged(parts):
    means, squares, counts = zip(*parts)
    count = sum(counts)
    mean = sum(n * m for n, m in zip(counts, means)) / jnp.maximum(count, 1.0)
    square = sum(squares) + sum(n * (m - mean) * (m - mean) for n, m in zip(counts, means))
    return mean, square, count


def rows_of(refs):
    return [[ref[copy, i : i + 1, :] for i in range(3)] for ref in refs for copy in range(ref.shape[0])]


def merge_kernel(stats_ref, out_ref):
    for i, row in enumerate(merged(rows_of([stats_ref]))):
        for copy in range(out_ref.shape[0]):
            out_ref[copy, i : i + 1, :] = row


def merge(stats, copies):
    return pl.pallas_call(
        merge_kernel,
        out_shape=jax.ShapeDtypeStruct((copies,) + stats.shape[1:], jnp.float32),
        in_specs=[pl.BlockSpec(memory_space=VMEM)],
        out_specs=pl.BlockSpec(memory_space=VMEM),
        compiler_params=params(8),
        cost_estimate=cost(10**8),
        name="merge",
    )(stats)


def back_kernel(stat_count, place_ref, gain_ref, shift_ref, *refs):
    stat_refs, refs = refs[:stat_count], refs[stat_count:]
    *conv_refs, out_ref, rows_out, sems, weights = refs
    convs, weight_refs = conv_refs[:3], conv_refs[3:]
    row_count, wide = convs[0].shape
    if len(weight_refs) > 1:
        depth = weight_refs[0].shape[0]
        for i, weight_ref in enumerate(weight_refs[:2]):
            at = pl.multiple_of(lax.bitwise_xor(place_ref[0], i) * depth, depth)
            weights[pl.ds(at, depth), :] = weight_ref[...]
        at, unit = 0, 16
        for weight_ref in weight_refs[2:]:
            rows = weight_ref.shape[0]
            start = lax.bitwise_xor(place_ref[0], 2 + at // depth) * depth + at % depth
            weights[pl.ds(pl.multiple_of(start, unit), rows), :] = weight_ref[...]
            at += rows
    else:
        weights[...] = weight_refs[0][...]
    mean, square, count = merged(rows_of(stat_refs))
    scale = lax.rsqrt(square / count + 1e-05) * gain_ref[...]
    shift = shift_ref[...]
    pieces, rows, columns = rows_out.shape
    across = out_ref.shape[1] // columns
    copies = []
    for piece in range(pieces // across):
        here = slice(piece * rows, (piece + 1) * rows)
        parts = []
        for i, conv_ref in enumerate(convs):
            lanes = slice(i * wide, (i + 1) * wide)
            scaled = (conv_ref[here, :] - mean[:, lanes]) * scale[:, lanes] + shift[:, lanes]
            parts.append((scaled * jax.nn.sigmoid(scaled)).astype(jnp.bfloat16))
        activated = jnp.concatenate(parts, axis=1)
        position = place_ref[1] + piece * rows + lax.broadcasted_iota(jnp.int32, (rows, 1), 0)
        for j in range(across):
            lanes = slice(j * columns, (j + 1) * columns)
            result = jnp.dot(activated, weights[:, lanes], preferred_element_type=jnp.float32)
            slot = piece * across + j
            rows_out[slot] = jnp.where(position < place_ref[2], result, 0.0).astype(jnp.bfloat16)
            copy = pltpu.make_async_copy(rows_out.at[slot], out_ref.at[here, lanes], sems.at[slot])
            copy.start()
            copies.append(copy)
    for copy in copies:
        copy.wait()


def back(place, stats, gain, shift, convs, weights):
    row_count = convs[0].shape[0]
    channels, width = gain.shape[1], weights[0].shape[1]
    pieces, across = 6, 3
    return pl.pallas_call(
        functools.partial(back_kernel, len(stats)),
        out_shape=jax.ShapeDtypeStruct((row_count, width), jnp.bfloat16),
        in_specs=[pl.BlockSpec(memory_space=pltpu.SMEM)]
        + [pl.BlockSpec(memory_space=VMEM)] * (2 + len(stats) + len(convs) + len(weights)),
        out_specs=pl.BlockSpec(memory_space=pl.ANY),
        scratch_shapes=[
            VMEM((pieces, row_count * across // pieces, width // across), jnp.bfloat16),
            pltpu.SemaphoreType.DMA((pieces,)),
            VMEM((channels, width), jnp.bfloat16),
        ],
        compiler_params=params(10),
        cost_estimate=cost(10**9),
        name="back",
    )(place, gain, shift, *stats, *convs, *weights)


def everyones(copies, groups):
    return lax.all_to_all(copies, ("fsdp", "ctx"), 0, 0, axis_index_groups=groups, tiled=True)


def tie(*values):
    return lax.optimization_barrier(values)


def body(frames, lengths, ln_gain, w_in, dw_kernel, bn_gain, bn_shift, w_out):
    _, row_count, model_width = frames.shape
    channels = dw_kernel.shape[1]
    wide = channels // 3
    ctx, fsdp = lax.axis_index("ctx"), lax.axis_index("fsdp")
    ctx_count, fsdp_count = lax.axis_size("ctx"), lax.axis_size("fsdp")
    direct = fsdp_count == 4 and ctx_count == 8
    rows = frames[0]
    gain = ln_gain[None]
    parity, pair = lax.rem(ctx, 2), lax.rem(ctx // 2, 2)
    place = jnp.stack([fsdp, ctx * row_count, lengths[0], parity, pair]).astype(jnp.int32)
    ends = ctx_count - 1
    down, up = [(i, i + 1) for i in range(ends)], [(i + 1, i) for i in range(ends)]
    both = ("fsdp", "ctx")
    member = lambda f, p: f * ctx_count + p

    def front(block, weights, *extra):
        return front_block(block, wide, place, normed, weights, dw_kernel, *extra)

    if direct:
        two, zero, one = cut(place, w_in, wide)
        two, zero, one = (swap(part, "fsdp", 2) for part in (two, zero, one))
        across = swap(w_in, "fsdp", 1)
        inner, outer = edge_rows(place, rows)
        part_rows = w_out.shape[0] // 12
        normed, *pieces = normalize_rows(rows, gain, w_out, [4 * part_rows, 8 * part_rows])
        inner = swap(inner, "ctx", 1)
        pairs = [(i, i + 1) for i in range(1, ends, 2)]
        outer = lax.ppermute(outer, "ctx", pairs + [(j, i) for i, j in pairs])
        normed, inner, outer, two, zero = tie(normed, inner, outer, two, zero)
        two, zero = [two, swap(two, "ctx", 1)], [zero, swap(zero, "ctx", 2)]
        normed, *partials = near_product(place, normed, inner, outer, gain, w_in, across)
        partials[2], two[0], zero[0] = tie(partials[2], two[0], zero[0])
        two.append(swap(two[0], "fsdp", 1))
        zero.append(swap(zero[0], "fsdp", 1))
        partials[2], *parts = tie(partials[2], *two, *zero, w_out)
        two, zero, w_out = parts[:3], parts[3:6], parts[6]
        two.append(swap(two[1], "fsdp", 1))
        zero.append(swap(zero[1], "fsdp", 1))
        partials[2], one = tie(partials[2], one)
        beyond_one = swap(one, "fsdp", 1)
        conv_two, stat_two = front(2, [partials[2], *two])
        conv_two, partials[0] = tie(conv_two, partials[0])
        pieces = [swap(piece, "fsdp", 2) for piece in pieces]
        conv_zero, stat_zero = front(0, [partials[0], *zero])
        conv_zero, partials[1] = tie(conv_zero, partials[1])
        conv_one, stats = front(1, [partials[1], one, beyond_one], (stat_two, stat_zero), 1)
        across_out = swap(w_out, "fsdp", 1)
        stats, pieces[0] = tie(stats, pieces[0])
        beyond = [swap(pieces[0], "fsdp", 1)]
        convs = [conv_zero, conv_one, conv_two]

        def others(flips):
            return [
                lax.ppermute(
                    stats,
                    both,
                    [(member(f, p), member(f ^ df, p ^ dp)) for f in range(4) for p in range(8)],
                )
                for df, dp in flips
            ]

        def union(parts):
            return jnp.stack(merged([[part[:, i] for i in range(3)] for part in parts]), 1)

        stats = union([stats] + others([(1, 0)]))
        stats = union([stats] + others([(0, 2)]))
        stats = union([stats] + others([(0, 4)]))
        stats = [stats] + others([(0, 1), (2, 0), (2, 1)])
        *stats, pieces[1] = tie(*stats, pieces[1])
        beyond.append(swap(pieces[1], "fsdp", 1))
        out_weights = [w_out, across_out, *pieces, *beyond]
    else:
        full_in = lax.all_gather(w_in, "fsdp", axis=0, tiled=True)
        out_weights = [lax.all_gather(w_out, "fsdp", axis=0, tiled=True)]
        before = lax.ppermute(rows[-HALO:], "ctx", down)
        after = lax.ppermute(rows[:HALO], "ctx", up)
        inner = jnp.where(parity == 0, after, before)
        outer = jnp.where(parity == 0, before, after)
        (normed,) = normalize_rows(rows, gain, w_out, ())
        (normed,) = near_product(place, normed, inner, outer, gain)
        near_by = 2 if ctx_count % 2 == 0 else 1
        groups = [
            [member(f, p + i) for f in range(fsdp_count) for i in range(near_by)]
            for p in range(0, ctx_count, near_by)
        ]
        convs, stats = [None] * 3, []
        for block in ORDER:
            extra = (stats, len(groups[0])) if block == ORDER[-1] else ()
            convs[block], stat = front(block, [full_in], *extra)
            stats.append(stat)
        stats = merge(everyones(stats[2], groups), len(groups))
        groups = [
            [member(f, p + i) for p in range(0, ctx_count, near_by)]
            for f in range(fsdp_count)
            for i in range(near_by)
        ]
        stats = [everyones(stats, groups)]
    result = back(place, stats, bn_gain[None], bn_shift[None], convs, out_weights)
    return result[None]


def solution(mesh):
    return jax.shard_map(
        body,
        mesh=mesh,
        in_specs=(
            P("fsdp", "ctx", None),
            P("fsdp"),
            P(),
            P("fsdp", None),
            P(),
            P(),
            P(),
            P("fsdp", None),
        ),
        out_specs=P("fsdp", "ctx", None),
        check_vma=False,
    )
```
